32 devices in a mesh: seq: 4 (over z), fsdp: 8 (over y, x, core).
Axes of the slice: x: 2, y: 2, z: 4, core: 2. Of those that a mesh axis runs over, the one named last changes fastest.
Arguments:
- inputs: bfloat16 [16, 1024, 1024], P('fsdp', 'seq'), may hold values from -6 to 6
- lengths: int32 [16], P('fsdp'), may hold values from 512 to 1024, as said below
- ffn_in: bfloat16 [2, 1024, 4096], P(None, 'fsdp'), may hold values from -0.1875 to 0.1875
- ffn_in_bias: bfloat16 [2, 4096], P(None, 'fsdp'), may hold values from -3 to 3
- ffn_out: bfloat16 [2, 4096, 1024], P(None, 'fsdp'), may hold values from -0.09375 to 0.09375
- qkv: bfloat16 [3, 1024, 1024], P(None, 'fsdp'), may hold values from -0.1875 to 0.1875
- attn_out: bfloat16 [1024, 1024], P('fsdp'), may hold values from -0.75 to 0.75
- conv_in: bfloat16 [1024, 2048], P('fsdp'), may hold values from -0.1875 to 0.1875
- conv_out: bfloat16 [1024, 1024], P('fsdp'), may hold values from -0.1875 to 0.1875
- depthwise: bfloat16 [31, 1024], P(None, 'fsdp'), may hold values from -1 to 1
- gains: bfloat16 [6, 1024], P(None, 'fsdp'), may hold values from 0.099609375 to 1.8984375
- shifts: bfloat16 [15, 1024], P(None, 'fsdp'), may hold values from -2 to 2
- distance: bfloat16 [73, 64], replicated, may hold values from -6 to 6
- grad_out: bfloat16 [16, 1024, 1024], P('fsdp', 'seq'), may hold values from -6 to 6
Outputs:
- outputs: bfloat16 [16, 1024, 1024], P('fsdp', 'seq')
- grad_inputs: bfloat16 [16, 1024, 1024], P('fsdp', 'seq')
- grad_ffn_in: float32 [2, 1024, 4096], P(None, 'fsdp')
- grad_ffn_in_bias: float32 [2, 4096], P(None, 'fsdp')
- grad_ffn_out: float32 [2, 4096, 1024], P(None, 'fsdp')
- grad_qkv: float32 [3, 1024, 1024], P(None, 'fsdp')
- grad_attn_out: float32 [1024, 1024], P('fsdp')
- grad_conv_in: float32 [1024, 2048], P('fsdp')
- grad_conv_out: float32 [1024, 1024], P('fsdp')
- grad_depthwise: float32 [31, 1024], P(None, 'fsdp')
- grad_gains: float32 [6, 1024], P(None, 'fsdp')
- grad_shifts: float32 [15, 1024], P(None, 'fsdp')
- grad_distance: float32 [73, 64], replicated
The draws below stay inside these ranges and needn't reach their ends.
Inputs may be any that keep to these rules, and one draw needn't show every extreme that they name: `lengths`: in each group of 2 sequences held by one index of fsdp, one sequence, drawn from the seed, has all 1024 tokens.
All inputs are finite; a program needn't handle non-finite values.
Results may differ from the reference program's by a relative error of at most 0.024.
Values may be sent and summed in bfloat16 or wider, within the bound.
A program may use at most 376 MiB of HBM per device.

```python
import jax
import jax.numpy as jnp
from jax import lax

D = 1024
FF = 4096
HEAD_DIM = 64
KERNEL = 31
LEFT = 64
RIGHT = 8
MICRO = 2
LEN = 1024
SEQS = 16
RELATIVE = 73


def draw_lengths(key, part):
    key = jax.random.fold_in(key, 11)
    first_key, second_key = jax.random.split(key)
    groups = SEQS // MICRO
    values = jax.random.randint(first_key, (groups, MICRO), LEN // 2, LEN + 1)
    picked = jax.random.randint(second_key, (groups, 1), 0, MICRO)
    filled = jnp.arange(MICRO)[None, :] == picked
    return jnp.where(filled, LEN, values).reshape(SEQS).astype(jnp.int32)


def level_of(stream_key, dims, shards, least, largest):
    def one(position, parts):
        steps = jax.random.uniform(jax.random.fold_in(jax.random.fold_in(stream_key, 6), position), (parts,), jnp.float32, least / len(shards), largest / len(shards))
        return jnp.repeat(jnp.exp(steps), dims[position] // parts).reshape((-1,) + (1,) * (len(dims) - position - 1))

    level = one(*shards[0])
    for cut in shards[1:]:
        level = level * one(*cut)
    return level


def noise(rng, shape, scale, limit, pieces=(), kind=jnp.bfloat16):
    loudness = level_of(rng, shape, pieces, -0.22, 0.18) if pieces else 1.0
    array = jax.random.normal(rng, shape, jnp.float32) * scale * loudness
    return jnp.minimum(jnp.maximum(array, -limit), limit).astype(kind)


def setup_inputs(seed: int = 0) -> dict:
    arg_keys = jax.random.split(jax.random.key(seed), 15)
    return {
        "inputs": noise(arg_keys[0], (SEQS, LEN, D), 1.0, 6.0, ((0, 8), (1, 4))),
        "lengths": draw_lengths(jax.random.fold_in(arg_keys[14], 71), 0),
        "ffn_in": noise(arg_keys[2], (2, D, FF), D ** -0.5, 0.1875, ((1, 8),)),
        "ffn_in_bias": noise(arg_keys[3], (2, FF), 0.5, 3.0, ((1, 8),)),
        "ffn_out": noise(arg_keys[4], (2, FF, D), FF ** -0.5, 0.09375, ((1, 8),)),
        "qkv": noise(arg_keys[5], (3, D, D), D ** -0.5, 0.1875, ((1, 8),)),
        "attn_out": noise(arg_keys[6], (D, D), (D // 16) ** -0.5, 0.75, ((0, 8),)),
        "conv_in": noise(arg_keys[7], (D, 2 * D), D ** -0.5, 0.1875, ((0, 8),)),
        "conv_out": noise(arg_keys[8], (D, D), D ** -0.5, 0.1875, ((0, 8),)),
        "depthwise": noise(arg_keys[9], (KERNEL, D), KERNEL ** -0.5, 1.0, ((1, 8),)),
        "gains": jnp.clip(1.0 + 0.18 * jax.random.normal(arg_keys[10], (6, D), jnp.float32), 0.099609375, 1.8984375).astype(jnp.bfloat16),
        "shifts": noise(arg_keys[11], (15, D), 0.3, 2.0, ((1, 8),)),
        "distance": noise(arg_keys[12], (RELATIVE, HEAD_DIM), 1.0, 6.0),
        "grad_out": noise(arg_keys[13], (SEQS, LEN, D), 1.0, 6.0, ((0, 8), (1, 4))),
    }


PRECISION = lax.Precision.HIGHEST
EPSILON = 1e-05

@jax.custom_vjp
def low(v):
    return lax.optimization_barrier(v.astype(jnp.bfloat16)).astype(jnp.float32)

@jax.custom_vjp
def low_back(v):
    return v

def low_keep(v):
    return (low(v), None)

def low_pass(kept, grad):
    return (grad,)

def back_keep(v):
    return (v, None)

def back_low(kept, grad):
    return (low(grad),)
low.defvjp(low_keep, low_pass)
low_back.defvjp(back_keep, back_low)

def product(left, right):
    return jnp.einsum('...d,df->...f', left, right, precision=PRECISION)

def layer_norm(values, gain, shift):
    centred = values - lax.optimization_barrier(jnp.mean(values, axis=-1, keepdims=True))
    spread = lax.optimization_barrier(jnp.mean(centred * centred, axis=-1, keepdims=True))
    return centred * lax.rsqrt(spread + EPSILON) * gain + shift

def feed_forward(values, w_inner, b_inner, w_outer, b_outer, gain, shift):
    normed = low(layer_norm(values, gain, shift))
    inner = low_back(product(normed, w_inner) + b_inner)
    active = low(jax.nn.silu(inner))
    return low_back(product(active, w_outer) + b_outer)

def front_part(tokens, w_inner, b_inner, w_outer, projections, gain_rows, shift_rows):
    first_sum = tokens + 0.5 * feed_forward(tokens, w_inner, b_inner, w_outer, shift_rows[6], gain_rows[0], shift_rows[0])
    normed = low(layer_norm(first_sum, gain_rows[1], shift_rows[1]))
    query = low(low_back(product(normed, projections[0]) + shift_rows[8]))
    key_rows = low(low_back(product(normed, projections[1])))
    value = low(low_back(product(normed, projections[2]) + shift_rows[9]))
    return (first_sum, query, key_rows, value)

def attend(query, key_rows, value, table, length):
    token_count = query.shape[0]
    heads_here = query.shape[1] // HEAD_DIM
    query_heads = query.reshape(token_count, heads_here, HEAD_DIM)
    key_heads = key_rows.reshape(token_count, heads_here, HEAD_DIM)
    value_heads = value.reshape(token_count, heads_here, HEAD_DIM)
    block_rows = min(512, token_count)
    positions = jnp.arange(token_count, dtype=jnp.int32)
    key_valid = positions < length

    def one_block(start):
        rows_query = lax.dynamic_slice_in_dim(query_heads, start, block_rows, 0)
        row_index = start + jnp.arange(block_rows, dtype=jnp.int32)
        offset = jnp.clip(positions[None, :] - row_index[:, None], -LEFT, RIGHT) + LEFT
        scores = jnp.einsum('bhd,nhd->hbn', rows_query, key_heads, precision=PRECISION)
        relative = jnp.einsum('bhd,rd->hbr', rows_query, table, precision=PRECISION)
        placed = jnp.take_along_axis(relative, jnp.broadcast_to(offset[None], (heads_here, block_rows, token_count)), axis=2)
        scores = low_back((scores + placed) * HEAD_DIM ** (-0.5))
        scores = jnp.where(key_valid[None, None, :], scores, -1e+30)
        row_max = lax.optimization_barrier(jnp.max(scores, axis=2, keepdims=True))
        probs = jnp.exp(scores - row_max)
        probs = probs / lax.optimization_barrier(jnp.sum(probs, axis=2, keepdims=True))
        mixed_rows = jnp.einsum('hbn,nhd->bhd', low(probs), value_heads, precision=PRECISION)
        return mixed_rows.reshape(block_rows, heads_here * HEAD_DIM)
    starts = jnp.arange(0, token_count, block_rows, dtype=jnp.int32)
    return lax.map(jax.checkpoint(one_block), starts).reshape(token_count, heads_here * HEAD_DIM)

def middle_part(first_sum, mixed, w_attn_out, w_conv_in, gain_rows, shift_rows):
    second_sum = first_sum + low_back(product(mixed, w_attn_out) + shift_rows[10])
    normed = low(layer_norm(second_sum, gain_rows[2], shift_rows[2]))
    bias_both = jnp.concatenate([shift_rows[11], shift_rows[12]])
    inner = low_back(product(normed, w_conv_in) + bias_both)
    width = first_sum.shape[-1]
    gated = low(inner[..., :width] * jax.nn.sigmoid(inner[..., width:]))
    return (second_sum, gated)

def back_part(second_sum, gated, halo, taps, w_conv_out, w_inner, b_inner, w_outer, gain_rows, shift_rows):
    count = second_sum.shape[-2]
    padded = jnp.concatenate([halo, gated], axis=-2)
    conv = shift_rows[13] + taps[0] * padded[..., 0:count, :]
    for tap in range(1, taps.shape[0]):
        conv = conv + taps[tap] * padded[..., tap:tap + count, :]
    active = low(jax.nn.silu(layer_norm(conv, gain_rows[3], shift_rows[3])))
    third_sum = second_sum + low_back(product(active, w_conv_out) + shift_rows[14])
    fourth_sum = third_sum + 0.5 * feed_forward(third_sum, w_inner, b_inner, w_outer, shift_rows[7], gain_rows[4], shift_rows[4])
    return layer_norm(fourth_sum, gain_rows[5], shift_rows[5])

def layer(tokens, weights, length):
    f_inner, f_bias, f_outer, projections, w_attn_out, w_conv_in, w_conv_out, taps, gain_rows, shift_rows, table = weights
    first_sum, query, key_rows, value = front_part(tokens, f_inner[0], f_bias[0], f_outer[0], projections, gain_rows, shift_rows)
    mixed = low(low_back(attend(query, key_rows, value, low(table), length)))
    second_sum, gated = middle_part(first_sum, mixed, w_attn_out, w_conv_in, gain_rows, shift_rows)
    halo = jnp.zeros((taps.shape[0] - 1, tokens.shape[-1]), jnp.float32)
    return back_part(second_sum, gated, halo, taps, w_conv_out, f_inner[1], f_bias[1], f_outer[1], gain_rows, shift_rows)

def reference(inputs, lengths, ffn_in, ffn_in_bias, ffn_out, qkv, attn_out, conv_in, conv_out, depthwise, gains, shifts, distance, grad_out):
    params = tuple((p.astype(jnp.float32) for p in (ffn_in, ffn_in_bias, ffn_out, qkv, attn_out, conv_in, conv_out, depthwise, gains, shifts, distance)))

    def step(summed, sequence):
        tokens, length, cotangent = sequence
        result, pullback = jax.vjp(lambda values, weights: layer(values, weights, length), tokens.astype(jnp.float32), params)
        grad_tokens, grad_weights = pullback(cotangent.astype(jnp.float32))
        summed = jax.tree.map(lambda first, second: first + second, summed, grad_weights)
        return (summed, (result.astype(jnp.bfloat16), grad_tokens.astype(jnp.bfloat16)))
    zeros = jax.tree.map(jnp.zeros_like, params)
    summed, (outputs, grad_inputs) = lax.scan(step, zeros, (inputs, lengths, grad_out))
    return (outputs, grad_inputs, summed[0], summed[1], summed[2], summed[3], summed[4], summed[5], summed[6], summed[7], summed[8], summed[9], summed[10])
```

```python
import functools

import jax
import jax.numpy as jnp
from jax import lax
from jax.experimental import pallas as pl
from jax.experimental.pallas import tpu as pltpu
from jax.sharding import PartitionSpec as P

HEAD_DIM=64; LEFT=64; RIGHT=8
F32=jnp.float32; BF=jnp.bfloat16
RB=256
PADL=128
WIN=512

def dot(a,b,ca,cb):
    return lax.dot_general(a,b,(((ca,),(cb,)),((),())),preferred_element_type=F32)

def lanes(shape):
    return lax.broadcasted_iota(jnp.int32,shape,1)

def band_offset():
    row=lax.broadcasted_iota(jnp.int32,(RB,WIN),0)
    col=lax.broadcasted_iota(jnp.int32,(RB,WIN),1)
    return col-row-LEFT

def fwd_kernel(len_ref,q_ref,k_ref,v_ref,wide_ref,ends_ref,p_ref,o_ref,s_ref,kx_ref):
    n=k_ref.shape[0]
    step=pl.program_id(1)
    i0=step*RB
    q2=q_ref[...]
    lane=lanes((RB,128))
    col=lanes((RB,128))
    t=lax.broadcasted_iota(jnp.int32,(n,128),0)
    c=lanes((n,128))
    left=(t<i0-128).astype(F32); right=(t>=i0+WIN-128).astype(F32)
    masked=jnp.where(t>=len_ref[0],-1e30,0.0)
    ext=jnp.where(c<2,left,jnp.where(c<4,right,jnp.where(c==4,masked,0.0)))
    kx_ref[...]=ext.astype(BF)
    outs=[]
    for h in range(2):
        mine=(lane<64) if h==0 else (lane>=64)
        qh=jnp.where(mine,q2,jnp.zeros_like(q2))
        ends=dot(qh,ends_ref[...],1,0)
        hi=ends.astype(BF).astype(F32)
        qx=jnp.where((col==0)|(col==2),hi,jnp.where((col==1)|(col==3),ends-hi,jnp.where(col==4,1.0,0.0))).astype(BF)
        s=dot(qh,k_ref[...],1,1)+dot(qx,kx_ref[...],1,1)
        s_ref[:,PADL:PADL+n]=s
        wide=dot(qh,wide_ref[...],1,0)
        band=pltpu.roll(wide,LEFT,1,stride=1,stride_axis=0)
        j=band_offset()
        band=jnp.where(j>=LEFT+RIGHT,wide[:,LEFT+RIGHT:LEFT+RIGHT+1],band)
        w=pl.ds(pl.multiple_of(i0,RB),WIN)
        s_ref[:,w]=s_ref[:,w]+band
        s=s_ref[:,PADL:PADL+n]
        m=jnp.max(s,axis=1,keepdims=True)
        e=jnp.exp(s-m)
        z=jnp.sum(e,axis=1,keepdims=True)
        p=(e*(1.0/z)).astype(BF)
        p_ref[h]=p
        outs.append(dot(p,v_ref[...],1,0))
    o_ref[...]=jnp.where(lane<64,outs[0],outs[1]).astype(BF)

def bwd_kernel(q_ref,k_ref,v_ref,do_ref,p_ref,wide_ref,dq_ref,dkt_ref,dvt_ref,de_ref,ds_ref,kx_ref,dka,dva,dea):
    n=k_ref.shape[0]
    step=pl.program_id(1)
    pair=pl.program_id(0)
    i0=step*RB
    q2=q_ref[...]; do2=do_ref[...]
    lane=lanes((RB,128))
    row=lax.broadcasted_iota(jnp.int32,(RB,128),0)
    t=lax.broadcasted_iota(jnp.int32,(n,128),0)
    c=lanes((n,128))
    left=(t<i0-128).astype(F32)
    kx_ref[...]=jnp.where(c==0,left,jnp.where(c==1,1.0,0.0)).astype(BF)
    @pl.when(step==0)
    def _():
        dka[...]=jnp.zeros_like(dka); dva[...]=jnp.zeros_like(dva)
    @pl.when((step==0)&(pair==0))
    def _():
        dea[...]=jnp.zeros_like(dea)
    ds_ref[:,0:PADL]=jnp.zeros((RB,PADL),F32)
    ds_ref[:,PADL+n:]=jnp.zeros((RB,ds_ref.shape[1]-PADL-n),F32)
    dqs=[]
    for h in range(2):
        mine=(lane<64) if h==0 else (lane>=64)
        doh=jnp.where(mine,do2,jnp.zeros_like(do2))
        qh=jnp.where(mine,q2,jnp.zeros_like(q2))
        p=p_ref[h]
        dp=dot(doh,v_ref[...],1,1)
        pf=p.astype(F32)
        d=jnp.sum(pf*dp,axis=1,keepdims=True)
        dsf=pf*(dp-d)
        ds=dsf.astype(BF)
        ds_ref[:,PADL:PADL+n]=ds.astype(F32)
        dva[...]+=dot(doh,p,0,0)
        dka[...]+=dot(qh,ds,0,0)
        dq=dot(ds,k_ref[...],1,0)
        sums=dot(ds,kx_ref[...],1,0)
        win=ds_ref[:,pl.ds(pl.multiple_of(i0,RB),WIN)]
        j=band_offset()
        inleft=jnp.sum(jnp.where(j<=0,win,0.0),axis=1,keepdims=True)
        drel=jnp.concatenate([win[8*g:8*g+8,LEFT+8*g:LEFT+8*g+128] for g in range(RB//8)],axis=0)
        for bit in (1,2,4):
            drel=jnp.where((row&bit)!=0,pltpu.roll(drel,128-bit,1),drel)
        drel=jnp.where((lane>0)&(lane<LEFT+RIGHT),drel,0.0)
        bandsum=jnp.sum(drel,axis=1,keepdims=True)
        l=sums[:,0:1]+inleft
        r=sums[:,1:2]-l-bandsum
        drel=jnp.where(lane==0,l,jnp.where(lane==LEFT+RIGHT,r,drel)).astype(BF)
        dq=dq+dot(drel,wide_ref[...],1,1)
        dqs.append(dq)
        dea[...]+=dot(drel,qh,0,0)
    dq_ref[...]=(jnp.where(lane<64,dqs[0],dqs[1])*HEAD_DIM**-0.5).astype(BF)
    @pl.when(step==pl.num_programs(1)-1)
    def _():
        dkt_ref[...]=jnp.transpose(dka[...]).astype(BF)
        dvt_ref[...]=jnp.transpose(dva[...]).astype(BF)
    @pl.when((step==pl.num_programs(1)-1)&(pair==pl.num_programs(0)-1))
    def _():
        de_ref[...]=dea[...]

def tables(distance):
    e=distance.T
    wide=jnp.concatenate([e,jnp.broadcast_to(e[:,72:73],(64,120)),jnp.broadcast_to(e[:,0:1],(64,WIN-193))],axis=1)
    wide=jnp.concatenate([wide,wide],axis=0)
    ends=jnp.concatenate([e[:,0:1],e[:,0:1],e[:,72:73],e[:,72:73],jnp.zeros((64,124),e.dtype)],axis=1)
    ends=jnp.concatenate([ends,ends],axis=0)
    return wide,ends

def attend(q,k,v,length,wide,ends):
    n,w=q.shape; pairs=w//128
    return pl.pallas_call(fwd_kernel,
        grid=(pairs,n//RB),
        in_specs=[pl.BlockSpec(memory_space=pltpu.SMEM),
            pl.BlockSpec((RB,128),lambda a,b:(b,a)),pl.BlockSpec((n,128),lambda a,b:(0,a)),pl.BlockSpec((n,128),lambda a,b:(0,a)),
            pl.BlockSpec((128,WIN),lambda a,b:(0,0)),pl.BlockSpec((128,128),lambda a,b:(0,0))],
        out_specs=[pl.BlockSpec((2,RB,n),lambda a,b:(a,b,0)),pl.BlockSpec((RB,128),lambda a,b:(b,a))],
        out_shape=[jax.ShapeDtypeStruct((2*pairs,n,n),BF),jax.ShapeDtypeStruct((n,w),BF)],
        scratch_shapes=[pltpu.VMEM((RB,PADL+n+256),F32),pltpu.VMEM((n,128),BF)],
        compiler_params=pltpu.CompilerParams(vmem_limit_bytes=32<<20),
        name="attend_fwd",
    )(length,q,k,v,wide,ends)

def attend_back(q,k,v,do,p,wide):
    n,w=q.shape; pairs=w//128
    rows=pl.BlockSpec((RB,128),lambda a,b:(b,a)); whole=pl.BlockSpec((n,128),lambda a,b:(0,a))
    return pl.pallas_call(bwd_kernel,
        grid=(pairs,n//RB),
        in_specs=[rows,whole,whole,rows,pl.BlockSpec((2,RB,n),lambda a,b:(a,b,0)),pl.BlockSpec((128,128),lambda a,b:(0,0))],
        out_specs=[rows,whole,whole,pl.BlockSpec((128,128),lambda a,b:(0,0))],
        out_shape=[jax.ShapeDtypeStruct((n,w),BF)]*3+[jax.ShapeDtypeStruct((128,128),F32)],
        scratch_shapes=[pltpu.VMEM((RB,PADL+n+256),F32),pltpu.VMEM((n,128),BF),pltpu.VMEM((128,n),F32),pltpu.VMEM((128,n),F32),pltpu.VMEM((128,128),F32)],
        compiler_params=pltpu.CompilerParams(vmem_limit_bytes=32<<20),
        name="attend_bwd",
    )(q,k,v,do,p,wide[:,0:128])

EPSILON = 1e-05
HALF = 0.5


def mm(a, b):
    return dot(a, b, 1, 0)


def mm_bt(a, b):
    return dot(a, b, 1, 1)


def mm_at(a, b):
    return dot(a, b, 0, 0)


def norm_stats(values):
    mean = jnp.mean(values, axis=-1, keepdims=True)
    centred = values - mean
    spread = jnp.mean(centred * centred, axis=-1, keepdims=True)
    return mean, lax.rsqrt(spread + EPSILON)


def normalized(values, stats):
    return (values - stats[0]) * stats[1]


def norm_back(dy, values, stats, gain):
    unit = normalized(values, stats)
    a = dy * gain
    dv = (a - jnp.mean(a, axis=-1, keepdims=True) - unit * jnp.mean(a * unit, axis=-1, keepdims=True)) * stats[1]
    return dv, jnp.sum(dy * unit, axis=0), jnp.sum(dy, axis=0)


def silu_slope(v):
    s = jax.nn.sigmoid(v)
    return s * (1.0 + v * (1.0 - s))


def xor_route(axis, mask):
    return [(i, i ^ mask) for i in range(lax.axis_size(axis))]


def swapped(block, axis, mask):
    return lax.ppermute(block, axis, xor_route(axis, mask))


def after(value, *marks):
    return lax.optimization_barrier((value,) + marks)[0]


class Cube:
    def __init__(self):
        self.me = lax.axis_index("fsdp")

    def gather(self, shard):
        rows = shard.shape[0]
        cut = rows // 2
        across_x = swapped(shard, "fsdp", 2)
        across_y = swapped(shard, "fsdp", 4)
        far_top = swapped(across_x[:cut], "fsdp", 4)
        far_low = swapped(across_y[cut:], "fsdp", 2)
        mine = [shard, across_x, across_y, far_top, far_low]
        other = [swapped(piece, "fsdp", 1) for piece in mine]
        return jnp.concatenate(
            [mine[0], other[0], mine[1], other[1], mine[2], other[2], mine[3], mine[4], other[3], other[4]], axis=0
        )

    def arrange(self, value):
        rows, cols = value.shape
        blocks = value.reshape(rows, 8, cols // 8)
        for bit in (1, 2, 4):
            order = [i ^ bit for i in range(8)]
            turned = jnp.stack([blocks[:, i] for i in order], axis=1)
            blocks = jnp.where((self.me & bit) != 0, turned, blocks)
        return blocks.reshape(rows, cols)

    def product_back(self, left, right):
        rows, cols = left.shape
        blocks = left.reshape(rows, 4, 2, cols // 8)
        odd = mm_at(blocks[:, :, 1].reshape(rows, cols // 2), right).astype(BF)
        even = mm_at(blocks[:, :, 0].reshape(rows, cols // 2), right)
        return odd, even

    def scatter(self, odd, even):
        size, cols = odd.shape
        rows, cut = size // 4, cols // 2
        here = (even + swapped(odd, "fsdp", 1).astype(F32)).reshape(4, rows, cols)
        one, two = here[:, :, :cut], here[:, :, cut:]
        got = swapped(one[1::2].astype(BF), "fsdp", 2)
        one = one[0::2] + got.astype(F32)
        got = swapped(two[2:].astype(BF), "fsdp", 4)
        two = two[:2] + got.astype(F32)
        one = one[0] + swapped(one[1].astype(BF), "fsdp", 4).astype(F32)
        two = two[0] + swapped(two[1].astype(BF), "fsdp", 2).astype(F32)
        return self.over_seq(jnp.concatenate([one, two], axis=1))

    def over_seq(self, part):
        rows = part.shape[0]
        place = lax.axis_index("seq")
        for mask in (1, 2):
            high = (place & mask) != 0
            half = part.shape[0] // 2
            first, second = part[:half], part[half:]
            sent = jnp.where(high, first, second).astype(BF)
            part = jnp.where(high, second, first) + swapped(sent, "seq", mask).astype(F32)
        part = part.astype(BF)
        for mask in (2, 1):
            high = (place & mask) != 0
            got = swapped(part, "seq", mask)
            part = jnp.where(high, jnp.concatenate([got, part], axis=0), jnp.concatenate([part, got], axis=0))
        return part.astype(F32)


class Plain:
    def gather(self, shard):
        return lax.all_gather(shard, "fsdp", axis=0, tiled=True)

    def arrange(self, value):
        return value

    def product_back(self, left, right):
        return None, mm_at(left, right)

    def scatter(self, odd, even):
        share = lax.psum_scatter(even.astype(BF), "fsdp", scatter_dimension=0, tiled=True)
        return lax.psum(share, "seq").astype(F32)


def to_pairs(array, place):
    one, two = array[0], array[1]
    got = lax.ppermute(jnp.where(place % 2 == 0, two, one), "seq", [(0, 2), (1, 0), (2, 3), (3, 1)])
    more = lax.ppermute(jnp.where(place == 1, two, one), "seq", [(1, 2), (2, 1)])
    first = jnp.where(place == 0, one, jnp.where(place == 1, more, got))
    second = jnp.where(place < 2, got, jnp.where(place == 2, more, two))
    return jnp.concatenate([first, second], axis=0)


def from_pairs(array, place):
    half = array.shape[0] // 2
    first, second = array[:half], array[half:]
    got = lax.ppermute(jnp.where(place < 2, second, first), "seq", [(2, 0), (0, 1), (3, 2), (1, 3)])
    more = lax.ppermute(jnp.where(place == 1, first, second), "seq", [(1, 2), (2, 1)])
    one = jnp.where(place == 0, first, jnp.where(place == 2, more, got))
    two = jnp.where(place == 3, second, jnp.where(place == 1, more, got))
    return jnp.stack([one, two])


def to_heads(array, odd):
    half = array.shape[1] // 2
    low, high = array[:, :half], array[:, half:]
    mine = jnp.where(odd, high, low)
    got = swapped(jnp.where(odd, low, high), "seq", 1)
    return jnp.concatenate([jnp.where(odd, got, mine), jnp.where(odd, mine, got)], axis=0)


def to_tokens(array, odd):
    half = array.shape[0] // 2
    low, high = array[:half], array[half:]
    mine = jnp.where(odd, high, low)
    got = swapped(jnp.where(odd, low, high), "seq", 1)
    return jnp.concatenate([jnp.where(odd, got, mine), jnp.where(odd, mine, got)], axis=1)


def on_device(
    inputs,
    lengths,
    ffn_in,
    ffn_in_bias,
    ffn_out,
    qkv,
    attn_out,
    conv_in,
    conv_out,
    depthwise,
    gains,
    shifts,
    distance,
    grad_out,
):
    shards = lax.axis_size("fsdp")
    me = lax.axis_index("fsdp")
    place = lax.axis_index("seq")
    odd = place % 2 == 1
    cube = Cube() if shards == 8 else Plain()
    reach = depthwise.shape[0] - 1
    inner_width = ffn_in.shape[2]
    width = inputs.shape[2]

    bias_rows = ffn_in_bias.shape[0] * inner_width // width
    small = jnp.concatenate(
        [gains, shifts, depthwise, ffn_in_bias.reshape(-1, width // shards)], axis=0
    )
    n_gain, n_shift, n_tap = gains.shape[0], shifts.shape[0], depthwise.shape[0]
    small = lax.all_gather(small, "fsdp", axis=0).astype(F32)
    rows = jnp.transpose(small, (1, 0, 2))
    gain = rows[:n_gain].reshape(n_gain, width)
    shift = rows[n_gain : n_gain + n_shift].reshape(n_shift, width)
    taps = rows[n_gain + n_shift : n_gain + n_shift + n_tap].reshape(n_tap, width)
    bias = small[:, n_gain + n_shift + n_tap :].reshape(shards, 2, -1).transpose(1, 0, 2).reshape(2, inner_width)

    w_in_a = cube.gather(ffn_in[0])
    w_out_a = cube.gather(ffn_out[0])
    w_qkv = cube.gather(jnp.concatenate([qkv[0], qkv[1], qkv[2]], axis=1))
    w_mid = cube.gather(jnp.concatenate([attn_out, conv_in, conv_out], axis=1))
    w_in_b = cube.gather(ffn_in[1])
    w_out_b = cube.gather(ffn_out[1])
    w_attn, w_conv_in, w_conv_out = w_mid[:, :width], w_mid[:, width : 3 * width], w_mid[:, 3 * width :]

    tokens = to_pairs(inputs, place).astype(F32)
    cotangent = to_pairs(grad_out, place)
    length = jnp.where(place < 2, lengths[0], lengths[1]).reshape(1)
    wide, ends = tables(distance)

    def prenorm(values, g):
        stats = norm_stats(values)
        unit = cube.arrange((normalized(values, stats) * gain[g] + shift[g]).astype(BF))
        return stats, unit

    def ffn(values, g, w_in, b_in, w_out, b_out):
        stats, unit = prenorm(values, g)
        inner = mm(unit, w_in) + b_in
        active = cube.arrange((inner * jax.nn.sigmoid(inner)).astype(BF))
        result = values + HALF * (mm(active, w_out) + b_out)
        return result, (stats, unit, inner.astype(BF), active)

    def ffn_back(dy, values, g, w_in, w_out, kept):
        stats, unit, inner, active = kept
        dout = (HALF * dy).astype(BF)
        d_out_w = cube.product_back(active, dout)
        dactive = cube.arrange(mm_bt(dout, w_out))
        dinner = (dactive * silu_slope(inner.astype(F32))).astype(BF)
        d_in_w = cube.product_back(unit, dinner)
        dunit = cube.arrange(mm_bt(dinner, w_in))
        dv, dgain, dshift = norm_back(dunit, values, stats, gain[g])
        return dy + dv, d_in_w, d_out_w, colsum(dinner), colsum(dout), dgain, dshift

    def colsum(v):
        return jnp.sum(v.astype(F32), axis=0)

    first, kept_a = ffn(tokens, 0, w_in_a, bias[0], w_out_a, shift[6])
    stats_1, unit_1 = prenorm(first, 1)
    query = ((mm(unit_1, w_qkv[:, :width]) + shift[8]).astype(BF) * jnp.asarray(HEAD_DIM**-0.5, BF)).astype(BF)
    key_rows = mm(unit_1, w_qkv[:, width : 2 * width]).astype(BF)
    value = (mm(unit_1, w_qkv[:, 2 * width :]) + shift[9]).astype(BF)
    query, key_rows, value = to_heads(query, odd), to_heads(key_rows, odd), to_heads(value, odd)
    probs, mixed = attend(query, key_rows, value, length, wide, ends)
    mixed = cube.arrange(to_tokens(mixed, odd))
    second = first + mm(mixed, w_attn) + shift[10]
    stats_2, unit_2 = prenorm(second, 2)
    glu = mm(unit_2, w_conv_in) + jnp.concatenate([shift[11], shift[12]])
    glu_value, glu_gate = glu[:, :width], jax.nn.sigmoid(glu[:, width:])
    gated = (glu_value * glu_gate).astype(BF)
    glu_value, glu_gate = glu_value.astype(BF), glu_gate.astype(BF)
    pairs = [(0, 1), (2, 3)]
    count = gated.shape[0]
    halo = lax.ppermute(gated[count - reach :], "seq", pairs)
    padded = jnp.concatenate([halo, gated], axis=0).astype(F32)
    conv = shift[13] + taps[0] * padded[0:count]
    for tap in range(1, n_tap):
        conv = conv + taps[tap] * padded[tap : tap + count]
    stats_3 = norm_stats(conv)
    normed = normalized(conv, stats_3) * gain[3] + shift[3]
    active_c = cube.arrange((normed * jax.nn.sigmoid(normed)).astype(BF))
    third = second + mm(active_c, w_conv_out) + shift[14]
    fourth, kept_b = ffn(third, 4, w_in_b, bias[1], w_out_b, shift[7])
    stats_5 = norm_stats(fourth)
    outputs = from_pairs((normalized(fourth, stats_5) * gain[5] + shift[5]).astype(BF), place)

    d4, dg5, db5 = norm_back(cotangent.astype(F32), fourth, stats_5, gain[5])
    d3, g_in_b, g_out_b, dbias_b, ds7, dg4, db4 = ffn_back(d4, third, 4, w_in_b, w_out_b, kept_b)
    share_out_b = cube.scatter(*g_out_b)
    share_in_b = cube.scatter(*g_in_b)
    dout = d3.astype(BF)
    ds14 = colsum(dout)
    g_conv_out = cube.product_back(active_c, dout)
    dactive = cube.arrange(mm_bt(dout, w_conv_out))
    dnormed = dactive * silu_slope(normalized(conv, stats_3) * gain[3] + shift[3])
    dconv, dg3, db3 = norm_back(dnormed, conv, stats_3, gain[3])
    ds13 = colsum(dconv)
    dtaps = jnp.stack([jnp.sum(dconv * padded[tap : tap + count], axis=0) for tap in range(n_tap)])
    follow = lax.ppermute(dconv[:reach], "seq", [(j, i) for i, j in pairs])
    dpadded = jnp.concatenate([dconv, follow], axis=0)
    dgated = taps[0] * dpadded[reach : reach + count]
    for tap in range(1, n_tap):
        dgated = dgated + taps[tap] * dpadded[reach - tap : reach - tap + count]
    val, sig = glu_value.astype(F32), glu_gate.astype(F32)
    dglu = jnp.concatenate([dgated * sig, dgated * val * sig * (1.0 - sig)], axis=1).astype(BF)
    ds11_12 = colsum(dglu)
    g_conv_in = cube.product_back(unit_2, dglu)
    dunit = cube.arrange(mm_bt(dglu, w_conv_in))
    dv, dg2, db2 = norm_back(dunit, second, stats_2, gain[2])
    d2 = d3 + dv
    dout = d2.astype(BF)
    ds10 = colsum(dout)
    g_attn = cube.product_back(mixed, dout)
    dmixed = cube.arrange(mm_bt(dout, w_attn)).astype(BF)
    dmixed = to_heads(dmixed, odd)
    dq, dk, dv_, dtable = attend_back(query, key_rows, value, dmixed, probs, wide)
    dq, dk, dv_ = to_tokens(dq, odd), to_tokens(dk, odd), to_tokens(dv_, odd)
    if shards == 8:
        g_mid = tuple(jnp.concatenate(parts, axis=1) for parts in zip(g_attn, g_conv_in, g_conv_out))
    else:
        g_mid = (None, jnp.concatenate([g_attn[1], g_conv_in[1], g_conv_out[1]], axis=1))
    share_mid = cube.scatter(*g_mid)
    ds8, ds9 = colsum(dq), colsum(dv_)
    dqkv = jnp.concatenate([dq, dk, dv_], axis=1)
    g_qkv = cube.product_back(unit_1, dqkv)
    dunit = cube.arrange(mm_bt(dqkv, w_qkv))
    dv, dg1, db1 = norm_back(dunit, first, stats_1, gain[1])
    d1 = d2 + dv
    share_qkv = cube.scatter(*g_qkv)
    d0, g_in_a, g_out_a, dbias_a, ds6, dg0, db0 = ffn_back(d1, tokens, 0, w_in_a, w_out_a, kept_a)
    share_out_a = cube.scatter(*g_out_a)
    share_in_a = cube.scatter(*g_in_a)
    grad_tokens = from_pairs(d0.astype(BF), place)

    dtable = (dtable[: distance.shape[0], :HEAD_DIM] + dtable[: distance.shape[0], HEAD_DIM:]).reshape(-1)
    pad = (-dtable.shape[0]) % width
    vectors = [dg0, dg1, dg2, dg3, dg4, dg5]
    vectors += [db0, db1, db2, db3, db4, db5, ds6, ds7, ds8, ds9, ds10, ds11_12, ds13, ds14]
    flat = jnp.concatenate(
        vectors + [dtaps.reshape(-1), dbias_a, dbias_b, dtable, jnp.zeros((pad,), F32)]
    ).reshape(-1, width)
    flat = lax.psum(flat, ("seq", "fsdp"))
    own = lax.dynamic_slice_in_dim(flat, me * (width // shards), width // shards, 1)
    at = n_gain + n_shift + n_tap
    biases = flat[at : at + bias_rows].reshape(2, inner_width)
    share_bias = lax.dynamic_slice_in_dim(biases, me * (inner_width // shards), inner_width // shards, 1)
    total_table = flat[at + bias_rows :].reshape(-1)[: distance.size].reshape(distance.shape)
    return (
        outputs,
        grad_tokens,
        jnp.stack([share_in_a, share_in_b]),
        share_bias,
        jnp.stack([share_out_a, share_out_b]),
        jnp.stack([share_qkv[:, :width], share_qkv[:, width : 2 * width], share_qkv[:, 2 * width :]]),
        share_mid[:, :width],
        share_mid[:, width : 3 * width],
        share_mid[:, 3 * width :],
        own[n_gain + n_shift : at],
        own[:n_gain],
        own[n_gain : n_gain + n_shift],
        total_table,
    )


def solution(mesh):
    return jax.shard_map(
        on_device,
        mesh=mesh,
        in_specs=(
            P("fsdp", "seq", None),
            P("fsdp"),
            P(None, "fsdp", None),
            P(None, "fsdp"),
            P(None, "fsdp", None),
            P(None, "fsdp", None),
            P("fsdp", None),
            P("fsdp", None),
            P("fsdp", None),
            P(None, "fsdp"),
            P(None, "fsdp"),
            P(None, "fsdp"),
            P(),
            P("fsdp", "seq", None),
        ),
        out_specs=(
            P("fsdp", "seq", None),
            P("fsdp", "seq", None),
            P(None, "fsdp", None),
            P(None, "fsdp"),
            P(None, "fsdp", None),
            P(None, "fsdp", None),
            P("fsdp", None),
            P("fsdp", None),
            P("fsdp", None),
            P(None, "fsdp"),
            P(None, "fsdp"),
            P(None, "fsdp"),
            P(),
        ),
        check_vma=False,
    )
```

```python
import functools

import jax
import jax.numpy as jnp
from jax import lax
from jax.experimental import pallas as pl
from jax.experimental.pallas import tpu as pltpu
from jax.sharding import PartitionSpec as P

HEAD_DIM=64; LEFT=64; RIGHT=8
F32=jnp.float32; BF=jnp.bfloat16
RB=256
PADL=128
WIN=512

def dot(a,b,ca,cb):
    return lax.dot_general(a,b,(((ca,),(cb,)),((),())),preferred_element_type=F32)

def lanes(shape):
    return lax.broadcasted_iota(jnp.int32,shape,1)

def band_offset():
    row=lax.broadcasted_iota(jnp.int32,(RB,WIN),0)
    col=lax.broadcasted_iota(jnp.int32,(RB,WIN),1)
    return col-row-LEFT


MESH = pl.DeviceIdType.MESH
STEPS = 4


def pair_place():
    place = lax.axis_index("seq")
    half = lax.rem(place, jnp.int32(2))
    return half, {"seq": place + 1 - 2 * half}


def meet(partner):
    barrier = pltpu.get_barrier_semaphore()
    pl.semaphore_signal(barrier, inc=1, device_id=partner, device_id_type=MESH)
    pl.semaphore_wait(barrier, 1)


def block_at(step, half):
    return lax.rem(step + 2 * (1 - half), jnp.int32(STEPS))


def fwd_kernel(len_ref,wide_ref,ends_ref,mine_ref,other_ref,p_ref,heads_ref,mixed_ref,s_ref,kx_ref,buf,mixed,stage,in_send,in_recv,in_load,out_send,out_recv):
    n=buf.shape[2]; own=n//2
    pair=pl.program_id(0); step=pl.program_id(1)
    pairs=buf.shape[0]
    half,partner=pair_place()
    at=pl.multiple_of(half*own,own)
    def arrive(a):
        return pltpu.make_async_remote_copy(src_ref=other_ref.at[a],dst_ref=buf.at[a,:,pl.ds(at,own)],send_sem=in_send.at[a],recv_sem=in_recv.at[a],device_id=partner,device_id_type=MESH)
    def load(a):
        return pltpu.make_async_copy(mine_ref.at[a],buf.at[a,:,pl.ds(at,own)],in_load.at[a])
    def leave(a,b):
        cols=pl.ds(pl.multiple_of(half*own+a*128,128),128)
        return pltpu.make_async_remote_copy(src_ref=stage.at[a,b],dst_ref=mixed.at[pl.ds(pl.multiple_of(b*RB,RB),RB),cols],send_sem=out_send.at[a,b],recv_sem=out_recv.at[a,b],device_id=partner,device_id_type=MESH)
    @pl.when((pair==0)&(step==0))
    def _():
        meet(partner)
        for a in range(pairs):
            load(a).start()
            arrive(a).start()
    @pl.when(step==0)
    def _():
        load(pair).wait()
        arrive(pair).wait()
        heads_ref[0]=buf[pair]
        kx_ref[:,0:128]=buf[pair,1]
    i0=pl.multiple_of(block_at(step,half)*RB,RB)
    q2=buf[pair,0,pl.ds(i0,RB)]
    v2=buf[pair,2]
    lane=lanes((RB,128))
    t=lax.broadcasted_iota(jnp.int32,(n,128),0)
    c=lanes((n,128))
    left=(t<i0-128).astype(F32); right=(t>=i0+WIN-128).astype(F32)
    masked=jnp.where(t>=len_ref[0],-1e30,0.0)
    ext=jnp.where(c<2,left,jnp.where(c<4,right,jnp.where(c==4,masked,0.0)))
    kx_ref[:,128:256]=ext.astype(BF)
    outs=[]
    for h in range(2):
        head=(lane<64) if h==0 else (lane>=64)
        qh=jnp.where(head,q2,jnp.zeros_like(q2))
        ends=dot(qh,ends_ref[...],1,0)
        hi=ends.astype(BF).astype(F32)
        qx=jnp.where((lane==0)|(lane==2),hi,jnp.where((lane==1)|(lane==3),ends-hi,jnp.where(lane==4,1.0,0.0))).astype(BF)
        s_ref[:,PADL:PADL+n]=dot(jnp.concatenate([qh,qx],axis=1),kx_ref[...],1,1)
        wide=dot(qh,wide_ref[...],1,0)
        band=pltpu.roll(wide,LEFT,1,stride=1,stride_axis=0)
        j=band_offset()
        band=jnp.where(j>=LEFT+RIGHT,wide[:,LEFT+RIGHT:LEFT+RIGHT+1],band)
        w=pl.ds(i0,WIN)
        s_ref[:,w]=s_ref[:,w]+band
        s=s_ref[:,PADL:PADL+n]
        m=jnp.max(s,axis=1,keepdims=True)
        e=jnp.exp(s-m)
        z=jnp.sum(e,axis=1,keepdims=True)
        p=(e*(1.0/z)).astype(BF)
        p_ref[h]=p
        outs.append(dot(p,v2,1,0))
    out=jnp.where(lane<64,outs[0],outs[1]).astype(BF)
    @pl.when(step<2)
    def _():
        stage[pair,step]=out
        leave(pair,step).start()
    @pl.when(step>=2)
    def _():
        cols=pl.ds(pl.multiple_of(half*own+pair*128,128),128)
        mixed[pl.ds(pl.multiple_of((step-2)*RB,RB),RB),cols]=out
    @pl.when((pair==pairs-1)&(step==STEPS-1))
    def _():
        for a in range(pairs):
            for b in range(2):
                leave(a,b).wait_send()
        for a in range(pairs):
            for b in range(2):
                arrived=pltpu.make_async_remote_copy(src_ref=stage.at[a,b],dst_ref=mixed.at[pl.ds(b*RB,RB),pl.ds(pl.multiple_of((1-half)*own+a*128,128),128)],send_sem=out_send.at[a,b],recv_sem=out_recv.at[a,b],device_id=partner,device_id_type=MESH)
                arrived.wait_recv()
        mixed_ref[...]=mixed[...]


def z_line(middle,to_1,to_2,whole,near,far,z_send,z_recv):
    def copy(i,stage):
        src=(whole,near,far)[stage]; dst=(near,far,near)[stage]
        return pltpu.make_async_remote_copy(src_ref=src.at[i],dst_ref=dst.at[i],send_sem=z_send.at[i,stage],recv_sem=z_recv.at[i,stage],device_id=to_2 if stage==1 else to_1,device_id_type=MESH)
    def begin(i):
        pl.when(middle==0)(lambda: copy(i,0).start())
    def step(i,stage):
        @pl.when(middle==1)
        def _():
            if stage==0:
                copy(i,0).wait_recv()
                near[i]=(whole[i].astype(F32)+near[i].astype(F32)).astype(BF)
                copy(i,1).start()
            elif stage==1:
                copy(i,1).wait()
                far[i]=(near[i].astype(F32)+far[i].astype(F32)).astype(BF)
                copy(i,2).start()
            else:
                copy(i,2).wait_send()
        if stage!=1:
            @pl.when(middle==0)
            def _():
                if stage==0:
                    copy(i,0).wait_send()
                else:
                    copy(i,2).wait_recv()
    return begin,step


def bwd_kernel(with_part,heads_ref,p_ref,wide_ref,mine_ref,other_ref,*rest):
    if with_part:
        part_ref,dqkv_ref,de_ref,out_ref,*rest=rest
        *rest,whole,near,far,part_sem,out_sem,z_send,z_recv=rest
    else:
        dqkv_ref,de_ref,*rest=rest
    ds_ref,kx_ref,dka,dva,dea,buf,dqkv,stage_q,stage_kv,in_send,in_recv,in_load,q_send,q_recv,kv_send,kv_recv=rest
    n=heads_ref.shape[2]; own=n//2
    pair=pl.program_id(0); step=pl.program_id(1)
    pairs=buf.shape[0]
    half,partner=pair_place()
    at=pl.multiple_of(half*own,own)
    width=2*own
    def columns(t,who,a):
        return pl.ds(pl.multiple_of(t*width+who*own+a*128,128),128)
    def arrive(a):
        return pltpu.make_async_remote_copy(src_ref=other_ref.at[a],dst_ref=buf.at[a,pl.ds(at,own)],send_sem=in_send.at[a],recv_sem=in_recv.at[a],device_id=partner,device_id_type=MESH)
    def load(a):
        return pltpu.make_async_copy(mine_ref.at[a],buf.at[a,pl.ds(at,own)],in_load.at[a])
    def leave_q(a,b,who):
        return pltpu.make_async_remote_copy(src_ref=stage_q.at[a,b],dst_ref=dqkv.at[pl.ds(pl.multiple_of(b*RB,RB),RB),columns(0,who,a)],send_sem=q_send.at[a,b],recv_sem=q_recv.at[a,b],device_id=partner,device_id_type=MESH)
    def leave_kv(a,t,who):
        return pltpu.make_async_remote_copy(src_ref=stage_kv.at[a,t],dst_ref=dqkv.at[:,columns(t+1,who,a)],send_sem=kv_send.at[a,t],recv_sem=kv_recv.at[a,t],device_id=partner,device_id_type=MESH)
    if with_part:
        n_part=part_ref.shape[0]
        place=lax.axis_index("seq")
        middle=lax.rem(lax.div(place+1,jnp.int32(2)),jnp.int32(2))
        across={"seq":3-place}
        z_begin,z_step=z_line(middle,partner,across,whole,near,far,z_send,z_recv)
        def part_copy(i):
            return pltpu.make_async_copy(part_ref.at[i],whole.at[i],part_sem.at[i])
        def result_do(i,act):
            for is_middle,src in ((1,far),(0,near)):
                copy=pltpu.make_async_copy(src.at[i],out_ref.at[i],out_sem.at[i])
                pl.when(middle==is_middle)(lambda copy=copy: act(copy))
        now=pair*STEPS+step
    @pl.when((pair==0)&(step==0))
    def _():
        if with_part:
            barrier=pltpu.get_barrier_semaphore()
            for device in (partner,across):
                pl.semaphore_signal(barrier,inc=1,device_id=device,device_id_type=MESH)
            pl.semaphore_wait(barrier,2)
        else:
            meet(partner)
        for a in range(pairs):
            load(a).start()
            arrive(a).start()
        if with_part:
            for i in range(n_part):
                part_copy(i).start()
        dea[...]=jnp.zeros_like(dea)
        ds_ref[:,0:PADL]=jnp.zeros((RB,PADL),F32)
        ds_ref[:,PADL+n:]=jnp.zeros((RB,ds_ref.shape[1]-PADL-n),F32)
    @pl.when(step==0)
    def _():
        load(pair).wait()
        arrive(pair).wait()
        kx_ref[:,0:128]=heads_ref[0,1]
        dka[...]=jnp.zeros_like(dka); dva[...]=jnp.zeros_like(dva)
    if with_part:
        for i in range(n_part):
            @pl.when(now==1+2*i)
            def _(i=i):
                part_copy(i).wait()
                z_begin(i)
            for stage in range(3):
                @pl.when(now==5+2*i+2*stage)
                def _(i=i,stage=stage):
                    z_step(i,stage)
                    if stage==2:
                        result_do(i,lambda copy: copy.start())
    i0=pl.multiple_of(block_at(step,half)*RB,RB)
    q2=heads_ref[0,0,pl.ds(i0,RB)]
    v2=heads_ref[0,2]
    do2=buf[pair,pl.ds(i0,RB)]
    lane=lanes((RB,128))
    row=lax.broadcasted_iota(jnp.int32,(RB,128),0)
    t=lax.broadcasted_iota(jnp.int32,(n,128),0)
    c=lanes((n,128))
    left=(t<i0-128).astype(F32)
    kx_ref[:,128:256]=jnp.where(c==0,left,jnp.where(c==1,1.0,0.0)).astype(BF)
    dqs=[]
    for h in range(2):
        head=(lane<64) if h==0 else (lane>=64)
        doh=jnp.where(head,do2,jnp.zeros_like(do2))
        qh=jnp.where(head,q2,jnp.zeros_like(q2))
        p=p_ref[h]
        dp=dot(doh,v2,1,1)
        pf=p.astype(F32)
        d=jnp.sum(pf*dp,axis=1,keepdims=True)
        dsf=pf*(dp-d)
        ds=dsf.astype(BF)
        ds_ref[:,PADL:PADL+n]=ds.astype(F32)
        dva[...]+=dot(doh,p,0,0)
        dka[...]+=dot(qh,ds,0,0)
        dqx=dot(ds,kx_ref[...],1,0)
        dq,sums=dqx[:,0:128],dqx[:,128:256]
        win=ds_ref[:,pl.ds(i0,WIN)]
        j=band_offset()
        inleft=jnp.sum(jnp.where(j<=0,win,0.0),axis=1,keepdims=True)
        drel=jnp.concatenate([win[8*g:8*g+8,LEFT+8*g:LEFT+8*g+128] for g in range(RB//8)],axis=0)
        for bit in (1,2,4):
            drel=jnp.where((row&bit)!=0,pltpu.roll(drel,128-bit,1),drel)
        drel=jnp.where((lane>0)&(lane<LEFT+RIGHT),drel,0.0)
        bandsum=jnp.sum(drel,axis=1,keepdims=True)
        l=sums[:,0:1]+inleft
        r=sums[:,1:2]-l-bandsum
        drel=jnp.where(lane==0,l,jnp.where(lane==LEFT+RIGHT,r,drel)).astype(BF)
        dq=dq+dot(drel,wide_ref[...],1,1)
        dqs.append(dq)
        dea[...]+=dot(drel,qh,0,0)
    dq=(jnp.where(lane<64,dqs[0],dqs[1])*HEAD_DIM**-0.5).astype(BF)
    @pl.when(step<2)
    def _():
        stage_q[pair,step]=dq
        leave_q(pair,step,half).start()
    @pl.when(step>=2)
    def _():
        dqkv[pl.ds(pl.multiple_of((step-2)*RB,RB),RB),columns(0,half,pair)]=dq
    @pl.when(step==STEPS-1)
    def _():
        for i,acc in enumerate((dka,dva)):
            mine=acc[:,pl.ds(at,own)]
            theirs=acc[:,pl.ds(pl.multiple_of((1-half)*own,own),own)]
            stage_kv[pair,i]=jnp.transpose(theirs).astype(BF)
            leave_kv(pair,i,half).start()
            dqkv[:,columns(i+1,half,pair)]=jnp.transpose(mine).astype(BF)
    @pl.when((pair==pairs-1)&(step==STEPS-1))
    def _():
        for a in range(pairs):
            for b in range(2):
                leave_q(a,b,half).wait_send()
                leave_kv(a,b,half).wait_send()
        for a in range(pairs):
            for b in range(2):
                leave_q(a,b,1-half).wait_recv()
                leave_kv(a,b,1-half).wait_recv()
        dqkv_ref[...]=dqkv[...]
        de_ref[...]=dea[...]
        if with_part:
            for i in range(n_part):
                result_do(i,lambda copy: copy.wait())


def tables(distance):
    e=distance.T
    wide=jnp.concatenate([e,jnp.broadcast_to(e[:,72:73],(64,120)),jnp.broadcast_to(e[:,0:1],(64,WIN-193))],axis=1)
    wide=jnp.concatenate([wide,wide],axis=0)
    ends=jnp.concatenate([e[:,0:1],e[:,0:1],e[:,72:73],e[:,72:73],jnp.zeros((64,124),e.dtype)],axis=1)
    ends=jnp.concatenate([ends,ends],axis=0)
    return wide,ends

def attend(mine,other,length,wide,ends):
    pairs,_,own,_=mine.shape; n=2*own
    dma=pltpu.SemaphoreType.DMA
    whole=lambda *shape: pl.BlockSpec(shape,lambda a,b:(0,)*len(shape))
    anywhere=pl.BlockSpec(memory_space=pl.ANY)
    return pl.pallas_call(fwd_kernel,
        grid=(pairs,STEPS),
        in_specs=[pl.BlockSpec(memory_space=pltpu.SMEM),whole(128,WIN),whole(128,128),anywhere,anywhere],
        out_specs=[pl.BlockSpec((2,RB,n),lambda a,b:(a,b,0)),pl.BlockSpec((1,3,n,128),lambda a,b:(a,0,0,0)),whole(own,2*own)],
        out_shape=[jax.ShapeDtypeStruct((2*pairs,n,n),BF),jax.ShapeDtypeStruct((pairs,3,n,128),BF),jax.ShapeDtypeStruct((own,2*own),BF)],
        scratch_shapes=[pltpu.VMEM((RB,PADL+n+256),F32),pltpu.VMEM((n,256),BF),pltpu.VMEM((pairs,3,n,128),BF),pltpu.VMEM((own,2*own),BF),pltpu.VMEM((pairs,2,RB,128),BF),
            dma((pairs,)),dma((pairs,)),dma((pairs,)),dma((pairs,2)),dma((pairs,2))],
        compiler_params=pltpu.CompilerParams(vmem_limit_bytes=58<<20,collective_id=1,has_side_effects=True),
        cost_estimate=pl.CostEstimate(flops=40_000_000_000,bytes_accessed=120_000_000,transcendentals=0),
        name="attend_fwd",
    )(length,wide,ends,mine,other)

def attend_back(heads,p,wide,mine,other,part=None):
    pairs,_,n,_=heads.shape; own=n//2
    dma=pltpu.SemaphoreType.DMA
    whole=lambda *shape: pl.BlockSpec(shape,lambda a,b:(0,)*len(shape))
    anywhere=pl.BlockSpec(memory_space=pl.ANY)
    with_part=part is not None
    extra=[pltpu.VMEM(part.shape,BF)]*3+[dma((part.shape[0],))]*2+[dma((part.shape[0],3))]*2 if with_part else []
    return pl.pallas_call(functools.partial(bwd_kernel,with_part),
        grid=(pairs,STEPS),
        in_specs=[pl.BlockSpec((1,3,n,128),lambda a,b:(a,0,0,0)),pl.BlockSpec((2,RB,n),lambda a,b:(a,b,0)),whole(128,128),anywhere,anywhere]+[anywhere]*with_part,
        out_specs=[whole(own,6*own),whole(128,128)]+[anywhere]*with_part,
        out_shape=[jax.ShapeDtypeStruct((own,6*own),BF),jax.ShapeDtypeStruct((128,128),F32)]+([jax.ShapeDtypeStruct(part.shape,BF)] if with_part else []),
        scratch_shapes=[pltpu.VMEM((RB,PADL+n+256),F32),pltpu.VMEM((n,256),BF),pltpu.VMEM((128,n),F32),pltpu.VMEM((128,n),F32),pltpu.VMEM((128,128),F32),
            pltpu.VMEM((pairs,n,128),BF),pltpu.VMEM((own,6*own),BF),pltpu.VMEM((pairs,2,RB,128),BF),pltpu.VMEM((pairs,2,own,128),BF),
            dma((pairs,)),dma((pairs,)),dma((pairs,)),dma((pairs,2)),dma((pairs,2)),dma((pairs,2)),dma((pairs,2))]+extra,
        compiler_params=pltpu.CompilerParams(vmem_limit_bytes=58<<20,collective_id=2,has_side_effects=True),
        cost_estimate=pl.CostEstimate(flops=50_000_000_000,bytes_accessed=150_000_000,transcendentals=0),
        name="attend_bwd",
    )(heads,p,wide[:,0:128],mine,other,*([part] if with_part else []))


EPSILON = 1e-05
HALF = 0.5
CUT = 256
VMEM = 56 << 20


def flat(ref):
    value = ref[...]
    return value.reshape(-1, value.shape[-1])


def cuts(count):
    return [pl.ds(i, CUT) for i in range(0, count, CUT)]


def normal(v):
    c = v - jnp.mean(v, axis=-1, keepdims=True)
    r = lax.rsqrt(jnp.mean(c * c, axis=-1, keepdims=True) + EPSILON)
    return c * r, r


def normal_back(dy, unit, r, gain):
    a = dy * gain
    return (a - jnp.mean(a, axis=-1, keepdims=True) - unit * jnp.mean(a * unit, axis=-1, keepdims=True)) * r


def total(v):
    return jnp.sum(v, axis=0, keepdims=True)


def silu_slope(v):
    s = jax.nn.sigmoid(v)
    return s * (1.0 + v * (1.0 - s))


def call(kernel, grid, ins, outs, scratch=(), name=None, aliases=None, flops=0, moved=0):
    def spec(shape, block, where):
        if block is None:
            return pl.BlockSpec(shape, lambda *_: (0,) * len(shape))
        if block == "smem":
            return pl.BlockSpec(memory_space=pltpu.SMEM)
        if block == "any":
            return pl.BlockSpec(memory_space=pl.ANY)
        return pl.BlockSpec(block, where)

    return pl.pallas_call(
        kernel,
        grid=grid,
        in_specs=[spec(a.shape, b, w) for a, b, w in ins],
        out_specs=[spec(s, b, w) for s, _, b, w in outs],
        out_shape=[jax.ShapeDtypeStruct(s, d) for s, d, _, _ in outs],
        scratch_shapes=list(scratch),
        input_output_aliases=aliases or {},
        compiler_params=pltpu.CompilerParams(vmem_limit_bytes=VMEM),
        cost_estimate=pl.CostEstimate(flops=flops, bytes_accessed=moved, transcendentals=0),
        name=name,
    )(*[a for a, _, _ in ins])


def scr(shape, dtype):
    return pltpu.VMEM(shape, dtype)


def in_kernel(x_ref, vec_ref, bias_ref, w_ref, inner_ref, act_ref, act_t_ref, unit_t_ref, unit):
    @pl.when(pl.program_id(0) == 0)
    def _():
        for rows in cuts(x_ref.shape[0]):
            n, _ = normal(x_ref[rows, :].astype(F32))
            u = (n * vec_ref[0:1, :] + vec_ref[1:2, :]).astype(BF)
            unit[rows, :] = u
            unit_t_ref[:, rows] = u.T

    w = flat(w_ref)
    for rows in cuts(x_ref.shape[0]):
        s = dot(unit[rows, :], w, 1, 0) + bias_ref[0]
        inner_ref[rows, :] = s.astype(BF)
        a = (s * jax.nn.sigmoid(s)).astype(BF)
        act_ref[rows, :] = a
        act_t_ref[:, rows] = a.T


def ffn_in_forward(x, vec, bias, w, unit0):
    t, d = x.shape
    n, _, r, _ = w.shape
    k = bias.shape[0] // d
    bias = bias.reshape(k, 1, d)
    return call(
        in_kernel,
        (k,),
        [
            (x, None, None),
            (vec, None, None),
            (bias, (1, 1, d), lambda j: (j, 0, 0)),
            (w, (n, 1, r, d), lambda j: (0, unit0 + j, 0, 0)),
        ],
        [
            ((t, k * d), BF, (t, d), lambda j: (0, j)),
            ((t, k * d), BF, (t, d), lambda j: (0, j)),
            ((k * d, t), BF, (d, t), lambda j: (j, 0)),
            ((d, t), BF, None, None),
        ],
        [scr((t, d), BF)],
        name="ffn_in",
        flops=2 * t * d * d * k,
        moved=2 * d * d * k + 6 * t * d * k,
    )


def out_qkv_kernel(odd_ref, x_ref, act_ref, w_out_ref, w_qkv_ref, vec_ref, first_ref, unit_t_ref, mine_ref, other_ref, unit, acc):
    s = pl.program_id(0)
    t = x_ref.shape[0]

    @pl.when(s < 4)
    def _():
        w = flat(w_out_ref)
        for rows in cuts(t):
            p = dot(act_ref[rows, :], w, 1, 0)
            acc[rows, :] = p + jnp.where(s == 0, 0.0, acc[rows, :])

    @pl.when(s == 3)
    def _():
        for rows in cuts(t):
            first = x_ref[rows, :].astype(F32) + HALF * (acc[rows, :] + vec_ref[0:1, :])
            first_ref[rows, :] = first
            n, _ = normal(first)
            u = (n * vec_ref[1:2, :] + vec_ref[2:3, :]).astype(BF)
            unit[rows, :] = u
            unit_t_ref[:, rows] = u.T

    @pl.when(s >= 4)
    def _():
        w = flat(w_qkv_ref)
        odd = odd_ref[0] == 1
        half = w.shape[1] // 2
        scale = jnp.where(s == 4, HEAD_DIM**-0.5, 1.0)
        b = jnp.where(s == 4, vec_ref[3:4, :], jnp.where(s == 6, vec_ref[4:5, :], 0.0))
        for rows in cuts(t):
            y = (dot(unit[rows, :], w, 1, 0) + b) * scale
            low, high = y[:, :half], y[:, half:]
            mine = jnp.where(odd, high, low).astype(BF)
            other = jnp.where(odd, low, high).astype(BF)
            for part in range(half // 128):
                cols = slice(part * 128, part * 128 + 128)
                mine_ref[part, 0, rows, :] = mine[:, cols]
                other_ref[part, 0, rows, :] = other[:, cols]


def out_qkv_forward(odd, x, act, w, vec):
    t, d = x.shape
    n, _, r, _ = w.shape
    return call(
        out_qkv_kernel,
        (7,),
        [
            (odd, "smem", None),
            (x, None, None),
            (act, (t, d), lambda s: (0, jnp.minimum(s, 3))),
            (w, (n // 4, 4, r, d), lambda s: (jnp.minimum(s, 3), 0, 0, 0)),
            (w, (n, 1, r, d), lambda s: (0, jnp.maximum(s, 4), 0, 0)),
            (vec, None, None),
        ],
        [
            ((t, d), F32, None, None),
            ((d, t), BF, None, None),
            ((d // 256, 3, t, 128), BF, (d // 256, 1, t, 128), lambda s: (0, jnp.maximum(s - 4, 0), 0, 0)),
            ((d // 256, 3, t, 128), BF, (d // 256, 1, t, 128), lambda s: (0, jnp.maximum(s - 4, 0), 0, 0)),
        ],
        [scr((t, d), BF), scr((t, d), F32)],
        name="out_qkv",
        flops=14 * t * d * d,
        moved=14 * d * d + 20 * t * d,
    )


def mid_kernel(first_ref, mixed_ref, w_attn_ref, w_in_ref, vec_ref, second_ref, mixed_t_ref, unit_t_ref, val_ref, sig_ref, gated_ref, unit, val):
    s = pl.program_id(0)
    t = first_ref.shape[0]

    @pl.when(s == 0)
    def _():
        w = flat(w_attn_ref)
        for rows in cuts(t):
            m = mixed_ref[rows, :]
            mixed_t_ref[:, rows] = m.T
            second = first_ref[rows, :] + dot(m, w, 1, 0) + vec_ref[0:1, :]
            second_ref[rows, :] = second
            n, _ = normal(second)
            u = (n * vec_ref[1:2, :] + vec_ref[2:3, :]).astype(BF)
            unit[rows, :] = u
            unit_t_ref[:, rows] = u.T

    @pl.when(s == 1)
    def _():
        w = flat(w_in_ref)
        for rows in cuts(t):
            v = dot(unit[rows, :], w, 1, 0) + vec_ref[3:4, :]
            val[rows, :] = v
            val_ref[rows, :] = v.astype(BF)

    @pl.when(s == 2)
    def _():
        w = flat(w_in_ref)
        for rows in cuts(t):
            g = jax.nn.sigmoid(dot(unit[rows, :], w, 1, 0) + vec_ref[4:5, :])
            sig_ref[rows, :] = g.astype(BF)
            gated_ref[rows, :] = (val[rows, :] * g).astype(BF)


def mid_forward(first, mixed, w, u_attn, u_in, vec):
    t, d = first.shape
    n, _, r, _ = w.shape
    return call(
        mid_kernel,
        (3,),
        [
            (first, None, None),
            (mixed, None, None),
            (w, (n, 1, r, d), lambda s: (0, u_attn, 0, 0)),
            (w, (n, 1, r, d), lambda s: (0, u_in + jnp.maximum(s - 1, 0), 0, 0)),
            (vec, None, None),
        ],
        [((t, d), F32, None, None), ((d, t), BF, None, None), ((d, t), BF, None, None)]
        + [((t, d), BF, None, None)] * 3,
        [scr((t, d), BF), scr((t, d), F32)],
        name="mid",
        flops=6 * t * d * d,
        moved=6 * d * d + 20 * t * d,
    )


ROWS = 32
COLS = 256


def shifted(window, b):
    return window if b == 0 else pltpu.roll(window, window.shape[0] - b, 0)


def fir(pad, taps, offset, count, width, start, write, turned=False):
    reach = taps.shape[0]
    for c in range(0, width, COLS):
        cols = slice(c, c + COLS)

        def body(i, _):
            base = pl.multiple_of(i * ROWS, ROWS)
            window = pad[pl.ds(base, ROWS + 32), cols]
            acc = start(cols)
            for b in range(8):
                sh = shifted(window, b)
                for a in range(0, 5):
                    m = 8 * a + b - offset
                    if 0 <= m < reach:
                        tap = reach - 1 - m if turned else m
                        acc = acc + taps[tap : tap + 1, cols] * sh[8 * a : 8 * a + ROWS]
            write(pl.ds(base, ROWS), cols, acc)
            return 0

        lax.fori_loop(0, count // ROWS, body, 0)


def conv_kernel(gated_ref, halo_ref, taps_ref, vec_ref, second_ref, w_ref, conv_ref, act_t_ref, third_ref, pad):
    t, d = gated_ref.shape
    pad[0:32, :] = halo_ref[...].astype(F32)
    for rows in cuts(t):
        pad[pl.ds(rows.start + 32, CUT), :] = gated_ref[rows, :].astype(F32)

    def write(rows, cols, acc):
        conv_ref[rows, cols] = acc

    fir(pad, taps_ref, 2, t, d, lambda cols: jnp.broadcast_to(vec_ref[0:1, cols], (ROWS, COLS)), write)
    w = flat(w_ref)
    for rows in cuts(t):
        n, _ = normal(conv_ref[rows, :])
        u = n * vec_ref[1:2, :] + vec_ref[2:3, :]
        a = (u * jax.nn.sigmoid(u)).astype(BF)
        act_t_ref[:, rows] = a.T
        third_ref[rows, :] = second_ref[rows, :] + dot(a, w, 1, 0) + vec_ref[3:4, :]


def conv_forward(gated, halo, taps, vec, second, w, unit0):
    t, d = gated.shape
    n, _, r, _ = w.shape
    return call(
        conv_kernel,
        (1,),
        [
            (gated, None, None),
            (halo, None, None),
            (taps, None, None),
            (vec, None, None),
            (second, None, None),
            (w, (n, 1, r, d), lambda s: (0, unit0, 0, 0)),
        ],
        [((t, d), F32, None, None), ((d, t), BF, None, None), ((t, d), F32, None, None)],
        [scr((t + 32, d), F32)],
        name="conv",
        flops=2 * t * d * d,
        moved=2 * d * d + 16 * t * d,
    )


def out_last_kernel(x_ref, act_ref, w_ref, cot_ref, vec_ref, out_ref, d_ref, sums_ref, acc):
    s = pl.program_id(0)
    t = x_ref.shape[0]
    w = flat(w_ref)
    for rows in cuts(t):
        p = dot(act_ref[rows, :], w, 1, 0)
        acc[rows, :] = p + jnp.where(s == 0, 0.0, acc[rows, :])

    @pl.when(s == 3)
    def _():
        sums_ref[...] = jnp.zeros_like(sums_ref)
        for rows in cuts(t):
            fourth = x_ref[rows, :] + HALF * (acc[rows, :] + vec_ref[0:1, :])
            n, r = normal(fourth)
            out_ref[rows, :] = (n * vec_ref[1:2, :] + vec_ref[2:3, :]).astype(BF)
            dy = cot_ref[rows, :].astype(F32)
            d_ref[rows, :] = normal_back(dy, n, r, vec_ref[1:2, :])
            sums_ref[0:1, :] += total(dy * n)
            sums_ref[1:2, :] += total(dy)


def out_last(x, act, w, block0, cot, vec):
    t, d = x.shape
    n, _, r, _ = w.shape
    return call(
        out_last_kernel,
        (4,),
        [
            (x, None, None),
            (act, (t, d), lambda s: (0, s)),
            (w, (n // 4, 4, r, d), lambda s: (s, block0, 0, 0)),
            (cot, None, None),
            (vec, None, None),
        ],
        [((t, d), BF, None, None), ((t, d), F32, None, None), ((8, d), F32, None, None)],
        [scr((t, d), F32)],
        name="out_last",
        flops=8 * t * d * d,
        moved=8 * d * d + 20 * t * d,
    )


def ffn_hidden_kernel(d_ref, inner_ref, w_ref, dinner_ref, dout_ref, dbias_ref, sums_ref):
    t = d_ref.shape[0]

    @pl.when(pl.program_id(0) == 0)
    def _():
        sums_ref[...] = jnp.zeros_like(sums_ref)
        for rows in cuts(t):
            v = (HALF * d_ref[rows, :]).astype(BF)
            dout_ref[rows, :] = v
            sums_ref[0:1, :] += total(v.astype(F32))

    w = flat(w_ref)
    dbias = 0.0
    for rows in cuts(t):
        da = dot(dout_ref[rows, :], w, 1, 1)
        v = (da * silu_slope(inner_ref[rows, :].astype(F32))).astype(BF)
        dinner_ref[rows, :] = v
        dbias = dbias + total(v.astype(F32))
    dbias_ref[0] = dbias


def ffn_hidden_back(dy, inner, w, block0):
    t, d = dy.shape
    n, _, r, _ = w.shape
    k = inner.shape[1] // d
    return call(
        ffn_hidden_kernel,
        (k,),
        [
            (dy, None, None),
            (inner, (t, d), lambda j: (0, j)),
            (w, (n // 4, 4, r, d), lambda j: (j, block0, 0, 0)),
        ],
        [
            ((t, k * d), BF, (t, d), lambda j: (0, j)),
            ((t, d), BF, None, None),
            ((k, 1, d), F32, (1, 1, d), lambda j: (j, 0, 0)),
            ((8, d), F32, None, None),
        ],
        name="ffn_hidden_back",
        flops=2 * t * d * d * k,
        moved=2 * d * d * k + 4 * t * d * k,
    )


def norm_input_kernel(k, dy_ref, g_ref, x_ref, w_ref, vec_ref, d_ref, sums_ref, acc):
    s = pl.program_id(0)
    t = x_ref.shape[0]
    w = flat(w_ref)
    for rows in cuts(t):
        p = dot(g_ref[rows, :], w, 1, 1)
        acc[rows, :] = p + jnp.where(s == 0, 0.0, acc[rows, :])

    @pl.when(s == k - 1)
    def _():
        sums_ref[...] = jnp.zeros_like(sums_ref)
        for rows in cuts(t):
            n, r = normal(x_ref[rows, :].astype(F32))
            du = acc[rows, :]
            d_ref[rows, :] = (dy_ref[rows, :] + normal_back(du, n, r, vec_ref[0:1, :])).astype(d_ref.dtype)
            sums_ref[0:1, :] += total(du * n)
            sums_ref[1:2, :] += total(du)


def norm_input_back(dy, g, x, w, unit0, gain, out_type=F32):
    t, d = dy.shape
    n, _, r, _ = w.shape
    k = g.shape[1] // d
    return call(
        functools.partial(norm_input_kernel, k),
        (k,),
        [
            (dy, None, None),
            (g, (t, d), lambda j: (0, j)),
            (x, None, None),
            (w, (n, 1, r, d), lambda j: (0, unit0 + j, 0, 0)),
            (gain, None, None),
        ],
        [((t, d), out_type, None, None), ((8, d), F32, None, None)],
        [scr((t, d), F32)],
        name="norm_input_back",
        flops=2 * t * d * d * k,
        moved=2 * d * d * k + 2 * t * d * k + 12 * t * d,
    )


def weight_kernel(left_ref, right_ref, *rest):
    out_ref = rest[-1]
    rows, d = left_ref.shape[0], out_ref.shape[-1]
    a, b, r, _ = out_ref.shape
    step = max(256, 4 * r)
    for i in range(0, rows, step):
        value = dot(left_ref[i : i + step, :], right_ref[...], 1, 0).astype(BF)
        if b == 1:
            out_ref[pl.ds(i // r, step // r), 0] = value.reshape(step // r, r, d)
        else:
            out_ref[pl.ds(i // (4 * r), step // (4 * r))] = value.reshape(step // (4 * r), 4, r, d)


def weight_grad(left_t, right, n, units, at, by_rows, into=None):
    d = 1024
    t = left_t.shape[1]
    r = d // n
    if by_rows:
        k = left_t.shape[0] // d
        ins = [(left_t, (d, t), lambda j: (j, 0)), (right, None, None)]
        block, where = (n // 4, 4, r, d), lambda j: (j, at // 4, 0, 0)
    else:
        k = right.shape[1] // d
        ins = [(left_t, None, None), (right, (t, d), lambda j: (0, j))]
        block, where = (n, 1, r, d), lambda j: (0, at + j, 0, 0)
    aliases = None
    if into is not None:
        ins.append((into, "any", None))
        aliases = {2: 0}
    return call(
        weight_kernel,
        (k,),
        ins,
        [((n, units, r, d), BF, block, where)],
        name="weight_grad",
        aliases=aliases,
        flops=2 * t * d * d * k,
        moved=2 * d * d * k + 2 * t * d * (k + 1),
    )[0]


def conv_out_kernel(d_ref, conv_ref, w_ref, vec_ref, dconv_ref, dout_ref, sums_ref):
    t = d_ref.shape[0]
    sums_ref[...] = jnp.zeros_like(sums_ref)
    w = flat(w_ref)
    for rows in cuts(t):
        dout = d_ref[rows, :].astype(BF)
        dout_ref[rows, :] = dout
        da = dot(dout, w, 1, 1)
        n, r = normal(conv_ref[rows, :])
        du = da * silu_slope(n * vec_ref[0:1, :] + vec_ref[1:2, :])
        dconv = normal_back(du, n, r, vec_ref[0:1, :])
        dconv_ref[rows, :] = dconv
        sums_ref[0:1, :] += total(dout.astype(F32))
        sums_ref[1:2, :] += total(du * n)
        sums_ref[2:3, :] += total(du)
        sums_ref[3:4, :] += total(dconv)


def conv_out_back(d3, conv, w, unit0, vec):
    t, d = d3.shape
    n, _, r, _ = w.shape
    return call(
        conv_out_kernel,
        (1,),
        [
            (d3, None, None),
            (conv, None, None),
            (w, (n, 1, r, d), lambda s: (0, unit0, 0, 0)),
            (vec, None, None),
        ],
        [((t, d), F32, None, None), ((t, d), BF, None, None), ((8, d), F32, None, None)],
        name="conv_out_back",
        flops=2 * t * d * d,
        moved=2 * d * d + 16 * t * d,
    )


def mid_back_kernel(odd_ref, dconv_ref, follow_ref, taps_ref, val_ref, sig_ref, second_ref, d3_ref, w_in_ref, w_attn_ref, vec_ref, d2_ref, dout_ref, dglu_ref, mine_ref, other_ref, sums_ref, pad, acc):
    s = pl.program_id(0)
    t, d = dconv_ref.shape

    @pl.when(s == 0)
    def _():
        for rows in cuts(t):
            pad[rows, :] = dconv_ref[rows, :]
        pad[t : t + 32, :] = follow_ref[...]

        def write(rows, cols, dgated):
            sig = sig_ref[rows, cols].astype(F32)
            dval = dgated * sig
            dglu_ref[rows, cols] = dval.astype(BF)
            dgate = dval * val_ref[rows, cols].astype(F32) * (1.0 - sig)
            dglu_ref[rows, cols.start + d : cols.stop + d] = dgate.astype(BF)

        fir(pad, taps_ref, 0, t, d, lambda cols: jnp.zeros((ROWS, COLS), F32), write, turned=True)
        sums_ref[...] = jnp.zeros_like(sums_ref)
        for rows in cuts(t):
            sums_ref[0:1, :] += total(dglu_ref[rows, :d].astype(F32))
            sums_ref[1:2, :] += total(dglu_ref[rows, d:].astype(F32))
        w = flat(w_in_ref)
        for rows in cuts(t):
            acc[rows, :] = dot(dglu_ref[rows, :d], w, 1, 1)

    @pl.when(s == 1)
    def _():
        w = flat(w_in_ref)
        w_attn = flat(w_attn_ref)
        odd = odd_ref[0] == 1
        half = d // 2
        for rows in cuts(t):
            du = acc[rows, :] + dot(dglu_ref[rows, d:], w, 1, 1)
            n, r = normal(second_ref[rows, :])
            d2 = d3_ref[rows, :] + normal_back(du, n, r, vec_ref[0:1, :])
            sums_ref[2:3, :] += total(du * n)
            sums_ref[3:4, :] += total(du)
            d2_ref[rows, :] = d2
            dout = d2.astype(BF)
            dout_ref[rows, :] = dout
            sums_ref[4:5, :] += total(dout.astype(F32))
            dm = dot(dout, w_attn, 1, 1)
            low, high = dm[:, :half], dm[:, half:]
            mine = jnp.where(odd, high, low).astype(BF)
            other = jnp.where(odd, low, high).astype(BF)
            for part in range(half // 128):
                cols = slice(part * 128, part * 128 + 128)
                mine_ref[part, rows, :] = mine[:, cols]
                other_ref[part, rows, :] = other[:, cols]


def mid_back(odd, dconv, follow, taps, val, sig, second, d3, w, u_attn, u_in, gain):
    t, d = d3.shape
    n, _, r, _ = w.shape
    return call(
        mid_back_kernel,
        (2,),
        [
            (odd, "smem", None),
            (dconv, None, None),
            (follow, None, None),
            (taps, None, None),
            (val, None, None),
            (sig, None, None),
            (second, None, None),
            (d3, None, None),
            (w, (n, 1, r, d), lambda s: (0, u_in + s, 0, 0)),
            (w, (n, 1, r, d), lambda s: (0, u_attn, 0, 0)),
            (gain, None, None),
        ],
        [
            ((t, d), F32, None, None),
            ((t, d), BF, None, None),
            ((t, 2 * d), BF, None, None),
            ((d // 256, t, 128), BF, None, None),
            ((d // 256, t, 128), BF, None, None),
            ((8, d), F32, None, None),
        ],
        [scr((t + 32, d), F32), scr((t, d), F32)],
        name="mid_back",
        flops=6 * t * d * d,
        moved=6 * d * d + 24 * t * d,
    )


def taps_kernel(dconv_ref, gated_ref, halo_ref, out_ref, pad, part):
    t, d = dconv_ref.shape
    reach = out_ref.shape[0]
    pad[0:32, :] = halo_ref[...].astype(F32)
    for rows in cuts(t):
        pad[pl.ds(rows.start + 32, CUT), :] = gated_ref[rows, :].astype(F32)
    part[...] = jnp.zeros_like(part)
    for c in range(0, d, COLS):
        cols = slice(c, c + COLS)

        def body(i, _):
            base = pl.multiple_of(i * ROWS, ROWS)
            window = pad[pl.ds(base, ROWS + 32), cols]
            here = dconv_ref[pl.ds(base, ROWS), cols]
            for b in range(8):
                sh = shifted(window, b)
                for a in range(0, 5):
                    m = 8 * a + b - 2
                    if 0 <= m < reach:
                        v = here * sh[8 * a : 8 * a + ROWS]
                        v = (v[0:8] + v[8:16]) + (v[16:24] + v[24:32])
                        part[8 * m : 8 * m + 8, cols] += v
            return 0

        lax.fori_loop(0, t // ROWS, body, 0)
    for m in range(reach):
        out_ref[m : m + 1, :] = total(part[8 * m : 8 * m + 8, :])


def taps_grad(dconv, gated, halo, reach):
    t, d = dconv.shape
    return call(
        taps_kernel,
        (1,),
        [(dconv, None, None), (gated, None, None), (halo, None, None)],
        [((reach, d), F32, None, None)],
        [scr((t + 32, d), F32), scr((8 * reach, d), F32)],
        name="taps_grad",
        flops=2 * t * d * reach,
        moved=6 * t * d,
    )[0]


ORDER = [
    ("q", 0), ("q", 1), ("q", 2), ("m", 0), ("m", 1), ("in", 0), ("m", 2), ("in", 1), ("m", 3),
    ("in", 2), ("out", 0), ("in", 3), ("out", 1), ("out", 2), ("out", 3),
]
N_CHUNK = len(ORDER)
FIRST_IN = 5
LAST_IN = 11
AHEAD = 2
HELD = 6


def flipped_bit(index, mask):
    return index + mask - 2 * mask * lax.rem(lax.div(index, jnp.int32(mask)), jnp.int32(2))


def thin(count):
    return [pl.ds(i, 128) for i in range(0, count, 128)]


def last_kernel(
    gain_ref, table_ref, sums_2_ref, sums_3_ref, sums_4_ref, sums_5_ref, sums_7_ref, dbias_ref,
    d2_ref, first_ref, x_ref, dconv_ref, gated_ref, halo_ref, part_ref, dqkv_ref, unit_q_ref, act_ref, unit_ref, inner_ref, w_out_ref, w_in_ref,
    mixed_ref, dout_2_ref, unit_2_ref, dglu_ref, act_c_ref, dout_3_ref,
    out_ref, out_part_ref, small_out_ref, table_out_ref, dx_ref,
    odd, even, core, first, second, whole, near, far,
    left, right, wo, wi, inner, dout, acc,
    small_0, small_y, small_x, small_c, small_z, table_got, d0, d1, some, dconv, gated, pad, taps,
    left_sem, right_sem, wo_sem, wi_sem, inner_sem, out_sem, part_sem, some_sem, taps_sem,
    core_send, core_recv, first_send, first_recv, second_send, second_recv,
    z_send, z_recv, small_send, small_recv, table_send, table_recv, dx_send, dx_recv, dx_sem, free_sem,
):
    r, d = out_ref.shape[1:]
    n_part = part_ref.shape[0]
    t = x_ref.shape[0]
    cut = r // 2
    me = lax.axis_index("fsdp")
    place = lax.axis_index("seq")
    two, four = jnp.int32(2), jnp.int32(4)
    chip = lax.div(me, two)
    bit_c, bit_x, bit_y = lax.rem(me, two), lax.rem(chip, two), lax.div(me, four)
    middle = lax.rem(lax.div(place + 1, two), two)
    to_c = {"fsdp": flipped_bit(me, 1)}
    to_x = {"fsdp": flipped_bit(me, 2)}
    to_y = {"fsdp": flipped_bit(me, 4)}
    to_1 = {"seq": flipped_bit(place, 1)}
    to_2 = {"seq": 3 - place}

    barrier = pltpu.get_barrier_semaphore()
    for device in (to_c, to_x, to_y, to_1, to_2, {"seq": flipped_bit(place, 2)}):
        pl.semaphore_signal(barrier, inc=1, device_id=device, device_id_type=MESH)
    pl.semaphore_wait(barrier, 6)

    def send(src, dst, send_sem, recv_sem, device):
        return pltpu.make_async_remote_copy(
            src_ref=src, dst_ref=dst, send_sem=send_sem, recv_sem=recv_sem, device_id=device, device_id_type=MESH
        )

    def at_2(c):
        return lax.rem(c, two)

    def at_3(c):
        return lax.rem(c, jnp.int32(3))

    def on(c, begin, end, work):
        pl.when((c >= begin) & (c < end))(lambda: work(c))

    def factor_copies(c, name, unit):
        cols = slice(unit * d, unit * d + d)
        lefts = {"q": unit_q_ref, "in": unit_ref, "m": (mixed_ref, unit_2_ref, unit_2_ref, act_c_ref)[unit % 4]}
        rights = {
            "q": lambda: dqkv_ref.at[:, cols],
            "m": lambda: (
                dout_2_ref if unit == 0 else dout_3_ref if unit == 3 else dglu_ref.at[:, (unit - 1) * d : unit * d]
            ),
        }
        src = act_ref.at[:, unit] if name == "out" else lefts[name]
        copies = [pltpu.make_async_copy(src, left.at[at_2(c)], left_sem.at[at_2(c)])]
        if name in rights:
            copies.append(pltpu.make_async_copy(rights[name](), right.at[at_3(c)], right_sem.at[at_3(c)]))
        return copies

    def fetch(c):
        for i, (name, unit) in enumerate(ORDER):

            @pl.when(c == i)
            def _(i=i, name=name, unit=unit):
                for copy in factor_copies(c, name, unit):
                    copy.start()

    def fetched(c):
        pltpu.make_async_copy(unit_ref, left.at[at_2(c)], left_sem.at[at_2(c)]).wait()
        has_right = functools.reduce(
            jnp.logical_or, [c == i for i, (name, _) in enumerate(ORDER) if name in ("q", "m")]
        )

        @pl.when(has_right)
        def _():
            pltpu.make_async_copy(dout_2_ref, right.at[at_3(c)], right_sem.at[at_3(c)]).wait()

    def is_in(c):
        return (c >= FIRST_IN) & (c <= LAST_IN) & (at_2(c) == FIRST_IN % 2)

    def wo_copy(j):
        return pltpu.make_async_copy(w_out_ref.at[pl.ds(2 * j, 2), pl.ds(0, 4)], wo, wo_sem)

    def wi_copy(j):
        return pltpu.make_async_copy(w_in_ref.at[:, j], wi, wi_sem)

    def wq_copy(i):
        return pltpu.make_async_copy(w_out_ref.at[:, 4 + i], wi, wi_sem)

    def inner_copy(j):
        return pltpu.make_async_copy(inner_ref.at[:, pl.ds(pl.multiple_of(j * d, d), d)], inner, inner_sem)

    def x_copy():
        return pltpu.make_async_copy(x_ref, inner, inner_sem)

    row = 53

    def hidden(c):
        j = lax.div(c - FIRST_IN, two)
        wo_copy(j).wait()
        inner_copy(j).wait()
        w = wo[...].reshape(d, d)
        dbias = jnp.zeros((1, d), F32)
        for rows in thin(t):
            da = dot(dout[rows, :], w, 1, 1)
            v = (da * silu_slope(inner[rows, :].astype(F32))).astype(BF)
            right[at_3(c), rows, :] = v
            dbias = dbias + total(v.astype(F32))
        for dev in range(2):
            for q in range(4):
                cols = pl.ds(pl.multiple_of((2 * j + dev) * r, r), r)
                small_0[row + 3 + q : row + 4 + q, cols] = dbias[:, dev * 4 * r + q * r : dev * 4 * r + (q + 1) * r]

        @pl.when(j < 3)
        def _():
            wo_copy(j + 1).start()
            inner_copy(j + 1).start()

        @pl.when(j == 3)
        def _():
            x_copy().start()

    def product(c):
        for i in range(4):
            value = dot(left[at_2(c), 2 * i : 2 * i + 2].reshape(2 * r, t), right[at_3(c)], 1, 0).astype(BF)
            low, high = value[:r], value[r:]
            p = i + bit_x - 2 * bit_x * (i % 2)
            p = p + 2 * bit_y - 4 * bit_y * lax.div(p, two)
            even[at_2(c), p] = jnp.where(bit_c == 0, low, high)
            odd[at_2(c), p] = jnp.where(bit_c == 0, high, low)

    def through(c, fresh):
        wi_copy(0).wait()
        w = wi[...].reshape(d, d)
        for rows in thin(t):
            p = dot(right[at_3(c), rows, :], w, 1, 1)
            acc[rows, :] = p + jnp.where(fresh, 0.0, acc[rows, :])

    def back(c):
        j = lax.div(c - FIRST_IN, two)
        through(c, j == 0)
        pl.when(j < 3)(lambda: wi_copy(j + 1).start())

    def back_q(c):
        through(c, c == 0)
        pl.when(c < 2)(lambda: wq_copy(c + 1).start())
        pl.when(c == 2)(lambda: wi_copy(0).start())
        column = total(right[at_3(c)].astype(F32))

        @pl.when(c == 0)
        def _():
            small_0[11:12, :] = column

        @pl.when(c == 2)
        def _():
            small_0[12:13, :] = column
            middle_gradient()

    def middle_gradient():
        pltpu.make_async_copy(d2_ref, d1, some_sem).wait()
        for rows in thin(t):
            copy = pltpu.make_async_copy(first_ref.at[rows], some, some_sem)
            copy.start()
            copy.wait()
            n, scale = normal(some[...])
            du = acc[rows, :]
            value = d1[rows, :] + normal_back(du, n, scale, gain_ref[1:2, :])
            d1[rows, :] = value
            small_0[0:1, :] += total(du * n)
            small_0[5:6, :] += total(du)
            v = (HALF * value).astype(BF)
            dout[rows, :] = v
            small_0[row + 2 : row + 3, :] += total(v.astype(F32))

    def taps_copies(b):
        cols = pl.ds(pl.multiple_of(b * COLS, COLS), COLS)
        return [
            pltpu.make_async_copy(dconv_ref.at[:, cols], dconv, taps_sem.at[0]),
            pltpu.make_async_copy(halo_ref.at[:, cols], gated.at[pl.ds(0, 32)], taps_sem.at[1]),
            pltpu.make_async_copy(gated_ref.at[:, cols], gated.at[pl.ds(32, t)], taps_sem.at[2]),
        ]

    def taps_columns(b):
        for copy in taps_copies(b):
            copy.wait()
        pad[...] = gated[...].astype(F32)
        taps[...] = jnp.zeros_like(taps)
        reach = taps.shape[0] // 8

        def body(i, _):
            base = pl.multiple_of(i * ROWS, ROWS)
            window = pad[pl.ds(base, ROWS + 32), :]
            here = dconv[pl.ds(base, ROWS), :]
            for q in range(8):
                sh = shifted(window, q)
                for a in range(0, 5):
                    m = 8 * a + q - 2
                    if 0 <= m < reach:
                        v = here * sh[8 * a : 8 * a + ROWS]
                        taps[8 * m : 8 * m + 8, :] += (v[0:8] + v[8:16]) + (v[16:24] + v[24:32])
            return 0

        lax.fori_loop(0, t // ROWS, body, 0)
        cols = pl.ds(pl.multiple_of(b * COLS, COLS), COLS)
        for m in range(reach):
            small_0[18 + m : 19 + m, cols] = total(taps[8 * m : 8 * m + 8, :])

        @pl.when(b < d // COLS - 1)
        def _():
            for copy in taps_copies(b + 1):
                copy.start()

    def held_at(c):
        return lax.rem(c, jnp.int32(HELD))

    def core_copy(c):
        return send(odd.at[at_2(c)], core.at[held_at(c)], core_send.at[c], core_recv.at[c], to_c)

    def make(c):
        fetch(c + 1)
        fetched(c)

        is_out = functools.reduce(jnp.logical_or, [c == i for i, (name, _) in enumerate(ORDER) if name == "out"])

        @pl.when(is_out)
        def _():
            right[at_3(c)] = dout[...]

        pl.when(is_in(c))(lambda: hidden(c))
        product(c)
        pl.when(c >= HELD)(lambda: pl.semaphore_wait(free_sem, 1))
        core_copy(c).start()

    def make_back(c):
        pl.when(is_in(c))(lambda: back(c))
        pl.when(c < 3)(lambda: back_q(c))

    def first_copies(c):
        top, rest = pl.ds(0, cut), pl.ds(cut, cut)
        o = held_at(c)
        return [
            send(core.at[o, 1, top], first.at[o, 0, 0], first_send.at[c, 0], first_recv.at[c, 0], to_x),
            send(core.at[o, 3, top], first.at[o, 0, 1], first_send.at[c, 1], first_recv.at[c, 1], to_x),
            send(core.at[o, 2, rest], first.at[o, 1, 0], first_send.at[c, 2], first_recv.at[c, 2], to_y),
            send(core.at[o, 3, rest], first.at[o, 1, 1], first_send.at[c, 3], first_recv.at[c, 3], to_y),
        ]

    def second_copies(c):
        o = held_at(c)
        return [
            send(first.at[o, 0, 1], second.at[o, 0], second_send.at[c, 0], second_recv.at[c, 0], to_y),
            send(first.at[o, 1, 1], second.at[o, 1], second_send.at[c, 1], second_recv.at[c, 1], to_x),
        ]

    def add_core(c):
        core_copy(c).wait()
        o = held_at(c)

        def rows(i, _):
            at = pl.ds(pl.multiple_of(i * 32, 32), 32)
            for b in range(4):
                core[o, b, at] = (core[o, b, at].astype(F32) + even[at_2(c), b, at].astype(F32)).astype(BF)
            return 0

        lax.fori_loop(0, r // 32, rows, 0)
        for copy in first_copies(c):
            copy.start()

    def add_first(c):
        for copy in first_copies(c):
            copy.wait()
        o = held_at(c)

        def rows(i, _):
            at = pl.ds(pl.multiple_of(i * 32, 32), 32)
            low_at = pl.ds(pl.multiple_of(cut + i * 32, 32), 32)
            for b in range(2):
                first[o, 0, b, at] = (first[o, 0, b, at].astype(F32) + core[o, 2 * b, at].astype(F32)).astype(BF)
                first[o, 1, b, at] = (first[o, 1, b, at].astype(F32) + core[o, b, low_at].astype(F32)).astype(BF)
            return 0

        lax.fori_loop(0, cut // 32, rows, 0)

        @pl.when(c < N_CHUNK - HELD)
        def _():
            pl.semaphore_signal(free_sem, inc=1, device_id=to_c, device_id_type=MESH)

        for copy in second_copies(c):
            copy.start()

    def add_second(c):
        for copy in second_copies(c):
            copy.wait()
        o = held_at(c)
        whole[c, 0:cut] = (first[o, 0, 0].astype(F32) + second[o, 0].astype(F32)).astype(BF)
        whole[c, cut:r] = (first[o, 1, 0].astype(F32) + second[o, 1].astype(F32)).astype(BF)
        z_begin(c)

    z_begin, z_step = z_line(middle, to_1, to_2, whole, near, far, z_send, z_recv)

    def result_do(i, act):
        for is_middle, src in ((1, far), (0, near)):
            chunk = pltpu.make_async_copy(src.at[i], out_ref.at[i], out_sem.at[i])
            part = pltpu.make_async_copy(src.at[i], out_part_ref.at[i - N_CHUNK], out_sem.at[i])
            pl.when((middle == is_middle) & (i < N_CHUNK))(lambda chunk=chunk: act(chunk))
            pl.when((middle == is_middle) & (i >= N_CHUNK))(lambda part=part: act(part))

    def z_stage(i, stage):
        z_step(i, stage)
        if stage == 2:
            result_do(i, lambda copy: copy.start())

    wide = [d // 2, d // 4, d // 8]
    bits = [bit_y, bit_x, bit_c]
    held = [small_0, small_y, small_x, small_c]
    partner = [to_y, to_x, to_c, to_1, to_2]

    def columns(step, bit):
        return pl.ds(pl.multiple_of(bit * wide[step], wide[step]), wide[step])

    def small_copy(step):
        sems = (small_send.at[step], small_recv.at[step])
        if step < 3:
            return send(held[step].at[:, columns(step, 1 - bits[step])], held[step + 1], *sems, partner[step])
        if step == 3:
            return send(small_c, small_z.at[0], *sems, partner[step])
        return send(small_z.at[0], small_z.at[1], *sems, partner[step])

    def small_step(step):
        small_copy(step).wait()
        if step < 3:
            held[step + 1][...] += held[step][:, columns(step, bits[step])]
        elif step == 3:
            small_z[0] = small_z[0] + small_c[...]
        else:
            small_out_ref[...] = small_z[0] + small_z[1]
        if step < 4:
            small_copy(step + 1).start()

    def table_copy(step):
        src = table_ref if step == 0 else table_got.at[step - 1]
        return send(src, table_got.at[step], table_send.at[step], table_recv.at[step], partner[step])

    def table_step(step):
        table_copy(step).wait()
        before = table_ref[...] if step == 0 else table_got[step - 1]
        table_got[step] = table_got[step] + before
        if step < 4:
            table_copy(step + 1).start()
        else:
            table_out_ref[...] = table_got[step]

    mine, seq = lax.rem(place, two), lax.div(place, two)

    def dx_copy(h):
        return send(d0.at[pl.ds(h * (t // 2), t // 2)], dx_ref.at[seq], dx_send.at[h], dx_recv.at[seq], {"seq": 2 * mine + h})

    def dx_keep(h):
        return pltpu.make_async_copy(d0.at[pl.ds(h * (t // 2), t // 2)], dx_ref.at[seq], dx_sem)

    def dx_arrived(s):
        return send(d0.at[pl.ds(0, t // 2)], dx_ref.at[s], dx_send.at[0], dx_recv.at[s], to_1)

    def input_gradient():
        x_copy().wait()
        for rows in thin(t):
            n, scale = normal(inner[rows, :].astype(F32))
            du = acc[rows, :]
            d0[rows, :] = (d1[rows, :] + normal_back(du, n, scale, gain_ref[0:1, :])).astype(BF)
            small_0[row : row + 1, :] += total(du * n)
            small_0[row + 1 : row + 2, :] += total(du)
        for h in range(2):
            away = 2 * mine + h != place
            pl.when(away)(lambda h=h: dx_copy(h).start())
            pl.when(jnp.logical_not(away))(lambda h=h: dx_keep(h).start())
        small_copy(0).start()

    def part_copy(i):
        return pltpu.make_async_copy(part_ref.at[i], whole.at[N_CHUNK + i], part_sem.at[i])

    fetch(jnp.int32(0))
    wq_copy(0).start()
    pltpu.make_async_copy(d2_ref, d1, some_sem).start()
    for copy in taps_copies(jnp.int32(0)):
        copy.start()
    for i in range(n_part):
        part_copy(i).start()
    table_copy(0).start()
    wo_copy(0).start()
    inner_copy(0).start()
    small_0[...] = jnp.zeros_like(small_0)
    here = {1: (sums_2_ref, 2), 2: (sums_3_ref, 1), 3: (sums_4_ref, 0), 4: (sums_5_ref, 0), 6: (sums_2_ref, 3)}
    here.update({7: (sums_3_ref, 2), 8: (sums_4_ref, 1), 9: (sums_5_ref, 1), 10: (sums_7_ref, 0), 13: (sums_2_ref, 4)})
    here.update({14: (sums_2_ref, 0), 15: (sums_2_ref, 1), 16: (sums_3_ref, 3), 17: (sums_3_ref, 0)})
    for at, (ref, i) in here.items():
        small_0[at : at + 1, :] = ref[i : i + 1, :]
    for j in range(4):
        for dev in range(2):
            for q in range(4):
                cols = slice((2 * j + dev) * r, (2 * j + dev + 1) * r)
                small_0[49 + q : 50 + q, cols] = dbias_ref[j, :, (4 * dev + q) * r : (4 * dev + q + 1) * r]
    for i in range(n_part):
        part_copy(i).wait()
    for c in range(AHEAD):
        make(jnp.int32(c))

    def slot(k, _):
        on(k, 0, N_CHUNK, add_core)
        on(k - 1, 0, N_CHUNK, add_first)
        on(k - 2, 0, N_CHUNK, add_second)
        for stage in range(3):
            on(k - 3 - stage, 0, N_CHUNK, lambda c, stage=stage: z_stage(c, stage))
        on(k, 0, n_part, lambda i: z_begin(N_CHUNK + i))
        for stage in range(3):
            on(k - 1 - stage, 0, n_part, lambda i, stage=stage: z_stage(N_CHUNK + i, stage))
        make_back(k)
        on(k + AHEAD, 0, N_CHUNK, make)
        pl.when(k == LAST_IN)(input_gradient)
        on(k - 1, 0, d // COLS, taps_columns)
        for step in range(5):
            pl.when(k == step)(lambda step=step: table_step(step))
            pl.when(k == LAST_IN + 1 + step)(lambda step=step: small_step(step))
        return 0

    lax.fori_loop(0, N_CHUNK + 5, slot, 0)
    for h in range(2):
        away = 2 * mine + h != place
        pl.when(away)(lambda h=h: dx_copy(h).wait_send())
        pl.when(jnp.logical_not(away))(lambda h=h: dx_keep(h).wait())
    for s in range(2):
        from_away = 2 * s + lax.div(place, two) != place
        pl.when(from_away)(lambda s=s: dx_arrived(s).wait_recv())

    def settle(i, _):
        result_do(i, lambda copy: copy.wait())
        return 0

    lax.fori_loop(0, N_CHUNK + n_part, settle, 0)


def last_reduced(
    gain, table, sums, dbias, d2, first, tokens, dconv, gated, halo, part, dqkv, unit_q, act_t, unit_t, inner, w_out, w_in, mixed_t, dout_2, unit_2, dglu, act_c, dout_3
):
    n, _, r, d = w_in.shape
    t = tokens.shape[0]
    rows = 64
    k = N_CHUNK
    m = part.shape[0]
    z = k + m
    dma = pltpu.SemaphoreType.DMA
    anywhere = pl.BlockSpec(memory_space=pl.ANY)
    vmem = pl.BlockSpec(memory_space=pltpu.VMEM)
    return pl.pallas_call(
        last_kernel,
        in_specs=[vmem] * 8 + [anywhere] * 20,
        out_specs=[anywhere, anywhere, vmem, vmem, anywhere],
        out_shape=[
            jax.ShapeDtypeStruct((k, r, d), BF),
            jax.ShapeDtypeStruct((m, r, d), BF),
            jax.ShapeDtypeStruct((rows, d // 8), F32),
            jax.ShapeDtypeStruct(table.shape, F32),
            jax.ShapeDtypeStruct((2, t // 2, d), BF),
        ],
        scratch_shapes=[
            scr((2, 4, r, d), BF),
            scr((2, 4, r, d), BF),
            scr((HELD, 4, r, d), BF),
            scr((HELD, 2, 2, r // 2, d), BF),
            scr((HELD, 2, r // 2, d), BF),
            scr((z, r, d), BF),
            scr((z, r, d), BF),
            scr((z, r, d), BF),
            scr((2, n, r, t), BF),
            scr((3, t, d), BF),
            scr((2, 4, r, d), BF),
            scr((n, r, d), BF),
            scr((t, d), BF),
            scr((t, d), BF),
            scr((t, d), F32),
            scr((rows, d), F32),
            scr((rows, d // 2), F32),
            scr((rows, d // 4), F32),
            scr((rows, d // 8), F32),
            scr((2, rows, d // 8), F32),
            scr((5,) + table.shape, F32),
            scr((t, d), BF),
            scr((t, d), F32),
            scr((128, d), F32),
            scr((t, COLS), F32),
            scr((t + 32, COLS), BF),
            scr((t + 32, COLS), F32),
            scr((8 * 31, COLS), F32),
            dma((2,)),
            dma((3,)),
            dma,
            dma,
            dma,
            dma((z,)),
            dma((m,)),
            dma,
            dma((3,)),
            dma((k,)),
            dma((k,)),
            dma((k, 4)),
            dma((k, 4)),
            dma((k, 2)),
            dma((k, 2)),
            dma((z, 3)),
            dma((z, 3)),
            dma((5,)),
            dma((5,)),
            dma((5,)),
            dma((5,)),
            dma((2,)),
            dma((2,)),
            dma,
            pltpu.SemaphoreType.REGULAR,
        ],
        compiler_params=pltpu.CompilerParams(vmem_limit_bytes=60 << 20, collective_id=0, has_side_effects=True),
        cost_estimate=pl.CostEstimate(flops=100_000_000_000, bytes_accessed=400_000_000, transcendentals=0),
        name="last",
    )(
        gain, table, *sums, dbias, d2, first, tokens, dconv, gated, halo, part, dqkv, unit_q.reshape(n, r, t), act_t.reshape(n, 4, r, t),
        unit_t.reshape(n, r, t), inner, w_out, w_in,
        mixed_t.reshape(n, r, t), dout_2, unit_2.reshape(n, r, t), dglu, act_c.reshape(n, r, t), dout_3,
    )


PLACE = {item: i for i, item in enumerate(ORDER)}


def finish_kernel(n_tap, main, in_b, out_b, small, table, g_in, g_out, g_qkv, g_attn, g_conv_in, g_conv_out, g_taps, g_gain, g_shift, g_bias, g_table):
    d = main.shape[-1]

    def of(name, unit):
        return main[PLACE[name, unit]].astype(F32)

    for u in range(4):
        cols = slice(u * d, (u + 1) * d)
        g_in[0, :, cols] = of("in", u)
        g_in[1, :, cols] = in_b[u].astype(F32)
        g_out[0, u] = of("out", u)
        g_out[1, u] = out_b[u].astype(F32)
    for u in range(3):
        g_qkv[u] = of("q", u)
    g_attn[...] = of("m", 0)
    g_conv_in[:, :d] = of("m", 1)
    g_conv_in[:, d:] = of("m", 2)
    g_conv_out[...] = of("m", 3)
    w = g_taps.shape[1]
    early, late = 0, 22 + n_tap
    g_taps[...] = small[18 : 18 + n_tap, :]
    g_gain[0:1, :] = small[late : late + 1, :]
    g_gain[1:6, :] = small[0:5, :]
    g_shift[0:1, :] = small[late + 1 : late + 2, :]
    g_shift[1:6, :] = small[5:10, :]
    g_shift[6:7, :] = small[late + 2 : late + 3, :]
    g_shift[7:15, :] = small[10:18, :]
    for u in range(4):
        g_bias[0:1, u * w : (u + 1) * w] = small[late + 3 + u : late + 4 + u, :]
        g_bias[1:2, u * w : (u + 1) * w] = small[18 + n_tap + u : 19 + n_tap + u, :]
    k, h = g_table.shape
    g_table[...] = table[0:k, 0:h] + table[0:k, h : 2 * h]


def finished(main, in_b, out_b, small, table, n_tap, table_shape):
    k, r, d = main.shape
    w = small.shape[1]
    step = min(r, 32)

    def rows(count):
        return pl.BlockSpec((count, step, d), lambda i: (0, i, 0))

    def whole(*shape):
        return pl.BlockSpec(shape, lambda i: (0,) * len(shape))

    outs = [
        ((2, r, 4 * d), pl.BlockSpec((2, step, 4 * d), lambda i: (0, i, 0))),
        ((2, 4, r, d), pl.BlockSpec((2, 4, step, d), lambda i: (0, 0, i, 0))),
        ((3, r, d), rows(3)),
        ((r, d), pl.BlockSpec((step, d), lambda i: (i, 0))),
        ((r, 2 * d), pl.BlockSpec((step, 2 * d), lambda i: (i, 0))),
        ((r, d), pl.BlockSpec((step, d), lambda i: (i, 0))),
        ((n_tap, w), whole(n_tap, w)),
        ((6, w), whole(6, w)),
        ((15, w), whole(15, w)),
        ((2, 4 * w), whole(2, 4 * w)),
        (table_shape, whole(*table_shape)),
    ]
    return pl.pallas_call(
        functools.partial(finish_kernel, n_tap),
        grid=(r // step,),
        in_specs=[rows(k), rows(4), rows(4), whole(*small.shape), whole(*table.shape)],
        out_specs=[b for _, b in outs],
        out_shape=[jax.ShapeDtypeStruct(s, F32) for s, _ in outs],
        compiler_params=pltpu.CompilerParams(vmem_limit_bytes=VMEM),
        cost_estimate=pl.CostEstimate(flops=0, bytes_accessed=18_000_000, transcendentals=0),
        name="finish",
    )(main, in_b, out_b, small, table)


def xor_route(axis, mask):
    return [(i, i ^ mask) for i in range(lax.axis_size(axis))]


def swapped(block, axis, mask):
    return lax.ppermute(block, axis, xor_route(axis, mask))


def after(value, *marks):
    return lax.optimization_barrier((value,) + marks)[0]


def over_seq(part):
    if lax.axis_size("seq") != 4 or part.shape[1] < 64:
        return lax.psum(part, "seq")
    place = lax.axis_index("seq")
    part = part.astype(F32)
    for mask in (1, 2):
        high = (place & mask) != 0
        half = part.shape[1] // 2
        first, second = part[:, :half], part[:, half:]
        sent = jnp.where(high, first, second).astype(BF)
        part = jnp.where(high, second, first) + swapped(sent, "seq", mask).astype(F32)
    part = part.astype(BF)
    for mask in (2, 1):
        high = (place & mask) != 0
        got = swapped(part, "seq", mask)
        part = jnp.where(high, jnp.concatenate([got, part], axis=1), jnp.concatenate([part, got], axis=1))
    return part


def reduced(g):
    return over_seq(lax.psum_scatter(g, "fsdp", scatter_dimension=0, tiled=False))


def small_reduced(rows):
    k, d = rows.shape
    n = lax.axis_size("fsdp")
    me = lax.axis_index("fsdp")
    rows = lax.psum(rows, ("seq", "fsdp"))
    return lax.dynamic_slice_in_dim(rows, me * (d // n), d // n, 1)


def to_pairs(array, place):
    one, two = array[0], array[1]
    got = lax.ppermute(jnp.where(place % 2 == 0, two, one), "seq", [(0, 2), (1, 0), (2, 3), (3, 1)])
    more = lax.ppermute(jnp.where(place == 1, two, one), "seq", [(1, 2), (2, 1)])
    first = jnp.where(place == 0, one, jnp.where(place == 1, more, got))
    second = jnp.where(place < 2, got, jnp.where(place == 2, more, two))
    return jnp.concatenate([first, second], axis=0)


def from_pairs(array, place):
    half = array.shape[0] // 2
    first, second = array[:half], array[half:]
    got = lax.ppermute(jnp.where(place < 2, second, first), "seq", [(2, 0), (0, 1), (3, 2), (1, 3)])
    more = lax.ppermute(jnp.where(place == 1, first, second), "seq", [(1, 2), (2, 1)])
    one = jnp.where(place == 0, first, jnp.where(place == 2, more, got))
    two = jnp.where(place == 3, second, jnp.where(place == 1, more, got))
    return jnp.stack([one, two])


def on_device(
    inputs,
    lengths,
    ffn_in,
    ffn_in_bias,
    ffn_out,
    qkv,
    attn_out,
    conv_in,
    conv_out,
    depthwise,
    gains,
    shifts,
    distance,
    grad_out,
):
    n = lax.axis_size("fsdp")
    me = lax.axis_index("fsdp")
    place = lax.axis_index("seq")
    odd = place % 2 == 1
    odd_word = (place % 2).astype(jnp.int32).reshape(1)
    me_word = me.astype(jnp.int32).reshape(1)
    width = inputs.shape[2]
    r = width // n
    inner_width = ffn_in.shape[2]
    n_gain, n_shift, n_tap = gains.shape[0], shifts.shape[0], depthwise.shape[0]
    cubed = n == 8 and lax.axis_size("seq") == 4

    def chunks(part):
        return [part[:, i : i + width] for i in range(0, part.shape[1], width)]

    shard_a = jnp.stack(chunks(ffn_in[0]))
    shard_b = jnp.concatenate([ffn_out[0].reshape(4, r, width), qkv], axis=0)
    shard_c = jnp.stack([attn_out] + chunks(conv_in) + [conv_out])
    shard_d = jnp.concatenate([jnp.stack(chunks(ffn_in[1])), ffn_out[1].reshape(4, r, width)], axis=0)
    small = jnp.concatenate([gains, shifts, depthwise, ffn_in_bias.reshape(-1, r)], axis=0)
    small = lax.all_gather(small, "fsdp", axis=0)
    w_a = lax.all_gather(shard_a, "fsdp", axis=0)

    small = small.astype(F32)
    rows = jnp.transpose(small, (1, 0, 2))
    n_plain = n_gain + n_shift + n_tap
    gain = rows[:n_gain].reshape(n_gain, width)
    shift = rows[n_gain : n_gain + n_shift].reshape(n_shift, width)
    taps = rows[n_gain + n_shift : n_plain].reshape(n_tap, width)
    bias = small[:, n_plain:].reshape(n, 2, -1).transpose(1, 0, 2).reshape(2, inner_width)

    tokens = to_pairs(inputs, place)
    cotangent = to_pairs(grad_out, place)
    length = jnp.where(place < 2, lengths[0], lengths[1]).reshape(1)
    wide, ends = tables(distance)
    pairs = [(0, 1), (2, 3)]

    w_b = lax.all_gather(after(shard_b, w_a, small, tokens), "fsdp", axis=0)
    inner_a, act_a, act_t_a, unit_t_a = ffn_in_forward(tokens, jnp.stack([gain[0], shift[0]]), bias[0], w_a, 0)
    w_c = lax.all_gather(after(shard_c, w_b, act_a), "fsdp", axis=0)
    first, unit_t_1, mine, other = out_qkv_forward(
        odd_word, tokens, act_a, w_b, jnp.stack([shift[6], gain[1], shift[1], shift[8], shift[9]])
    )
    w_d = lax.all_gather(after(shard_d, other), "fsdp", axis=0)
    probs, heads, mixed = attend(mine, other, length, wide, ends)
    second, mixed_t, unit_t_2, val, sig, gated = mid_forward(
        first, mixed, w_c, 0, 1, jnp.stack([shift[10], gain[2], shift[2], shift[11], shift[12]])
    )
    count = gated.shape[0]
    halo = lax.ppermute(gated[count - 32 :], "seq", pairs)
    conv, act_t_c, third = conv_forward(
        gated, halo, taps, jnp.stack([shift[13], gain[3], shift[3], shift[14]]), second, w_c, 3
    )
    inner_b, act_b, act_t_b, unit_t_b = ffn_in_forward(third, jnp.stack([gain[4], shift[4]]), bias[1], w_d, 0)
    outputs, d4, sums_5 = out_last(third, act_b, w_d, 1, cotangent, jnp.stack([shift[7], gain[5], shift[5]]))
    outputs = from_pairs(outputs, place)

    dinner, dout, dbias_b, sums_7 = ffn_hidden_back(d4, inner_b, w_d, 1)
    g_out_b = weight_grad(act_t_b, dout, n, 4, 0, True)
    g_in_b = weight_grad(unit_t_b, after(dinner, g_out_b), n, 4, 0, False)
    part_out_b = lax.psum_scatter(g_out_b, "fsdp", scatter_dimension=0, tiled=False)
    part_in_b = lax.psum_scatter(g_in_b, "fsdp", scatter_dimension=0, tiled=False)
    dinner = after(dinner, g_in_b)
    d3, sums_4 = norm_input_back(d4, dinner, third, w_d, 0, gain[4:5])
    d3, outputs = lax.optimization_barrier((d3, outputs))
    dconv, dout_3, sums_3 = conv_out_back(d3, conv, w_c, 3, jnp.stack([gain[3], shift[3]]))
    follow = lax.ppermute(dconv[:32], "seq", [(j, i) for i, j in pairs])
    d2, dout_2, dglu, mine, other, sums_2 = mid_back(
        odd_word, dconv, follow, taps, val, sig, second, d3, w_c, 0, 1, gain[2:3]
    )
    if cubed:
        dqkv, dtable, share_out_b = attend_back(heads, probs, wide, mine, other, part_out_b)
    else:
        dqkv, dtable = attend_back(heads, probs, wide, mine, other)
        share_out_b, share_in_b = over_seq(part_out_b), over_seq(part_in_b)

    def biases(part):
        return part.reshape(n, 4, r).transpose(1, 0, 2).reshape(4, width)

    if cubed:
        main, share_in_b, small, table, grad_tokens = last_reduced(
            gain[0:2], dtable, (sums_2, sums_3, sums_4, sums_5, sums_7), dbias_b, d2, first, tokens, dconv, gated, halo,
            part_in_b, dqkv, unit_t_1, act_t_a, unit_t_a, inner_a, w_b, w_a,
            mixed_t, dout_2, unit_t_2, dglu, act_t_c, dout_3,
        )
    else:
        d1, sums_1 = norm_input_back(d2, dqkv, first, w_b, 4, gain[1:2])
        bias_sums = jnp.sum(dqkv.astype(F32), axis=0)
        dtaps = taps_grad(dconv, gated, halo, n_tap)
        early = jnp.concatenate(
            [
                jnp.stack([sums_1[0], sums_2[2], sums_3[1], sums_4[0], sums_5[0]]),
                jnp.stack([sums_1[1], sums_2[3], sums_3[2], sums_4[1], sums_5[1]]),
                jnp.stack(
                    [
                        sums_7[0],
                        bias_sums[:width],
                        bias_sums[2 * width :],
                        sums_2[4],
                        sums_2[0],
                        sums_2[1],
                        sums_3[3],
                        sums_3[0],
                    ]
                ),
                dtaps,
                biases(dbias_b),
            ],
            axis=0,
        )
        dinner, dout, dbias_a, sums_6 = ffn_hidden_back(d1, inner_a, w_b, 0)
        g_m = weight_grad(unit_t_2, dglu, n, 4, 1, False)
        g_m = weight_grad(mixed_t, dout_2, n, 4, 0, False, into=g_m)
        g_m = weight_grad(act_t_c, dout_3, n, 4, 3, False, into=g_m)
        shares = {
            "m": reduced(g_m),
            "q": reduced(weight_grad(unit_t_1, dqkv, n, 3, 0, False)),
            "out": reduced(weight_grad(act_t_a, dout, n, 4, 0, True)),
            "in": reduced(weight_grad(unit_t_a, dinner, n, 4, 0, False)),
        }
        main = jnp.stack([shares[name][unit] for name, unit in ORDER])
        d0, sums_0 = norm_input_back(d1, dinner, tokens, w_a, 0, gain[0:1], BF)
        grad_tokens = from_pairs(d0, place)
        late = jnp.concatenate([jnp.stack([sums_0[0], sums_0[1], sums_6[0]]), biases(dbias_a)], axis=0)
        small = small_reduced(jnp.concatenate([early, late], axis=0))
        table = lax.psum(dtable, ("seq", "fsdp"))
    g_in, g_out, g_qkv, g_attn, g_conv_in, g_conv_out, g_taps, g_gain, g_shift, g_bias, total_table = finished(
        main, share_in_b, share_out_b, small, table, n_tap, distance.shape
    )
    return (
        outputs,
        grad_tokens,
        g_in,
        g_bias,
        g_out.reshape(2, 4 * r, width),
        g_qkv,
        g_attn,
        g_conv_in,
        g_conv_out,
        g_taps,
        g_gain,
        g_shift,
        total_table,
    )


def solution(mesh):
    return jax.shard_map(
        on_device,
        mesh=mesh,
        in_specs=(
            P("fsdp", "seq", None),
            P("fsdp"),
            P(None, "fsdp", None),
            P(None, "fsdp"),
            P(None, "fsdp", None),
            P(None, "fsdp", None),
            P("fsdp", None),
            P("fsdp", None),
            P("fsdp", None),
            P(None, "fsdp"),
            P(None, "fsdp"),
            P(None, "fsdp"),
            P(),
            P("fsdp", "seq", None),
        ),
        out_specs=(
            P("fsdp", "seq", None),
            P("fsdp", "seq", None),
            P(None, "fsdp", None),
            P(None, "fsdp"),
            P(None, "fsdp", None),
            P(None, "fsdp", None),
            P("fsdp", None),
            P("fsdp", None),
            P("fsdp", None),
            P(None, "fsdp"),
            P(None, "fsdp"),
            P(None, "fsdp"),
            P(),
        ),
        check_vma=False,
    )
```

```python
import functools

import jax
import jax.numpy as jnp
from jax import lax
from jax.experimental import pallas as pl
from jax.experimental.pallas import tpu as pltpu
from jax.sharding import PartitionSpec as P

HEAD_DIM=64; LEFT=64; RIGHT=8
F32=jnp.float32; BF=jnp.bfloat16
RB=256
PADL=128
WIN=512

def dot(a,b,ca,cb):
    return lax.dot_general(a,b,(((ca,),(cb,)),((),())),preferred_element_type=F32)

def lanes(shape):
    return lax.broadcasted_iota(jnp.int32,shape,1)

def band_offset():
    row=lax.broadcasted_iota(jnp.int32,(RB,WIN),0)
    col=lax.broadcasted_iota(jnp.int32,(RB,WIN),1)
    return col-row-LEFT


MESH = pl.DeviceIdType.MESH
STEPS = 4


def pair_place():
    place = lax.axis_index("seq")
    half = lax.rem(place, jnp.int32(2))
    return half, {"seq": place + 1 - 2 * half}


def meet(partner):
    barrier = pltpu.get_barrier_semaphore()
    pl.semaphore_signal(barrier, inc=1, device_id=partner, device_id_type=MESH)
    pl.semaphore_wait(barrier, 1)


def block_at(step, half):
    return lax.rem(step + 2 * (1 - half), jnp.int32(STEPS))


def fwd_kernel(len_ref,wide_ref,ends_ref,mine_ref,other_ref,p_ref,heads_ref,mixed_ref,s_ref,kx_ref,buf,mixed,stage,in_send,in_recv,in_load,out_send,out_recv):
    n=buf.shape[2]; own=n//2
    pair=pl.program_id(0); step=pl.program_id(1)
    pairs=buf.shape[0]
    half,partner=pair_place()
    at=pl.multiple_of(half*own,own)
    def arrive(a):
        return pltpu.make_async_remote_copy(src_ref=other_ref.at[a],dst_ref=buf.at[a,:,pl.ds(at,own)],send_sem=in_send.at[a],recv_sem=in_recv.at[a],device_id=partner,device_id_type=MESH)
    def load(a):
        return pltpu.make_async_copy(mine_ref.at[a],buf.at[a,:,pl.ds(at,own)],in_load.at[a])
    def leave(a,b):
        cols=pl.ds(pl.multiple_of(half*own+a*128,128),128)
        return pltpu.make_async_remote_copy(src_ref=stage.at[a,b],dst_ref=mixed.at[pl.ds(pl.multiple_of(b*RB,RB),RB),cols],send_sem=out_send.at[a,b],recv_sem=out_recv.at[a,b],device_id=partner,device_id_type=MESH)
    @pl.when((pair==0)&(step==0))
    def _():
        meet(partner)
        for a in range(pairs):
            load(a).start()
            arrive(a).start()
    @pl.when(step==0)
    def _():
        load(pair).wait()
        arrive(pair).wait()
        heads_ref[0]=buf[pair]
        kx_ref[:,0:128]=buf[pair,1]
    i0=pl.multiple_of(block_at(step,half)*RB,RB)
    q2=buf[pair,0,pl.ds(i0,RB)]
    v2=buf[pair,2]
    lane=lanes((RB,128))
    t=lax.broadcasted_iota(jnp.int32,(n,128),0)
    c=lanes((n,128))
    left=(t<i0-128).astype(F32); right=(t>=i0+WIN-128).astype(F32)
    masked=jnp.where(t>=len_ref[0],-1e30,0.0)
    ext=jnp.where(c<2,left,jnp.where(c<4,right,jnp.where(c==4,masked,0.0)))
    kx_ref[:,128:256]=ext.astype(BF)
    outs=[]
    for h in range(2):
        head=(lane<64) if h==0 else (lane>=64)
        qh=jnp.where(head,q2,jnp.zeros_like(q2))
        ends=dot(qh,ends_ref[...],1,0)
        hi=ends.astype(BF).astype(F32)
        qx=jnp.where((lane==0)|(lane==2),hi,jnp.where((lane==1)|(lane==3),ends-hi,jnp.where(lane==4,1.0,0.0))).astype(BF)
        s_ref[:,PADL:PADL+n]=dot(jnp.concatenate([qh,qx],axis=1),kx_ref[...],1,1)
        wide=dot(qh,wide_ref[...],1,0)
        band=pltpu.roll(wide,LEFT,1,stride=1,stride_axis=0)
        j=band_offset()
        band=jnp.where(j>=LEFT+RIGHT,wide[:,LEFT+RIGHT:LEFT+RIGHT+1],band)
        w=pl.ds(i0,WIN)
        s_ref[:,w]=s_ref[:,w]+band
        s=s_ref[:,PADL:PADL+n]
        m=jnp.max(s,axis=1,keepdims=True)
        e=jnp.exp(s-m)
        z=jnp.sum(e,axis=1,keepdims=True)
        p=(e*(1.0/z)).astype(BF)
        p_ref[h]=p
        outs.append(dot(p,v2,1,0))
    out=jnp.where(lane<64,outs[0],outs[1]).astype(BF)
    @pl.when(step<2)
    def _():
        stage[pair,step]=out
        leave(pair,step).start()
    @pl.when(step>=2)
    def _():
        cols=pl.ds(pl.multiple_of(half*own+pair*128,128),128)
        mixed[pl.ds(pl.multiple_of((step-2)*RB,RB),RB),cols]=out
    @pl.when((pair==pairs-1)&(step==STEPS-1))
    def _():
        for a in range(pairs):
            for b in range(2):
                leave(a,b).wait_send()
        for a in range(pairs):
            for b in range(2):
                arrived=pltpu.make_async_remote_copy(src_ref=stage.at[a,b],dst_ref=mixed.at[pl.ds(b*RB,RB),pl.ds(pl.multiple_of((1-half)*own+a*128,128),128)],send_sem=out_send.at[a,b],recv_sem=out_recv.at[a,b],device_id=partner,device_id_type=MESH)
                arrived.wait_recv()
        mixed_ref[...]=mixed[...]


def z_line(middle,to_1,to_2,whole,near,far,z_send,z_recv):
    def copy(i,stage):
        src=(whole,near,far)[stage]; dst=(near,far,near)[stage]
        return pltpu.make_async_remote_copy(src_ref=src.at[i],dst_ref=dst.at[i],send_sem=z_send.at[i,stage],recv_sem=z_recv.at[i,stage],device_id=to_2 if stage==1 else to_1,device_id_type=MESH)
    def begin(i):
        pl.when(middle==0)(lambda: copy(i,0).start())
    def step(i,stage):
        @pl.when(middle==1)
        def _():
            if stage==0:
                copy(i,0).wait_recv()
                near[i]=(whole[i].astype(F32)+near[i].astype(F32)).astype(BF)
                copy(i,1).start()
            elif stage==1:
                copy(i,1).wait()
                far[i]=(near[i].astype(F32)+far[i].astype(F32)).astype(BF)
                copy(i,2).start()
            else:
                copy(i,2).wait_send()
        if stage!=1:
            @pl.when(middle==0)
            def _():
                if stage==0:
                    copy(i,0).wait_send()
                else:
                    copy(i,2).wait_recv()
    return begin,step


def bwd_kernel(with_part,heads_ref,p_ref,wide_ref,mine_ref,other_ref,*rest):
    if with_part:
        part_ref,dqkv_ref,de_ref,out_ref,*rest=rest
        *rest,whole,near,far,part_sem,out_sem,z_send,z_recv=rest
    else:
        dqkv_ref,de_ref,*rest=rest
    ds_ref,kx_ref,dka,dva,dea,buf,dqkv,stage_q,stage_kv,in_send,in_recv,in_load,q_send,q_recv,kv_send,kv_recv=rest
    n=heads_ref.shape[2]; own=n//2
    pair=pl.program_id(0); step=pl.program_id(1)
    pairs=buf.shape[0]
    half,partner=pair_place()
    at=pl.multiple_of(half*own,own)
    width=2*own
    def columns(t,who,a):
        return pl.ds(pl.multiple_of(t*width+who*own+a*128,128),128)
    def arrive(a):
        return pltpu.make_async_remote_copy(src_ref=other_ref.at[a],dst_ref=buf.at[a,pl.ds(at,own)],send_sem=in_send.at[a],recv_sem=in_recv.at[a],device_id=partner,device_id_type=MESH)
    def load(a):
        return pltpu.make_async_copy(mine_ref.at[a],buf.at[a,pl.ds(at,own)],in_load.at[a])
    def leave_q(a,b,who):
        return pltpu.make_async_remote_copy(src_ref=stage_q.at[a,b],dst_ref=dqkv.at[pl.ds(pl.multiple_of(b*RB,RB),RB),columns(0,who,a)],send_sem=q_send.at[a,b],recv_sem=q_recv.at[a,b],device_id=partner,device_id_type=MESH)
    def leave_kv(a,t,who):
        return pltpu.make_async_remote_copy(src_ref=stage_kv.at[a,t],dst_ref=dqkv.at[:,columns(t+1,who,a)],send_sem=kv_send.at[a,t],recv_sem=kv_recv.at[a,t],device_id=partner,device_id_type=MESH)
    if with_part:
        n_part=part_ref.shape[0]
        place=lax.axis_index("seq")
        middle=lax.rem(lax.div(place+1,jnp.int32(2)),jnp.int32(2))
        across={"seq":3-place}
        z_begin,z_step=z_line(middle,partner,across,whole,near,far,z_send,z_recv)
        def part_copy(i):
            return pltpu.make_async_copy(part_ref.at[i],whole.at[i],part_sem.at[i])
        def result_do(i,act):
            for is_middle,src in ((1,far),(0,near)):
                copy=pltpu.make_async_copy(src.at[i],out_ref.at[i],out_sem.at[i])
                pl.when(middle==is_middle)(lambda copy=copy: act(copy))
        now=pair*STEPS+step
    @pl.when((pair==0)&(step==0))
    def _():
        if with_part:
            barrier=pltpu.get_barrier_semaphore()
            for device in (partner,across):
                pl.semaphore_signal(barrier,inc=1,device_id=device,device_id_type=MESH)
            pl.semaphore_wait(barrier,2)
        else:
            meet(partner)
        for a in range(pairs):
            load(a).start()
            arrive(a).start()
        if with_part:
            for i in range(n_part):
                part_copy(i).start()
        dea[...]=jnp.zeros_like(dea)
        ds_ref[:,0:PADL]=jnp.zeros((RB,PADL),F32)
        ds_ref[:,PADL+n:]=jnp.zeros((RB,ds_ref.shape[1]-PADL-n),F32)
    @pl.when(step==0)
    def _():
        load(pair).wait()
        arrive(pair).wait()
        kx_ref[:,0:128]=heads_ref[0,1]
        dka[...]=jnp.zeros_like(dka); dva[...]=jnp.zeros_like(dva)
    if with_part:
        for i in range(n_part):
            @pl.when(now==1+2*i)
            def _(i=i):
                part_copy(i).wait()
                z_begin(i)
            for stage in range(3):
                @pl.when(now==5+2*i+2*stage)
                def _(i=i,stage=stage):
                    z_step(i,stage)
                    if stage==2:
                        result_do(i,lambda copy: copy.start())
    i0=pl.multiple_of(block_at(step,half)*RB,RB)
    q2=heads_ref[0,0,pl.ds(i0,RB)]
    v2=heads_ref[0,2]
    do2=buf[pair,pl.ds(i0,RB)]
    lane=lanes((RB,128))
    row=lax.broadcasted_iota(jnp.int32,(RB,128),0)
    t=lax.broadcasted_iota(jnp.int32,(n,128),0)
    c=lanes((n,128))
    left=(t<i0-128).astype(F32)
    kx_ref[:,128:256]=jnp.where(c==0,left,jnp.where(c==1,1.0,0.0)).astype(BF)
    dqs=[]
    for h in range(2):
        head=(lane<64) if h==0 else (lane>=64)
        doh=jnp.where(head,do2,jnp.zeros_like(do2))
        qh=jnp.where(head,q2,jnp.zeros_like(q2))
        p=p_ref[h]
        dp=dot(doh,v2,1,1)
        pf=p.astype(F32)
        d=jnp.sum(pf*dp,axis=1,keepdims=True)
        dsf=pf*(dp-d)
        ds=dsf.astype(BF)
        ds_ref[:,PADL:PADL+n]=ds.astype(F32)
        dva[...]+=dot(doh,p,0,0)
        dka[...]+=dot(qh,ds,0,0)
        dqx=dot(ds,kx_ref[...],1,0)
        dq,sums=dqx[:,0:128],dqx[:,128:256]
        win=ds_ref[:,pl.ds(i0,WIN)]
        j=band_offset()
        inleft=jnp.sum(jnp.where(j<=0,win,0.0),axis=1,keepdims=True)
        drel=jnp.concatenate([win[8*g:8*g+8,LEFT+8*g:LEFT+8*g+128] for g in range(RB//8)],axis=0)
        for bit in (1,2,4):
            drel=jnp.where((row&bit)!=0,pltpu.roll(drel,128-bit,1),drel)
        drel=jnp.where((lane>0)&(lane<LEFT+RIGHT),drel,0.0)
        bandsum=jnp.sum(drel,axis=1,keepdims=True)
        l=sums[:,0:1]+inleft
        r=sums[:,1:2]-l-bandsum
        drel=jnp.where(lane==0,l,jnp.where(lane==LEFT+RIGHT,r,drel)).astype(BF)
        dq=dq+dot(drel,wide_ref[...],1,1)
        dqs.append(dq)
        dea[...]+=dot(drel,qh,0,0)
    dq=(jnp.where(lane<64,dqs[0],dqs[1])*HEAD_DIM**-0.5).astype(BF)
    @pl.when(step<2)
    def _():
        stage_q[pair,step]=dq
        leave_q(pair,step,half).start()
    @pl.when(step>=2)
    def _():
        dqkv[pl.ds(pl.multiple_of((step-2)*RB,RB),RB),columns(0,half,pair)]=dq
    @pl.when(step==STEPS-1)
    def _():
        for i,acc in enumerate((dka,dva)):
            mine=acc[:,pl.ds(at,own)]
            theirs=acc[:,pl.ds(pl.multiple_of((1-half)*own,own),own)]
            stage_kv[pair,i]=jnp.transpose(theirs).astype(BF)
            leave_kv(pair,i,half).start()
            dqkv[:,columns(i+1,half,pair)]=jnp.transpose(mine).astype(BF)
    @pl.when((pair==pairs-1)&(step==STEPS-1))
    def _():
        for a in range(pairs):
            for b in range(2):
                leave_q(a,b,half).wait_send()
                leave_kv(a,b,half).wait_send()
        for a in range(pairs):
            for b in range(2):
                leave_q(a,b,1-half).wait_recv()
                leave_kv(a,b,1-half).wait_recv()
        dqkv_ref[...]=dqkv[...]
        de_ref[...]=dea[...]
        if with_part:
            for i in range(n_part):
                result_do(i,lambda copy: copy.wait())


def tables(distance):
    e=distance.T
    wide=jnp.concatenate([e,jnp.broadcast_to(e[:,72:73],(64,120)),jnp.broadcast_to(e[:,0:1],(64,WIN-193))],axis=1)
    wide=jnp.concatenate([wide,wide],axis=0)
    ends=jnp.concatenate([e[:,0:1],e[:,0:1],e[:,72:73],e[:,72:73],jnp.zeros((64,124),e.dtype)],axis=1)
    ends=jnp.concatenate([ends,ends],axis=0)
    return wide,ends

def attend(mine,other,length,wide,ends):
    pairs,_,own,_=mine.shape; n=2*own
    dma=pltpu.SemaphoreType.DMA
    whole=lambda *shape: pl.BlockSpec(shape,lambda a,b:(0,)*len(shape))
    anywhere=pl.BlockSpec(memory_space=pl.ANY)
    return pl.pallas_call(fwd_kernel,
        grid=(pairs,STEPS),
        in_specs=[pl.BlockSpec(memory_space=pltpu.SMEM),whole(128,WIN),whole(128,128),anywhere,anywhere],
        out_specs=[pl.BlockSpec((2,RB,n),lambda a,b:(a,b,0)),pl.BlockSpec((1,3,n,128),lambda a,b:(a,0,0,0)),whole(own,2*own)],
        out_shape=[jax.ShapeDtypeStruct((2*pairs,n,n),BF),jax.ShapeDtypeStruct((pairs,3,n,128),BF),jax.ShapeDtypeStruct((own,2*own),BF)],
        scratch_shapes=[pltpu.VMEM((RB,PADL+n+256),F32),pltpu.VMEM((n,256),BF),pltpu.VMEM((pairs,3,n,128),BF),pltpu.VMEM((own,2*own),BF),pltpu.VMEM((pairs,2,RB,128),BF),
            dma((pairs,)),dma((pairs,)),dma((pairs,)),dma((pairs,2)),dma((pairs,2))],
        compiler_params=pltpu.CompilerParams(vmem_limit_bytes=58<<20,collective_id=1,has_side_effects=True),
        cost_estimate=pl.CostEstimate(flops=40_000_000_000,bytes_accessed=120_000_000,transcendentals=0),
        name="attend_fwd",
    )(length,wide,ends,mine,other)

def attend_back(heads,p,wide,mine,other,part=None):
    pairs,_,n,_=heads.shape; own=n//2
    dma=pltpu.SemaphoreType.DMA
    whole=lambda *shape: pl.BlockSpec(shape,lambda a,b:(0,)*len(shape))
    anywhere=pl.BlockSpec(memory_space=pl.ANY)
    with_part=part is not None
    extra=[pltpu.VMEM(part.shape,BF)]*3+[dma((part.shape[0],))]*2+[dma((part.shape[0],3))]*2 if with_part else []
    return pl.pallas_call(functools.partial(bwd_kernel,with_part),
        grid=(pairs,STEPS),
        in_specs=[pl.BlockSpec((1,3,n,128),lambda a,b:(a,0,0,0)),pl.BlockSpec((2,RB,n),lambda a,b:(a,b,0)),whole(128,128),anywhere,anywhere]+[anywhere]*with_part,
        out_specs=[whole(own,6*own),whole(128,128)]+[anywhere]*with_part,
        out_shape=[jax.ShapeDtypeStruct((own,6*own),BF),jax.ShapeDtypeStruct((128,128),F32)]+([jax.ShapeDtypeStruct(part.shape,BF)] if with_part else []),
        scratch_shapes=[pltpu.VMEM((RB,PADL+n+256),F32),pltpu.VMEM((n,256),BF),pltpu.VMEM((128,n),F32),pltpu.VMEM((128,n),F32),pltpu.VMEM((128,128),F32),
            pltpu.VMEM((pairs,n,128),BF),pltpu.VMEM((own,6*own),BF),pltpu.VMEM((pairs,2,RB,128),BF),pltpu.VMEM((pairs,2,own,128),BF),
            dma((pairs,)),dma((pairs,)),dma((pairs,)),dma((pairs,2)),dma((pairs,2)),dma((pairs,2)),dma((pairs,2))]+extra,
        compiler_params=pltpu.CompilerParams(vmem_limit_bytes=58<<20,collective_id=2,has_side_effects=True),
        cost_estimate=pl.CostEstimate(flops=50_000_000_000,bytes_accessed=150_000_000,transcendentals=0),
        name="attend_bwd",
    )(heads,p,wide[:,0:128],mine,other,*([part] if with_part else []))


EPSILON = 1e-05
HALF = 0.5
CUT = 256
VMEM = 56 << 20


def flat(ref):
    value = ref[...]
    return value.reshape(-1, value.shape[-1])


def cuts(count):
    return [pl.ds(i, CUT) for i in range(0, count, CUT)]


def normal(v):
    c = v - jnp.mean(v, axis=-1, keepdims=True)
    r = lax.rsqrt(jnp.mean(c * c, axis=-1, keepdims=True) + EPSILON)
    return c * r, r


def normal_back(dy, unit, r, gain):
    a = dy * gain
    return (a - jnp.mean(a, axis=-1, keepdims=True) - unit * jnp.mean(a * unit, axis=-1, keepdims=True)) * r


def total(v):
    return jnp.sum(v, axis=0, keepdims=True)


def silu_slope(v):
    s = jax.nn.sigmoid(v)
    return s * (1.0 + v * (1.0 - s))


def call(kernel, grid, ins, outs, scratch=(), name=None, aliases=None, flops=0, moved=0):
    def spec(shape, block, where):
        if block is None:
            return pl.BlockSpec(shape, lambda *_: (0,) * len(shape))
        if block == "smem":
            return pl.BlockSpec(memory_space=pltpu.SMEM)
        if block == "any":
            return pl.BlockSpec(memory_space=pl.ANY)
        return pl.BlockSpec(block, where)

    return pl.pallas_call(
        kernel,
        grid=grid,
        in_specs=[spec(a.shape, b, w) for a, b, w in ins],
        out_specs=[spec(s, b, w) for s, _, b, w in outs],
        out_shape=[jax.ShapeDtypeStruct(s, d) for s, d, _, _ in outs],
        scratch_shapes=list(scratch),
        input_output_aliases=aliases or {},
        compiler_params=pltpu.CompilerParams(vmem_limit_bytes=VMEM),
        cost_estimate=pl.CostEstimate(flops=flops, bytes_accessed=moved, transcendentals=0),
        name=name,
    )(*[a for a, _, _ in ins])


def scr(shape, dtype):
    return pltpu.VMEM(shape, dtype)


def in_kernel(x_ref, vec_ref, bias_ref, w_ref, inner_ref, act_ref, act_t_ref, unit_t_ref, unit):
    @pl.when(pl.program_id(0) == 0)
    def _():
        for rows in cuts(x_ref.shape[0]):
            n, _ = normal(x_ref[rows, :].astype(F32))
            u = (n * vec_ref[0:1, :] + vec_ref[1:2, :]).astype(BF)
            unit[rows, :] = u
            unit_t_ref[:, rows] = u.T

    w = flat(w_ref)
    for rows in cuts(x_ref.shape[0]):
        s = dot(unit[rows, :], w, 1, 0) + bias_ref[0]
        inner_ref[rows, :] = s.astype(BF)
        a = (s * jax.nn.sigmoid(s)).astype(BF)
        act_ref[rows, :] = a
        act_t_ref[:, rows] = a.T


def ffn_in_forward(x, vec, bias, w, unit0):
    t, d = x.shape
    n, _, r, _ = w.shape
    k = bias.shape[0] // d
    bias = bias.reshape(k, 1, d)
    return call(
        in_kernel,
        (k,),
        [
            (x, None, None),
            (vec, None, None),
            (bias, (1, 1, d), lambda j: (j, 0, 0)),
            (w, (n, 1, r, d), lambda j: (0, unit0 + j, 0, 0)),
        ],
        [
            ((t, k * d), BF, (t, d), lambda j: (0, j)),
            ((t, k * d), BF, (t, d), lambda j: (0, j)),
            ((k * d, t), BF, (d, t), lambda j: (j, 0)),
            ((d, t), BF, None, None),
        ],
        [scr((t, d), BF)],
        name="ffn_in",
        flops=2 * t * d * d * k,
        moved=2 * d * d * k + 6 * t * d * k,
    )


def out_qkv_kernel(odd_ref, x_ref, act_ref, w_out_ref, w_qkv_ref, vec_ref, first_ref, unit_t_ref, mine_ref, other_ref, unit, acc):
    s = pl.program_id(0)
    t = x_ref.shape[0]

    @pl.when(s < 4)
    def _():
        w = flat(w_out_ref)
        for rows in cuts(t):
            p = dot(act_ref[rows, :], w, 1, 0)
            acc[rows, :] = p + jnp.where(s == 0, 0.0, acc[rows, :])

    @pl.when(s == 3)
    def _():
        for rows in cuts(t):
            first = x_ref[rows, :].astype(F32) + HALF * (acc[rows, :] + vec_ref[0:1, :])
            first_ref[rows, :] = first
            n, _ = normal(first)
            u = (n * vec_ref[1:2, :] + vec_ref[2:3, :]).astype(BF)
            unit[rows, :] = u
            unit_t_ref[:, rows] = u.T

    @pl.when(s >= 4)
    def _():
        w = flat(w_qkv_ref)
        odd = odd_ref[0] == 1
        half = w.shape[1] // 2
        scale = jnp.where(s == 4, HEAD_DIM**-0.5, 1.0)
        b = jnp.where(s == 4, vec_ref[3:4, :], jnp.where(s == 6, vec_ref[4:5, :], 0.0))
        for rows in cuts(t):
            y = (dot(unit[rows, :], w, 1, 0) + b) * scale
            low, high = y[:, :half], y[:, half:]
            mine = jnp.where(odd, high, low).astype(BF)
            other = jnp.where(odd, low, high).astype(BF)
            for part in range(half // 128):
                cols = slice(part * 128, part * 128 + 128)
                mine_ref[part, 0, rows, :] = mine[:, cols]
                other_ref[part, 0, rows, :] = other[:, cols]


def out_qkv_forward(odd, x, act, w, vec):
    t, d = x.shape
    n, _, r, _ = w.shape
    return call(
        out_qkv_kernel,
        (7,),
        [
            (odd, "smem", None),
            (x, None, None),
            (act, (t, d), lambda s: (0, jnp.minimum(s, 3))),
            (w, (n // 4, 4, r, d), lambda s: (jnp.minimum(s, 3), 0, 0, 0)),
            (w, (n, 1, r, d), lambda s: (0, jnp.maximum(s, 4), 0, 0)),
            (vec, None, None),
        ],
        [
            ((t, d), F32, None, None),
            ((d, t), BF, None, None),
            ((d // 256, 3, t, 128), BF, (d // 256, 1, t, 128), lambda s: (0, jnp.maximum(s - 4, 0), 0, 0)),
            ((d // 256, 3, t, 128), BF, (d // 256, 1, t, 128), lambda s: (0, jnp.maximum(s - 4, 0), 0, 0)),
        ],
        [scr((t, d), BF), scr((t, d), F32)],
        name="out_qkv",
        flops=14 * t * d * d,
        moved=14 * d * d + 20 * t * d,
    )


def mid_kernel(first_ref, mixed_ref, w_attn_ref, w_in_ref, vec_ref, second_ref, mixed_t_ref, unit_t_ref, val_ref, sig_ref, gated_ref, unit, val):
    s = pl.program_id(0)
    t = first_ref.shape[0]

    @pl.when(s == 0)
    def _():
        w = flat(w_attn_ref)
        for rows in cuts(t):
            m = mixed_ref[rows, :]
            mixed_t_ref[:, rows] = m.T
            second = first_ref[rows, :] + dot(m, w, 1, 0) + vec_ref[0:1, :]
            second_ref[rows, :] = second
            n, _ = normal(second)
            u = (n * vec_ref[1:2, :] + vec_ref[2:3, :]).astype(BF)
            unit[rows, :] = u
            unit_t_ref[:, rows] = u.T

    @pl.when(s == 1)
    def _():
        w = flat(w_in_ref)
        for rows in cuts(t):
            v = dot(unit[rows, :], w, 1, 0) + vec_ref[3:4, :]
            val[rows, :] = v
            val_ref[rows, :] = v.astype(BF)

    @pl.when(s == 2)
    def _():
        w = flat(w_in_ref)
        for rows in cuts(t):
            g = jax.nn.sigmoid(dot(unit[rows, :], w, 1, 0) + vec_ref[4:5, :])
            sig_ref[rows, :] = g.astype(BF)
            gated_ref[rows, :] = (val[rows, :] * g).astype(BF)


def mid_forward(first, mixed, w, u_attn, u_in, vec):
    t, d = first.shape
    n, _, r, _ = w.shape
    return call(
        mid_kernel,
        (3,),
        [
            (first, None, None),
            (mixed, None, None),
            (w, (n, 1, r, d), lambda s: (0, u_attn, 0, 0)),
            (w, (n, 1, r, d), lambda s: (0, u_in + jnp.maximum(s - 1, 0), 0, 0)),
            (vec, None, None),
        ],
        [((t, d), F32, None, None), ((d, t), BF, None, None), ((d, t), BF, None, None)]
        + [((t, d), BF, None, None)] * 3,
        [scr((t, d), BF), scr((t, d), F32)],
        name="mid",
        flops=6 * t * d * d,
        moved=6 * d * d + 20 * t * d,
    )


ROWS = 32
COLS = 256


def shifted(window, b):
    return window if b == 0 else pltpu.roll(window, window.shape[0] - b, 0)


def fir(pad, taps, offset, count, width, start, write, turned=False):
    reach = taps.shape[0]
    for c in range(0, width, COLS):
        cols = slice(c, c + COLS)

        def body(i, _):
            base = pl.multiple_of(i * ROWS, ROWS)
            window = pad[pl.ds(base, ROWS + 32), cols]
            acc = start(cols)
            for b in range(8):
                sh = shifted(window, b)
                for a in range(0, 5):
                    m = 8 * a + b - offset
                    if 0 <= m < reach:
                        tap = reach - 1 - m if turned else m
                        acc = acc + taps[tap : tap + 1, cols] * sh[8 * a : 8 * a + ROWS]
            write(pl.ds(base, ROWS), cols, acc)
            return 0

        lax.fori_loop(0, count // ROWS, body, 0)


def conv_kernel(gated_ref, halo_ref, taps_ref, vec_ref, second_ref, w_ref, conv_ref, act_t_ref, third_ref, pad):
    t, d = gated_ref.shape
    pad[0:32, :] = halo_ref[...].astype(F32)
    for rows in cuts(t):
        pad[pl.ds(rows.start + 32, CUT), :] = gated_ref[rows, :].astype(F32)

    def write(rows, cols, acc):
        conv_ref[rows, cols] = acc

    fir(pad, taps_ref, 2, t, d, lambda cols: jnp.broadcast_to(vec_ref[0:1, cols], (ROWS, COLS)), write)
    w = flat(w_ref)
    for rows in cuts(t):
        n, _ = normal(conv_ref[rows, :])
        u = n * vec_ref[1:2, :] + vec_ref[2:3, :]
        a = (u * jax.nn.sigmoid(u)).astype(BF)
        act_t_ref[:, rows] = a.T
        third_ref[rows, :] = second_ref[rows, :] + dot(a, w, 1, 0) + vec_ref[3:4, :]


def conv_forward(gated, halo, taps, vec, second, w, unit0):
    t, d = gated.shape
    n, _, r, _ = w.shape
    return call(
        conv_kernel,
        (1,),
        [
            (gated, None, None),
            (halo, None, None),
            (taps, None, None),
            (vec, None, None),
            (second, None, None),
            (w, (n, 1, r, d), lambda s: (0, unit0, 0, 0)),
        ],
        [((t, d), F32, None, None), ((d, t), BF, None, None), ((t, d), F32, None, None)],
        [scr((t + 32, d), F32)],
        name="conv",
        flops=2 * t * d * d,
        moved=2 * d * d + 16 * t * d,
    )


def out_last_kernel(x_ref, act_ref, w_ref, cot_ref, vec_ref, out_ref, d_ref, sums_ref, acc):
    s = pl.program_id(0)
    t = x_ref.shape[0]
    w = flat(w_ref)
    for rows in cuts(t):
        p = dot(act_ref[rows, :], w, 1, 0)
        acc[rows, :] = p + jnp.where(s == 0, 0.0, acc[rows, :])

    @pl.when(s == 3)
    def _():
        sums_ref[...] = jnp.zeros_like(sums_ref)
        for rows in cuts(t):
            fourth = x_ref[rows, :] + HALF * (acc[rows, :] + vec_ref[0:1, :])
            n, r = normal(fourth)
            out_ref[rows, :] = (n * vec_ref[1:2, :] + vec_ref[2:3, :]).astype(BF)
            dy = cot_ref[rows, :].astype(F32)
            d_ref[rows, :] = normal_back(dy, n, r, vec_ref[1:2, :])
            sums_ref[0:1, :] += total(dy * n)
            sums_ref[1:2, :] += total(dy)


def out_last(x, act, w, block0, cot, vec):
    t, d = x.shape
    n, _, r, _ = w.shape
    return call(
        out_last_kernel,
        (4,),
        [
            (x, None, None),
            (act, (t, d), lambda s: (0, s)),
            (w, (n // 4, 4, r, d), lambda s: (s, block0, 0, 0)),
            (cot, None, None),
            (vec, None, None),
        ],
        [((t, d), BF, None, None), ((t, d), F32, None, None), ((8, d), F32, None, None)],
        [scr((t, d), F32)],
        name="out_last",
        flops=8 * t * d * d,
        moved=8 * d * d + 20 * t * d,
    )


def ffn_hidden_kernel(d_ref, inner_ref, w_ref, dinner_ref, dout_ref, dbias_ref, sums_ref):
    t = d_ref.shape[0]

    @pl.when(pl.program_id(0) == 0)
    def _():
        sums_ref[...] = jnp.zeros_like(sums_ref)
        for rows in cuts(t):
            v = (HALF * d_ref[rows, :]).astype(BF)
            dout_ref[rows, :] = v
            sums_ref[0:1, :] += total(v.astype(F32))

    w = flat(w_ref)
    dbias = 0.0
    for rows in cuts(t):
        da = dot(dout_ref[rows, :], w, 1, 1)
        v = (da * silu_slope(inner_ref[rows, :].astype(F32))).astype(BF)
        dinner_ref[rows, :] = v
        dbias = dbias + total(v.astype(F32))
    dbias_ref[0] = dbias


def ffn_hidden_back(dy, inner, w, block0):
    t, d = dy.shape
    n, _, r, _ = w.shape
    k = inner.shape[1] // d
    return call(
        ffn_hidden_kernel,
        (k,),
        [
            (dy, None, None),
            (inner, (t, d), lambda j: (0, j)),
            (w, (n // 4, 4, r, d), lambda j: (j, block0, 0, 0)),
        ],
        [
            ((t, k * d), BF, (t, d), lambda j: (0, j)),
            ((t, d), BF, None, None),
            ((k, 1, d), F32, (1, 1, d), lambda j: (j, 0, 0)),
            ((8, d), F32, None, None),
        ],
        name="ffn_hidden_back",
        flops=2 * t * d * d * k,
        moved=2 * d * d * k + 4 * t * d * k,
    )


def norm_input_kernel(k, dy_ref, g_ref, x_ref, w_ref, vec_ref, d_ref, sums_ref, acc):
    s = pl.program_id(0)
    t = x_ref.shape[0]
    w = flat(w_ref)
    for rows in cuts(t):
        p = dot(g_ref[rows, :], w, 1, 1)
        acc[rows, :] = p + jnp.where(s == 0, 0.0, acc[rows, :])

    @pl.when(s == k - 1)
    def _():
        sums_ref[...] = jnp.zeros_like(sums_ref)
        for rows in cuts(t):
            n, r = normal(x_ref[rows, :].astype(F32))
            du = acc[rows, :]
            d_ref[rows, :] = (dy_ref[rows, :] + normal_back(du, n, r, vec_ref[0:1, :])).astype(d_ref.dtype)
            sums_ref[0:1, :] += total(du * n)
            sums_ref[1:2, :] += total(du)


def norm_input_back(dy, g, x, w, unit0, gain, out_type=F32):
    t, d = dy.shape
    n, _, r, _ = w.shape
    k = g.shape[1] // d
    return call(
        functools.partial(norm_input_kernel, k),
        (k,),
        [
            (dy, None, None),
            (g, (t, d), lambda j: (0, j)),
            (x, None, None),
            (w, (n, 1, r, d), lambda j: (0, unit0 + j, 0, 0)),
            (gain, None, None),
        ],
        [((t, d), out_type, None, None), ((8, d), F32, None, None)],
        [scr((t, d), F32)],
        name="norm_input_back",
        flops=2 * t * d * d * k,
        moved=2 * d * d * k + 2 * t * d * k + 12 * t * d,
    )


def weight_kernel(left_ref, right_ref, *rest):
    out_ref = rest[-1]
    rows, d = left_ref.shape[0], out_ref.shape[-1]
    a, b, r, _ = out_ref.shape
    step = max(256, 4 * r)
    for i in range(0, rows, step):
        value = dot(left_ref[i : i + step, :], right_ref[...], 1, 0).astype(BF)
        if b == 1:
            out_ref[pl.ds(i // r, step // r), 0] = value.reshape(step // r, r, d)
        else:
            out_ref[pl.ds(i // (4 * r), step // (4 * r))] = value.reshape(step // (4 * r), 4, r, d)


def weight_grad(left_t, right, n, units, at, by_rows, into=None):
    d = 1024
    t = left_t.shape[1]
    r = d // n
    if by_rows:
        k = left_t.shape[0] // d
        ins = [(left_t, (d, t), lambda j: (j, 0)), (right, None, None)]
        block, where = (n // 4, 4, r, d), lambda j: (j, at // 4, 0, 0)
    else:
        k = right.shape[1] // d
        ins = [(left_t, None, None), (right, (t, d), lambda j: (0, j))]
        block, where = (n, 1, r, d), lambda j: (0, at + j, 0, 0)
    aliases = None
    if into is not None:
        ins.append((into, "any", None))
        aliases = {2: 0}
    return call(
        weight_kernel,
        (k,),
        ins,
        [((n, units, r, d), BF, block, where)],
        name="weight_grad",
        aliases=aliases,
        flops=2 * t * d * d * k,
        moved=2 * d * d * k + 2 * t * d * (k + 1),
    )[0]


def conv_out_kernel(d_ref, conv_ref, w_ref, vec_ref, dconv_ref, dout_ref, sums_ref):
    t = d_ref.shape[0]
    sums_ref[...] = jnp.zeros_like(sums_ref)
    w = flat(w_ref)
    for rows in cuts(t):
        dout = d_ref[rows, :].astype(BF)
        dout_ref[rows, :] = dout
        da = dot(dout, w, 1, 1)
        n, r = normal(conv_ref[rows, :])
        du = da * silu_slope(n * vec_ref[0:1, :] + vec_ref[1:2, :])
        dconv = normal_back(du, n, r, vec_ref[0:1, :])
        dconv_ref[rows, :] = dconv
        sums_ref[0:1, :] += total(dout.astype(F32))
        sums_ref[1:2, :] += total(du * n)
        sums_ref[2:3, :] += total(du)
        sums_ref[3:4, :] += total(dconv)


def conv_out_back(d3, conv, w, unit0, vec):
    t, d = d3.shape
    n, _, r, _ = w.shape
    return call(
        conv_out_kernel,
        (1,),
        [
            (d3, None, None),
            (conv, None, None),
            (w, (n, 1, r, d), lambda s: (0, unit0, 0, 0)),
            (vec, None, None),
        ],
        [((t, d), F32, None, None), ((t, d), BF, None, None), ((8, d), F32, None, None)],
        name="conv_out_back",
        flops=2 * t * d * d,
        moved=2 * d * d + 16 * t * d,
    )


def mid_back_kernel(odd_ref, dconv_ref, follow_ref, taps_ref, val_ref, sig_ref, second_ref, d3_ref, w_in_ref, w_attn_ref, vec_ref, d2_ref, dout_ref, dglu_ref, mine_ref, other_ref, sums_ref, pad, acc):
    s = pl.program_id(0)
    t, d = dconv_ref.shape

    @pl.when(s == 0)
    def _():
        for rows in cuts(t):
            pad[rows, :] = dconv_ref[rows, :]
        pad[t : t + 32, :] = follow_ref[...]

        def write(rows, cols, dgated):
            sig = sig_ref[rows, cols].astype(F32)
            dval = dgated * sig
            dglu_ref[rows, cols] = dval.astype(BF)
            dgate = dval * val_ref[rows, cols].astype(F32) * (1.0 - sig)
            dglu_ref[rows, cols.start + d : cols.stop + d] = dgate.astype(BF)

        fir(pad, taps_ref, 0, t, d, lambda cols: jnp.zeros((ROWS, COLS), F32), write, turned=True)
        sums_ref[...] = jnp.zeros_like(sums_ref)
        for rows in cuts(t):
            sums_ref[0:1, :] += total(dglu_ref[rows, :d].astype(F32))
            sums_ref[1:2, :] += total(dglu_ref[rows, d:].astype(F32))
        w = flat(w_in_ref)
        for rows in cuts(t):
            acc[rows, :] = dot(dglu_ref[rows, :d], w, 1, 1)

    @pl.when(s == 1)
    def _():
        w = flat(w_in_ref)
        w_attn = flat(w_attn_ref)
        odd = odd_ref[0] == 1
        half = d // 2
        for rows in cuts(t):
            du = acc[rows, :] + dot(dglu_ref[rows, d:], w, 1, 1)
            n, r = normal(second_ref[rows, :])
            d2 = d3_ref[rows, :] + normal_back(du, n, r, vec_ref[0:1, :])
            sums_ref[2:3, :] += total(du * n)
            sums_ref[3:4, :] += total(du)
            d2_ref[rows, :] = d2
            dout = d2.astype(BF)
            dout_ref[rows, :] = dout
            sums_ref[4:5, :] += total(dout.astype(F32))
            dm = dot(dout, w_attn, 1, 1)
            low, high = dm[:, :half], dm[:, half:]
            mine = jnp.where(odd, high, low).astype(BF)
            other = jnp.where(odd, low, high).astype(BF)
            for part in range(half // 128):
                cols = slice(part * 128, part * 128 + 128)
                mine_ref[part, rows, :] = mine[:, cols]
                other_ref[part, rows, :] = other[:, cols]


def mid_back(odd, dconv, follow, taps, val, sig, second, d3, w, u_attn, u_in, gain):
    t, d = d3.shape
    n, _, r, _ = w.shape
    return call(
        mid_back_kernel,
        (2,),
        [
            (odd, "smem", None),
            (dconv, None, None),
            (follow, None, None),
            (taps, None, None),
            (val, None, None),
            (sig, None, None),
            (second, None, None),
            (d3, None, None),
            (w, (n, 1, r, d), lambda s: (0, u_in + s, 0, 0)),
            (w, (n, 1, r, d), lambda s: (0, u_attn, 0, 0)),
            (gain, None, None),
        ],
        [
            ((t, d), F32, None, None),
            ((t, d), BF, None, None),
            ((t, 2 * d), BF, None, None),
            ((d // 256, t, 128), BF, None, None),
            ((d // 256, t, 128), BF, None, None),
            ((8, d), F32, None, None),
        ],
        [scr((t + 32, d), F32), scr((t, d), F32)],
        name="mid_back",
        flops=6 * t * d * d,
        moved=6 * d * d + 24 * t * d,
    )


def taps_kernel(dconv_ref, gated_ref, halo_ref, out_ref, pad, part):
    t, d = dconv_ref.shape
    reach = out_ref.shape[0]
    pad[0:32, :] = halo_ref[...].astype(F32)
    for rows in cuts(t):
        pad[pl.ds(rows.start + 32, CUT), :] = gated_ref[rows, :].astype(F32)
    part[...] = jnp.zeros_like(part)
    for c in range(0, d, COLS):
        cols = slice(c, c + COLS)

        def body(i, _):
            base = pl.multiple_of(i * ROWS, ROWS)
            window = pad[pl.ds(base, ROWS + 32), cols]
            here = dconv_ref[pl.ds(base, ROWS), cols]
            for b in range(8):
                sh = shifted(window, b)
                for a in range(0, 5):
                    m = 8 * a + b - 2
                    if 0 <= m < reach:
                        v = here * sh[8 * a : 8 * a + ROWS]
                        v = (v[0:8] + v[8:16]) + (v[16:24] + v[24:32])
                        part[8 * m : 8 * m + 8, cols] += v
            return 0

        lax.fori_loop(0, t // ROWS, body, 0)
    for m in range(reach):
        out_ref[m : m + 1, :] = total(part[8 * m : 8 * m + 8, :])


def taps_grad(dconv, gated, halo, reach):
    t, d = dconv.shape
    return call(
        taps_kernel,
        (1,),
        [(dconv, None, None), (gated, None, None), (halo, None, None)],
        [((reach, d), F32, None, None)],
        [scr((t + 32, d), F32), scr((8 * reach, d), F32)],
        name="taps_grad",
        flops=2 * t * d * reach,
        moved=6 * t * d,
    )[0]


def flipped_bit(index, mask):
    return index + mask - 2 * mask * lax.rem(lax.div(index, jnp.int32(mask)), jnp.int32(2))


def first_kernel(
    x_ref, w_ref, gains_ref, shifts_ref, taps_ref, bias_ref,
    inner_ref, act_ref, act_t_ref, unit_t_ref, tokens_ref, small_out_ref, w_out_ref,
    w, small, small_ref, tokens, unit, vec,
    own_send, own_recv, far_send, far_recv, core_send, core_recv, x_send, x_recv, x_load, w_leave,
):
    j = pl.program_id(0)
    n, k, r, d = w.shape
    t = tokens.shape[0]
    cut, thin_cut = r // 2, small.shape[1] // 2
    me, place = lax.axis_index("fsdp"), lax.axis_index("seq")
    two = jnp.int32(2)
    other_x, other_y, other_c = flipped_bit(me, 2), flipped_bit(me, 4), flipped_bit(me, 1)
    other_xy = flipped_bit(other_x, 4)
    to_x, to_y, to_c = {"fsdp": other_x}, {"fsdp": other_y}, {"fsdp": other_c}

    def send(src, dst, send_sem, recv_sem, device):
        return pltpu.make_async_remote_copy(
            src_ref=src, dst_ref=dst, send_sem=send_sem, recv_sem=recv_sem, device_id=device, device_id_type=MESH
        )

    def held(dev, u, rows=None):
        if u == k:
            return small.at[dev] if rows is None else small.at[dev, rows]
        return w.at[dev, u] if rows is None else w.at[dev, u, rows]

    def own(u):
        return small_ref if u == k else w_ref.at[u]

    def own_copies(u):
        return [
            send(own(u), held(me, u), own_send.at[i, u], own_recv.at[i, u], device)
            for i, device in enumerate((to_x, to_y, to_c))
        ]

    def keep_copy(u):
        return pltpu.make_async_copy(own(u), held(me, u), x_load.at[2 + u])

    def far_copies(u):
        half = thin_cut if u == k else cut
        top, low = pl.ds(0, half), pl.ds(half, half)
        return [
            send(held(other_x, u, top), held(other_x, u, top), far_send.at[0, u], far_recv.at[0, u], to_y),
            send(held(other_y, u, low), held(other_y, u, low), far_send.at[1, u], far_recv.at[1, u], to_x),
        ]

    def core_copy(i, u):
        dev = (other_x, other_y, other_xy)[i]
        return send(held(dev, u), held(dev, u), core_send.at[i, u], core_recv.at[i, u], to_c)

    def gather_begin(u):
        keep_copy(u).start()
        for copy in own_copies(u):
            copy.start()

    def gather_forward(u):
        across = own_copies(u)
        far = far_copies(u)
        across[0].wait_recv()
        far[0].start()
        core_copy(0, u).start()
        across[1].wait_recv()
        far[1].start()
        core_copy(1, u).start()

    def gather_far(u):
        for copy in far_copies(u):
            copy.wait_recv()
        core_copy(2, u).start()

    def gather_end(u):
        keep_copy(u).wait()
        own_copies(u)[2].wait_recv()
        for i in range(3):
            core_copy(i, u).wait_recv()

    def gather_sent(u):
        for copy in own_copies(u) + far_copies(u) + [core_copy(i, u) for i in range(3)]:
            copy.wait_send()

    side, half_of = lax.div(place, two), lax.rem(place, two)

    def token_rows(h):
        return pl.ds(pl.multiple_of(h * (t // 2), t // 2), t // 2)

    def token_copy(s):
        return send(x_ref.at[s], tokens.at[token_rows(half_of)], x_send.at[s], x_recv.at[half_of], {"seq": 2 * s + side})

    def token_keep(s):
        return pltpu.make_async_copy(x_ref.at[s], tokens.at[token_rows(half_of)], x_load.at[s])

    def token_arrived(h):
        return send(x_ref.at[0], tokens.at[token_rows(h)], x_send.at[0], x_recv.at[h], {"seq": flipped_bit(place, 1)})

    @pl.when(j == 0)
    def _():
        small_ref[...] = jnp.zeros_like(small_ref)
        at = 0
        for ref in (gains_ref, shifts_ref, taps_ref):
            small_ref[at : at + ref.shape[0], :] = ref[...]
            at += ref.shape[0]
        for layer in range(2):
            for q in range(4):
                row = at + 4 * layer + q
                small_ref[row : row + 1, :] = bias_ref[layer : layer + 1, q * r : (q + 1) * r]
        barrier = pltpu.get_barrier_semaphore()
        devices = [to_x, to_y, to_c, {"seq": flipped_bit(place, 1)}, {"seq": flipped_bit(place, 2)}, {"seq": 3 - place}]
        for device in devices:
            pl.semaphore_signal(barrier, inc=1, device_id=device, device_id_type=MESH)
        pl.semaphore_wait(barrier, 6)
        gather_begin(k)
        for s in range(2):
            away = 2 * s + side != place
            pl.when(away)(lambda s=s: token_copy(s).start())
            pl.when(jnp.logical_not(away))(lambda s=s: token_keep(s).start())
        for u in range(k):
            gather_begin(u)
        gather_forward(k)
        gather_far(k)
        gather_end(k)
        for dev in range(n):
            cols = slice(dev * r, (dev + 1) * r)
            vec[0:1, cols] = small[dev, 0:1, :].astype(F32)
            vec[1:2, cols] = small[dev, 6:7, :].astype(F32)
            for q in range(4):
                at = 4 * (dev % 2) + q
                vec[2 + dev // 2 : 3 + dev // 2, at * r : (at + 1) * r] = small[dev, 52 + q : 53 + q, :].astype(F32)
        gather_forward(0)
        gather_forward(1)
        for s in range(2):
            away = 2 * s + side != place
            pl.when(away)(lambda s=s: token_copy(s).wait_send())
            pl.when(jnp.logical_not(away))(lambda s=s: token_keep(s).wait())
        for h in range(2):
            pl.when(2 * half_of + h != place)(lambda h=h: token_arrived(h).wait_recv())
        gather_forward(2)
        gather_forward(3)
        for rows in cuts(t):
            c, _ = normal(tokens[rows, :].astype(F32))
            v = (c * vec[0:1, :] + vec[1:2, :]).astype(BF)
            unit[rows, :] = v
            unit_t_ref[:, rows] = v.T
        tokens_ref[...] = tokens[...]
        small_out_ref[...] = small[...]
        for u in range(k):
            gather_far(u)

    def leave(u):
        return pltpu.make_async_copy(w.at[:, u], w_out_ref.at[:, u], w_leave.at[u])

    for u in range(k):

        @pl.when(j == u)
        def _(u=u):
            gather_end(u)
            leave(u).start()

    weights = w[:, j].reshape(d, d)
    for rows in cuts(t):
        s = dot(unit[rows, :], weights, 1, 0) + vec[pl.ds(2 + j, 1), :]
        inner_ref[rows, :] = s.astype(BF)
        a = (s * jax.nn.sigmoid(s)).astype(BF)
        act_ref[rows, :] = a
        act_t_ref[:, rows] = a.T

    @pl.when(j == k - 1)
    def _():
        for u in range(k + 1):
            gather_sent(u)
        for u in range(k):
            leave(u).wait()


def first_forward(x, w, gains, shifts, taps, bias):
    _, half, d = x.shape
    k, r, _ = w.shape
    n, t = 8, 2 * half
    rows = 64
    dma = pltpu.SemaphoreType.DMA
    anywhere = pl.BlockSpec(memory_space=pl.ANY)

    def whole(*shape):
        return pl.BlockSpec(shape, lambda j: (0,) * len(shape))

    return pl.pallas_call(
        first_kernel,
        grid=(k,),
        in_specs=[anywhere] * 2 + [whole(*a.shape) for a in (gains, shifts, taps, bias)],
        out_specs=[
            pl.BlockSpec((t, d), lambda j: (0, j)),
            pl.BlockSpec((t, d), lambda j: (0, j)),
            pl.BlockSpec((d, t), lambda j: (j, 0)),
            whole(d, t),
            whole(t, d),
            whole(n, rows, r),
            anywhere,
        ],
        out_shape=[
            jax.ShapeDtypeStruct((t, k * d), BF),
            jax.ShapeDtypeStruct((t, k * d), BF),
            jax.ShapeDtypeStruct((k * d, t), BF),
            jax.ShapeDtypeStruct((d, t), BF),
            jax.ShapeDtypeStruct((t, d), BF),
            jax.ShapeDtypeStruct((n, rows, r), BF),
            jax.ShapeDtypeStruct((n, k, r, d), BF),
        ],
        scratch_shapes=[
            scr((n, k, r, d), BF),
            scr((n, rows, r), BF),
            scr((rows, r), BF),
            scr((t, d), BF),
            scr((t, d), BF),
            scr((8, d), F32),
            dma((3, k + 1)),
            dma((3, k + 1)),
            dma((2, k + 1)),
            dma((2, k + 1)),
            dma((3, k + 1)),
            dma((3, k + 1)),
            dma((2,)),
            dma((2,)),
            dma((2 + k + 1,)),
            dma((k,)),
        ],
        compiler_params=pltpu.CompilerParams(vmem_limit_bytes=VMEM, collective_id=3, has_side_effects=True),
        cost_estimate=pl.CostEstimate(flops=30_000_000_000, bytes_accessed=100_000_000, transcendentals=0),
        name="first",
    )(x, w, gains, shifts, taps, bias)


ORDER = [
    ("q", 0), ("q", 1), ("q", 2), ("m", 0), ("m", 1), ("in", 0), ("m", 2), ("in", 1), ("m", 3),
    ("in", 2), ("out", 0), ("in", 3), ("out", 1), ("out", 2), ("out", 3),
]
N_CHUNK = len(ORDER)
FIRST_IN = 5
LAST_IN = 11
AHEAD = 2
HELD = 6


def thin(count):
    return [pl.ds(i, 128) for i in range(0, count, 128)]


def last_kernel(
    gain_ref, table_ref, sums_2_ref, sums_3_ref, sums_4_ref, sums_5_ref, sums_7_ref, dbias_ref,
    d2_ref, first_ref, x_ref, dconv_ref, gated_ref, halo_ref, part_ref, dqkv_ref, unit_q_ref, act_ref, unit_ref, inner_ref, w_out_ref, w_in_ref,
    mixed_ref, dout_2_ref, unit_2_ref, dglu_ref, act_c_ref, dout_3_ref,
    out_ref, out_part_ref, small_out_ref, table_out_ref, dx_ref,
    odd, even, core, first, second, whole, near, far,
    left, right, wo, wi, inner, dout, acc,
    small_0, small_y, small_x, small_c, small_z, table_got, d0, d1, some, dconv, gated, pad, taps,
    left_sem, right_sem, wo_sem, wi_sem, inner_sem, out_sem, part_sem, some_sem, taps_sem,
    core_send, core_recv, first_send, first_recv, second_send, second_recv,
    z_send, z_recv, small_send, small_recv, table_send, table_recv, dx_send, dx_recv, dx_sem, free_sem,
):
    r, d = out_ref.shape[1:]
    n_part = part_ref.shape[0]
    t = x_ref.shape[0]
    cut = r // 2
    me = lax.axis_index("fsdp")
    place = lax.axis_index("seq")
    two, four = jnp.int32(2), jnp.int32(4)
    chip = lax.div(me, two)
    bit_c, bit_x, bit_y = lax.rem(me, two), lax.rem(chip, two), lax.div(me, four)
    middle = lax.rem(lax.div(place + 1, two), two)
    to_c = {"fsdp": flipped_bit(me, 1)}
    to_x = {"fsdp": flipped_bit(me, 2)}
    to_y = {"fsdp": flipped_bit(me, 4)}
    to_1 = {"seq": flipped_bit(place, 1)}
    to_2 = {"seq": 3 - place}

    barrier = pltpu.get_barrier_semaphore()
    for device in (to_c, to_x, to_y, to_1, to_2, {"seq": flipped_bit(place, 2)}):
        pl.semaphore_signal(barrier, inc=1, device_id=device, device_id_type=MESH)
    pl.semaphore_wait(barrier, 6)

    def send(src, dst, send_sem, recv_sem, device):
        return pltpu.make_async_remote_copy(
            src_ref=src, dst_ref=dst, send_sem=send_sem, recv_sem=recv_sem, device_id=device, device_id_type=MESH
        )

    def at_2(c):
        return lax.rem(c, two)

    def at_3(c):
        return lax.rem(c, jnp.int32(3))

    def on(c, begin, end, work):
        pl.when((c >= begin) & (c < end))(lambda: work(c))

    def factor_copies(c, name, unit):
        cols = slice(unit * d, unit * d + d)
        lefts = {"q": unit_q_ref, "in": unit_ref, "m": (mixed_ref, unit_2_ref, unit_2_ref, act_c_ref)[unit % 4]}
        rights = {
            "q": lambda: dqkv_ref.at[:, cols],
            "m": lambda: (
                dout_2_ref if unit == 0 else dout_3_ref if unit == 3 else dglu_ref.at[:, (unit - 1) * d : unit * d]
            ),
        }
        src = act_ref.at[:, unit] if name == "out" else lefts[name]
        copies = [pltpu.make_async_copy(src, left.at[at_2(c)], left_sem.at[at_2(c)])]
        if name in rights:
            copies.append(pltpu.make_async_copy(rights[name](), right.at[at_3(c)], right_sem.at[at_3(c)]))
        return copies

    def fetch(c):
        for i, (name, unit) in enumerate(ORDER):

            @pl.when(c == i)
            def _(i=i, name=name, unit=unit):
                for copy in factor_copies(c, name, unit):
                    copy.start()

    def fetched(c):
        pltpu.make_async_copy(unit_ref, left.at[at_2(c)], left_sem.at[at_2(c)]).wait()
        has_right = functools.reduce(
            jnp.logical_or, [c == i for i, (name, _) in enumerate(ORDER) if name in ("q", "m")]
        )

        @pl.when(has_right)
        def _():
            pltpu.make_async_copy(dout_2_ref, right.at[at_3(c)], right_sem.at[at_3(c)]).wait()

    def is_in(c):
        return (c >= FIRST_IN) & (c <= LAST_IN) & (at_2(c) == FIRST_IN % 2)

    def wo_copy(j):
        return pltpu.make_async_copy(w_out_ref.at[pl.ds(2 * j, 2), pl.ds(0, 4)], wo, wo_sem)

    def wi_copy(j):
        return pltpu.make_async_copy(w_in_ref.at[:, j], wi, wi_sem)

    def wq_copy(i):
        return pltpu.make_async_copy(w_out_ref.at[:, 4 + i], wi, wi_sem)

    def inner_copy(j):
        return pltpu.make_async_copy(inner_ref.at[:, pl.ds(pl.multiple_of(j * d, d), d)], inner, inner_sem)

    def x_copy():
        return pltpu.make_async_copy(x_ref, inner, inner_sem)

    row = 53

    def hidden(c):
        j = lax.div(c - FIRST_IN, two)
        wo_copy(j).wait()
        inner_copy(j).wait()
        w = wo[...].reshape(d, d)
        dbias = jnp.zeros((1, d), F32)
        for rows in thin(t):
            da = dot(dout[rows, :], w, 1, 1)
            v = (da * silu_slope(inner[rows, :].astype(F32))).astype(BF)
            right[at_3(c), rows, :] = v
            dbias = dbias + total(v.astype(F32))
        for dev in range(2):
            for q in range(4):
                cols = pl.ds(pl.multiple_of((2 * j + dev) * r, r), r)
                small_0[row + 3 + q : row + 4 + q, cols] = dbias[:, dev * 4 * r + q * r : dev * 4 * r + (q + 1) * r]

        @pl.when(j < 3)
        def _():
            wo_copy(j + 1).start()
            inner_copy(j + 1).start()

        @pl.when(j == 3)
        def _():
            x_copy().start()

    def product(c):
        for i in range(4):
            value = dot(left[at_2(c), 2 * i : 2 * i + 2].reshape(2 * r, t), right[at_3(c)], 1, 0).astype(BF)
            low, high = value[:r], value[r:]
            p = i + bit_x - 2 * bit_x * (i % 2)
            p = p + 2 * bit_y - 4 * bit_y * lax.div(p, two)
            even[at_2(c), p] = jnp.where(bit_c == 0, low, high)
            odd[at_2(c), p] = jnp.where(bit_c == 0, high, low)

    def through(c, fresh):
        wi_copy(0).wait()
        w = wi[...].reshape(d, d)
        for rows in thin(t):
            p = dot(right[at_3(c), rows, :], w, 1, 1)
            acc[rows, :] = p + jnp.where(fresh, 0.0, acc[rows, :])

    def back(c):
        j = lax.div(c - FIRST_IN, two)
        through(c, j == 0)
        pl.when(j < 3)(lambda: wi_copy(j + 1).start())

    def back_q(c):
        through(c, c == 0)
        pl.when(c < 2)(lambda: wq_copy(c + 1).start())
        pl.when(c == 2)(lambda: wi_copy(0).start())
        column = total(right[at_3(c)].astype(F32))

        @pl.when(c == 0)
        def _():
            small_0[11:12, :] = column

        @pl.when(c == 2)
        def _():
            small_0[12:13, :] = column
            middle_gradient()

    def middle_gradient():
        pltpu.make_async_copy(d2_ref, d1, some_sem).wait()
        for rows in thin(t):
            copy = pltpu.make_async_copy(first_ref.at[rows], some, some_sem)
            copy.start()
            copy.wait()
            n, scale = normal(some[...])
            du = acc[rows, :]
            value = d1[rows, :] + normal_back(du, n, scale, gain_ref[1:2, :])
            d1[rows, :] = value
            small_0[0:1, :] += total(du * n)
            small_0[5:6, :] += total(du)
            v = (HALF * value).astype(BF)
            dout[rows, :] = v
            small_0[row + 2 : row + 3, :] += total(v.astype(F32))

    def taps_copies(b):
        cols = pl.ds(pl.multiple_of(b * COLS, COLS), COLS)
        return [
            pltpu.make_async_copy(dconv_ref.at[:, cols], dconv, taps_sem.at[0]),
            pltpu.make_async_copy(halo_ref.at[:, cols], gated.at[pl.ds(0, 32)], taps_sem.at[1]),
            pltpu.make_async_copy(gated_ref.at[:, cols], gated.at[pl.ds(32, t)], taps_sem.at[2]),
        ]

    def taps_columns(b):
        for copy in taps_copies(b):
            copy.wait()
        pad[...] = gated[...].astype(F32)
        taps[...] = jnp.zeros_like(taps)
        reach = taps.shape[0] // 8

        def body(i, _):
            base = pl.multiple_of(i * ROWS, ROWS)
            window = pad[pl.ds(base, ROWS + 32), :]
            here = dconv[pl.ds(base, ROWS), :]
            for q in range(8):
                sh = shifted(window, q)
                for a in range(0, 5):
                    m = 8 * a + q - 2
                    if 0 <= m < reach:
                        v = here * sh[8 * a : 8 * a + ROWS]
                        taps[8 * m : 8 * m + 8, :] += (v[0:8] + v[8:16]) + (v[16:24] + v[24:32])
            return 0

        lax.fori_loop(0, t // ROWS, body, 0)
        cols = pl.ds(pl.multiple_of(b * COLS, COLS), COLS)
        for m in range(reach):
            small_0[18 + m : 19 + m, cols] = total(taps[8 * m : 8 * m + 8, :])

        @pl.when(b < d // COLS - 1)
        def _():
            for copy in taps_copies(b + 1):
                copy.start()

    def held_at(c):
        return lax.rem(c, jnp.int32(HELD))

    def core_copy(c):
        return send(odd.at[at_2(c)], core.at[held_at(c)], core_send.at[c], core_recv.at[c], to_c)

    def make(c):
        fetch(c + 1)
        fetched(c)

        is_out = functools.reduce(jnp.logical_or, [c == i for i, (name, _) in enumerate(ORDER) if name == "out"])

        @pl.when(is_out)
        def _():
            right[at_3(c)] = dout[...]

        pl.when(is_in(c))(lambda: hidden(c))
        product(c)
        pl.when(c >= HELD)(lambda: pl.semaphore_wait(free_sem, 1))
        core_copy(c).start()

    def make_back(c):
        pl.when(is_in(c))(lambda: back(c))
        pl.when(c < 3)(lambda: back_q(c))

    def first_copies(c):
        top, rest = pl.ds(0, cut), pl.ds(cut, cut)
        o = held_at(c)
        return [
            send(core.at[o, 1, top], first.at[o, 0, 0], first_send.at[c, 0], first_recv.at[c, 0], to_x),
            send(core.at[o, 3, top], first.at[o, 0, 1], first_send.at[c, 1], first_recv.at[c, 1], to_x),
            send(core.at[o, 2, rest], first.at[o, 1, 0], first_send.at[c, 2], first_recv.at[c, 2], to_y),
            send(core.at[o, 3, rest], first.at[o, 1, 1], first_send.at[c, 3], first_recv.at[c, 3], to_y),
        ]

    def second_copies(c):
        o = held_at(c)
        return [
            send(first.at[o, 0, 1], second.at[o, 0], second_send.at[c, 0], second_recv.at[c, 0], to_y),
            send(first.at[o, 1, 1], second.at[o, 1], second_send.at[c, 1], second_recv.at[c, 1], to_x),
        ]

    def add_core(c):
        core_copy(c).wait()
        o = held_at(c)

        def rows(i, _):
            at = pl.ds(pl.multiple_of(i * 32, 32), 32)
            for b in range(4):
                core[o, b, at] = (core[o, b, at].astype(F32) + even[at_2(c), b, at].astype(F32)).astype(BF)
            return 0

        lax.fori_loop(0, r // 32, rows, 0)
        for copy in first_copies(c):
            copy.start()

    def add_first(c):
        for copy in first_copies(c):
            copy.wait()
        o = held_at(c)

        def rows(i, _):
            at = pl.ds(pl.multiple_of(i * 32, 32), 32)
            low_at = pl.ds(pl.multiple_of(cut + i * 32, 32), 32)
            for b in range(2):
                first[o, 0, b, at] = (first[o, 0, b, at].astype(F32) + core[o, 2 * b, at].astype(F32)).astype(BF)
                first[o, 1, b, at] = (first[o, 1, b, at].astype(F32) + core[o, b, low_at].astype(F32)).astype(BF)
            return 0

        lax.fori_loop(0, cut // 32, rows, 0)

        @pl.when(c < N_CHUNK - HELD)
        def _():
            pl.semaphore_signal(free_sem, inc=1, device_id=to_c, device_id_type=MESH)

        for copy in second_copies(c):
            copy.start()

    def add_second(c):
        for copy in second_copies(c):
            copy.wait()
        o = held_at(c)
        whole[c, 0:cut] = (first[o, 0, 0].astype(F32) + second[o, 0].astype(F32)).astype(BF)
        whole[c, cut:r] = (first[o, 1, 0].astype(F32) + second[o, 1].astype(F32)).astype(BF)
        z_begin(c)

    z_begin, z_step = z_line(middle, to_1, to_2, whole, near, far, z_send, z_recv)

    def result_do(i, act):
        for is_middle, src in ((1, far), (0, near)):
            chunk = pltpu.make_async_copy(src.at[i], out_ref.at[i], out_sem.at[i])
            part = pltpu.make_async_copy(src.at[i], out_part_ref.at[i - N_CHUNK], out_sem.at[i])
            pl.when((middle == is_middle) & (i < N_CHUNK))(lambda chunk=chunk: act(chunk))
            pl.when((middle == is_middle) & (i >= N_CHUNK))(lambda part=part: act(part))

    def z_stage(i, stage):
        z_step(i, stage)
        if stage == 2:
            result_do(i, lambda copy: copy.start())

    wide = [d // 2, d // 4, d // 8]
    bits = [bit_y, bit_x, bit_c]
    held = [small_0, small_y, small_x, small_c]
    partner = [to_y, to_x, to_c, to_1, to_2]

    def columns(step, bit):
        return pl.ds(pl.multiple_of(bit * wide[step], wide[step]), wide[step])

    def small_copy(step):
        sems = (small_send.at[step], small_recv.at[step])
        if step < 3:
            return send(held[step].at[:, columns(step, 1 - bits[step])], held[step + 1], *sems, partner[step])
        if step == 3:
            return send(small_c, small_z.at[0], *sems, partner[step])
        return send(small_z.at[0], small_z.at[1], *sems, partner[step])

    def small_step(step):
        small_copy(step).wait()
        if step < 3:
            held[step + 1][...] += held[step][:, columns(step, bits[step])]
        elif step == 3:
            small_z[0] = small_z[0] + small_c[...]
        else:
            small_out_ref[...] = small_z[0] + small_z[1]
        if step < 4:
            small_copy(step + 1).start()

    def table_copy(step):
        src = table_ref if step == 0 else table_got.at[step - 1]
        return send(src, table_got.at[step], table_send.at[step], table_recv.at[step], partner[step])

    def table_step(step):
        table_copy(step).wait()
        before = table_ref[...] if step == 0 else table_got[step - 1]
        table_got[step] = table_got[step] + before
        if step < 4:
            table_copy(step + 1).start()
        else:
            table_out_ref[...] = table_got[step]

    mine, seq = lax.rem(place, two), lax.div(place, two)

    def dx_copy(h):
        return send(d0.at[pl.ds(h * (t // 2), t // 2)], dx_ref.at[seq], dx_send.at[h], dx_recv.at[seq], {"seq": 2 * mine + h})

    def dx_keep(h):
        return pltpu.make_async_copy(d0.at[pl.ds(h * (t // 2), t // 2)], dx_ref.at[seq], dx_sem)

    def dx_arrived(s):
        return send(d0.at[pl.ds(0, t // 2)], dx_ref.at[s], dx_send.at[0], dx_recv.at[s], to_1)

    def input_gradient():
        x_copy().wait()
        for rows in thin(t):
            n, scale = normal(inner[rows, :].astype(F32))
            du = acc[rows, :]
            d0[rows, :] = (d1[rows, :] + normal_back(du, n, scale, gain_ref[0:1, :])).astype(BF)
            small_0[row : row + 1, :] += total(du * n)
            small_0[row + 1 : row + 2, :] += total(du)
        for h in range(2):
            away = 2 * mine + h != place
            pl.when(away)(lambda h=h: dx_copy(h).start())
            pl.when(jnp.logical_not(away))(lambda h=h: dx_keep(h).start())
        small_copy(0).start()

    def part_copy(i):
        return pltpu.make_async_copy(part_ref.at[i], whole.at[N_CHUNK + i], part_sem.at[i])

    fetch(jnp.int32(0))
    wq_copy(0).start()
    pltpu.make_async_copy(d2_ref, d1, some_sem).start()
    for copy in taps_copies(jnp.int32(0)):
        copy.start()
    for i in range(n_part):
        part_copy(i).start()
    table_copy(0).start()
    wo_copy(0).start()
    inner_copy(0).start()
    small_0[...] = jnp.zeros_like(small_0)
    here = {1: (sums_2_ref, 2), 2: (sums_3_ref, 1), 3: (sums_4_ref, 0), 4: (sums_5_ref, 0), 6: (sums_2_ref, 3)}
    here.update({7: (sums_3_ref, 2), 8: (sums_4_ref, 1), 9: (sums_5_ref, 1), 10: (sums_7_ref, 0), 13: (sums_2_ref, 4)})
    here.update({14: (sums_2_ref, 0), 15: (sums_2_ref, 1), 16: (sums_3_ref, 3), 17: (sums_3_ref, 0)})
    for at, (ref, i) in here.items():
        small_0[at : at + 1, :] = ref[i : i + 1, :]
    for j in range(4):
        for dev in range(2):
            for q in range(4):
                cols = slice((2 * j + dev) * r, (2 * j + dev + 1) * r)
                small_0[49 + q : 50 + q, cols] = dbias_ref[j, :, (4 * dev + q) * r : (4 * dev + q + 1) * r]
    for i in range(n_part):
        part_copy(i).wait()
    for c in range(AHEAD):
        make(jnp.int32(c))

    def slot(k, _):
        on(k, 0, N_CHUNK, add_core)
        on(k - 1, 0, N_CHUNK, add_first)
        on(k - 2, 0, N_CHUNK, add_second)
        for stage in range(3):
            on(k - 3 - stage, 0, N_CHUNK, lambda c, stage=stage: z_stage(c, stage))
        on(k, 0, n_part, lambda i: z_begin(N_CHUNK + i))
        for stage in range(3):
            on(k - 1 - stage, 0, n_part, lambda i, stage=stage: z_stage(N_CHUNK + i, stage))
        make_back(k)
        on(k + AHEAD, 0, N_CHUNK, make)
        pl.when(k == LAST_IN)(input_gradient)
        on(k - 1, 0, d // COLS, taps_columns)
        for step in range(5):
            pl.when(k == step)(lambda step=step: table_step(step))
            pl.when(k == LAST_IN + 1 + step)(lambda step=step: small_step(step))
        return 0

    lax.fori_loop(0, N_CHUNK + 5, slot, 0)
    for h in range(2):
        away = 2 * mine + h != place
        pl.when(away)(lambda h=h: dx_copy(h).wait_send())
        pl.when(jnp.logical_not(away))(lambda h=h: dx_keep(h).wait())
    for s in range(2):
        from_away = 2 * s + lax.div(place, two) != place
        pl.when(from_away)(lambda s=s: dx_arrived(s).wait_recv())

    def settle(i, _):
        result_do(i, lambda copy: copy.wait())
        return 0

    lax.fori_loop(0, N_CHUNK + n_part, settle, 0)


def last_reduced(
    gain, table, sums, dbias, d2, first, tokens, dconv, gated, halo, part, dqkv, unit_q, act_t, unit_t, inner, w_out, w_in, mixed_t, dout_2, unit_2, dglu, act_c, dout_3
):
    n, _, r, d = w_in.shape
    t = tokens.shape[0]
    rows = 64
    k = N_CHUNK
    m = part.shape[0]
    z = k + m
    dma = pltpu.SemaphoreType.DMA
    anywhere = pl.BlockSpec(memory_space=pl.ANY)
    vmem = pl.BlockSpec(memory_space=pltpu.VMEM)
    return pl.pallas_call(
        last_kernel,
        in_specs=[vmem] * 8 + [anywhere] * 20,
        out_specs=[anywhere, anywhere, vmem, vmem, anywhere],
        out_shape=[
            jax.ShapeDtypeStruct((k, r, d), BF),
            jax.ShapeDtypeStruct((m, r, d), BF),
            jax.ShapeDtypeStruct((rows, d // 8), F32),
            jax.ShapeDtypeStruct(table.shape, F32),
            jax.ShapeDtypeStruct((2, t // 2, d), BF),
        ],
        scratch_shapes=[
            scr((2, 4, r, d), BF),
            scr((2, 4, r, d), BF),
            scr((HELD, 4, r, d), BF),
            scr((HELD, 2, 2, r // 2, d), BF),
            scr((HELD, 2, r // 2, d), BF),
            scr((z, r, d), BF),
            scr((z, r, d), BF),
            scr((z, r, d), BF),
            scr((2, n, r, t), BF),
            scr((3, t, d), BF),
            scr((2, 4, r, d), BF),
            scr((n, r, d), BF),
            scr((t, d), BF),
            scr((t, d), BF),
            scr((t, d), F32),
            scr((rows, d), F32),
            scr((rows, d // 2), F32),
            scr((rows, d // 4), F32),
            scr((rows, d // 8), F32),
            scr((2, rows, d // 8), F32),
            scr((5,) + table.shape, F32),
            scr((t, d), BF),
            scr((t, d), F32),
            scr((128, d), F32),
            scr((t, COLS), F32),
            scr((t + 32, COLS), BF),
            scr((t + 32, COLS), F32),
            scr((8 * 31, COLS), F32),
            dma((2,)),
            dma((3,)),
            dma,
            dma,
            dma,
            dma((z,)),
            dma((m,)),
            dma,
            dma((3,)),
            dma((k,)),
            dma((k,)),
            dma((k, 4)),
            dma((k, 4)),
            dma((k, 2)),
            dma((k, 2)),
            dma((z, 3)),
            dma((z, 3)),
            dma((5,)),
            dma((5,)),
            dma((5,)),
            dma((5,)),
            dma((2,)),
            dma((2,)),
            dma,
            pltpu.SemaphoreType.REGULAR,
        ],
        compiler_params=pltpu.CompilerParams(vmem_limit_bytes=60 << 20, collective_id=0, has_side_effects=True),
        cost_estimate=pl.CostEstimate(flops=100_000_000_000, bytes_accessed=400_000_000, transcendentals=0),
        name="last",
    )(
        gain, table, *sums, dbias, d2, first, tokens, dconv, gated, halo, part, dqkv, unit_q.reshape(n, r, t), act_t.reshape(n, 4, r, t),
        unit_t.reshape(n, r, t), inner, w_out, w_in,
        mixed_t.reshape(n, r, t), dout_2, unit_2.reshape(n, r, t), dglu, act_c.reshape(n, r, t), dout_3,
    )


PLACE = {item: i for i, item in enumerate(ORDER)}


def finish_kernel(n_tap, main, in_b, out_b, small, table, g_in, g_out, g_qkv, g_attn, g_conv_in, g_conv_out, g_taps, g_gain, g_shift, g_bias, g_table):
    d = main.shape[-1]

    def of(name, unit):
        return main[PLACE[name, unit]].astype(F32)

    for u in range(4):
        cols = slice(u * d, (u + 1) * d)
        g_in[0, :, cols] = of("in", u)
        g_in[1, :, cols] = in_b[u].astype(F32)
        g_out[0, u] = of("out", u)
        g_out[1, u] = out_b[u].astype(F32)
    for u in range(3):
        g_qkv[u] = of("q", u)
    g_attn[...] = of("m", 0)
    g_conv_in[:, :d] = of("m", 1)
    g_conv_in[:, d:] = of("m", 2)
    g_conv_out[...] = of("m", 3)
    w = g_taps.shape[1]
    early, late = 0, 22 + n_tap
    g_taps[...] = small[18 : 18 + n_tap, :]
    g_gain[0:1, :] = small[late : late + 1, :]
    g_gain[1:6, :] = small[0:5, :]
    g_shift[0:1, :] = small[late + 1 : late + 2, :]
    g_shift[1:6, :] = small[5:10, :]
    g_shift[6:7, :] = small[late + 2 : late + 3, :]
    g_shift[7:15, :] = small[10:18, :]
    for u in range(4):
        g_bias[0:1, u * w : (u + 1) * w] = small[late + 3 + u : late + 4 + u, :]
        g_bias[1:2, u * w : (u + 1) * w] = small[18 + n_tap + u : 19 + n_tap + u, :]
    k, h = g_table.shape
    g_table[...] = table[0:k, 0:h] + table[0:k, h : 2 * h]


def finished(main, in_b, out_b, small, table, n_tap, table_shape):
    k, r, d = main.shape
    w = small.shape[1]
    step = min(r, 32)

    def rows(count):
        return pl.BlockSpec((count, step, d), lambda i: (0, i, 0))

    def whole(*shape):
        return pl.BlockSpec(shape, lambda i: (0,) * len(shape))

    outs = [
        ((2, r, 4 * d), pl.BlockSpec((2, step, 4 * d), lambda i: (0, i, 0))),
        ((2, 4, r, d), pl.BlockSpec((2, 4, step, d), lambda i: (0, 0, i, 0))),
        ((3, r, d), rows(3)),
        ((r, d), pl.BlockSpec((step, d), lambda i: (i, 0))),
        ((r, 2 * d), pl.BlockSpec((step, 2 * d), lambda i: (i, 0))),
        ((r, d), pl.BlockSpec((step, d), lambda i: (i, 0))),
        ((n_tap, w), whole(n_tap, w)),
        ((6, w), whole(6, w)),
        ((15, w), whole(15, w)),
        ((2, 4 * w), whole(2, 4 * w)),
        (table_shape, whole(*table_shape)),
    ]
    return pl.pallas_call(
        functools.partial(finish_kernel, n_tap),
        grid=(r // step,),
        in_specs=[rows(k), rows(4), rows(4), whole(*small.shape), whole(*table.shape)],
        out_specs=[b for _, b in outs],
        out_shape=[jax.ShapeDtypeStruct(s, F32) for s, _ in outs],
        compiler_params=pltpu.CompilerParams(vmem_limit_bytes=VMEM),
        cost_estimate=pl.CostEstimate(flops=0, bytes_accessed=18_000_000, transcendentals=0),
        name="finish",
    )(main, in_b, out_b, small, table)


def xor_route(axis, mask):
    return [(i, i ^ mask) for i in range(lax.axis_size(axis))]


def swapped(block, axis, mask):
    return lax.ppermute(block, axis, xor_route(axis, mask))


def after(value, *marks):
    return lax.optimization_barrier((value,) + marks)[0]


def over_seq(part):
    if lax.axis_size("seq") != 4 or part.shape[1] < 64:
        return lax.psum(part, "seq")
    place = lax.axis_index("seq")
    part = part.astype(F32)
    for mask in (1, 2):
        high = (place & mask) != 0
        half = part.shape[1] // 2
        first, second = part[:, :half], part[:, half:]
        sent = jnp.where(high, first, second).astype(BF)
        part = jnp.where(high, second, first) + swapped(sent, "seq", mask).astype(F32)
    part = part.astype(BF)
    for mask in (2, 1):
        high = (place & mask) != 0
        got = swapped(part, "seq", mask)
        part = jnp.where(high, jnp.concatenate([got, part], axis=1), jnp.concatenate([part, got], axis=1))
    return part


def reduced(g):
    return over_seq(lax.psum_scatter(g, "fsdp", scatter_dimension=0, tiled=False))


def small_reduced(rows):
    k, d = rows.shape
    n = lax.axis_size("fsdp")
    me = lax.axis_index("fsdp")
    rows = lax.psum(rows, ("seq", "fsdp"))
    return lax.dynamic_slice_in_dim(rows, me * (d // n), d // n, 1)


def to_pairs(array, place):
    one, two = array[0], array[1]
    got = lax.ppermute(jnp.where(place % 2 == 0, two, one), "seq", [(0, 2), (1, 0), (2, 3), (3, 1)])
    more = lax.ppermute(jnp.where(place == 1, two, one), "seq", [(1, 2), (2, 1)])
    first = jnp.where(place == 0, one, jnp.where(place == 1, more, got))
    second = jnp.where(place < 2, got, jnp.where(place == 2, more, two))
    return jnp.concatenate([first, second], axis=0)


def from_pairs(array, place):
    half = array.shape[0] // 2
    first, second = array[:half], array[half:]
    got = lax.ppermute(jnp.where(place < 2, second, first), "seq", [(2, 0), (0, 1), (3, 2), (1, 3)])
    more = lax.ppermute(jnp.where(place == 1, first, second), "seq", [(1, 2), (2, 1)])
    one = jnp.where(place == 0, first, jnp.where(place == 2, more, got))
    two = jnp.where(place == 3, second, jnp.where(place == 1, more, got))
    return jnp.stack([one, two])


def on_device(
    inputs,
    lengths,
    ffn_in,
    ffn_in_bias,
    ffn_out,
    qkv,
    attn_out,
    conv_in,
    conv_out,
    depthwise,
    gains,
    shifts,
    distance,
    grad_out,
):
    n = lax.axis_size("fsdp")
    me = lax.axis_index("fsdp")
    place = lax.axis_index("seq")
    odd = place % 2 == 1
    odd_word = (place % 2).astype(jnp.int32).reshape(1)
    me_word = me.astype(jnp.int32).reshape(1)
    width = inputs.shape[2]
    r = width // n
    inner_width = ffn_in.shape[2]
    n_gain, n_shift, n_tap = gains.shape[0], shifts.shape[0], depthwise.shape[0]
    cubed = n == 8 and lax.axis_size("seq") == 4

    def chunks(part):
        return [part[:, i : i + width] for i in range(0, part.shape[1], width)]

    shard_a = jnp.stack(chunks(ffn_in[0]))
    shard_b = jnp.concatenate([ffn_out[0].reshape(4, r, width), qkv], axis=0)
    shard_c = jnp.stack(chunks(ffn_in[1]) + [attn_out] + chunks(conv_in) + [conv_out])
    shard_d = ffn_out[1].reshape(4, r, width)
    if cubed:
        w_b = lax.all_gather(shard_b, "fsdp", axis=0)
        inner_a, act_a, act_t_a, unit_t_a, tokens, small, w_a = first_forward(
            inputs, after(shard_a, shard_b), gains, shifts, depthwise, ffn_in_bias
        )
        cotangent = to_pairs(after(grad_out, act_a), place)
    else:
        small = jnp.concatenate([gains, shifts, depthwise, ffn_in_bias.reshape(-1, r)], axis=0)
        small = lax.all_gather(small, "fsdp", axis=0)
        w_a = lax.all_gather(shard_a, "fsdp", axis=0)
        w_b = lax.all_gather(shard_b, "fsdp", axis=0)
        tokens, cotangent = to_pairs(inputs, place), to_pairs(grad_out, place)

    small = small.astype(F32)
    rows = jnp.transpose(small, (1, 0, 2))
    n_plain = n_gain + n_shift + n_tap
    gain = rows[:n_gain].reshape(n_gain, width)
    shift = rows[n_gain : n_gain + n_shift].reshape(n_shift, width)
    taps = rows[n_gain + n_shift : n_plain].reshape(n_tap, width)
    bias = small[:, n_plain : n_plain + 8].reshape(n, 2, -1).transpose(1, 0, 2).reshape(2, inner_width)

    length = jnp.where(place < 2, lengths[0], lengths[1]).reshape(1)
    wide, ends = tables(distance)
    pairs = [(0, 1), (2, 3)]

    if not cubed:
        inner_a, act_a, act_t_a, unit_t_a = ffn_in_forward(tokens, jnp.stack([gain[0], shift[0]]), bias[0], w_a, 0)
    w_c = lax.all_gather(after(shard_c, w_b, cotangent, act_a), "fsdp", axis=0)
    first, unit_t_1, mine, other = out_qkv_forward(
        odd_word, tokens, act_a, w_b, jnp.stack([shift[6], gain[1], shift[1], shift[8], shift[9]])
    )
    probs, heads, mixed = attend(mine, other, length, wide, ends)
    w_d = lax.all_gather(after(shard_d, w_c, mixed), "fsdp", axis=0)
    second, mixed_t, unit_t_2, val, sig, gated = mid_forward(
        first, mixed, w_c, 4, 5, jnp.stack([shift[10], gain[2], shift[2], shift[11], shift[12]])
    )
    count = gated.shape[0]
    halo = lax.ppermute(gated[count - 32 :], "seq", pairs)
    conv, act_t_c, third = conv_forward(
        gated, halo, taps, jnp.stack([shift[13], gain[3], shift[3], shift[14]]), second, w_c, 7
    )
    inner_b, act_b, act_t_b, unit_t_b = ffn_in_forward(third, jnp.stack([gain[4], shift[4]]), bias[1], w_c, 0)
    outputs, d4, sums_5 = out_last(third, act_b, w_d, 0, cotangent, jnp.stack([shift[7], gain[5], shift[5]]))
    outputs = from_pairs(outputs, place)

    dinner, dout, dbias_b, sums_7 = ffn_hidden_back(d4, inner_b, w_d, 0)
    g_out_b = weight_grad(act_t_b, dout, n, 4, 0, True)
    g_in_b = weight_grad(unit_t_b, after(dinner, g_out_b), n, 4, 0, False)
    part_out_b = lax.psum_scatter(g_out_b, "fsdp", scatter_dimension=0, tiled=False)
    part_in_b = lax.psum_scatter(g_in_b, "fsdp", scatter_dimension=0, tiled=False)
    dinner = after(dinner, g_in_b)
    d3, sums_4 = norm_input_back(d4, dinner, third, w_c, 0, gain[4:5])
    d3, outputs = lax.optimization_barrier((d3, outputs))
    dconv, dout_3, sums_3 = conv_out_back(d3, conv, w_c, 7, jnp.stack([gain[3], shift[3]]))
    follow = lax.ppermute(dconv[:32], "seq", [(j, i) for i, j in pairs])
    d2, dout_2, dglu, mine, other, sums_2 = mid_back(
        odd_word, dconv, follow, taps, val, sig, second, d3, w_c, 4, 5, gain[2:3]
    )
    if cubed:
        dqkv, dtable, share_out_b = attend_back(heads, probs, wide, mine, other, part_out_b)
    else:
        dqkv, dtable = attend_back(heads, probs, wide, mine, other)
        share_out_b, share_in_b = over_seq(part_out_b), over_seq(part_in_b)

    def biases(part):
        return part.reshape(n, 4, r).transpose(1, 0, 2).reshape(4, width)

    if cubed:
        main, share_in_b, small, table, grad_tokens = last_reduced(
            gain[0:2], dtable, (sums_2, sums_3, sums_4, sums_5, sums_7), dbias_b, d2, first, tokens, dconv, gated, halo,
            part_in_b, dqkv, unit_t_1, act_t_a, unit_t_a, inner_a, w_b, w_a,
            mixed_t, dout_2, unit_t_2, dglu, act_t_c, dout_3,
        )
    else:
        d1, sums_1 = norm_input_back(d2, dqkv, first, w_b, 4, gain[1:2])
        bias_sums = jnp.sum(dqkv.astype(F32), axis=0)
        dtaps = taps_grad(dconv, gated, halo, n_tap)
        early = jnp.concatenate(
            [
                jnp.stack([sums_1[0], sums_2[2], sums_3[1], sums_4[0], sums_5[0]]),
                jnp.stack([sums_1[1], sums_2[3], sums_3[2], sums_4[1], sums_5[1]]),
                jnp.stack(
                    [
                        sums_7[0],
                        bias_sums[:width],
                        bias_sums[2 * width :],
                        sums_2[4],
                        sums_2[0],
                        sums_2[1],
                        sums_3[3],
                        sums_3[0],
                    ]
                ),
                dtaps,
                biases(dbias_b),
            ],
            axis=0,
        )
        dinner, dout, dbias_a, sums_6 = ffn_hidden_back(d1, inner_a, w_b, 0)
        g_m = weight_grad(unit_t_2, dglu, n, 4, 1, False)
        g_m = weight_grad(mixed_t, dout_2, n, 4, 0, False, into=g_m)
        g_m = weight_grad(act_t_c, dout_3, n, 4, 3, False, into=g_m)
        shares = {
            "m": reduced(g_m),
            "q": reduced(weight_grad(unit_t_1, dqkv, n, 3, 0, False)),
            "out": reduced(weight_grad(act_t_a, dout, n, 4, 0, True)),
            "in": reduced(weight_grad(unit_t_a, dinner, n, 4, 0, False)),
        }
        main = jnp.stack([shares[name][unit] for name, unit in ORDER])
        d0, sums_0 = norm_input_back(d1, dinner, tokens, w_a, 0, gain[0:1], BF)
        grad_tokens = from_pairs(d0, place)
        late = jnp.concatenate([jnp.stack([sums_0[0], sums_0[1], sums_6[0]]), biases(dbias_a)], axis=0)
        small = small_reduced(jnp.concatenate([early, late], axis=0))
        table = lax.psum(dtable, ("seq", "fsdp"))
    g_in, g_out, g_qkv, g_attn, g_conv_in, g_conv_out, g_taps, g_gain, g_shift, g_bias, total_table = finished(
        main, share_in_b, share_out_b, small, table, n_tap, distance.shape
    )
    return (
        outputs,
        grad_tokens,
        g_in,
        g_bias,
        g_out.reshape(2, 4 * r, width),
        g_qkv,
        g_attn,
        g_conv_in,
        g_conv_out,
        g_taps,
        g_gain,
        g_shift,
        total_table,
    )


def solution(mesh):
    return jax.shard_map(
        on_device,
        mesh=mesh,
        in_specs=(
            P("fsdp", "seq", None),
            P("fsdp"),
            P(None, "fsdp", None),
            P(None, "fsdp"),
            P(None, "fsdp", None),
            P(None, "fsdp", None),
            P("fsdp", None),
            P("fsdp", None),
            P("fsdp", None),
            P(None, "fsdp"),
            P(None, "fsdp"),
            P(None, "fsdp"),
            P(),
            P("fsdp", "seq", None),
        ),
        out_specs=(
            P("fsdp", "seq", None),
            P("fsdp", "seq", None),
            P(None, "fsdp", None),
            P(None, "fsdp"),
            P(None, "fsdp", None),
            P(None, "fsdp", None),
            P("fsdp", None),
            P("fsdp", None),
            P("fsdp", None),
            P(None, "fsdp"),
            P(None, "fsdp"),
            P(None, "fsdp"),
            P(),
        ),
        check_vma=False,
    )
```

```python
import functools

import jax
import jax.numpy as jnp
from jax import lax
from jax.experimental import pallas as pl
from jax.experimental.pallas import tpu as pltpu
from jax.sharding import PartitionSpec as P

HEAD_DIM=64; LEFT=64; RIGHT=8
F32=jnp.float32; BF=jnp.bfloat16
RB=256
PADL=128
WIN=512

def dot(a,b,ca,cb):
    return lax.dot_general(a,b,(((ca,),(cb,)),((),())),preferred_element_type=F32)

def lanes(shape):
    return lax.broadcasted_iota(jnp.int32,shape,1)

def band_offset():
    row=lax.broadcasted_iota(jnp.int32,(RB,WIN),0)
    col=lax.broadcasted_iota(jnp.int32,(RB,WIN),1)
    return col-row-LEFT


MESH = pl.DeviceIdType.MESH
STEPS = 4


def pair_place():
    place = lax.axis_index("seq")
    half = lax.rem(place, jnp.int32(2))
    return half, {"seq": place + 1 - 2 * half}


def meet(partner):
    barrier = pltpu.get_barrier_semaphore()
    pl.semaphore_signal(barrier, inc=1, device_id=partner, device_id_type=MESH)
    pl.semaphore_wait(barrier, 1)


def block_at(step, half):
    return lax.rem(step + 2 * (1 - half), jnp.int32(STEPS))


def fwd_kernel(len_ref,wide_ref,ends_ref,mine_ref,other_ref,p_ref,heads_ref,mixed_ref,s_ref,kx_ref,buf,mixed,stage,in_send,in_recv,in_load,out_send,out_recv):
    n=buf.shape[2]; own=n//2
    pair=pl.program_id(0); step=pl.program_id(1)
    pairs=buf.shape[0]
    half,partner=pair_place()
    at=pl.multiple_of(half*own,own)
    def arrive(a):
        return pltpu.make_async_remote_copy(src_ref=other_ref.at[a],dst_ref=buf.at[a,:,pl.ds(at,own)],send_sem=in_send.at[a],recv_sem=in_recv.at[a],device_id=partner,device_id_type=MESH)
    def load(a):
        return pltpu.make_async_copy(mine_ref.at[a],buf.at[a,:,pl.ds(at,own)],in_load.at[a])
    def leave(a,b):
        cols=pl.ds(pl.multiple_of(half*own+a*128,128),128)
        return pltpu.make_async_remote_copy(src_ref=stage.at[a,b],dst_ref=mixed.at[pl.ds(pl.multiple_of(b*RB,RB),RB),cols],send_sem=out_send.at[a,b],recv_sem=out_recv.at[a,b],device_id=partner,device_id_type=MESH)
    @pl.when((pair==0)&(step==0))
    def _():
        meet(partner)
        for a in range(pairs):
            load(a).start()
            arrive(a).start()
    @pl.when(step==0)
    def _():
        load(pair).wait()
        arrive(pair).wait()
        heads_ref[0]=buf[pair]
        kx_ref[:,0:128]=buf[pair,1]
    i0=pl.multiple_of(block_at(step,half)*RB,RB)
    q2=buf[pair,0,pl.ds(i0,RB)]
    v2=buf[pair,2]
    lane=lanes((RB,128))
    t=lax.broadcasted_iota(jnp.int32,(n,128),0)
    c=lanes((n,128))
    left=(t<i0-128).astype(F32); right=(t>=i0+WIN-128).astype(F32)
    masked=jnp.where(t>=len_ref[0],-1e30,0.0)
    ext=jnp.where(c<2,left,jnp.where(c<4,right,jnp.where(c==4,masked,0.0)))
    kx_ref[:,128:256]=ext.astype(BF)
    outs=[]
    for h in range(2):
        head=(lane<64) if h==0 else (lane>=64)
        qh=jnp.where(head,q2,jnp.zeros_like(q2))
        ends=dot(qh,ends_ref[...],1,0)
        hi=ends.astype(BF).astype(F32)
        qx=jnp.where((lane==0)|(lane==2),hi,jnp.where((lane==1)|(lane==3),ends-hi,jnp.where(lane==4,1.0,0.0))).astype(BF)
        s_ref[:,PADL:PADL+n]=dot(jnp.concatenate([qh,qx],axis=1),kx_ref[...],1,1)
        wide=dot(qh,wide_ref[...],1,0)
        band=pltpu.roll(wide,LEFT,1,stride=1,stride_axis=0)
        j=band_offset()
        band=jnp.where(j>=LEFT+RIGHT,wide[:,LEFT+RIGHT:LEFT+RIGHT+1],band)
        w=pl.ds(i0,WIN)
        s_ref[:,w]=s_ref[:,w]+band
        s=s_ref[:,PADL:PADL+n]
        m=jnp.max(s,axis=1,keepdims=True)
        e=jnp.exp(s-m)
        z=jnp.sum(e,axis=1,keepdims=True)
        p=(e*(1.0/z)).astype(BF)
        p_ref[h]=p
        outs.append(dot(p,v2,1,0))
    out=jnp.where(lane<64,outs[0],outs[1]).astype(BF)
    @pl.when(step<2)
    def _():
        stage[pair,step]=out
        leave(pair,step).start()
    @pl.when(step>=2)
    def _():
        cols=pl.ds(pl.multiple_of(half*own+pair*128,128),128)
        mixed[pl.ds(pl.multiple_of((step-2)*RB,RB),RB),cols]=out
    @pl.when((pair==pairs-1)&(step==STEPS-1))
    def _():
        for a in range(pairs):
            for b in range(2):
                leave(a,b).wait_send()
        for a in range(pairs):
            for b in range(2):
                arrived=pltpu.make_async_remote_copy(src_ref=stage.at[a,b],dst_ref=mixed.at[pl.ds(b*RB,RB),pl.ds(pl.multiple_of((1-half)*own+a*128,128),128)],send_sem=out_send.at[a,b],recv_sem=out_recv.at[a,b],device_id=partner,device_id_type=MESH)
                arrived.wait_recv()
        mixed_ref[...]=mixed[...]


def z_line(middle,to_1,to_2,whole,near,far,z_send,z_recv):
    def copy(i,stage):
        src=(whole,near,far)[stage]; dst=(near,far,near)[stage]
        return pltpu.make_async_remote_copy(src_ref=src.at[i],dst_ref=dst.at[i],send_sem=z_send.at[i,stage],recv_sem=z_recv.at[i,stage],device_id=to_2 if stage==1 else to_1,device_id_type=MESH)
    def begin(i):
        pl.when(middle==0)(lambda: copy(i,0).start())
    def step(i,stage):
        @pl.when(middle==1)
        def _():
            if stage==0:
                copy(i,0).wait_recv()
                near[i]=(whole[i].astype(F32)+near[i].astype(F32)).astype(BF)
                copy(i,1).start()
            elif stage==1:
                copy(i,1).wait()
                far[i]=(near[i].astype(F32)+far[i].astype(F32)).astype(BF)
                copy(i,2).start()
            else:
                copy(i,2).wait_send()
        if stage!=1:
            @pl.when(middle==0)
            def _():
                if stage==0:
                    copy(i,0).wait_send()
                else:
                    copy(i,2).wait_recv()
    return begin,step


def bwd_kernel(with_part,heads_ref,p_ref,wide_ref,mine_ref,other_ref,*rest):
    if with_part:
        part_ref,dqkv_ref,de_ref,out_ref,*rest=rest
        *rest,whole,near,far,part_sem,out_sem,z_send,z_recv=rest
    else:
        dqkv_ref,de_ref,*rest=rest
    ds_ref,kx_ref,dka,dva,dea,buf,dqkv,stage_q,stage_kv,in_send,in_recv,in_load,q_send,q_recv,kv_send,kv_recv=rest
    n=heads_ref.shape[2]; own=n//2
    pair=pl.program_id(0); step=pl.program_id(1)
    pairs=buf.shape[0]
    half,partner=pair_place()
    at=pl.multiple_of(half*own,own)
    width=2*own
    def columns(t,who,a):
        return pl.ds(pl.multiple_of(t*width+who*own+a*128,128),128)
    def arrive(a):
        return pltpu.make_async_remote_copy(src_ref=other_ref.at[a],dst_ref=buf.at[a,pl.ds(at,own)],send_sem=in_send.at[a],recv_sem=in_recv.at[a],device_id=partner,device_id_type=MESH)
    def load(a):
        return pltpu.make_async_copy(mine_ref.at[a],buf.at[a,pl.ds(at,own)],in_load.at[a])
    def leave_q(a,b,who):
        return pltpu.make_async_remote_copy(src_ref=stage_q.at[a,b],dst_ref=dqkv.at[pl.ds(pl.multiple_of(b*RB,RB),RB),columns(0,who,a)],send_sem=q_send.at[a,b],recv_sem=q_recv.at[a,b],device_id=partner,device_id_type=MESH)
    def leave_kv(a,t,who):
        return pltpu.make_async_remote_copy(src_ref=stage_kv.at[a,t],dst_ref=dqkv.at[:,columns(t+1,who,a)],send_sem=kv_send.at[a,t],recv_sem=kv_recv.at[a,t],device_id=partner,device_id_type=MESH)
    if with_part:
        n_part=part_ref.shape[0]
        place=lax.axis_index("seq")
        middle=lax.rem(lax.div(place+1,jnp.int32(2)),jnp.int32(2))
        across={"seq":3-place}
        z_begin,z_step=z_line(middle,partner,across,whole,near,far,z_send,z_recv)
        def part_copy(i):
            return pltpu.make_async_copy(part_ref.at[i],whole.at[i],part_sem.at[i])
        def result_do(i,act):
            for is_middle,src in ((1,far),(0,near)):
                copy=pltpu.make_async_copy(src.at[i],out_ref.at[i],out_sem.at[i])
                pl.when(middle==is_middle)(lambda copy=copy: act(copy))
        now=pair*STEPS+step
    @pl.when((pair==0)&(step==0))
    def _():
        if with_part:
            barrier=pltpu.get_barrier_semaphore()
            for device in (partner,across):
                pl.semaphore_signal(barrier,inc=1,device_id=device,device_id_type=MESH)
            pl.semaphore_wait(barrier,2)
        else:
            meet(partner)
        for a in range(pairs):
            load(a).start()
            arrive(a).start()
        if with_part:
            for i in range(n_part):
                part_copy(i).start()
        dea[...]=jnp.zeros_like(dea)
        ds_ref[:,0:PADL]=jnp.zeros((RB,PADL),F32)
        ds_ref[:,PADL+n:]=jnp.zeros((RB,ds_ref.shape[1]-PADL-n),F32)
    @pl.when(step==0)
    def _():
        load(pair).wait()
        pl.when(pair>0)(lambda: arrive(pair).wait())
        kx_ref[:,0:128]=heads_ref[0,1]
        dka[...]=jnp.zeros_like(dka); dva[...]=jnp.zeros_like(dva)
    if with_part:
        for i in range(n_part):
            @pl.when(now==1+2*i)
            def _(i=i):
                part_copy(i).wait()
                z_begin(i)
            for stage in range(3):
                @pl.when(now==5+2*i+2*stage)
                def _(i=i,stage=stage):
                    z_step(i,stage)
                    if stage==2:
                        result_do(i,lambda copy: copy.start())
    @pl.when((pair==0)&(step==2))
    def _():
        arrive(pair).wait()
    turned=lax.rem(step+2*jnp.where(pair==0,1,0),jnp.int32(STEPS))
    i0=pl.multiple_of(block_at(turned,half)*RB,RB)
    q2=heads_ref[0,0,pl.ds(i0,RB)]
    v2=heads_ref[0,2]
    do2=buf[pair,pl.ds(i0,RB)]
    lane=lanes((RB,128))
    row=lax.broadcasted_iota(jnp.int32,(RB,128),0)
    t=lax.broadcasted_iota(jnp.int32,(n,128),0)
    c=lanes((n,128))
    left=(t<i0-128).astype(F32)
    kx_ref[:,128:256]=jnp.where(c==0,left,jnp.where(c==1,1.0,0.0)).astype(BF)
    dqs=[]
    for h in range(2):
        head=(lane<64) if h==0 else (lane>=64)
        doh=jnp.where(head,do2,jnp.zeros_like(do2))
        qh=jnp.where(head,q2,jnp.zeros_like(q2))
        p=p_ref[h]
        dp=dot(doh,v2,1,1)
        pf=p.astype(F32)
        d=jnp.sum(pf*dp,axis=1,keepdims=True)
        dsf=pf*(dp-d)
        ds=dsf.astype(BF)
        ds_ref[:,PADL:PADL+n]=ds.astype(F32)
        dva[...]+=dot(doh,p,0,0)
        dka[...]+=dot(qh,ds,0,0)
        dqx=dot(ds,kx_ref[...],1,0)
        dq,sums=dqx[:,0:128],dqx[:,128:256]
        win=ds_ref[:,pl.ds(i0,WIN)]
        j=band_offset()
        inleft=jnp.sum(jnp.where(j<=0,win,0.0),axis=1,keepdims=True)
        drel=jnp.concatenate([win[8*g:8*g+8,LEFT+8*g:LEFT+8*g+128] for g in range(RB//8)],axis=0)
        for bit in (1,2,4):
            drel=jnp.where((row&bit)!=0,pltpu.roll(drel,128-bit,1),drel)
        drel=jnp.where((lane>0)&(lane<LEFT+RIGHT),drel,0.0)
        bandsum=jnp.sum(drel,axis=1,keepdims=True)
        l=sums[:,0:1]+inleft
        r=sums[:,1:2]-l-bandsum
        drel=jnp.where(lane==0,l,jnp.where(lane==LEFT+RIGHT,r,drel)).astype(BF)
        dq=dq+dot(drel,wide_ref[...],1,1)
        dqs.append(dq)
        dea[...]+=dot(drel,qh,0,0)
    dq=(jnp.where(lane<64,dqs[0],dqs[1])*HEAD_DIM**-0.5).astype(BF)
    @pl.when(turned<2)
    def _():
        stage_q[pair,turned]=dq
        leave_q(pair,turned,half).start()
    @pl.when(turned>=2)
    def _():
        dqkv[pl.ds(pl.multiple_of((turned-2)*RB,RB),RB),columns(0,half,pair)]=dq
    @pl.when(step==STEPS-1)
    def _():
        for i,acc in enumerate((dka,dva)):
            mine=acc[:,pl.ds(at,own)]
            theirs=acc[:,pl.ds(pl.multiple_of((1-half)*own,own),own)]
            stage_kv[pair,i]=jnp.transpose(theirs).astype(BF)
            leave_kv(pair,i,half).start()
            dqkv[:,columns(i+1,half,pair)]=jnp.transpose(mine).astype(BF)
    @pl.when((pair==pairs-1)&(step==STEPS-1))
    def _():
        for a in range(pairs):
            for b in range(2):
                leave_q(a,b,half).wait_send()
                leave_kv(a,b,half).wait_send()
        for a in range(pairs):
            for b in range(2):
                leave_q(a,b,1-half).wait_recv()
                leave_kv(a,b,1-half).wait_recv()
        dqkv_ref[...]=dqkv[...]
        de_ref[...]=dea[...]
        if with_part:
            for i in range(n_part):
                result_do(i,lambda copy: copy.wait())


def tables(distance):
    e=distance.T
    wide=jnp.concatenate([e,jnp.broadcast_to(e[:,72:73],(64,120)),jnp.broadcast_to(e[:,0:1],(64,WIN-193))],axis=1)
    wide=jnp.concatenate([wide,wide],axis=0)
    ends=jnp.concatenate([e[:,0:1],e[:,0:1],e[:,72:73],e[:,72:73],jnp.zeros((64,124),e.dtype)],axis=1)
    ends=jnp.concatenate([ends,ends],axis=0)
    return wide,ends

def attend(mine,other,length,wide,ends):
    pairs,_,own,_=mine.shape; n=2*own
    dma=pltpu.SemaphoreType.DMA
    whole=lambda *shape: pl.BlockSpec(shape,lambda a,b:(0,)*len(shape))
    anywhere=pl.BlockSpec(memory_space=pl.ANY)
    return pl.pallas_call(fwd_kernel,
        grid=(pairs,STEPS),
        in_specs=[pl.BlockSpec(memory_space=pltpu.SMEM),whole(128,WIN),whole(128,128),anywhere,anywhere],
        out_specs=[pl.BlockSpec((2,RB,n),lambda a,b:(a,b,0)),pl.BlockSpec((1,3,n,128),lambda a,b:(a,0,0,0)),whole(own,2*own)],
        out_shape=[jax.ShapeDtypeStruct((2*pairs,n,n),BF),jax.ShapeDtypeStruct((pairs,3,n,128),BF),jax.ShapeDtypeStruct((own,2*own),BF)],
        scratch_shapes=[pltpu.VMEM((RB,PADL+n+256),F32),pltpu.VMEM((n,256),BF),pltpu.VMEM((pairs,3,n,128),BF),pltpu.VMEM((own,2*own),BF),pltpu.VMEM((pairs,2,RB,128),BF),
            dma((pairs,)),dma((pairs,)),dma((pairs,)),dma((pairs,2)),dma((pairs,2))],
        compiler_params=pltpu.CompilerParams(vmem_limit_bytes=58<<20,collective_id=1,has_side_effects=True),
        cost_estimate=pl.CostEstimate(flops=40_000_000_000,bytes_accessed=120_000_000,transcendentals=0),
        name="attend_fwd",
    )(length,wide,ends,mine,other)

def attend_back(heads,p,wide,mine,other,part=None):
    pairs,_,n,_=heads.shape; own=n//2
    dma=pltpu.SemaphoreType.DMA
    whole=lambda *shape: pl.BlockSpec(shape,lambda a,b:(0,)*len(shape))
    anywhere=pl.BlockSpec(memory_space=pl.ANY)
    with_part=part is not None
    extra=[pltpu.VMEM(part.shape,BF)]*3+[dma((part.shape[0],))]*2+[dma((part.shape[0],3))]*2 if with_part else []
    return pl.pallas_call(functools.partial(bwd_kernel,with_part),
        grid=(pairs,STEPS),
        in_specs=[pl.BlockSpec((1,3,n,128),lambda a,b:(a,0,0,0)),pl.BlockSpec((2,RB,n),lambda a,b:(a,jnp.where(a==0,lax.rem(b+2,STEPS),b),0)),whole(128,128),anywhere,anywhere]+[anywhere]*with_part,
        out_specs=[whole(own,6*own),whole(128,128)]+[anywhere]*with_part,
        out_shape=[jax.ShapeDtypeStruct((own,6*own),BF),jax.ShapeDtypeStruct((128,128),F32)]+([jax.ShapeDtypeStruct(part.shape,BF)] if with_part else []),
        scratch_shapes=[pltpu.VMEM((RB,PADL+n+256),F32),pltpu.VMEM((n,256),BF),pltpu.VMEM((128,n),F32),pltpu.VMEM((128,n),F32),pltpu.VMEM((128,128),F32),
            pltpu.VMEM((pairs,n,128),BF),pltpu.VMEM((own,6*own),BF),pltpu.VMEM((pairs,2,RB,128),BF),pltpu.VMEM((pairs,2,own,128),BF),
            dma((pairs,)),dma((pairs,)),dma((pairs,)),dma((pairs,2)),dma((pairs,2)),dma((pairs,2)),dma((pairs,2))]+extra,
        compiler_params=pltpu.CompilerParams(vmem_limit_bytes=58<<20,collective_id=2,has_side_effects=True),
        cost_estimate=pl.CostEstimate(flops=50_000_000_000,bytes_accessed=150_000_000,transcendentals=0),
        name="attend_bwd",
    )(heads,p,wide[:,0:128],mine,other,*([part] if with_part else []))


EPSILON = 1e-05
HALF = 0.5
CUT = 256
VMEM = 56 << 20


def flat(ref):
    value = ref[...]
    return value.reshape(-1, value.shape[-1])


def cuts(count):
    return [pl.ds(i, CUT) for i in range(0, count, CUT)]


def normal(v):
    c = v - jnp.mean(v, axis=-1, keepdims=True)
    r = lax.rsqrt(jnp.mean(c * c, axis=-1, keepdims=True) + EPSILON)
    return c * r, r


def normal_back(dy, unit, r, gain):
    a = dy * gain
    return (a - jnp.mean(a, axis=-1, keepdims=True) - unit * jnp.mean(a * unit, axis=-1, keepdims=True)) * r


def total(v):
    return jnp.sum(v, axis=0, keepdims=True)


def silu_slope(v):
    s = jax.nn.sigmoid(v)
    return s * (1.0 + v * (1.0 - s))


def call(kernel, grid, ins, outs, scratch=(), name=None, aliases=None, flops=0, moved=0):
    def spec(shape, block, where):
        if block is None:
            return pl.BlockSpec(shape, lambda *_: (0,) * len(shape))
        if block == "smem":
            return pl.BlockSpec(memory_space=pltpu.SMEM)
        if block == "any":
            return pl.BlockSpec(memory_space=pl.ANY)
        return pl.BlockSpec(block, where)

    return pl.pallas_call(
        kernel,
        grid=grid,
        in_specs=[spec(a.shape, b, w) for a, b, w in ins],
        out_specs=[spec(s, b, w) for s, _, b, w in outs],
        out_shape=[jax.ShapeDtypeStruct(s, d) for s, d, _, _ in outs],
        scratch_shapes=list(scratch),
        input_output_aliases=aliases or {},
        compiler_params=pltpu.CompilerParams(vmem_limit_bytes=VMEM),
        cost_estimate=pl.CostEstimate(flops=flops, bytes_accessed=moved, transcendentals=0),
        name=name,
    )(*[a for a, _, _ in ins])


def scr(shape, dtype):
    return pltpu.VMEM(shape, dtype)


def in_kernel(x_ref, vec_ref, bias_ref, w_ref, inner_ref, act_ref, act_t_ref, unit_t_ref, unit):
    @pl.when(pl.program_id(0) == 0)
    def _():
        for rows in cuts(x_ref.shape[0]):
            n, _ = normal(x_ref[rows, :].astype(F32))
            u = (n * vec_ref[0:1, :] + vec_ref[1:2, :]).astype(BF)
            unit[rows, :] = u
            unit_t_ref[:, rows] = u.T

    w = flat(w_ref)
    for rows in cuts(x_ref.shape[0]):
        s = dot(unit[rows, :], w, 1, 0) + bias_ref[0]
        inner_ref[rows, :] = s.astype(BF)
        a = (s * jax.nn.sigmoid(s)).astype(BF)
        act_ref[rows, :] = a
        act_t_ref[:, rows] = a.T


def ffn_in_forward(x, vec, bias, w, unit0):
    t, d = x.shape
    n, _, r, _ = w.shape
    k = bias.shape[0] // d
    bias = bias.reshape(k, 1, d)
    return call(
        in_kernel,
        (k,),
        [
            (x, None, None),
            (vec, None, None),
            (bias, (1, 1, d), lambda j: (j, 0, 0)),
            (w, (n, 1, r, d), lambda j: (0, unit0 + j, 0, 0)),
        ],
        [
            ((t, k * d), BF, (t, d), lambda j: (0, j)),
            ((t, k * d), BF, (t, d), lambda j: (0, j)),
            ((k * d, t), BF, (d, t), lambda j: (j, 0)),
            ((d, t), BF, None, None),
        ],
        [scr((t, d), BF)],
        name="ffn_in",
        flops=2 * t * d * d * k,
        moved=2 * d * d * k + 6 * t * d * k,
    )


def out_qkv_kernel(odd_ref, x_ref, act_ref, w_out_ref, w_qkv_ref, vec_ref, first_ref, unit_t_ref, mine_ref, other_ref, unit, acc):
    s = pl.program_id(0)
    t = x_ref.shape[0]

    @pl.when(s < 4)
    def _():
        w = flat(w_out_ref)
        for rows in cuts(t):
            p = dot(act_ref[rows, :], w, 1, 0)
            acc[rows, :] = p + jnp.where(s == 0, 0.0, acc[rows, :])

    @pl.when(s == 3)
    def _():
        for rows in cuts(t):
            first = x_ref[rows, :].astype(F32) + HALF * (acc[rows, :] + vec_ref[0:1, :])
            first_ref[rows, :] = first
            n, _ = normal(first)
            u = (n * vec_ref[1:2, :] + vec_ref[2:3, :]).astype(BF)
            unit[rows, :] = u
            unit_t_ref[:, rows] = u.T

    @pl.when(s >= 4)
    def _():
        w = flat(w_qkv_ref)
        odd = odd_ref[0] == 1
        half = w.shape[1] // 2
        scale = jnp.where(s == 4, HEAD_DIM**-0.5, 1.0)
        b = jnp.where(s == 4, vec_ref[3:4, :], jnp.where(s == 6, vec_ref[4:5, :], 0.0))
        for rows in cuts(t):
            y = (dot(unit[rows, :], w, 1, 0) + b) * scale
            low, high = y[:, :half], y[:, half:]
            mine = jnp.where(odd, high, low).astype(BF)
            other = jnp.where(odd, low, high).astype(BF)
            for part in range(half // 128):
                cols = slice(part * 128, part * 128 + 128)
                mine_ref[part, 0, rows, :] = mine[:, cols]
                other_ref[part, 0, rows, :] = other[:, cols]


def out_qkv_forward(odd, x, act, w, vec):
    t, d = x.shape
    n, _, r, _ = w.shape
    return call(
        out_qkv_kernel,
        (7,),
        [
            (odd, "smem", None),
            (x, None, None),
            (act, (t, d), lambda s: (0, jnp.minimum(s, 3))),
            (w, (n // 4, 4, r, d), lambda s: (jnp.minimum(s, 3), 0, 0, 0)),
            (w, (n, 1, r, d), lambda s: (0, jnp.maximum(s, 4), 0, 0)),
            (vec, None, None),
        ],
        [
            ((t, d), F32, None, None),
            ((d, t), BF, None, None),
            ((d // 256, 3, t, 128), BF, (d // 256, 1, t, 128), lambda s: (0, jnp.maximum(s - 4, 0), 0, 0)),
            ((d // 256, 3, t, 128), BF, (d // 256, 1, t, 128), lambda s: (0, jnp.maximum(s - 4, 0), 0, 0)),
        ],
        [scr((t, d), BF), scr((t, d), F32)],
        name="out_qkv",
        flops=14 * t * d * d,
        moved=14 * d * d + 20 * t * d,
    )


def mid_kernel(first_ref, mixed_ref, w_attn_ref, w_in_ref, vec_ref, second_ref, mixed_t_ref, unit_t_ref, val_ref, sig_ref, gated_ref, unit, val):
    s = pl.program_id(0)
    t = first_ref.shape[0]

    @pl.when(s == 0)
    def _():
        w = flat(w_attn_ref)
        for rows in cuts(t):
            m = mixed_ref[rows, :]
            mixed_t_ref[:, rows] = m.T
            second = first_ref[rows, :] + dot(m, w, 1, 0) + vec_ref[0:1, :]
            second_ref[rows, :] = second
            n, _ = normal(second)
            u = (n * vec_ref[1:2, :] + vec_ref[2:3, :]).astype(BF)
            unit[rows, :] = u
            unit_t_ref[:, rows] = u.T

    @pl.when(s == 1)
    def _():
        w = flat(w_in_ref)
        for rows in cuts(t):
            v = dot(unit[rows, :], w, 1, 0) + vec_ref[3:4, :]
            val[rows, :] = v
            val_ref[rows, :] = v.astype(BF)

    @pl.when(s == 2)
    def _():
        w = flat(w_in_ref)
        for rows in cuts(t):
            g = jax.nn.sigmoid(dot(unit[rows, :], w, 1, 0) + vec_ref[4:5, :])
            sig_ref[rows, :] = g.astype(BF)
            gated_ref[rows, :] = (val[rows, :] * g).astype(BF)


def mid_forward(first, mixed, w, u_attn, u_in, vec):
    t, d = first.shape
    n, _, r, _ = w.shape
    return call(
        mid_kernel,
        (3,),
        [
            (first, None, None),
            (mixed, None, None),
            (w, (n, 1, r, d), lambda s: (0, u_attn, 0, 0)),
            (w, (n, 1, r, d), lambda s: (0, u_in + jnp.maximum(s - 1, 0), 0, 0)),
            (vec, None, None),
        ],
        [((t, d), F32, None, None), ((d, t), BF, None, None), ((d, t), BF, None, None)]
        + [((t, d), BF, None, None)] * 3,
        [scr((t, d), BF), scr((t, d), F32)],
        name="mid",
        flops=6 * t * d * d,
        moved=6 * d * d + 20 * t * d,
    )


ROWS = 32
COLS = 256


def shifted(window, b):
    return window if b == 0 else pltpu.roll(window, window.shape[0] - b, 0)


def fir(pad, taps, offset, count, width, start, write, turned=False):
    reach = taps.shape[0]
    for c in range(0, width, COLS):
        cols = slice(c, c + COLS)

        def body(i, _):
            base = pl.multiple_of(i * ROWS, ROWS)
            window = pad[pl.ds(base, ROWS + 32), cols]
            acc = start(cols)
            for b in range(8):
                sh = shifted(window, b)
                for a in range(0, 5):
                    m = 8 * a + b - offset
                    if 0 <= m < reach:
                        tap = reach - 1 - m if turned else m
                        acc = acc + taps[tap : tap + 1, cols] * sh[8 * a : 8 * a + ROWS]
            write(pl.ds(base, ROWS), cols, acc)
            return 0

        lax.fori_loop(0, count // ROWS, body, 0)


def conv_kernel(gated_ref, halo_ref, taps_ref, vec_ref, second_ref, w_ref, conv_ref, act_t_ref, third_ref, pad):
    t, d = gated_ref.shape
    pad[0:32, :] = halo_ref[...].astype(F32)
    for rows in cuts(t):
        pad[pl.ds(rows.start + 32, CUT), :] = gated_ref[rows, :].astype(F32)

    def write(rows, cols, acc):
        conv_ref[rows, cols] = acc

    fir(pad, taps_ref, 2, t, d, lambda cols: jnp.broadcast_to(vec_ref[0:1, cols], (ROWS, COLS)), write)
    w = flat(w_ref)
    for rows in cuts(t):
        n, _ = normal(conv_ref[rows, :])
        u = n * vec_ref[1:2, :] + vec_ref[2:3, :]
        a = (u * jax.nn.sigmoid(u)).astype(BF)
        act_t_ref[:, rows] = a.T
        third_ref[rows, :] = second_ref[rows, :] + dot(a, w, 1, 0) + vec_ref[3:4, :]


def conv_forward(gated, halo, taps, vec, second, w, unit0):
    t, d = gated.shape
    n, _, r, _ = w.shape
    return call(
        conv_kernel,
        (1,),
        [
            (gated, None, None),
            (halo, None, None),
            (taps, None, None),
            (vec, None, None),
            (second, None, None),
            (w, (n, 1, r, d), lambda s: (0, unit0, 0, 0)),
        ],
        [((t, d), F32, None, None), ((d, t), BF, None, None), ((t, d), F32, None, None)],
        [scr((t + 32, d), F32)],
        name="conv",
        flops=2 * t * d * d,
        moved=2 * d * d + 16 * t * d,
    )


def out_last_kernel(x_ref, act_ref, w_ref, cot_ref, vec_ref, out_ref, d_ref, dout_ref, sums_ref, acc):
    s = pl.program_id(0)
    t = x_ref.shape[0]
    w = flat(w_ref)
    for rows in cuts(t):
        p = dot(act_ref[rows, :], w, 1, 0)
        acc[rows, :] = p + jnp.where(s == 0, 0.0, acc[rows, :])

    @pl.when(s == 3)
    def _():
        sums_ref[...] = jnp.zeros_like(sums_ref)
        for rows in cuts(t):
            fourth = x_ref[rows, :] + HALF * (acc[rows, :] + vec_ref[0:1, :])
            n, r = normal(fourth)
            out_ref[rows, :] = (n * vec_ref[1:2, :] + vec_ref[2:3, :]).astype(BF)
            dy = cot_ref[rows, :].astype(F32)
            d = normal_back(dy, n, r, vec_ref[1:2, :])
            d_ref[rows, :] = d
            dout_ref[rows, :] = (HALF * d).astype(BF)
            sums_ref[0:1, :] += total(dy * n)
            sums_ref[1:2, :] += total(dy)


def out_last(x, act, w, block0, cot, vec):
    t, d = x.shape
    n, _, r, _ = w.shape
    return call(
        out_last_kernel,
        (4,),
        [
            (x, None, None),
            (act, (t, d), lambda s: (0, s)),
            (w, (n // 4, 4, r, d), lambda s: (s, block0, 0, 0)),
            (cot, None, None),
            (vec, None, None),
        ],
        [((t, d), BF, None, None), ((t, d), F32, None, None), ((t, d), BF, None, None), ((8, d), F32, None, None)],
        [scr((t, d), F32)],
        name="out_last",
        flops=8 * t * d * d,
        moved=8 * d * d + 20 * t * d,
    )


def ffn_hidden_kernel(d_ref, inner_ref, w_ref, dinner_ref, dout_ref, dbias_ref, sums_ref):
    t = d_ref.shape[0]

    @pl.when(pl.program_id(0) == 0)
    def _():
        sums_ref[...] = jnp.zeros_like(sums_ref)
        for rows in cuts(t):
            v = d_ref[rows, :] if d_ref.dtype == BF else (HALF * d_ref[rows, :]).astype(BF)
            dout_ref[rows, :] = v
            sums_ref[0:1, :] += total(v.astype(F32))

    w = flat(w_ref)
    dbias = 0.0
    for rows in cuts(t):
        da = dot(dout_ref[rows, :], w, 1, 1)
        v = (da * silu_slope(inner_ref[rows, :].astype(F32))).astype(BF)
        dinner_ref[rows, :] = v
        dbias = dbias + total(v.astype(F32))
    dbias_ref[0] = dbias


def ffn_hidden_back(dy, inner, w, block0):
    t, d = dy.shape
    n, _, r, _ = w.shape
    k = inner.shape[1] // d
    return call(
        ffn_hidden_kernel,
        (k,),
        [
            (dy, None, None),
            (inner, (t, d), lambda j: (0, j)),
            (w, (n // 4, 4, r, d), lambda j: (j, block0, 0, 0)),
        ],
        [
            ((t, k * d), BF, (t, d), lambda j: (0, j)),
            ((t, d), BF, None, None),
            ((k, 1, d), F32, (1, 1, d), lambda j: (j, 0, 0)),
            ((8, d), F32, None, None),
        ],
        name="ffn_hidden_back",
        flops=2 * t * d * d * k,
        moved=2 * d * d * k + 4 * t * d * k,
    )


def norm_input_kernel(k, dy_ref, g_ref, x_ref, w_ref, vec_ref, d_ref, sums_ref, acc):
    s = pl.program_id(0)
    t = x_ref.shape[0]
    w = flat(w_ref)
    for rows in cuts(t):
        p = dot(g_ref[rows, :], w, 1, 1)
        acc[rows, :] = p + jnp.where(s == 0, 0.0, acc[rows, :])

    @pl.when(s == k - 1)
    def _():
        sums_ref[...] = jnp.zeros_like(sums_ref)
        for rows in cuts(t):
            n, r = normal(x_ref[rows, :].astype(F32))
            du = acc[rows, :]
            d_ref[rows, :] = (dy_ref[rows, :] + normal_back(du, n, r, vec_ref[0:1, :])).astype(d_ref.dtype)
            sums_ref[0:1, :] += total(du * n)
            sums_ref[1:2, :] += total(du)


def norm_input_back(dy, g, x, w, unit0, gain, out_type=F32):
    t, d = dy.shape
    n, _, r, _ = w.shape
    k = g.shape[1] // d
    return call(
        functools.partial(norm_input_kernel, k),
        (k,),
        [
            (dy, None, None),
            (g, (t, d), lambda j: (0, j)),
            (x, None, None),
            (w, (n, 1, r, d), lambda j: (0, unit0 + j, 0, 0)),
            (gain, None, None),
        ],
        [((t, d), out_type, None, None), ((8, d), F32, None, None)],
        [scr((t, d), F32)],
        name="norm_input_back",
        flops=2 * t * d * d * k,
        moved=2 * d * d * k + 2 * t * d * k + 12 * t * d,
    )


def weight_kernel(left_ref, right_ref, *rest):
    out_ref = rest[-1]
    rows, d = left_ref.shape[0], out_ref.shape[-1]
    a, b, r, _ = out_ref.shape
    step = max(256, 4 * r)
    for i in range(0, rows, step):
        value = dot(left_ref[i : i + step, :], right_ref[...], 1, 0).astype(BF)
        if b == 1:
            out_ref[pl.ds(i // r, step // r), 0] = value.reshape(step // r, r, d)
        else:
            out_ref[pl.ds(i // (4 * r), step // (4 * r))] = value.reshape(step // (4 * r), 4, r, d)


def weight_grad(left_t, right, n, units, at, by_rows, into=None):
    d = 1024
    t = left_t.shape[1]
    r = d // n
    if by_rows:
        k = left_t.shape[0] // d
        ins = [(left_t, (d, t), lambda j: (j, 0)), (right, None, None)]
        block, where = (n // 4, 4, r, d), lambda j: (j, at // 4, 0, 0)
    else:
        k = right.shape[1] // d
        ins = [(left_t, None, None), (right, (t, d), lambda j: (0, j))]
        block, where = (n, 1, r, d), lambda j: (0, at + j, 0, 0)
    aliases = None
    if into is not None:
        ins.append((into, "any", None))
        aliases = {2: 0}
    return call(
        weight_kernel,
        (k,),
        ins,
        [((n, units, r, d), BF, block, where)],
        name="weight_grad",
        aliases=aliases,
        flops=2 * t * d * d * k,
        moved=2 * d * d * k + 2 * t * d * (k + 1),
    )[0]


def conv_out_kernel(d_ref, conv_ref, w_ref, vec_ref, dconv_ref, dout_ref, sums_ref):
    t = d_ref.shape[0]
    sums_ref[...] = jnp.zeros_like(sums_ref)
    w = flat(w_ref)
    for rows in cuts(t):
        dout = d_ref[rows, :].astype(BF)
        dout_ref[rows, :] = dout
        da = dot(dout, w, 1, 1)
        n, r = normal(conv_ref[rows, :])
        du = da * silu_slope(n * vec_ref[0:1, :] + vec_ref[1:2, :])
        dconv = normal_back(du, n, r, vec_ref[0:1, :])
        dconv_ref[rows, :] = dconv
        sums_ref[0:1, :] += total(dout.astype(F32))
        sums_ref[1:2, :] += total(du * n)
        sums_ref[2:3, :] += total(du)
        sums_ref[3:4, :] += total(dconv)


def conv_out_back(d3, conv, w, unit0, vec):
    t, d = d3.shape
    n, _, r, _ = w.shape
    return call(
        conv_out_kernel,
        (1,),
        [
            (d3, None, None),
            (conv, None, None),
            (w, (n, 1, r, d), lambda s: (0, unit0, 0, 0)),
            (vec, None, None),
        ],
        [((t, d), F32, None, None), ((t, d), BF, None, None), ((8, d), F32, None, None)],
        name="conv_out_back",
        flops=2 * t * d * d,
        moved=2 * d * d + 16 * t * d,
    )


def mid_back_kernel(odd_ref, dconv_ref, follow_ref, taps_ref, val_ref, sig_ref, second_ref, d3_ref, w_in_ref, w_attn_ref, vec_ref, d2_ref, dout_ref, dglu_ref, mine_ref, other_ref, sums_ref, pad, acc):
    s = pl.program_id(0)
    t, d = dconv_ref.shape

    @pl.when(s == 0)
    def _():
        for rows in cuts(t):
            pad[rows, :] = dconv_ref[rows, :]
        pad[t : t + 32, :] = follow_ref[...]

        def write(rows, cols, dgated):
            sig = sig_ref[rows, cols].astype(F32)
            dval = dgated * sig
            dglu_ref[rows, cols] = dval.astype(BF)
            dgate = dval * val_ref[rows, cols].astype(F32) * (1.0 - sig)
            dglu_ref[rows, cols.start + d : cols.stop + d] = dgate.astype(BF)

        fir(pad, taps_ref, 0, t, d, lambda cols: jnp.zeros((ROWS, COLS), F32), write, turned=True)
        sums_ref[...] = jnp.zeros_like(sums_ref)
        for rows in cuts(t):
            sums_ref[0:1, :] += total(dglu_ref[rows, :d].astype(F32))
            sums_ref[1:2, :] += total(dglu_ref[rows, d:].astype(F32))
        w = flat(w_in_ref)
        for rows in cuts(t):
            acc[rows, :] = dot(dglu_ref[rows, :d], w, 1, 1)

    @pl.when(s == 1)
    def _():
        w = flat(w_in_ref)
        w_attn = flat(w_attn_ref)
        odd = odd_ref[0] == 1
        half = d // 2
        for rows in cuts(t):
            du = acc[rows, :] + dot(dglu_ref[rows, d:], w, 1, 1)
            n, r = normal(second_ref[rows, :])
            d2 = d3_ref[rows, :] + normal_back(du, n, r, vec_ref[0:1, :])
            sums_ref[2:3, :] += total(du * n)
            sums_ref[3:4, :] += total(du)
            d2_ref[rows, :] = d2
            dout = d2.astype(BF)
            dout_ref[rows, :] = dout
            sums_ref[4:5, :] += total(dout.astype(F32))
            dm = dot(dout, w_attn, 1, 1)
            low, high = dm[:, :half], dm[:, half:]
            mine = jnp.where(odd, high, low).astype(BF)
            other = jnp.where(odd, low, high).astype(BF)
            for part in range(half // 128):
                cols = slice(part * 128, part * 128 + 128)
                mine_ref[part, rows, :] = mine[:, cols]
                other_ref[part, rows, :] = other[:, cols]


def mid_back(odd, dconv, follow, taps, val, sig, second, d3, w, u_attn, u_in, gain):
    t, d = d3.shape
    n, _, r, _ = w.shape
    return call(
        mid_back_kernel,
        (2,),
        [
            (odd, "smem", None),
            (dconv, None, None),
            (follow, None, None),
            (taps, None, None),
            (val, None, None),
            (sig, None, None),
            (second, None, None),
            (d3, None, None),
            (w, (n, 1, r, d), lambda s: (0, u_in + s, 0, 0)),
            (w, (n, 1, r, d), lambda s: (0, u_attn, 0, 0)),
            (gain, None, None),
        ],
        [
            ((t, d), F32, None, None),
            ((t, d), BF, None, None),
            ((t, 2 * d), BF, None, None),
            ((d // 256, t, 128), BF, None, None),
            ((d // 256, t, 128), BF, None, None),
            ((8, d), F32, None, None),
        ],
        [scr((t + 32, d), F32), scr((t, d), F32)],
        name="mid_back",
        flops=6 * t * d * d,
        moved=6 * d * d + 24 * t * d,
    )


def taps_kernel(dconv_ref, gated_ref, halo_ref, out_ref, pad, part):
    t, d = dconv_ref.shape
    reach = out_ref.shape[0]
    pad[0:32, :] = halo_ref[...].astype(F32)
    for rows in cuts(t):
        pad[pl.ds(rows.start + 32, CUT), :] = gated_ref[rows, :].astype(F32)
    part[...] = jnp.zeros_like(part)
    for c in range(0, d, COLS):
        cols = slice(c, c + COLS)

        def body(i, _):
            base = pl.multiple_of(i * ROWS, ROWS)
            window = pad[pl.ds(base, ROWS + 32), cols]
            here = dconv_ref[pl.ds(base, ROWS), cols]
            for b in range(8):
                sh = shifted(window, b)
                for a in range(0, 5):
                    m = 8 * a + b - 2
                    if 0 <= m < reach:
                        v = here * sh[8 * a : 8 * a + ROWS]
                        v = (v[0:8] + v[8:16]) + (v[16:24] + v[24:32])
                        part[8 * m : 8 * m + 8, cols] += v
            return 0

        lax.fori_loop(0, t // ROWS, body, 0)
    for m in range(reach):
        out_ref[m : m + 1, :] = total(part[8 * m : 8 * m + 8, :])


def taps_grad(dconv, gated, halo, reach):
    t, d = dconv.shape
    return call(
        taps_kernel,
        (1,),
        [(dconv, None, None), (gated, None, None), (halo, None, None)],
        [((reach, d), F32, None, None)],
        [scr((t + 32, d), F32), scr((8 * reach, d), F32)],
        name="taps_grad",
        flops=2 * t * d * reach,
        moved=6 * t * d,
    )[0]


def flipped_bit(index, mask):
    return index + mask - 2 * mask * lax.rem(lax.div(index, jnp.int32(mask)), jnp.int32(2))


def first_kernel(
    x_ref, w_ref, gains_ref, shifts_ref, taps_ref, bias_ref,
    inner_ref, act_ref, act_t_ref, unit_t_ref, tokens_ref, small_out_ref, w_out_ref,
    w, small, small_ref, tokens, unit, vec,
    own_send, own_recv, far_send, far_recv, core_send, core_recv, x_send, x_recv, x_load, w_leave,
):
    j = pl.program_id(0)
    n, k, r, d = w.shape
    t = tokens.shape[0]
    cut, thin_cut = r // 2, small.shape[1] // 2
    me, place = lax.axis_index("fsdp"), lax.axis_index("seq")
    two = jnp.int32(2)
    other_x, other_y, other_c = flipped_bit(me, 2), flipped_bit(me, 4), flipped_bit(me, 1)
    other_xy = flipped_bit(other_x, 4)
    to_x, to_y, to_c = {"fsdp": other_x}, {"fsdp": other_y}, {"fsdp": other_c}

    def send(src, dst, send_sem, recv_sem, device):
        return pltpu.make_async_remote_copy(
            src_ref=src, dst_ref=dst, send_sem=send_sem, recv_sem=recv_sem, device_id=device, device_id_type=MESH
        )

    def held(dev, u, rows=None):
        if u == k:
            return small.at[dev] if rows is None else small.at[dev, rows]
        return w.at[dev, u] if rows is None else w.at[dev, u, rows]

    def own(u):
        return small_ref if u == k else w_ref.at[u]

    def own_copies(u):
        return [
            send(own(u), held(me, u), own_send.at[i, u], own_recv.at[i, u], device)
            for i, device in enumerate((to_x, to_y, to_c))
        ]

    def keep_copy(u):
        return pltpu.make_async_copy(own(u), held(me, u), x_load.at[2 + u])

    def far_copies(u):
        half = thin_cut if u == k else cut
        top, low = pl.ds(0, half), pl.ds(half, half)
        return [
            send(held(other_x, u, top), held(other_x, u, top), far_send.at[0, u], far_recv.at[0, u], to_y),
            send(held(other_y, u, low), held(other_y, u, low), far_send.at[1, u], far_recv.at[1, u], to_x),
        ]

    def core_copy(i, u):
        dev = (other_x, other_y, other_xy)[i]
        return send(held(dev, u), held(dev, u), core_send.at[i, u], core_recv.at[i, u], to_c)

    def gather_begin(u):
        keep_copy(u).start()
        for copy in own_copies(u):
            copy.start()

    def gather_forward(u):
        across = own_copies(u)
        far = far_copies(u)
        across[0].wait_recv()
        far[0].start()
        core_copy(0, u).start()
        across[1].wait_recv()
        far[1].start()
        core_copy(1, u).start()

    def gather_far(u):
        for copy in far_copies(u):
            copy.wait_recv()
        core_copy(2, u).start()

    def gather_end(u):
        keep_copy(u).wait()
        own_copies(u)[2].wait_recv()
        for i in range(3):
            core_copy(i, u).wait_recv()

    def gather_sent(u):
        for copy in own_copies(u) + far_copies(u) + [core_copy(i, u) for i in range(3)]:
            copy.wait_send()

    side, half_of = lax.div(place, two), lax.rem(place, two)

    def token_rows(h):
        return pl.ds(pl.multiple_of(h * (t // 2), t // 2), t // 2)

    def token_copy(s):
        return send(x_ref.at[s], tokens.at[token_rows(half_of)], x_send.at[s], x_recv.at[half_of], {"seq": 2 * s + side})

    def token_keep(s):
        return pltpu.make_async_copy(x_ref.at[s], tokens.at[token_rows(half_of)], x_load.at[s])

    def token_arrived(h):
        return send(x_ref.at[0], tokens.at[token_rows(h)], x_send.at[0], x_recv.at[h], {"seq": flipped_bit(place, 1)})

    @pl.when(j == 0)
    def _():
        small_ref[...] = jnp.zeros_like(small_ref)
        at = 0
        for ref in (gains_ref, shifts_ref, taps_ref):
            small_ref[at : at + ref.shape[0], :] = ref[...]
            at += ref.shape[0]
        for layer in range(2):
            for q in range(4):
                row = at + 4 * layer + q
                small_ref[row : row + 1, :] = bias_ref[layer : layer + 1, q * r : (q + 1) * r]
        barrier = pltpu.get_barrier_semaphore()
        devices = [to_x, to_y, to_c, {"seq": flipped_bit(place, 1)}, {"seq": flipped_bit(place, 2)}, {"seq": 3 - place}]
        for device in devices:
            pl.semaphore_signal(barrier, inc=1, device_id=device, device_id_type=MESH)
        pl.semaphore_wait(barrier, 6)
        gather_begin(k)
        for s in range(2):
            away = 2 * s + side != place
            pl.when(away)(lambda s=s: token_copy(s).start())
            pl.when(jnp.logical_not(away))(lambda s=s: token_keep(s).start())
        for u in range(k):
            gather_begin(u)
        gather_forward(k)
        gather_far(k)
        gather_end(k)
        for dev in range(n):
            cols = slice(dev * r, (dev + 1) * r)
            vec[0:1, cols] = small[dev, 0:1, :].astype(F32)
            vec[1:2, cols] = small[dev, 6:7, :].astype(F32)
            for q in range(4):
                at = 4 * (dev % 2) + q
                vec[2 + dev // 2 : 3 + dev // 2, at * r : (at + 1) * r] = small[dev, 52 + q : 53 + q, :].astype(F32)
        gather_forward(0)
        gather_forward(1)
        for s in range(2):
            away = 2 * s + side != place
            pl.when(away)(lambda s=s: token_copy(s).wait_send())
            pl.when(jnp.logical_not(away))(lambda s=s: token_keep(s).wait())
        for h in range(2):
            pl.when(2 * half_of + h != place)(lambda h=h: token_arrived(h).wait_recv())
        gather_forward(2)
        gather_forward(3)
        for rows in cuts(t):
            c, _ = normal(tokens[rows, :].astype(F32))
            v = (c * vec[0:1, :] + vec[1:2, :]).astype(BF)
            unit[rows, :] = v
            unit_t_ref[:, rows] = v.T
        tokens_ref[...] = tokens[...]
        small_out_ref[...] = small[...]
        for u in range(k):
            gather_far(u)

    def leave(u):
        return pltpu.make_async_copy(w.at[:, u], w_out_ref.at[:, u], w_leave.at[u])

    for u in range(k):

        @pl.when(j == u)
        def _(u=u):
            gather_end(u)
            leave(u).start()

    weights = w[:, j].reshape(d, d)
    for rows in cuts(t):
        s = dot(unit[rows, :], weights, 1, 0) + vec[pl.ds(2 + j, 1), :]
        inner_ref[rows, :] = s.astype(BF)
        a = (s * jax.nn.sigmoid(s)).astype(BF)
        act_ref[rows, :] = a
        act_t_ref[:, rows] = a.T

    @pl.when(j == k - 1)
    def _():
        for u in range(k + 1):
            gather_sent(u)
        for u in range(k):
            leave(u).wait()


def first_forward(x, w, gains, shifts, taps, bias):
    _, half, d = x.shape
    k, r, _ = w.shape
    n, t = 8, 2 * half
    rows = 64
    dma = pltpu.SemaphoreType.DMA
    anywhere = pl.BlockSpec(memory_space=pl.ANY)

    def whole(*shape):
        return pl.BlockSpec(shape, lambda j: (0,) * len(shape))

    return pl.pallas_call(
        first_kernel,
        grid=(k,),
        in_specs=[anywhere] * 2 + [whole(*a.shape) for a in (gains, shifts, taps, bias)],
        out_specs=[
            pl.BlockSpec((t, d), lambda j: (0, j)),
            pl.BlockSpec((t, d), lambda j: (0, j)),
            pl.BlockSpec((d, t), lambda j: (j, 0)),
            whole(d, t),
            whole(t, d),
            whole(n, rows, r),
            anywhere,
        ],
        out_shape=[
            jax.ShapeDtypeStruct((t, k * d), BF),
            jax.ShapeDtypeStruct((t, k * d), BF),
            jax.ShapeDtypeStruct((k * d, t), BF),
            jax.ShapeDtypeStruct((d, t), BF),
            jax.ShapeDtypeStruct((t, d), BF),
            jax.ShapeDtypeStruct((n, rows, r), BF),
            jax.ShapeDtypeStruct((n, k, r, d), BF),
        ],
        scratch_shapes=[
            scr((n, k, r, d), BF),
            scr((n, rows, r), BF),
            scr((rows, r), BF),
            scr((t, d), BF),
            scr((t, d), BF),
            scr((8, d), F32),
            dma((3, k + 1)),
            dma((3, k + 1)),
            dma((2, k + 1)),
            dma((2, k + 1)),
            dma((3, k + 1)),
            dma((3, k + 1)),
            dma((2,)),
            dma((2,)),
            dma((2 + k + 1,)),
            dma((k,)),
        ],
        compiler_params=pltpu.CompilerParams(vmem_limit_bytes=VMEM, collective_id=3, has_side_effects=True),
        cost_estimate=pl.CostEstimate(flops=30_000_000_000, bytes_accessed=100_000_000, transcendentals=0),
        name="first",
    )(x, w, gains, shifts, taps, bias)


def middle_kernel(
    g_ref, w_ref, w_attn_ref, taps_ref, vec_ref, dy_in, third_in, conv_in, val_in, sig_in, second_in, result_ref,
    d2_ref, dout_2_ref, mine_ref, other_ref, sums_4_ref, sums_3_ref, sums_2_ref, dconv_out, dout_3_out, dglu_out, outputs_ref,
    dy_ref, third_ref, conv_ref, val_ref, sig_ref, second_ref, dout_3_ref, dglu_ref,
    acc, d3, pad, load_sem, leave_sem, halo_send, halo_recv, out_send, out_recv, out_keep,
):
    s = pl.program_id(0)
    t, d = third_ref.shape

    def load(i):
        src = (dy_in, third_in, conv_in, val_in, sig_in, second_in)[i]
        dst = (dy_ref, third_ref, conv_ref, val_ref, sig_ref, second_ref)[i]
        return pltpu.make_async_copy(src, dst, load_sem.at[i])

    def leave(i):
        src = (pad.at[pl.ds(0, t)], dout_3_ref, dglu_ref)[i]
        return pltpu.make_async_copy(src, (dconv_out, dout_3_out, dglu_out)[i], leave_sem.at[i])

    place = lax.axis_index("seq")
    two = jnp.int32(2)
    odd, seq = lax.rem(place, two), lax.div(place, two)
    partner = {"seq": flipped_bit(place, 1)}
    half = d // 2

    def halo_copy():
        return pltpu.make_async_remote_copy(
            src_ref=pad.at[pl.ds(0, 32)],
            dst_ref=pad.at[pl.ds(t, 32)],
            send_sem=halo_send,
            recv_sem=halo_recv,
            device_id=partner,
            device_id_type=MESH,
        )

    def out_copy(h, to, s):
        return pltpu.make_async_remote_copy(
            src_ref=result_ref.at[pl.ds(h * (t // 2), t // 2)],
            dst_ref=outputs_ref.at[s],
            send_sem=out_send.at[h],
            recv_sem=out_recv.at[s],
            device_id={"seq": to},
            device_id_type=MESH,
        )

    def out_stay(h):
        return pltpu.make_async_copy(result_ref.at[pl.ds(h * (t // 2), t // 2)], outputs_ref.at[seq], out_keep)

    @pl.when(s == 0)
    def _():
        for i in range(6):
            load(i).start()
        barrier = pltpu.get_barrier_semaphore()
        for device in (partner, {"seq": flipped_bit(place, 2)}, {"seq": 3 - place}):
            pl.semaphore_signal(barrier, inc=1, device_id=device, device_id_type=MESH)
        pl.semaphore_wait(barrier, 3)
        for h in range(2):
            away = 2 * odd + h != place
            pl.when(away)(lambda h=h: out_copy(h, 2 * odd + h, seq).start())
            pl.when(jnp.logical_not(away))(lambda h=h: out_stay(h).start())
        for ref in (sums_4_ref, sums_3_ref, sums_2_ref):
            ref[...] = jnp.zeros_like(ref)

    w = flat(w_ref)

    @pl.when(s < 4)
    def _():
        for rows in cuts(t):
            p = dot(g_ref[rows, :], w, 1, 1)
            acc[rows, :] = p + jnp.where(s == 0, 0.0, acc[rows, :])

    @pl.when(s == 3)
    def _():
        load(0).wait()
        load(1).wait()
        for rows in cuts(t):
            n, r = normal(third_ref[rows, :])
            du = acc[rows, :]
            value = dy_ref[rows, :] + normal_back(du, n, r, vec_ref[0:1, :])
            d3[rows, :] = value
            dout = value.astype(BF)
            dout_3_ref[rows, :] = dout
            sums_4_ref[0:1, :] += total(du * n)
            sums_4_ref[1:2, :] += total(du)
            sums_3_ref[0:1, :] += total(dout.astype(F32))
        leave(1).start()

    @pl.when(s == 4)
    def _():
        load(2).wait()
        for i, rows in enumerate(cuts(t)):
            da = dot(dout_3_ref[rows, :], w, 1, 1)
            n, r = normal(conv_ref[rows, :])
            du = da * silu_slope(n * vec_ref[1:2, :] + vec_ref[2:3, :])
            dconv = normal_back(du, n, r, vec_ref[1:2, :])
            pad[rows, :] = dconv
            sums_3_ref[1:2, :] += total(du * n)
            sums_3_ref[2:3, :] += total(du)
            sums_3_ref[3:4, :] += total(dconv)
            if i == 0:

                @pl.when(odd == 1)
                def _():
                    halo_copy().start()
                    pad[t : t + 32, :] = jnp.zeros((32, d), F32)

        leave(0).start()

    @pl.when(s == 5)
    def _():
        load(3).wait()
        load(4).wait()
        pl.when(odd == 1)(lambda: halo_copy().wait_send())
        pl.when(odd == 0)(lambda: halo_copy().wait_recv())

        def write(rows, cols, dgated):
            sig = sig_ref[rows, cols].astype(F32)
            dval = dgated * sig
            dglu_ref[rows, cols] = dval.astype(BF)
            dgate = dval * val_ref[rows, cols].astype(F32) * (1.0 - sig)
            dglu_ref[rows, cols.start + d : cols.stop + d] = dgate.astype(BF)

        fir(pad, taps_ref, 0, t, d, lambda cols: jnp.zeros((ROWS, COLS), F32), write, turned=True)
        for rows in cuts(t):
            sums_2_ref[0:1, :] += total(dglu_ref[rows, :d].astype(F32))
            sums_2_ref[1:2, :] += total(dglu_ref[rows, d:].astype(F32))
            acc[rows, :] = dot(dglu_ref[rows, :d], w, 1, 1)
        leave(2).start()

    @pl.when(s == 6)
    def _():
        load(5).wait()
        w_attn = flat(w_attn_ref)
        for rows in cuts(t):
            du = acc[rows, :] + dot(dglu_ref[rows, d:], w, 1, 1)
            n, r = normal(second_ref[rows, :])
            d2 = d3[rows, :] + normal_back(du, n, r, vec_ref[3:4, :])
            sums_2_ref[2:3, :] += total(du * n)
            sums_2_ref[3:4, :] += total(du)
            d2_ref[rows, :] = d2
            dout = d2.astype(BF)
            dout_2_ref[rows, :] = dout
            sums_2_ref[4:5, :] += total(dout.astype(F32))
            dm = dot(dout, w_attn, 1, 1)
            low, high = dm[:, :half], dm[:, half:]
            mine = jnp.where(odd == 1, high, low).astype(BF)
            other = jnp.where(odd == 1, low, high).astype(BF)
            for part in range(half // 128):
                cols = slice(part * 128, part * 128 + 128)
                mine_ref[part, rows, :] = mine[:, cols]
                other_ref[part, rows, :] = other[:, cols]
        for i in range(3):
            leave(i).wait()
        for h in range(2):
            away = 2 * odd + h != place
            pl.when(away)(lambda h=h: out_copy(h, 2 * odd + h, seq).wait_send())
            pl.when(jnp.logical_not(away))(lambda h=h: out_stay(h).wait())
        for q in range(2):
            pl.when(2 * q + seq != place)(lambda q=q: out_copy(0, flipped_bit(place, 1), q).wait_recv())


def middle_back(dy, g, third, conv, val, sig, second, w, taps, vec, result):
    t, d = dy.shape
    n, _, r, _ = w.shape
    dma = pltpu.SemaphoreType.DMA

    def whole(*shape):
        return pl.BlockSpec(shape, lambda s: (0,) * len(shape))

    anywhere = pl.BlockSpec(memory_space=pl.ANY)
    outs = [
        ((t, d), F32), ((t, d), BF), ((d // 256, t, 128), BF), ((d // 256, t, 128), BF),
        ((8, d), F32), ((8, d), F32), ((8, d), F32),
    ]
    far = [((t, d), F32), ((t, d), BF), ((t, 2 * d), BF), ((2, t // 2, d), BF)]
    d2, dout_2, mine, other, sums_4, sums_3, sums_2, dconv, dout_3, dglu, result = pl.pallas_call(
        middle_kernel,
        grid=(7,),
        in_specs=[
            pl.BlockSpec((t, d), lambda s: (0, jnp.minimum(s, 3))),
            pl.BlockSpec((n, 1, r, d), lambda s: (0, jnp.where(s == 4, 7, s), 0, 0)),
            pl.BlockSpec((n, 1, r, d), lambda s: (0, 4, 0, 0)),
            whole(*taps.shape),
            whole(*vec.shape),
        ]
        + [anywhere] * 7,
        out_specs=[whole(*shape) for shape, _ in outs] + [anywhere] * 4,
        out_shape=[jax.ShapeDtypeStruct(shape, kind) for shape, kind in outs + far],
        scratch_shapes=[
            scr((t, d), F32), scr((t, d), F32), scr((t, d), F32), scr((t, d), BF), scr((t, d), BF), scr((t, d), F32),
            scr((t, d), BF), scr((t, 2 * d), BF),
            scr((t, d), F32), scr((t, d), F32), scr((t + 32, d), F32),
            dma((6,)), dma((3,)), dma, dma, dma((2,)), dma((2,)), dma,
        ],
        compiler_params=pltpu.CompilerParams(vmem_limit_bytes=58 << 20, collective_id=4, has_side_effects=True),
        cost_estimate=pl.CostEstimate(flops=40_000_000_000, bytes_accessed=120_000_000, transcendentals=0),
        name="middle_back",
    )(g, w, w, taps, vec, dy, third, conv, val, sig, second, result)
    return dconv, dout_3, d2, dout_2, dglu, mine, other, sums_4, sums_3, sums_2, result


ORDER = [
    ("q", 0), ("q", 1), ("q", 2), ("m", 0), ("m", 1), ("in", 0), ("m", 2), ("in", 1), ("m", 3),
    ("in", 2), ("out", 0), ("in", 3), ("out", 1), ("out", 2), ("out", 3),
]
N_CHUNK = len(ORDER)
FIRST_IN = 5
LAST_IN = 11
AHEAD = 2
HELD = 6


def thin(count):
    return [pl.ds(i, 128) for i in range(0, count, 128)]


def last_kernel(
    gain_ref, table_ref, sums_2_ref, sums_3_ref, sums_4_ref, sums_5_ref, sums_7_ref, dbias_ref,
    d2_ref, first_ref, x_ref, dconv_ref, gated_ref, halo_ref, part_ref, dqkv_ref, unit_q_ref, act_ref, unit_ref, inner_ref, w_out_ref, w_in_ref,
    mixed_ref, dout_2_ref, unit_2_ref, dglu_ref, act_c_ref, dout_3_ref,
    out_ref, out_part_ref, small_out_ref, table_out_ref, dx_ref,
    odd, even, core, first, second, whole, near, far,
    left, right, wo, wi, inner, dout, acc,
    small_0, small_y, small_x, small_c, small_z, table_got, d0, d1, some, dconv, gated, pad, taps,
    left_sem, right_sem, wo_sem, wi_sem, inner_sem, out_sem, part_sem, d1_sem, some_sem, taps_sem,
    core_send, core_recv, first_send, first_recv, second_send, second_recv,
    z_send, z_recv, small_send, small_recv, table_send, table_recv, dx_send, dx_recv, dx_sem, free_sem,
):
    r, d = out_ref.shape[1:]
    n_part = part_ref.shape[0]
    t = x_ref.shape[0]
    cut = r // 2
    me = lax.axis_index("fsdp")
    place = lax.axis_index("seq")
    two, four = jnp.int32(2), jnp.int32(4)
    chip = lax.div(me, two)
    bit_c, bit_x, bit_y = lax.rem(me, two), lax.rem(chip, two), lax.div(me, four)
    middle = lax.rem(lax.div(place + 1, two), two)
    to_c = {"fsdp": flipped_bit(me, 1)}
    to_x = {"fsdp": flipped_bit(me, 2)}
    to_y = {"fsdp": flipped_bit(me, 4)}
    to_1 = {"seq": flipped_bit(place, 1)}
    to_2 = {"seq": 3 - place}

    barrier = pltpu.get_barrier_semaphore()
    for device in (to_c, to_x, to_y, to_1, to_2, {"seq": flipped_bit(place, 2)}):
        pl.semaphore_signal(barrier, inc=1, device_id=device, device_id_type=MESH)

    def send(src, dst, send_sem, recv_sem, device):
        return pltpu.make_async_remote_copy(
            src_ref=src, dst_ref=dst, send_sem=send_sem, recv_sem=recv_sem, device_id=device, device_id_type=MESH
        )

    def at_2(c):
        return lax.rem(c, two)

    def at_3(c):
        return lax.rem(c, jnp.int32(3))

    def on(c, begin, end, work):
        pl.when((c >= begin) & (c < end))(lambda: work(c))

    def factor_copies(c, name, unit):
        cols = slice(unit * d, unit * d + d)
        lefts = {"q": unit_q_ref, "in": unit_ref, "m": (mixed_ref, unit_2_ref, unit_2_ref, act_c_ref)[unit % 4]}
        rights = {
            "q": lambda: dqkv_ref.at[:, cols],
            "m": lambda: (
                dout_2_ref if unit == 0 else dout_3_ref if unit == 3 else dglu_ref.at[:, (unit - 1) * d : unit * d]
            ),
        }
        src = act_ref.at[:, unit] if name == "out" else lefts[name]
        copies = [pltpu.make_async_copy(src, left.at[at_2(c)], left_sem.at[at_2(c)])]
        if name in rights:
            copies.append(pltpu.make_async_copy(rights[name](), right.at[at_3(c)], right_sem.at[at_3(c)]))
        return copies

    def fetch(c):
        for i, (name, unit) in enumerate(ORDER):

            @pl.when(c == i)
            def _(i=i, name=name, unit=unit):
                for copy in factor_copies(c, name, unit):
                    copy.start()

    def fetched(c):
        pltpu.make_async_copy(unit_ref, left.at[at_2(c)], left_sem.at[at_2(c)]).wait()
        has_right = functools.reduce(
            jnp.logical_or, [c == i for i, (name, _) in enumerate(ORDER) if name in ("q", "m")]
        )

        @pl.when(has_right)
        def _():
            pltpu.make_async_copy(dout_2_ref, right.at[at_3(c)], right_sem.at[at_3(c)]).wait()

    def is_in(c):
        return (c >= FIRST_IN) & (c <= LAST_IN) & (at_2(c) == FIRST_IN % 2)

    def wo_copy(j):
        return pltpu.make_async_copy(w_out_ref.at[pl.ds(2 * j, 2), pl.ds(0, 4)], wo, wo_sem)

    def wi_copy(j):
        return pltpu.make_async_copy(w_in_ref.at[:, j], wi, wi_sem)

    def wq_copy(i):
        return pltpu.make_async_copy(w_out_ref.at[:, 4 + i], wi, wi_sem)

    def inner_copy(j):
        return pltpu.make_async_copy(inner_ref.at[:, pl.ds(pl.multiple_of(j * d, d), d)], inner, inner_sem)

    def x_copy():
        return pltpu.make_async_copy(x_ref, inner, inner_sem)

    row = 53

    def hidden(c):
        j = lax.div(c - FIRST_IN, two)
        wo_copy(j).wait()
        inner_copy(j).wait()
        w = wo[...].reshape(d, d)
        dbias = jnp.zeros((1, d), F32)
        for rows in thin(t):
            da = dot(dout[rows, :], w, 1, 1)
            v = (da * silu_slope(inner[rows, :].astype(F32))).astype(BF)
            right[at_3(c), rows, :] = v
            dbias = dbias + total(v.astype(F32))
        for dev in range(2):
            for q in range(4):
                cols = pl.ds(pl.multiple_of((2 * j + dev) * r, r), r)
                small_0[row + 3 + q : row + 4 + q, cols] = dbias[:, dev * 4 * r + q * r : dev * 4 * r + (q + 1) * r]

        @pl.when(j < 3)
        def _():
            wo_copy(j + 1).start()
            inner_copy(j + 1).start()

        @pl.when(j == 3)
        def _():
            x_copy().start()

    def product(c):
        for i in range(4):
            value = dot(left[at_2(c), 2 * i : 2 * i + 2].reshape(2 * r, t), right[at_3(c)], 1, 0).astype(BF)
            low, high = value[:r], value[r:]
            p = i + bit_x - 2 * bit_x * (i % 2)
            p = p + 2 * bit_y - 4 * bit_y * lax.div(p, two)
            even[at_2(c), p] = jnp.where(bit_c == 0, low, high)
            odd[at_2(c), p] = jnp.where(bit_c == 0, high, low)

    def through(c, fresh):
        wi_copy(0).wait()
        w = wi[...].reshape(d, d)
        for rows in thin(t):
            p = dot(right[at_3(c), rows, :], w, 1, 1)
            acc[rows, :] = p + jnp.where(fresh, 0.0, acc[rows, :])

    def back(c):
        j = lax.div(c - FIRST_IN, two)
        through(c, j == 0)
        pl.when(j < 3)(lambda: wi_copy(j + 1).start())

    def back_q(c):
        through(c, c == 0)
        pl.when(c < 2)(lambda: wq_copy(c + 1).start())
        pl.when(c == 2)(lambda: wi_copy(0).start())
        column = total(right[at_3(c)].astype(F32))

        @pl.when(c == 0)
        def _():
            small_0[11:12, :] = column

        @pl.when(c == 2)
        def _():
            small_0[12:13, :] = column
            middle_gradient()

    def middle_gradient():
        pltpu.make_async_copy(d2_ref, d1, d1_sem).wait()
        copies = [
            pltpu.make_async_copy(first_ref.at[rows], some.at[i % 2], some_sem.at[i % 2]) for i, rows in enumerate(thin(t))
        ]
        for i, rows in enumerate(thin(t)):
            copies[i].wait()
            n, scale = normal(some[i % 2])
            du = acc[rows, :]
            value = d1[rows, :] + normal_back(du, n, scale, gain_ref[1:2, :])
            d1[rows, :] = value
            small_0[0:1, :] += total(du * n)
            small_0[5:6, :] += total(du)
            v = (HALF * value).astype(BF)
            dout[rows, :] = v
            small_0[row + 2 : row + 3, :] += total(v.astype(F32))
            if i + 2 < len(copies):
                copies[i + 2].start()

    def first_rows(i):
        return pltpu.make_async_copy(first_ref.at[pl.ds(128 * i, 128)], some.at[i], some_sem.at[i])

    def taps_copies(b):
        cols = pl.ds(pl.multiple_of(b * COLS, COLS), COLS)
        return [
            pltpu.make_async_copy(dconv_ref.at[:, cols], dconv, taps_sem.at[0]),
            pltpu.make_async_copy(halo_ref.at[:, cols], gated.at[pl.ds(0, 32)], taps_sem.at[1]),
            pltpu.make_async_copy(gated_ref.at[:, cols], gated.at[pl.ds(32, t)], taps_sem.at[2]),
        ]

    def taps_columns(b):
        for copy in taps_copies(b):
            copy.wait()
        pad[...] = gated[...].astype(F32)
        taps[...] = jnp.zeros_like(taps)
        reach = taps.shape[0] // 8

        def body(i, _):
            base = pl.multiple_of(i * ROWS, ROWS)
            window = pad[pl.ds(base, ROWS + 32), :]
            here = dconv[pl.ds(base, ROWS), :]
            for q in range(8):
                sh = shifted(window, q)
                for a in range(0, 5):
                    m = 8 * a + q - 2
                    if 0 <= m < reach:
                        v = here * sh[8 * a : 8 * a + ROWS]
                        taps[8 * m : 8 * m + 8, :] += (v[0:8] + v[8:16]) + (v[16:24] + v[24:32])
            return 0

        lax.fori_loop(0, t // ROWS, body, 0)
        cols = pl.ds(pl.multiple_of(b * COLS, COLS), COLS)
        for m in range(reach):
            small_0[18 + m : 19 + m, cols] = total(taps[8 * m : 8 * m + 8, :])

        @pl.when(b < d // COLS - 1)
        def _():
            for copy in taps_copies(b + 1):
                copy.start()

    def held_at(c):
        return lax.rem(c, jnp.int32(HELD))

    def core_copy(c):
        return send(odd.at[at_2(c)], core.at[held_at(c)], core_send.at[c], core_recv.at[c], to_c)

    def make(c):
        fetch(c + 1)
        fetched(c)

        is_out = functools.reduce(jnp.logical_or, [c == i for i, (name, _) in enumerate(ORDER) if name == "out"])

        @pl.when(is_out)
        def _():
            right[at_3(c)] = dout[...]

        pl.when(is_in(c))(lambda: hidden(c))
        product(c)
        pl.when(c >= HELD)(lambda: pl.semaphore_wait(free_sem, 1))
        core_copy(c).start()

    def make_back(c):
        pl.when(is_in(c))(lambda: back(c))
        pl.when(c < 3)(lambda: back_q(c))

    def first_copies(c):
        top, rest = pl.ds(0, cut), pl.ds(cut, cut)
        o = held_at(c)
        return [
            send(core.at[o, 1, top], first.at[o, 0, 0], first_send.at[c, 0], first_recv.at[c, 0], to_x),
            send(core.at[o, 3, top], first.at[o, 0, 1], first_send.at[c, 1], first_recv.at[c, 1], to_x),
            send(core.at[o, 2, rest], first.at[o, 1, 0], first_send.at[c, 2], first_recv.at[c, 2], to_y),
            send(core.at[o, 3, rest], first.at[o, 1, 1], first_send.at[c, 3], first_recv.at[c, 3], to_y),
        ]

    def second_copies(c):
        o = held_at(c)
        return [
            send(first.at[o, 0, 1], second.at[o, 0], second_send.at[c, 0], second_recv.at[c, 0], to_y),
            send(first.at[o, 1, 1], second.at[o, 1], second_send.at[c, 1], second_recv.at[c, 1], to_x),
        ]

    def add_core(c):
        core_copy(c).wait()
        o = held_at(c)

        def rows(i, _):
            at = pl.ds(pl.multiple_of(i * 32, 32), 32)
            for b in range(4):
                core[o, b, at] = (core[o, b, at].astype(F32) + even[at_2(c), b, at].astype(F32)).astype(BF)
            return 0

        lax.fori_loop(0, r // 32, rows, 0)
        for copy in first_copies(c):
            copy.start()

    def add_first(c):
        for copy in first_copies(c):
            copy.wait()
        o = held_at(c)

        def rows(i, _):
            at = pl.ds(pl.multiple_of(i * 32, 32), 32)
            low_at = pl.ds(pl.multiple_of(cut + i * 32, 32), 32)
            for b in range(2):
                first[o, 0, b, at] = (first[o, 0, b, at].astype(F32) + core[o, 2 * b, at].astype(F32)).astype(BF)
                first[o, 1, b, at] = (first[o, 1, b, at].astype(F32) + core[o, b, low_at].astype(F32)).astype(BF)
            return 0

        lax.fori_loop(0, cut // 32, rows, 0)

        @pl.when(c < N_CHUNK - HELD)
        def _():
            pl.semaphore_signal(free_sem, inc=1, device_id=to_c, device_id_type=MESH)

        for copy in second_copies(c):
            copy.start()

    def add_second(c):
        for copy in second_copies(c):
            copy.wait()
        o = held_at(c)
        whole[c, 0:cut] = (first[o, 0, 0].astype(F32) + second[o, 0].astype(F32)).astype(BF)
        whole[c, cut:r] = (first[o, 1, 0].astype(F32) + second[o, 1].astype(F32)).astype(BF)
        z_begin(c)

    z_begin, z_step = z_line(middle, to_1, to_2, whole, near, far, z_send, z_recv)

    def result_do(i, act):
        for is_middle, src in ((1, far), (0, near)):
            chunk = pltpu.make_async_copy(src.at[i], out_ref.at[i], out_sem.at[i])
            part = pltpu.make_async_copy(src.at[i], out_part_ref.at[i - N_CHUNK], out_sem.at[i])
            pl.when((middle == is_middle) & (i < N_CHUNK))(lambda chunk=chunk: act(chunk))
            pl.when((middle == is_middle) & (i >= N_CHUNK))(lambda part=part: act(part))

    def z_stage(i, stage):
        z_step(i, stage)
        if stage == 2:
            result_do(i, lambda copy: copy.start())

    wide = [d // 2, d // 4, d // 8]
    bits = [bit_y, bit_x, bit_c]
    held = [small_0, small_y, small_x, small_c]
    partner = [to_y, to_x, to_c, to_1, to_2]

    def columns(step, bit):
        return pl.ds(pl.multiple_of(bit * wide[step], wide[step]), wide[step])

    def small_copy(step):
        sems = (small_send.at[step], small_recv.at[step])
        if step < 3:
            return send(held[step].at[:, columns(step, 1 - bits[step])], held[step + 1], *sems, partner[step])
        if step == 3:
            return send(small_c, small_z.at[0], *sems, partner[step])
        return send(small_z.at[0], small_z.at[1], *sems, partner[step])

    def small_step(step):
        small_copy(step).wait()
        if step < 3:
            held[step + 1][...] += held[step][:, columns(step, bits[step])]
        elif step == 3:
            small_z[0] = small_z[0] + small_c[...]
        else:
            small_out_ref[...] = small_z[0] + small_z[1]
        if step < 4:
            small_copy(step + 1).start()

    def table_copy(step):
        src = table_ref if step == 0 else table_got.at[step - 1]
        return send(src, table_got.at[step], table_send.at[step], table_recv.at[step], partner[step])

    def table_step(step):
        table_copy(step).wait()
        before = table_ref[...] if step == 0 else table_got[step - 1]
        table_got[step] = table_got[step] + before
        if step < 4:
            table_copy(step + 1).start()
        else:
            table_out_ref[...] = table_got[step]

    mine, seq = lax.rem(place, two), lax.div(place, two)

    def dx_copy(h):
        return send(d0.at[pl.ds(h * (t // 2), t // 2)], dx_ref.at[seq], dx_send.at[h], dx_recv.at[seq], {"seq": 2 * mine + h})

    def dx_keep(h):
        return pltpu.make_async_copy(d0.at[pl.ds(h * (t // 2), t // 2)], dx_ref.at[seq], dx_sem)

    def dx_arrived(s):
        return send(d0.at[pl.ds(0, t // 2)], dx_ref.at[s], dx_send.at[0], dx_recv.at[s], to_1)

    def input_gradient():
        x_copy().wait()
        for rows in thin(t):
            n, scale = normal(inner[rows, :].astype(F32))
            du = acc[rows, :]
            d0[rows, :] = (d1[rows, :] + normal_back(du, n, scale, gain_ref[0:1, :])).astype(BF)
            small_0[row : row + 1, :] += total(du * n)
            small_0[row + 1 : row + 2, :] += total(du)
        for h in range(2):
            away = 2 * mine + h != place
            pl.when(away)(lambda h=h: dx_copy(h).start())
            pl.when(jnp.logical_not(away))(lambda h=h: dx_keep(h).start())
        small_copy(0).start()

    def part_copy(i):
        return pltpu.make_async_copy(part_ref.at[i], whole.at[N_CHUNK + i], part_sem.at[i])

    def part_begin(i):
        part_copy(i).wait()
        z_begin(N_CHUNK + i)

    fetch(jnp.int32(0))
    wq_copy(0).start()
    pltpu.make_async_copy(d2_ref, d1, d1_sem).start()
    for i in range(2):
        first_rows(i).start()
    for copy in taps_copies(jnp.int32(0)):
        copy.start()
    for i in range(n_part):
        part_copy(i).start()
    wo_copy(0).start()
    inner_copy(0).start()
    small_0[...] = jnp.zeros_like(small_0)
    here = {1: (sums_2_ref, 2), 2: (sums_3_ref, 1), 3: (sums_4_ref, 0), 4: (sums_5_ref, 0), 6: (sums_2_ref, 3)}
    here.update({7: (sums_3_ref, 2), 8: (sums_4_ref, 1), 9: (sums_5_ref, 1), 10: (sums_7_ref, 0), 13: (sums_2_ref, 4)})
    here.update({14: (sums_2_ref, 0), 15: (sums_2_ref, 1), 16: (sums_3_ref, 3), 17: (sums_3_ref, 0)})
    for at, (ref, i) in here.items():
        small_0[at : at + 1, :] = ref[i : i + 1, :]
    for j in range(4):
        for dev in range(2):
            for q in range(4):
                cols = slice((2 * j + dev) * r, (2 * j + dev + 1) * r)
                small_0[49 + q : 50 + q, cols] = dbias_ref[j, :, (4 * dev + q) * r : (4 * dev + q + 1) * r]
    pl.semaphore_wait(barrier, 6)
    table_copy(0).start()
    for c in range(AHEAD):
        make(jnp.int32(c))

    def slot(k, _):
        on(k, 0, N_CHUNK, add_core)
        on(k - 1, 0, N_CHUNK, add_first)
        on(k - 2, 0, N_CHUNK, add_second)
        for stage in range(3):
            on(k - 3 - stage, 0, N_CHUNK, lambda c, stage=stage: z_stage(c, stage))
        on(k, 0, n_part, part_begin)
        for stage in range(3):
            on(k - 1 - stage, 0, n_part, lambda i, stage=stage: z_stage(N_CHUNK + i, stage))
        make_back(k)
        on(k + AHEAD, 0, N_CHUNK, make)
        pl.when(k == LAST_IN)(input_gradient)
        for b in range(d // COLS):
            pl.when(k == 4 + 2 * b)(lambda b=b: taps_columns(jnp.int32(b)))
        for step in range(5):
            pl.when(k == step)(lambda step=step: table_step(step))
            pl.when(k == LAST_IN + 1 + step)(lambda step=step: small_step(step))
        return 0

    lax.fori_loop(0, N_CHUNK + 5, slot, 0)
    for h in range(2):
        away = 2 * mine + h != place
        pl.when(away)(lambda h=h: dx_copy(h).wait_send())
        pl.when(jnp.logical_not(away))(lambda h=h: dx_keep(h).wait())
    for s in range(2):
        from_away = 2 * s + lax.div(place, two) != place
        pl.when(from_away)(lambda s=s: dx_arrived(s).wait_recv())

    def settle(i, _):
        result_do(i, lambda copy: copy.wait())
        return 0

    lax.fori_loop(0, N_CHUNK + n_part, settle, 0)


def last_reduced(
    gain, table, sums, dbias, d2, first, tokens, dconv, gated, halo, part, dqkv, unit_q, act_t, unit_t, inner, w_out, w_in, mixed_t, dout_2, unit_2, dglu, act_c, dout_3
):
    n, _, r, d = w_in.shape
    t = tokens.shape[0]
    rows = 64
    k = N_CHUNK
    m = part.shape[0]
    z = k + m
    dma = pltpu.SemaphoreType.DMA
    anywhere = pl.BlockSpec(memory_space=pl.ANY)
    vmem = pl.BlockSpec(memory_space=pltpu.VMEM)
    return pl.pallas_call(
        last_kernel,
        in_specs=[vmem] * 8 + [anywhere] * 20,
        out_specs=[anywhere, anywhere, vmem, vmem, anywhere],
        out_shape=[
            jax.ShapeDtypeStruct((k, r, d), BF),
            jax.ShapeDtypeStruct((m, r, d), BF),
            jax.ShapeDtypeStruct((rows, d // 8), F32),
            jax.ShapeDtypeStruct(table.shape, F32),
            jax.ShapeDtypeStruct((2, t // 2, d), BF),
        ],
        scratch_shapes=[
            scr((2, 4, r, d), BF),
            scr((2, 4, r, d), BF),
            scr((HELD, 4, r, d), BF),
            scr((HELD, 2, 2, r // 2, d), BF),
            scr((HELD, 2, r // 2, d), BF),
            scr((z, r, d), BF),
            scr((z, r, d), BF),
            scr((z, r, d), BF),
            scr((2, n, r, t), BF),
            scr((3, t, d), BF),
            scr((2, 4, r, d), BF),
            scr((n, r, d), BF),
            scr((t, d), BF),
            scr((t, d), BF),
            scr((t, d), F32),
            scr((rows, d), F32),
            scr((rows, d // 2), F32),
            scr((rows, d // 4), F32),
            scr((rows, d // 8), F32),
            scr((2, rows, d // 8), F32),
            scr((5,) + table.shape, F32),
            scr((t, d), BF),
            scr((t, d), F32),
            scr((2, 128, d), F32),
            scr((t, COLS), F32),
            scr((t + 32, COLS), BF),
            scr((t + 32, COLS), F32),
            scr((8 * 31, COLS), F32),
            dma((2,)),
            dma((3,)),
            dma,
            dma,
            dma,
            dma((z,)),
            dma((m,)),
            dma,
            dma((2,)),
            dma((3,)),
            dma((k,)),
            dma((k,)),
            dma((k, 4)),
            dma((k, 4)),
            dma((k, 2)),
            dma((k, 2)),
            dma((z, 3)),
            dma((z, 3)),
            dma((5,)),
            dma((5,)),
            dma((5,)),
            dma((5,)),
            dma((2,)),
            dma((2,)),
            dma,
            pltpu.SemaphoreType.REGULAR,
        ],
        compiler_params=pltpu.CompilerParams(vmem_limit_bytes=60 << 20, collective_id=0, has_side_effects=True),
        cost_estimate=pl.CostEstimate(flops=100_000_000_000, bytes_accessed=400_000_000, transcendentals=0),
        name="last",
    )(
        gain, table, *sums, dbias, d2, first, tokens, dconv, gated, halo, part, dqkv, unit_q.reshape(n, r, t), act_t.reshape(n, 4, r, t),
        unit_t.reshape(n, r, t), inner, w_out, w_in,
        mixed_t.reshape(n, r, t), dout_2, unit_2.reshape(n, r, t), dglu, act_c.reshape(n, r, t), dout_3,
    )


PLACE = {item: i for i, item in enumerate(ORDER)}


def finish_kernel(n_tap, main, in_b, out_b, small, table, g_in, g_out, g_qkv, g_attn, g_conv_in, g_conv_out, g_taps, g_gain, g_shift, g_bias, g_table):
    d = main.shape[-1]

    def of(name, unit):
        return main[PLACE[name, unit]].astype(F32)

    for u in range(4):
        cols = slice(u * d, (u + 1) * d)
        g_in[0, :, cols] = of("in", u)
        g_in[1, :, cols] = in_b[u].astype(F32)
        g_out[0, u] = of("out", u)
        g_out[1, u] = out_b[u].astype(F32)
    for u in range(3):
        g_qkv[u] = of("q", u)
    g_attn[...] = of("m", 0)
    g_conv_in[:, :d] = of("m", 1)
    g_conv_in[:, d:] = of("m", 2)
    g_conv_out[...] = of("m", 3)
    w = g_taps.shape[1]
    early, late = 0, 22 + n_tap
    g_taps[...] = small[18 : 18 + n_tap, :]
    g_gain[0:1, :] = small[late : late + 1, :]
    g_gain[1:6, :] = small[0:5, :]
    g_shift[0:1, :] = small[late + 1 : late + 2, :]
    g_shift[1:6, :] = small[5:10, :]
    g_shift[6:7, :] = small[late + 2 : late + 3, :]
    g_shift[7:15, :] = small[10:18, :]
    for u in range(4):
        g_bias[0:1, u * w : (u + 1) * w] = small[late + 3 + u : late + 4 + u, :]
        g_bias[1:2, u * w : (u + 1) * w] = small[18 + n_tap + u : 19 + n_tap + u, :]
    k, h = g_table.shape
    g_table[...] = table[0:k, 0:h] + table[0:k, h : 2 * h]


def finished(main, in_b, out_b, small, table, n_tap, table_shape):
    k, r, d = main.shape
    w = small.shape[1]
    step = min(r, 32)

    def rows(count):
        return pl.BlockSpec((count, step, d), lambda i: (0, i, 0))

    def whole(*shape):
        return pl.BlockSpec(shape, lambda i: (0,) * len(shape))

    outs = [
        ((2, r, 4 * d), pl.BlockSpec((2, step, 4 * d), lambda i: (0, i, 0))),
        ((2, 4, r, d), pl.BlockSpec((2, 4, step, d), lambda i: (0, 0, i, 0))),
        ((3, r, d), rows(3)),
        ((r, d), pl.BlockSpec((step, d), lambda i: (i, 0))),
        ((r, 2 * d), pl.BlockSpec((step, 2 * d), lambda i: (i, 0))),
        ((r, d), pl.BlockSpec((step, d), lambda i: (i, 0))),
        ((n_tap, w), whole(n_tap, w)),
        ((6, w), whole(6, w)),
        ((15, w), whole(15, w)),
        ((2, 4 * w), whole(2, 4 * w)),
        (table_shape, whole(*table_shape)),
    ]
    return pl.pallas_call(
        functools.partial(finish_kernel, n_tap),
        grid=(r // step,),
        in_specs=[rows(k), rows(4), rows(4), whole(*small.shape), whole(*table.shape)],
        out_specs=[b for _, b in outs],
        out_shape=[jax.ShapeDtypeStruct(s, F32) for s, _ in outs],
        compiler_params=pltpu.CompilerParams(vmem_limit_bytes=VMEM),
        cost_estimate=pl.CostEstimate(flops=0, bytes_accessed=18_000_000, transcendentals=0),
        name="finish",
    )(main, in_b, out_b, small, table)


def xor_route(axis, mask):
    return [(i, i ^ mask) for i in range(lax.axis_size(axis))]


def swapped(block, axis, mask):
    return lax.ppermute(block, axis, xor_route(axis, mask))


def after(value, *marks):
    return lax.optimization_barrier((value,) + marks)[0]


def over_seq(part):
    if lax.axis_size("seq") != 4 or part.shape[1] < 64:
        return lax.psum(part, "seq")
    place = lax.axis_index("seq")
    part = part.astype(F32)
    for mask in (1, 2):
        high = (place & mask) != 0
        half = part.shape[1] // 2
        first, second = part[:, :half], part[:, half:]
        sent = jnp.where(high, first, second).astype(BF)
        part = jnp.where(high, second, first) + swapped(sent, "seq", mask).astype(F32)
    part = part.astype(BF)
    for mask in (2, 1):
        high = (place & mask) != 0
        got = swapped(part, "seq", mask)
        part = jnp.where(high, jnp.concatenate([got, part], axis=1), jnp.concatenate([part, got], axis=1))
    return part


def reduced(g):
    return over_seq(lax.psum_scatter(g, "fsdp", scatter_dimension=0, tiled=False))


def small_reduced(rows):
    k, d = rows.shape
    n = lax.axis_size("fsdp")
    me = lax.axis_index("fsdp")
    rows = lax.psum(rows, ("seq", "fsdp"))
    return lax.dynamic_slice_in_dim(rows, me * (d // n), d // n, 1)


def to_pairs(array, place):
    one, two = array[0], array[1]
    got = lax.ppermute(jnp.where(place % 2 == 0, two, one), "seq", [(0, 2), (1, 0), (2, 3), (3, 1)])
    more = lax.ppermute(jnp.where(place == 1, two, one), "seq", [(1, 2), (2, 1)])
    first = jnp.where(place == 0, one, jnp.where(place == 1, more, got))
    second = jnp.where(place < 2, got, jnp.where(place == 2, more, two))
    return jnp.concatenate([first, second], axis=0)


def from_pairs(array, place):
    half = array.shape[0] // 2
    first, second = array[:half], array[half:]
    got = lax.ppermute(jnp.where(place < 2, second, first), "seq", [(2, 0), (0, 1), (3, 2), (1, 3)])
    more = lax.ppermute(jnp.where(place == 1, first, second), "seq", [(1, 2), (2, 1)])
    one = jnp.where(place == 0, first, jnp.where(place == 2, more, got))
    two = jnp.where(place == 3, second, jnp.where(place == 1, more, got))
    return jnp.stack([one, two])


def on_device(
    inputs,
    lengths,
    ffn_in,
    ffn_in_bias,
    ffn_out,
    qkv,
    attn_out,
    conv_in,
    conv_out,
    depthwise,
    gains,
    shifts,
    distance,
    grad_out,
):
    n = lax.axis_size("fsdp")
    me = lax.axis_index("fsdp")
    place = lax.axis_index("seq")
    odd = place % 2 == 1
    odd_word = (place % 2).astype(jnp.int32).reshape(1)
    me_word = me.astype(jnp.int32).reshape(1)
    width = inputs.shape[2]
    r = width // n
    inner_width = ffn_in.shape[2]
    n_gain, n_shift, n_tap = gains.shape[0], shifts.shape[0], depthwise.shape[0]
    cubed = n == 8 and lax.axis_size("seq") == 4

    def chunks(part):
        return [part[:, i : i + width] for i in range(0, part.shape[1], width)]

    shard_a = jnp.stack(chunks(ffn_in[0]))
    shard_b = jnp.concatenate([ffn_out[0].reshape(4, r, width), qkv], axis=0)
    shard_c = jnp.stack(chunks(ffn_in[1]) + [attn_out] + chunks(conv_in) + [conv_out])
    shard_d = ffn_out[1].reshape(4, r, width)
    if cubed:
        w_b = lax.all_gather(shard_b, "fsdp", axis=0)
        inner_a, act_a, act_t_a, unit_t_a, tokens, small, w_a = first_forward(
            inputs, after(shard_a, shard_b), gains, shifts, depthwise, ffn_in_bias
        )
        cotangent = to_pairs(after(grad_out, act_a), place)
    else:
        small = jnp.concatenate([gains, shifts, depthwise, ffn_in_bias.reshape(-1, r)], axis=0)
        small = lax.all_gather(small, "fsdp", axis=0)
        w_a = lax.all_gather(shard_a, "fsdp", axis=0)
        w_b = lax.all_gather(shard_b, "fsdp", axis=0)
        tokens, cotangent = to_pairs(inputs, place), to_pairs(grad_out, place)

    small = small.astype(F32)
    rows = jnp.transpose(small, (1, 0, 2))
    n_plain = n_gain + n_shift + n_tap
    gain = rows[:n_gain].reshape(n_gain, width)
    shift = rows[n_gain : n_gain + n_shift].reshape(n_shift, width)
    taps = rows[n_gain + n_shift : n_plain].reshape(n_tap, width)
    bias = small[:, n_plain : n_plain + 8].reshape(n, 2, -1).transpose(1, 0, 2).reshape(2, inner_width)

    length = jnp.where(place < 2, lengths[0], lengths[1]).reshape(1)
    wide, ends = tables(distance)
    pairs = [(0, 1), (2, 3)]

    if not cubed:
        inner_a, act_a, act_t_a, unit_t_a = ffn_in_forward(tokens, jnp.stack([gain[0], shift[0]]), bias[0], w_a, 0)
    w_c = lax.all_gather(after(shard_c, w_b, cotangent, act_a), "fsdp", axis=0)
    first, unit_t_1, mine, other = out_qkv_forward(
        odd_word, tokens, act_a, w_b, jnp.stack([shift[6], gain[1], shift[1], shift[8], shift[9]])
    )
    probs, heads, mixed = attend(mine, other, length, wide, ends)
    w_d = lax.all_gather(after(shard_d, w_c, mixed), "fsdp", axis=0)
    second, mixed_t, unit_t_2, val, sig, gated = mid_forward(
        first, mixed, w_c, 4, 5, jnp.stack([shift[10], gain[2], shift[2], shift[11], shift[12]])
    )
    count = gated.shape[0]
    halo = lax.ppermute(gated[count - 32 :], "seq", pairs)
    conv, act_t_c, third = conv_forward(
        gated, halo, taps, jnp.stack([shift[13], gain[3], shift[3], shift[14]]), second, w_c, 7
    )
    inner_b, act_b, act_t_b, unit_t_b = ffn_in_forward(third, jnp.stack([gain[4], shift[4]]), bias[1], w_c, 0)
    outputs, d4, dout, sums_5 = out_last(third, act_b, w_d, 0, cotangent, jnp.stack([shift[7], gain[5], shift[5]]))

    g_out_b = weight_grad(act_t_b, dout, n, 4, 0, True)
    part_out_b = lax.psum_scatter(g_out_b, "fsdp", scatter_dimension=0, tiled=False)
    dinner, dout, dbias_b, sums_7 = ffn_hidden_back(after(dout, g_out_b), inner_b, w_d, 0)
    g_in_b = weight_grad(unit_t_b, dinner, n, 4, 0, False)
    part_in_b = lax.psum_scatter(g_in_b, "fsdp", scatter_dimension=0, tiled=False)
    dinner = after(dinner, g_in_b)
    if cubed:
        vec = jnp.stack([gain[4], gain[3], shift[3], gain[2]])
        dconv, dout_3, d2, dout_2, dglu, mine, other, sums_4, sums_3, sums_2, outputs = middle_back(
            d4, dinner, third, conv, val, sig, second, w_c, taps, vec, outputs
        )
    else:
        outputs = from_pairs(outputs, place)
        d3, sums_4 = norm_input_back(d4, dinner, third, w_c, 0, gain[4:5])
        dconv, dout_3, sums_3 = conv_out_back(d3, conv, w_c, 7, jnp.stack([gain[3], shift[3]]))
        follow = lax.ppermute(dconv[:32], "seq", [(j, i) for i, j in pairs])
        d2, dout_2, dglu, mine, other, sums_2 = mid_back(
            odd_word, dconv, follow, taps, val, sig, second, d3, w_c, 4, 5, gain[2:3]
        )
    if cubed:
        dqkv, dtable, share_out_b = attend_back(heads, probs, wide, mine, other, part_out_b)
    else:
        dqkv, dtable = attend_back(heads, probs, wide, mine, other)
        share_out_b, share_in_b = over_seq(part_out_b), over_seq(part_in_b)

    def biases(part):
        return part.reshape(n, 4, r).transpose(1, 0, 2).reshape(4, width)

    if cubed:
        main, share_in_b, small, table, grad_tokens = last_reduced(
            gain[0:2], dtable, (sums_2, sums_3, sums_4, sums_5, sums_7), dbias_b, d2, first, tokens, dconv, gated, halo,
            part_in_b, dqkv, unit_t_1, act_t_a, unit_t_a, inner_a, w_b, w_a,
            mixed_t, dout_2, unit_t_2, dglu, act_t_c, dout_3,
        )
    else:
        d1, sums_1 = norm_input_back(d2, dqkv, first, w_b, 4, gain[1:2])
        bias_sums = jnp.sum(dqkv.astype(F32), axis=0)
        dtaps = taps_grad(dconv, gated, halo, n_tap)
        early = jnp.concatenate(
            [
                jnp.stack([sums_1[0], sums_2[2], sums_3[1], sums_4[0], sums_5[0]]),
                jnp.stack([sums_1[1], sums_2[3], sums_3[2], sums_4[1], sums_5[1]]),
                jnp.stack(
                    [
                        sums_7[0],
                        bias_sums[:width],
                        bias_sums[2 * width :],
                        sums_2[4],
                        sums_2[0],
                        sums_2[1],
                        sums_3[3],
                        sums_3[0],
                    ]
                ),
                dtaps,
                biases(dbias_b),
            ],
            axis=0,
        )
        dinner, dout, dbias_a, sums_6 = ffn_hidden_back(d1, inner_a, w_b, 0)
        g_m = weight_grad(unit_t_2, dglu, n, 4, 1, False)
        g_m = weight_grad(mixed_t, dout_2, n, 4, 0, False, into=g_m)
        g_m = weight_grad(act_t_c, dout_3, n, 4, 3, False, into=g_m)
        shares = {
            "m": reduced(g_m),
            "q": reduced(weight_grad(unit_t_1, dqkv, n, 3, 0, False)),
            "out": reduced(weight_grad(act_t_a, dout, n, 4, 0, True)),
            "in": reduced(weight_grad(unit_t_a, dinner, n, 4, 0, False)),
        }
        main = jnp.stack([shares[name][unit] for name, unit in ORDER])
        d0, sums_0 = norm_input_back(d1, dinner, tokens, w_a, 0, gain[0:1], BF)
        grad_tokens = from_pairs(d0, place)
        late = jnp.concatenate([jnp.stack([sums_0[0], sums_0[1], sums_6[0]]), biases(dbias_a)], axis=0)
        small = small_reduced(jnp.concatenate([early, late], axis=0))
        table = lax.psum(dtable, ("seq", "fsdp"))
    g_in, g_out, g_qkv, g_attn, g_conv_in, g_conv_out, g_taps, g_gain, g_shift, g_bias, total_table = finished(
        main, share_in_b, share_out_b, small, table, n_tap, distance.shape
    )
    return (
        outputs,
        grad_tokens,
        g_in,
        g_bias,
        g_out.reshape(2, 4 * r, width),
        g_qkv,
        g_attn,
        g_conv_in,
        g_conv_out,
        g_taps,
        g_gain,
        g_shift,
        total_table,
    )


def solution(mesh):
    return jax.shard_map(
        on_device,
        mesh=mesh,
        in_specs=(
            P("fsdp", "seq", None),
            P("fsdp"),
            P(None, "fsdp", None),
            P(None, "fsdp"),
            P(None, "fsdp", None),
            P(None, "fsdp", None),
            P("fsdp", None),
            P("fsdp", None),
            P("fsdp", None),
            P(None, "fsdp"),
            P(None, "fsdp"),
            P(None, "fsdp"),
            P(),
            P("fsdp", "seq", None),
        ),
        out_specs=(
            P("fsdp", "seq", None),
            P("fsdp", "seq", None),
            P(None, "fsdp", None),
            P(None, "fsdp"),
            P(None, "fsdp", None),
            P(None, "fsdp", None),
            P("fsdp", None),
            P("fsdp", None),
            P("fsdp", None),
            P(None, "fsdp"),
            P(None, "fsdp"),
            P(None, "fsdp"),
            P(),
        ),
        check_vma=False,
    )
```

```python
import functools

import jax
import jax.numpy as jnp
from jax import lax
from jax.experimental import pallas as pl
from jax.experimental.pallas import tpu as pltpu
from jax.sharding import PartitionSpec as P

HEAD_DIM=64; LEFT=64; RIGHT=8
F32=jnp.float32; BF=jnp.bfloat16
RB=256
PADL=128
WIN=512

def dot(a,b,ca,cb):
    return lax.dot_general(a,b,(((ca,),(cb,)),((),())),preferred_element_type=F32)

def lanes(shape):
    return lax.broadcasted_iota(jnp.int32,shape,1)

def band_offset():
    row=lax.broadcasted_iota(jnp.int32,(RB,WIN),0)
    col=lax.broadcasted_iota(jnp.int32,(RB,WIN),1)
    return col-row-LEFT


MESH = pl.DeviceIdType.MESH
STEPS = 4


def pair_place():
    place = lax.axis_index("seq")
    half = lax.rem(place, jnp.int32(2))
    return half, {"seq": place + 1 - 2 * half}


def meet(partner):
    barrier = pltpu.get_barrier_semaphore()
    pl.semaphore_signal(barrier, inc=1, device_id=partner, device_id_type=MESH)
    pl.semaphore_wait(barrier, 1)


def block_at(step, half):
    return lax.rem(step + 2 * (1 - half), jnp.int32(STEPS))


def fwd_kernel(len_ref,wide_ref,ends_ref,mine_ref,other_ref,p_ref,heads_ref,mixed_ref,s_ref,kx_ref,buf,mixed,stage,in_send,in_recv,in_load,out_send,out_recv):
    n=buf.shape[2]; own=n//2
    pair=pl.program_id(0); step=pl.program_id(1)
    pairs=buf.shape[0]
    half,partner=pair_place()
    at=pl.multiple_of(half*own,own)
    def arrive(a):
        return pltpu.make_async_remote_copy(src_ref=other_ref.at[a],dst_ref=buf.at[a,:,pl.ds(at,own)],send_sem=in_send.at[a],recv_sem=in_recv.at[a],device_id=partner,device_id_type=MESH)
    def load(a):
        return pltpu.make_async_copy(mine_ref.at[a],buf.at[a,:,pl.ds(at,own)],in_load.at[a])
    def leave(a,b):
        cols=pl.ds(pl.multiple_of(half*own+a*128,128),128)
        return pltpu.make_async_remote_copy(src_ref=stage.at[a,b],dst_ref=mixed.at[pl.ds(pl.multiple_of(b*RB,RB),RB),cols],send_sem=out_send.at[a,b],recv_sem=out_recv.at[a,b],device_id=partner,device_id_type=MESH)
    @pl.when((pair==0)&(step==0))
    def _():
        meet(partner)
        for a in range(pairs):
            load(a).start()
            arrive(a).start()
    @pl.when(step==0)
    def _():
        load(pair).wait()
        arrive(pair).wait()
        heads_ref[0]=buf[pair]
        kx_ref[:,0:128]=buf[pair,1]
    i0=pl.multiple_of(block_at(step,half)*RB,RB)
    q2=buf[pair,0,pl.ds(i0,RB)]
    v2=buf[pair,2]
    lane=lanes((RB,128))
    t=lax.broadcasted_iota(jnp.int32,(n,128),0)
    c=lanes((n,128))
    left=(t<i0-128).astype(F32); right=(t>=i0+WIN-128).astype(F32)
    masked=jnp.where(t>=len_ref[0],-1e30,0.0)
    ext=jnp.where(c<2,left,jnp.where(c<4,right,jnp.where(c==4,masked,0.0)))
    kx_ref[:,128:256]=ext.astype(BF)
    qhs,qxs=[],[]
    for h in range(2):
        head=(lane<64) if h==0 else (lane>=64)
        qh=jnp.where(head,q2,jnp.zeros_like(q2))
        ends=dot(qh,ends_ref[...],1,0)
        hi=ends.astype(BF).astype(F32)
        qx=jnp.where((lane==0)|(lane==2),hi,jnp.where((lane==1)|(lane==3),ends-hi,jnp.where(lane==4,1.0,0.0))).astype(BF)
        qhs.append(qh); qxs.append(jnp.concatenate([qh,qx],axis=1))
    for h in range(2):
        s_ref[h,:,PADL:PADL+n]=dot(qxs[h],kx_ref[...],1,1)
    j=band_offset()
    w=pl.ds(i0,WIN)
    for h in range(2):
        wide=dot(qhs[h],wide_ref[...],1,0)
        band=pltpu.roll(wide,LEFT,1,stride=1,stride_axis=0)
        band=jnp.where(j>=LEFT+RIGHT,wide[:,LEFT+RIGHT:LEFT+RIGHT+1],band)
        s_ref[h,:,w]=s_ref[h,:,w]+band
    for h in range(2):
        s=s_ref[h,:,PADL:PADL+n]
        m=jnp.max(s,axis=1,keepdims=True)
        e=jnp.exp(s-m)
        z=jnp.sum(e,axis=1,keepdims=True)
        p_ref[h]=(e*(1.0/z)).astype(BF)
    outs=[dot(p_ref[h],v2,1,0) for h in range(2)]
    out=jnp.where(lane<64,outs[0],outs[1]).astype(BF)
    @pl.when(step<2)
    def _():
        stage[pair,step]=out
        leave(pair,step).start()
    @pl.when(step>=2)
    def _():
        cols=pl.ds(pl.multiple_of(half*own+pair*128,128),128)
        mixed[pl.ds(pl.multiple_of((step-2)*RB,RB),RB),cols]=out
    @pl.when((pair==pairs-1)&(step==STEPS-1))
    def _():
        for a in range(pairs):
            for b in range(2):
                leave(a,b).wait_send()
        for a in range(pairs):
            for b in range(2):
                arrived=pltpu.make_async_remote_copy(src_ref=stage.at[a,b],dst_ref=mixed.at[pl.ds(b*RB,RB),pl.ds(pl.multiple_of((1-half)*own+a*128,128),128)],send_sem=out_send.at[a,b],recv_sem=out_recv.at[a,b],device_id=partner,device_id_type=MESH)
                arrived.wait_recv()
        mixed_ref[...]=mixed[...]


def z_line(middle,to_1,to_2,whole,near,far,z_send,z_recv):
    def copy(i,stage):
        src=(whole,near,far)[stage]; dst=(near,far,near)[stage]
        return pltpu.make_async_remote_copy(src_ref=src.at[i],dst_ref=dst.at[i],send_sem=z_send.at[i,stage],recv_sem=z_recv.at[i,stage],device_id=to_2 if stage==1 else to_1,device_id_type=MESH)
    def begin(i):
        pl.when(middle==0)(lambda: copy(i,0).start())
    def step(i,stage):
        @pl.when(middle==1)
        def _():
            if stage==0:
                copy(i,0).wait_recv()
                near[i]=(whole[i].astype(F32)+near[i].astype(F32)).astype(BF)
                copy(i,1).start()
            elif stage==1:
                copy(i,1).wait()
                far[i]=(near[i].astype(F32)+far[i].astype(F32)).astype(BF)
                copy(i,2).start()
            else:
                copy(i,2).wait_send()
        if stage!=1:
            @pl.when(middle==0)
            def _():
                if stage==0:
                    copy(i,0).wait_send()
                else:
                    copy(i,2).wait_recv()
    return begin,step


def bwd_kernel(with_part,heads_ref,p_ref,wide_ref,mine_ref,other_ref,*rest):
    if with_part:
        part_ref,dqkv_ref,de_ref,out_ref,*rest=rest
        *rest,whole,near,far,part_sem,out_sem,z_send,z_recv=rest
    else:
        dqkv_ref,de_ref,*rest=rest
    ds_ref,kx_ref,dka,dva,dea,buf,dqkv,stage_q,stage_kv,in_send,in_recv,in_load,q_send,q_recv,kv_send,kv_recv=rest
    n=heads_ref.shape[2]; own=n//2
    pair=pl.program_id(0); step=pl.program_id(1)
    pairs=buf.shape[0]
    half,partner=pair_place()
    at=pl.multiple_of(half*own,own)
    width=2*own
    def columns(t,who,a):
        return pl.ds(pl.multiple_of(t*width+who*own+a*128,128),128)
    def arrive(a):
        return pltpu.make_async_remote_copy(src_ref=other_ref.at[a],dst_ref=buf.at[a,pl.ds(at,own)],send_sem=in_send.at[a],recv_sem=in_recv.at[a],device_id=partner,device_id_type=MESH)
    def load(a):
        return pltpu.make_async_copy(mine_ref.at[a],buf.at[a,pl.ds(at,own)],in_load.at[a])
    def leave_q(a,b,who):
        return pltpu.make_async_remote_copy(src_ref=stage_q.at[a,b],dst_ref=dqkv.at[pl.ds(pl.multiple_of(b*RB,RB),RB),columns(0,who,a)],send_sem=q_send.at[a,b],recv_sem=q_recv.at[a,b],device_id=partner,device_id_type=MESH)
    def leave_kv(a,t,who):
        return pltpu.make_async_remote_copy(src_ref=stage_kv.at[a,t],dst_ref=dqkv.at[:,columns(t+1,who,a)],send_sem=kv_send.at[a,t],recv_sem=kv_recv.at[a,t],device_id=partner,device_id_type=MESH)
    if with_part:
        n_part=part_ref.shape[0]
        place=lax.axis_index("seq")
        middle=lax.rem(lax.div(place+1,jnp.int32(2)),jnp.int32(2))
        across={"seq":3-place}
        z_begin,z_step=z_line(middle,partner,across,whole,near,far,z_send,z_recv)
        def part_copy(i):
            return pltpu.make_async_copy(part_ref.at[i],whole.at[i],part_sem.at[i])
        def result_do(i,act):
            for is_middle,src in ((1,far),(0,near)):
                copy=pltpu.make_async_copy(src.at[i],out_ref.at[i],out_sem.at[i])
                pl.when(middle==is_middle)(lambda copy=copy: act(copy))
        now=pair*STEPS+step
    @pl.when((pair==0)&(step==0))
    def _():
        if with_part:
            barrier=pltpu.get_barrier_semaphore()
            for device in (partner,across):
                pl.semaphore_signal(barrier,inc=1,device_id=device,device_id_type=MESH)
            pl.semaphore_wait(barrier,2)
        else:
            meet(partner)
        for a in range(pairs):
            load(a).start()
            arrive(a).start()
        if with_part:
            for i in range(n_part):
                part_copy(i).start()
        dea[...]=jnp.zeros_like(dea)
        for h in range(2):
            ds_ref[h,:,0:PADL]=jnp.zeros((RB,PADL),F32)
            ds_ref[h,:,PADL+n:]=jnp.zeros((RB,ds_ref.shape[2]-PADL-n),F32)
    @pl.when(step==0)
    def _():
        load(pair).wait()
        pl.when(pair>0)(lambda: arrive(pair).wait())
        kx_ref[:,0:128]=heads_ref[0,1]
        dka[...]=jnp.zeros_like(dka); dva[...]=jnp.zeros_like(dva)
    if with_part:
        for i in range(n_part):
            @pl.when(now==1+2*i)
            def _(i=i):
                part_copy(i).wait()
                z_begin(i)
            for stage in range(3):
                @pl.when(now==5+2*i+2*stage)
                def _(i=i,stage=stage):
                    z_step(i,stage)
                    if stage==2:
                        result_do(i,lambda copy: copy.start())
    @pl.when((pair==0)&(step==2))
    def _():
        arrive(pair).wait()
    turned=lax.rem(step+2*jnp.where(pair==0,1,0),jnp.int32(STEPS))
    i0=pl.multiple_of(block_at(turned,half)*RB,RB)
    q2=heads_ref[0,0,pl.ds(i0,RB)]
    v2=heads_ref[0,2]
    do2=buf[pair,pl.ds(i0,RB)]
    lane=lanes((RB,128))
    row=lax.broadcasted_iota(jnp.int32,(RB,128),0)
    t=lax.broadcasted_iota(jnp.int32,(n,128),0)
    c=lanes((n,128))
    left=(t<i0-128).astype(F32)
    kx_ref[:,128:256]=jnp.where(c==0,left,jnp.where(c==1,1.0,0.0)).astype(BF)
    heads=[]
    for h in range(2):
        head=(lane<64) if h==0 else (lane>=64)
        heads.append((jnp.where(head,do2,jnp.zeros_like(do2)),jnp.where(head,q2,jnp.zeros_like(q2))))
    dps=[dot(doh,v2,1,1) for doh,_ in heads]
    dss=[]
    for h in range(2):
        pf=p_ref[h].astype(F32)
        d=jnp.sum(pf*dps[h],axis=1,keepdims=True)
        dsf=pf*(dps[h]-d)
        ds_ref[h,:,PADL:PADL+n]=dsf
        dss.append(dsf.astype(BF))
    dva[...]+=dot(heads[0][0],p_ref[0],0,0)+dot(heads[1][0],p_ref[1],0,0)
    dka[...]+=dot(heads[0][1],dss[0],0,0)+dot(heads[1][1],dss[1],0,0)
    dqxs=[dot(ds,kx_ref[...],1,0) for ds in dss]
    j=band_offset()
    drels=[]
    for h in range(2):
        sums=dqxs[h][:,128:256]
        win=ds_ref[h,:,pl.ds(i0,WIN)]
        inleft=jnp.sum(jnp.where(j<=0,win,0.0),axis=1,keepdims=True)
        drel=jnp.concatenate([win[8*g:8*g+8,LEFT+8*g:LEFT+8*g+128] for g in range(RB//8)],axis=0)
        for bit in (1,2,4):
            drel=jnp.where((row&bit)!=0,pltpu.roll(drel,128-bit,1),drel)
        drel=jnp.where((lane>0)&(lane<LEFT+RIGHT),drel,0.0)
        bandsum=jnp.sum(drel,axis=1,keepdims=True)
        l=sums[:,0:1]+inleft
        r=sums[:,1:2]-l-bandsum
        drels.append(jnp.where(lane==0,l,jnp.where(lane==LEFT+RIGHT,r,drel)).astype(BF))
    dqs=[dqxs[h][:,0:128]+dot(drels[h],wide_ref[...],1,1) for h in range(2)]
    dea[...]+=dot(drels[0],heads[0][1],0,0)+dot(drels[1],heads[1][1],0,0)
    dq=(jnp.where(lane<64,dqs[0],dqs[1])*HEAD_DIM**-0.5).astype(BF)
    @pl.when(turned<2)
    def _():
        stage_q[pair,turned]=dq
        leave_q(pair,turned,half).start()
    @pl.when(turned>=2)
    def _():
        dqkv[pl.ds(pl.multiple_of((turned-2)*RB,RB),RB),columns(0,half,pair)]=dq
    @pl.when(step==STEPS-1)
    def _():
        for i,acc in enumerate((dka,dva)):
            mine=acc[:,pl.ds(at,own)]
            theirs=acc[:,pl.ds(pl.multiple_of((1-half)*own,own),own)]
            stage_kv[pair,i]=jnp.transpose(theirs).astype(BF)
            leave_kv(pair,i,half).start()
            dqkv[:,columns(i+1,half,pair)]=jnp.transpose(mine).astype(BF)
    @pl.when((pair==pairs-1)&(step==STEPS-1))
    def _():
        for a in range(pairs):
            for b in range(2):
                leave_q(a,b,half).wait_send()
                leave_kv(a,b,half).wait_send()
        for a in range(pairs):
            for b in range(2):
                leave_q(a,b,1-half).wait_recv()
                leave_kv(a,b,1-half).wait_recv()
        dqkv_ref[...]=dqkv[...]
        de_ref[...]=dea[...]
        if with_part:
            for i in range(n_part):
                result_do(i,lambda copy: copy.wait())


def tables(distance):
    e=distance.T
    wide=jnp.concatenate([e,jnp.broadcast_to(e[:,72:73],(64,120)),jnp.broadcast_to(e[:,0:1],(64,WIN-193))],axis=1)
    wide=jnp.concatenate([wide,wide],axis=0)
    ends=jnp.concatenate([e[:,0:1],e[:,0:1],e[:,72:73],e[:,72:73],jnp.zeros((64,124),e.dtype)],axis=1)
    ends=jnp.concatenate([ends,ends],axis=0)
    return wide,ends

def attend(mine,other,length,wide,ends):
    pairs,_,own,_=mine.shape; n=2*own
    dma=pltpu.SemaphoreType.DMA
    whole=lambda *shape: pl.BlockSpec(shape,lambda a,b:(0,)*len(shape))
    anywhere=pl.BlockSpec(memory_space=pl.ANY)
    return pl.pallas_call(fwd_kernel,
        grid=(pairs,STEPS),
        in_specs=[pl.BlockSpec(memory_space=pltpu.SMEM),whole(128,WIN),whole(128,128),anywhere,anywhere],
        out_specs=[pl.BlockSpec((2,RB,n),lambda a,b:(a,b,0)),pl.BlockSpec((1,3,n,128),lambda a,b:(a,0,0,0)),whole(own,2*own)],
        out_shape=[jax.ShapeDtypeStruct((2*pairs,n,n),BF),jax.ShapeDtypeStruct((pairs,3,n,128),BF),jax.ShapeDtypeStruct((own,2*own),BF)],
        scratch_shapes=[pltpu.VMEM((2,RB,PADL+n+256),F32),pltpu.VMEM((n,256),BF),pltpu.VMEM((pairs,3,n,128),BF),pltpu.VMEM((own,2*own),BF),pltpu.VMEM((pairs,2,RB,128),BF),
            dma((pairs,)),dma((pairs,)),dma((pairs,)),dma((pairs,2)),dma((pairs,2))],
        compiler_params=pltpu.CompilerParams(vmem_limit_bytes=58<<20,collective_id=1,has_side_effects=True),
        cost_estimate=pl.CostEstimate(flops=40_000_000_000,bytes_accessed=120_000_000,transcendentals=0),
        name="attend_fwd",
    )(length,wide,ends,mine,other)

def attend_back(heads,p,wide,mine,other,part=None):
    pairs,_,n,_=heads.shape; own=n//2
    dma=pltpu.SemaphoreType.DMA
    whole=lambda *shape: pl.BlockSpec(shape,lambda a,b:(0,)*len(shape))
    anywhere=pl.BlockSpec(memory_space=pl.ANY)
    with_part=part is not None
    extra=[pltpu.VMEM(part.shape,BF)]*3+[dma((part.shape[0],))]*2+[dma((part.shape[0],3))]*2 if with_part else []
    return pl.pallas_call(functools.partial(bwd_kernel,with_part),
        grid=(pairs,STEPS),
        in_specs=[pl.BlockSpec((1,3,n,128),lambda a,b:(a,0,0,0)),pl.BlockSpec((2,RB,n),lambda a,b:(a,jnp.where(a==0,lax.rem(b+2,STEPS),b),0)),whole(128,128),anywhere,anywhere]+[anywhere]*with_part,
        out_specs=[whole(own,6*own),whole(128,128)]+[anywhere]*with_part,
        out_shape=[jax.ShapeDtypeStruct((own,6*own),BF),jax.ShapeDtypeStruct((128,128),F32)]+([jax.ShapeDtypeStruct(part.shape,BF)] if with_part else []),
        scratch_shapes=[pltpu.VMEM((2,RB,PADL+n+256),F32),pltpu.VMEM((n,256),BF),pltpu.VMEM((128,n),F32),pltpu.VMEM((128,n),F32),pltpu.VMEM((128,128),F32),
            pltpu.VMEM((pairs,n,128),BF),pltpu.VMEM((own,6*own),BF),pltpu.VMEM((pairs,2,RB,128),BF),pltpu.VMEM((pairs,2,own,128),BF),
            dma((pairs,)),dma((pairs,)),dma((pairs,)),dma((pairs,2)),dma((pairs,2)),dma((pairs,2)),dma((pairs,2))]+extra,
        compiler_params=pltpu.CompilerParams(vmem_limit_bytes=58<<20,collective_id=2,has_side_effects=True),
        cost_estimate=pl.CostEstimate(flops=50_000_000_000,bytes_accessed=150_000_000,transcendentals=0),
        name="attend_bwd",
    )(heads,p,wide[:,0:128],mine,other,*([part] if with_part else []))


EPSILON = 1e-05
HALF = 0.5
CUT = 256
VMEM = 56 << 20


def flat(ref):
    value = ref[...]
    return value.reshape(-1, value.shape[-1])


def cuts(count):
    return [pl.ds(i, CUT) for i in range(0, count, CUT)]


def normal(v):
    c = v - jnp.mean(v, axis=-1, keepdims=True)
    r = lax.rsqrt(jnp.mean(c * c, axis=-1, keepdims=True) + EPSILON)
    return c * r, r


def normal_back(dy, unit, r, gain):
    a = dy * gain
    return (a - jnp.mean(a, axis=-1, keepdims=True) - unit * jnp.mean(a * unit, axis=-1, keepdims=True)) * r


def total(v):
    return jnp.sum(v, axis=0, keepdims=True)


def silu_slope(v):
    s = jax.nn.sigmoid(v)
    return s * (1.0 + v * (1.0 - s))


def call(kernel, grid, ins, outs, scratch=(), name=None, aliases=None, flops=0, moved=0):
    def spec(shape, block, where):
        if block is None:
            return pl.BlockSpec(shape, lambda *_: (0,) * len(shape))
        if block == "smem":
            return pl.BlockSpec(memory_space=pltpu.SMEM)
        if block == "any":
            return pl.BlockSpec(memory_space=pl.ANY)
        return pl.BlockSpec(block, where)

    return pl.pallas_call(
        kernel,
        grid=grid,
        in_specs=[spec(a.shape, b, w) for a, b, w in ins],
        out_specs=[spec(s, b, w) for s, _, b, w in outs],
        out_shape=[jax.ShapeDtypeStruct(s, d) for s, d, _, _ in outs],
        scratch_shapes=list(scratch),
        input_output_aliases=aliases or {},
        compiler_params=pltpu.CompilerParams(vmem_limit_bytes=VMEM),
        cost_estimate=pl.CostEstimate(flops=flops, bytes_accessed=moved, transcendentals=0),
        name=name,
    )(*[a for a, _, _ in ins])


def scr(shape, dtype):
    return pltpu.VMEM(shape, dtype)


def in_kernel(x_ref, vec_ref, bias_ref, w_ref, inner_ref, act_ref, act_t_ref, unit_t_ref, unit):
    @pl.when(pl.program_id(0) == 0)
    def _():
        for rows in cuts(x_ref.shape[0]):
            n, _ = normal(x_ref[rows, :].astype(F32))
            u = (n * vec_ref[0:1, :] + vec_ref[1:2, :]).astype(BF)
            unit[rows, :] = u
            unit_t_ref[:, rows] = u.T

    w = flat(w_ref)
    for rows in cuts(x_ref.shape[0]):
        s = dot(unit[rows, :], w, 1, 0) + bias_ref[0]
        inner_ref[rows, :] = s.astype(BF)
        a = (s * jax.nn.sigmoid(s)).astype(BF)
        act_ref[rows, :] = a
        act_t_ref[:, rows] = a.T


def ffn_in_forward(x, vec, bias, w, unit0):
    t, d = x.shape
    n, _, r, _ = w.shape
    k = bias.shape[0] // d
    bias = bias.reshape(k, 1, d)
    return call(
        in_kernel,
        (k,),
        [
            (x, None, None),
            (vec, None, None),
            (bias, (1, 1, d), lambda j: (j, 0, 0)),
            (w, (n, 1, r, d), lambda j: (0, unit0 + j, 0, 0)),
        ],
        [
            ((t, k * d), BF, (t, d), lambda j: (0, j)),
            ((t, k * d), BF, (t, d), lambda j: (0, j)),
            ((k * d, t), BF, (d, t), lambda j: (j, 0)),
            ((d, t), BF, None, None),
        ],
        [scr((t, d), BF)],
        name="ffn_in",
        flops=2 * t * d * d * k,
        moved=2 * d * d * k + 6 * t * d * k,
    )


def out_qkv_kernel(odd_ref, x_ref, act_ref, w_out_ref, w_qkv_ref, vec_ref, first_ref, unit_t_ref, mine_ref, other_ref, unit, acc):
    s = pl.program_id(0)
    t = x_ref.shape[0]

    @pl.when(s < 4)
    def _():
        w = flat(w_out_ref)
        for rows in cuts(t):
            p = dot(act_ref[rows, :], w, 1, 0)
            acc[rows, :] = p + jnp.where(s == 0, 0.0, acc[rows, :])

    @pl.when(s == 3)
    def _():
        for rows in cuts(t):
            first = x_ref[rows, :].astype(F32) + HALF * (acc[rows, :] + vec_ref[0:1, :])
            first_ref[rows, :] = first
            n, _ = normal(first)
            u = (n * vec_ref[1:2, :] + vec_ref[2:3, :]).astype(BF)
            unit[rows, :] = u
            unit_t_ref[:, rows] = u.T

    @pl.when(s >= 4)
    def _():
        w = flat(w_qkv_ref)
        odd = odd_ref[0] == 1
        half = w.shape[1] // 2
        scale = jnp.where(s == 4, HEAD_DIM**-0.5, 1.0)
        b = jnp.where(s == 4, vec_ref[3:4, :], jnp.where(s == 6, vec_ref[4:5, :], 0.0))
        for rows in cuts(t):
            y = (dot(unit[rows, :], w, 1, 0) + b) * scale
            low, high = y[:, :half], y[:, half:]
            mine = jnp.where(odd, high, low).astype(BF)
            other = jnp.where(odd, low, high).astype(BF)
            for part in range(half // 128):
                cols = slice(part * 128, part * 128 + 128)
                mine_ref[part, 0, rows, :] = mine[:, cols]
                other_ref[part, 0, rows, :] = other[:, cols]


def out_qkv_forward(odd, x, act, w, vec):
    t, d = x.shape
    n, _, r, _ = w.shape
    return call(
        out_qkv_kernel,
        (7,),
        [
            (odd, "smem", None),
            (x, None, None),
            (act, (t, d), lambda s: (0, jnp.minimum(s, 3))),
            (w, (n // 4, 4, r, d), lambda s: (jnp.minimum(s, 3), 0, 0, 0)),
            (w, (n, 1, r, d), lambda s: (0, jnp.maximum(s, 4), 0, 0)),
            (vec, None, None),
        ],
        [
            ((t, d), F32, None, None),
            ((d, t), BF, None, None),
            ((d // 256, 3, t, 128), BF, (d // 256, 1, t, 128), lambda s: (0, jnp.maximum(s - 4, 0), 0, 0)),
            ((d // 256, 3, t, 128), BF, (d // 256, 1, t, 128), lambda s: (0, jnp.maximum(s - 4, 0), 0, 0)),
        ],
        [scr((t, d), BF), scr((t, d), F32)],
        name="out_qkv",
        flops=14 * t * d * d,
        moved=14 * d * d + 20 * t * d,
    )


def mid_kernel(first_ref, mixed_ref, w_attn_ref, w_in_ref, vec_ref, second_ref, mixed_t_ref, unit_t_ref, val_ref, sig_ref, gated_ref, unit, val):
    s = pl.program_id(0)
    t = first_ref.shape[0]

    @pl.when(s == 0)
    def _():
        w = flat(w_attn_ref)
        for rows in cuts(t):
            m = mixed_ref[rows, :]
            mixed_t_ref[:, rows] = m.T
            second = first_ref[rows, :] + dot(m, w, 1, 0) + vec_ref[0:1, :]
            second_ref[rows, :] = second
            n, _ = normal(second)
            u = (n * vec_ref[1:2, :] + vec_ref[2:3, :]).astype(BF)
            unit[rows, :] = u
            unit_t_ref[:, rows] = u.T

    @pl.when(s == 1)
    def _():
        w = flat(w_in_ref)
        for rows in cuts(t):
            v = dot(unit[rows, :], w, 1, 0) + vec_ref[3:4, :]
            val[rows, :] = v
            val_ref[rows, :] = v.astype(BF)

    @pl.when(s == 2)
    def _():
        w = flat(w_in_ref)
        for rows in cuts(t):
            g = jax.nn.sigmoid(dot(unit[rows, :], w, 1, 0) + vec_ref[4:5, :])
            sig_ref[rows, :] = g.astype(BF)
            gated_ref[rows, :] = (val[rows, :] * g).astype(BF)


def mid_forward(first, mixed, w, u_attn, u_in, vec):
    t, d = first.shape
    n, _, r, _ = w.shape
    return call(
        mid_kernel,
        (3,),
        [
            (first, None, None),
            (mixed, None, None),
            (w, (n, 1, r, d), lambda s: (0, u_attn, 0, 0)),
            (w, (n, 1, r, d), lambda s: (0, u_in + jnp.maximum(s - 1, 0), 0, 0)),
            (vec, None, None),
        ],
        [((t, d), F32, None, None), ((d, t), BF, None, None), ((d, t), BF, None, None)]
        + [((t, d), BF, None, None)] * 3,
        [scr((t, d), BF), scr((t, d), F32)],
        name="mid",
        flops=6 * t * d * d,
        moved=6 * d * d + 20 * t * d,
    )


ROWS = 32
COLS = 256
FIR_ROWS = 64
FIR_COLS = 128


def shifted(window, b):
    return window if b == 0 else pltpu.roll(window, window.shape[0] - b, 0)


def fir(pad, taps, offset, count, width, start, write, turned=False):
    reach = taps.shape[0]
    for c in range(0, width, FIR_COLS):
        cols = slice(c, c + FIR_COLS)

        def body(i, _):
            base = pl.multiple_of(i * FIR_ROWS, FIR_ROWS)
            window = pad[pl.ds(base, FIR_ROWS + 32), cols]
            acc = start(cols)
            for b in range(8):
                sh = shifted(window, b)
                for a in range(0, 5):
                    m = 8 * a + b - offset
                    if 0 <= m < reach:
                        tap = reach - 1 - m if turned else m
                        acc = acc + taps[tap : tap + 1, cols] * sh[8 * a : 8 * a + FIR_ROWS]
            write(pl.ds(base, FIR_ROWS), cols, acc)
            return 0

        lax.fori_loop(0, count // FIR_ROWS, body, 0)


def conv_kernel(gated_ref, halo_ref, taps_ref, vec_ref, second_ref, w_ref, conv_ref, act_t_ref, third_ref, pad):
    t, d = gated_ref.shape
    pad[0:32, :] = halo_ref[...].astype(F32)
    for rows in cuts(t):
        pad[pl.ds(rows.start + 32, CUT), :] = gated_ref[rows, :].astype(F32)

    def write(rows, cols, acc):
        conv_ref[rows, cols] = acc

    fir(pad, taps_ref, 2, t, d, lambda cols: jnp.broadcast_to(vec_ref[0:1, cols], (FIR_ROWS, FIR_COLS)), write)
    w = flat(w_ref)
    for rows in cuts(t):
        n, _ = normal(conv_ref[rows, :])
        u = n * vec_ref[1:2, :] + vec_ref[2:3, :]
        a = (u * jax.nn.sigmoid(u)).astype(BF)
        act_t_ref[:, rows] = a.T
        third_ref[rows, :] = second_ref[rows, :] + dot(a, w, 1, 0) + vec_ref[3:4, :]


def conv_forward(gated, halo, taps, vec, second, w, unit0):
    t, d = gated.shape
    n, _, r, _ = w.shape
    return call(
        conv_kernel,
        (1,),
        [
            (gated, None, None),
            (halo, None, None),
            (taps, None, None),
            (vec, None, None),
            (second, None, None),
            (w, (n, 1, r, d), lambda s: (0, unit0, 0, 0)),
        ],
        [((t, d), F32, None, None), ((d, t), BF, None, None), ((t, d), F32, None, None)],
        [scr((t + 32, d), F32)],
        name="conv",
        flops=2 * t * d * d,
        moved=2 * d * d + 16 * t * d,
    )


def out_last_kernel(x_ref, act_ref, w_ref, cot_ref, vec_ref, out_ref, d_ref, dout_ref, sums_ref, acc):
    s = pl.program_id(0)
    t = x_ref.shape[0]
    w = flat(w_ref)
    for rows in cuts(t):
        p = dot(act_ref[rows, :], w, 1, 0)
        acc[rows, :] = p + jnp.where(s == 0, 0.0, acc[rows, :])

    @pl.when(s == 3)
    def _():
        sums_ref[...] = jnp.zeros_like(sums_ref)
        for rows in cuts(t):
            fourth = x_ref[rows, :] + HALF * (acc[rows, :] + vec_ref[0:1, :])
            n, r = normal(fourth)
            out_ref[rows, :] = (n * vec_ref[1:2, :] + vec_ref[2:3, :]).astype(BF)
            dy = cot_ref[rows, :].astype(F32)
            d = normal_back(dy, n, r, vec_ref[1:2, :])
            d_ref[rows, :] = d
            dout_ref[rows, :] = (HALF * d).astype(BF)
            sums_ref[0:1, :] += total(dy * n)
            sums_ref[1:2, :] += total(dy)


def out_last(x, act, w, block0, cot, vec):
    t, d = x.shape
    n, _, r, _ = w.shape
    return call(
        out_last_kernel,
        (4,),
        [
            (x, None, None),
            (act, (t, d), lambda s: (0, s)),
            (w, (n // 4, 4, r, d), lambda s: (s, block0, 0, 0)),
            (cot, None, None),
            (vec, None, None),
        ],
        [((t, d), BF, None, None), ((t, d), F32, None, None), ((t, d), BF, None, None), ((8, d), F32, None, None)],
        [scr((t, d), F32)],
        name="out_last",
        flops=8 * t * d * d,
        moved=8 * d * d + 20 * t * d,
    )


def ffn_hidden_kernel(d_ref, inner_ref, w_ref, dinner_ref, dout_ref, dbias_ref, sums_ref):
    t = d_ref.shape[0]

    @pl.when(pl.program_id(0) == 0)
    def _():
        sums_ref[...] = jnp.zeros_like(sums_ref)
        for rows in cuts(t):
            v = d_ref[rows, :] if d_ref.dtype == BF else (HALF * d_ref[rows, :]).astype(BF)
            dout_ref[rows, :] = v
            sums_ref[0:1, :] += total(v.astype(F32))

    w = flat(w_ref)
    dbias = 0.0
    for rows in cuts(t):
        da = dot(dout_ref[rows, :], w, 1, 1)
        v = (da * silu_slope(inner_ref[rows, :].astype(F32))).astype(BF)
        dinner_ref[rows, :] = v
        dbias = dbias + total(v.astype(F32))
    dbias_ref[0] = dbias


def ffn_hidden_back(dy, inner, w, block0):
    t, d = dy.shape
    n, _, r, _ = w.shape
    k = inner.shape[1] // d
    return call(
        ffn_hidden_kernel,
        (k,),
        [
            (dy, None, None),
            (inner, (t, d), lambda j: (0, j)),
            (w, (n // 4, 4, r, d), lambda j: (j, block0, 0, 0)),
        ],
        [
            ((t, k * d), BF, (t, d), lambda j: (0, j)),
            ((t, d), BF, None, None),
            ((k, 1, d), F32, (1, 1, d), lambda j: (j, 0, 0)),
            ((8, d), F32, None, None),
        ],
        name="ffn_hidden_back",
        flops=2 * t * d * d * k,
        moved=2 * d * d * k + 4 * t * d * k,
    )


def norm_input_kernel(k, dy_ref, g_ref, x_ref, w_ref, vec_ref, d_ref, sums_ref, acc):
    s = pl.program_id(0)
    t = x_ref.shape[0]
    w = flat(w_ref)
    for rows in cuts(t):
        p = dot(g_ref[rows, :], w, 1, 1)
        acc[rows, :] = p + jnp.where(s == 0, 0.0, acc[rows, :])

    @pl.when(s == k - 1)
    def _():
        sums_ref[...] = jnp.zeros_like(sums_ref)
        for rows in cuts(t):
            n, r = normal(x_ref[rows, :].astype(F32))
            du = acc[rows, :]
            d_ref[rows, :] = (dy_ref[rows, :] + normal_back(du, n, r, vec_ref[0:1, :])).astype(d_ref.dtype)
            sums_ref[0:1, :] += total(du * n)
            sums_ref[1:2, :] += total(du)


def norm_input_back(dy, g, x, w, unit0, gain, out_type=F32):
    t, d = dy.shape
    n, _, r, _ = w.shape
    k = g.shape[1] // d
    return call(
        functools.partial(norm_input_kernel, k),
        (k,),
        [
            (dy, None, None),
            (g, (t, d), lambda j: (0, j)),
            (x, None, None),
            (w, (n, 1, r, d), lambda j: (0, unit0 + j, 0, 0)),
            (gain, None, None),
        ],
        [((t, d), out_type, None, None), ((8, d), F32, None, None)],
        [scr((t, d), F32)],
        name="norm_input_back",
        flops=2 * t * d * d * k,
        moved=2 * d * d * k + 2 * t * d * k + 12 * t * d,
    )


def weight_kernel(left_ref, right_ref, *rest):
    out_ref = rest[-1]
    rows, d = left_ref.shape[0], out_ref.shape[-1]
    a, b, r, _ = out_ref.shape
    step = max(256, 4 * r)
    for i in range(0, rows, step):
        value = dot(left_ref[i : i + step, :], right_ref[...], 1, 0).astype(BF)
        if b == 1:
            out_ref[pl.ds(i // r, step // r), 0] = value.reshape(step // r, r, d)
        else:
            out_ref[pl.ds(i // (4 * r), step // (4 * r))] = value.reshape(step // (4 * r), 4, r, d)


def weight_grad(left_t, right, n, units, at, by_rows, into=None):
    d = 1024
    t = left_t.shape[1]
    r = d // n
    if by_rows:
        k = left_t.shape[0] // d
        ins = [(left_t, (d, t), lambda j: (j, 0)), (right, None, None)]
        block, where = (n // 4, 4, r, d), lambda j: (j, at // 4, 0, 0)
    else:
        k = right.shape[1] // d
        ins = [(left_t, None, None), (right, (t, d), lambda j: (0, j))]
        block, where = (n, 1, r, d), lambda j: (0, at + j, 0, 0)
    aliases = None
    if into is not None:
        ins.append((into, "any", None))
        aliases = {2: 0}
    return call(
        weight_kernel,
        (k,),
        ins,
        [((n, units, r, d), BF, block, where)],
        name="weight_grad",
        aliases=aliases,
        flops=2 * t * d * d * k,
        moved=2 * d * d * k + 2 * t * d * (k + 1),
    )[0]


def conv_out_kernel(d_ref, conv_ref, w_ref, vec_ref, dconv_ref, dout_ref, sums_ref):
    t = d_ref.shape[0]
    sums_ref[...] = jnp.zeros_like(sums_ref)
    w = flat(w_ref)
    for rows in cuts(t):
        dout = d_ref[rows, :].astype(BF)
        dout_ref[rows, :] = dout
        da = dot(dout, w, 1, 1)
        n, r = normal(conv_ref[rows, :])
        du = da * silu_slope(n * vec_ref[0:1, :] + vec_ref[1:2, :])
        dconv = normal_back(du, n, r, vec_ref[0:1, :])
        dconv_ref[rows, :] = dconv
        sums_ref[0:1, :] += total(dout.astype(F32))
        sums_ref[1:2, :] += total(du * n)
        sums_ref[2:3, :] += total(du)
        sums_ref[3:4, :] += total(dconv)


def conv_out_back(d3, conv, w, unit0, vec):
    t, d = d3.shape
    n, _, r, _ = w.shape
    return call(
        conv_out_kernel,
        (1,),
        [
            (d3, None, None),
            (conv, None, None),
            (w, (n, 1, r, d), lambda s: (0, unit0, 0, 0)),
            (vec, None, None),
        ],
        [((t, d), F32, None, None), ((t, d), BF, None, None), ((8, d), F32, None, None)],
        name="conv_out_back",
        flops=2 * t * d * d,
        moved=2 * d * d + 16 * t * d,
    )


def mid_back_kernel(odd_ref, dconv_ref, follow_ref, taps_ref, val_ref, sig_ref, second_ref, d3_ref, w_in_ref, w_attn_ref, vec_ref, d2_ref, dout_ref, dglu_ref, mine_ref, other_ref, sums_ref, pad, acc):
    s = pl.program_id(0)
    t, d = dconv_ref.shape

    @pl.when(s == 0)
    def _():
        for rows in cuts(t):
            pad[rows, :] = dconv_ref[rows, :]
        pad[t : t + 32, :] = follow_ref[...]

        def write(rows, cols, dgated):
            sig = sig_ref[rows, cols].astype(F32)
            dval = dgated * sig
            dglu_ref[rows, cols] = dval.astype(BF)
            dgate = dval * val_ref[rows, cols].astype(F32) * (1.0 - sig)
            dglu_ref[rows, cols.start + d : cols.stop + d] = dgate.astype(BF)

        fir(pad, taps_ref, 0, t, d, lambda cols: jnp.zeros((FIR_ROWS, FIR_COLS), F32), write, turned=True)
        sums_ref[...] = jnp.zeros_like(sums_ref)
        for rows in cuts(t):
            sums_ref[0:1, :] += total(dglu_ref[rows, :d].astype(F32))
            sums_ref[1:2, :] += total(dglu_ref[rows, d:].astype(F32))
        w = flat(w_in_ref)
        for rows in cuts(t):
            acc[rows, :] = dot(dglu_ref[rows, :d], w, 1, 1)

    @pl.when(s == 1)
    def _():
        w = flat(w_in_ref)
        w_attn = flat(w_attn_ref)
        odd = odd_ref[0] == 1
        half = d // 2
        for rows in cuts(t):
            du = acc[rows, :] + dot(dglu_ref[rows, d:], w, 1, 1)
            n, r = normal(second_ref[rows, :])
            d2 = d3_ref[rows, :] + normal_back(du, n, r, vec_ref[0:1, :])
            sums_ref[2:3, :] += total(du * n)
            sums_ref[3:4, :] += total(du)
            d2_ref[rows, :] = d2
            dout = d2.astype(BF)
            dout_ref[rows, :] = dout
            sums_ref[4:5, :] += total(dout.astype(F32))
            dm = dot(dout, w_attn, 1, 1)
            low, high = dm[:, :half], dm[:, half:]
            mine = jnp.where(odd, high, low).astype(BF)
            other = jnp.where(odd, low, high).astype(BF)
            for part in range(half // 128):
                cols = slice(part * 128, part * 128 + 128)
                mine_ref[part, rows, :] = mine[:, cols]
                other_ref[part, rows, :] = other[:, cols]


def mid_back(odd, dconv, follow, taps, val, sig, second, d3, w, u_attn, u_in, gain):
    t, d = d3.shape
    n, _, r, _ = w.shape
    return call(
        mid_back_kernel,
        (2,),
        [
            (odd, "smem", None),
            (dconv, None, None),
            (follow, None, None),
            (taps, None, None),
            (val, None, None),
            (sig, None, None),
            (second, None, None),
            (d3, None, None),
            (w, (n, 1, r, d), lambda s: (0, u_in + s, 0, 0)),
            (w, (n, 1, r, d), lambda s: (0, u_attn, 0, 0)),
            (gain, None, None),
        ],
        [
            ((t, d), F32, None, None),
            ((t, d), BF, None, None),
            ((t, 2 * d), BF, None, None),
            ((d // 256, t, 128), BF, None, None),
            ((d // 256, t, 128), BF, None, None),
            ((8, d), F32, None, None),
        ],
        [scr((t + 32, d), F32), scr((t, d), F32)],
        name="mid_back",
        flops=6 * t * d * d,
        moved=6 * d * d + 24 * t * d,
    )


def taps_kernel(dconv_ref, gated_ref, halo_ref, out_ref, pad, part):
    t, d = dconv_ref.shape
    reach = out_ref.shape[0]
    pad[0:32, :] = halo_ref[...].astype(F32)
    for rows in cuts(t):
        pad[pl.ds(rows.start + 32, CUT), :] = gated_ref[rows, :].astype(F32)
    part[...] = jnp.zeros_like(part)
    for c in range(0, d, COLS):
        cols = slice(c, c + COLS)

        def body(i, _):
            base = pl.multiple_of(i * ROWS, ROWS)
            window = pad[pl.ds(base, ROWS + 32), cols]
            here = dconv_ref[pl.ds(base, ROWS), cols]
            for b in range(8):
                sh = shifted(window, b)
                for a in range(0, 5):
                    m = 8 * a + b - 2
                    if 0 <= m < reach:
                        v = here * sh[8 * a : 8 * a + ROWS]
                        v = (v[0:8] + v[8:16]) + (v[16:24] + v[24:32])
                        part[8 * m : 8 * m + 8, cols] += v
            return 0

        lax.fori_loop(0, t // ROWS, body, 0)
    for m in range(reach):
        out_ref[m : m + 1, :] = total(part[8 * m : 8 * m + 8, :])


def taps_grad(dconv, gated, halo, reach):
    t, d = dconv.shape
    return call(
        taps_kernel,
        (1,),
        [(dconv, None, None), (gated, None, None), (halo, None, None)],
        [((reach, d), F32, None, None)],
        [scr((t + 32, d), F32), scr((8 * reach, d), F32)],
        name="taps_grad",
        flops=2 * t * d * reach,
        moved=6 * t * d,
    )[0]


def flipped_bit(index, mask):
    return index + mask - 2 * mask * lax.rem(lax.div(index, jnp.int32(mask)), jnp.int32(2))


def first_kernel(
    x_ref, w_ref, gains_ref, shifts_ref, taps_ref, bias_ref,
    inner_ref, act_ref, act_t_ref, unit_t_ref, tokens_ref, small_out_ref, w_out_ref,
    w, small, small_ref, tokens, unit, vec,
    own_send, own_recv, far_send, far_recv, core_send, core_recv, x_send, x_recv, x_load, w_leave,
):
    j = pl.program_id(0)
    n, k, r, d = w.shape
    t = tokens.shape[0]
    cut, thin_cut = r // 2, small.shape[1] // 2
    me, place = lax.axis_index("fsdp"), lax.axis_index("seq")
    two = jnp.int32(2)
    other_x, other_y, other_c = flipped_bit(me, 2), flipped_bit(me, 4), flipped_bit(me, 1)
    other_xy = flipped_bit(other_x, 4)
    to_x, to_y, to_c = {"fsdp": other_x}, {"fsdp": other_y}, {"fsdp": other_c}

    def send(src, dst, send_sem, recv_sem, device):
        return pltpu.make_async_remote_copy(
            src_ref=src, dst_ref=dst, send_sem=send_sem, recv_sem=recv_sem, device_id=device, device_id_type=MESH
        )

    def held(dev, u, rows=None):
        if u == k:
            return small.at[dev] if rows is None else small.at[dev, rows]
        return w.at[dev, u] if rows is None else w.at[dev, u, rows]

    def own(u):
        return small_ref if u == k else w_ref.at[u]

    def own_copies(u):
        return [
            send(own(u), held(me, u), own_send.at[i, u], own_recv.at[i, u], device)
            for i, device in enumerate((to_x, to_y, to_c))
        ]

    def keep_copy(u):
        return pltpu.make_async_copy(own(u), held(me, u), x_load.at[2 + u])

    def far_copies(u):
        half = thin_cut if u == k else cut
        top, low = pl.ds(0, half), pl.ds(half, half)
        return [
            send(held(other_x, u, top), held(other_x, u, top), far_send.at[0, u], far_recv.at[0, u], to_y),
            send(held(other_y, u, low), held(other_y, u, low), far_send.at[1, u], far_recv.at[1, u], to_x),
        ]

    def core_copy(i, u):
        dev = (other_x, other_y, other_xy)[i]
        return send(held(dev, u), held(dev, u), core_send.at[i, u], core_recv.at[i, u], to_c)

    def gather_begin(u):
        keep_copy(u).start()
        for copy in own_copies(u):
            copy.start()

    def gather_forward(u):
        across = own_copies(u)
        far = far_copies(u)
        across[0].wait_recv()
        far[0].start()
        core_copy(0, u).start()
        across[1].wait_recv()
        far[1].start()
        core_copy(1, u).start()

    def gather_far(u):
        for copy in far_copies(u):
            copy.wait_recv()
        core_copy(2, u).start()

    def gather_end(u):
        keep_copy(u).wait()
        own_copies(u)[2].wait_recv()
        for i in range(3):
            core_copy(i, u).wait_recv()

    def gather_sent(u):
        for copy in own_copies(u) + far_copies(u) + [core_copy(i, u) for i in range(3)]:
            copy.wait_send()

    side, half_of = lax.div(place, two), lax.rem(place, two)

    def token_rows(h):
        return pl.ds(pl.multiple_of(h * (t // 2), t // 2), t // 2)

    def token_copy(s):
        return send(x_ref.at[s], tokens.at[token_rows(half_of)], x_send.at[s], x_recv.at[half_of], {"seq": 2 * s + side})

    def token_keep(s):
        return pltpu.make_async_copy(x_ref.at[s], tokens.at[token_rows(half_of)], x_load.at[s])

    def token_arrived(h):
        return send(x_ref.at[0], tokens.at[token_rows(h)], x_send.at[0], x_recv.at[h], {"seq": flipped_bit(place, 1)})

    @pl.when(j == 0)
    def _():
        small_ref[...] = jnp.zeros_like(small_ref)
        at = 0
        for ref in (gains_ref, shifts_ref, taps_ref):
            small_ref[at : at + ref.shape[0], :] = ref[...]
            at += ref.shape[0]
        for layer in range(2):
            for q in range(4):
                row = at + 4 * layer + q
                small_ref[row : row + 1, :] = bias_ref[layer : layer + 1, q * r : (q + 1) * r]
        barrier = pltpu.get_barrier_semaphore()
        devices = [to_x, to_y, to_c, {"seq": flipped_bit(place, 1)}, {"seq": flipped_bit(place, 2)}, {"seq": 3 - place}]
        for device in devices:
            pl.semaphore_signal(barrier, inc=1, device_id=device, device_id_type=MESH)
        pl.semaphore_wait(barrier, 6)
        gather_begin(k)
        for s in range(2):
            away = 2 * s + side != place
            pl.when(away)(lambda s=s: token_copy(s).start())
            pl.when(jnp.logical_not(away))(lambda s=s: token_keep(s).start())
        for u in range(k):
            gather_begin(u)
        gather_forward(k)
        gather_far(k)
        gather_end(k)
        for dev in range(n):
            cols = slice(dev * r, (dev + 1) * r)
            vec[0:1, cols] = small[dev, 0:1, :].astype(F32)
            vec[1:2, cols] = small[dev, 6:7, :].astype(F32)
            for q in range(4):
                at = 4 * (dev % 2) + q
                vec[2 + dev // 2 : 3 + dev // 2, at * r : (at + 1) * r] = small[dev, 52 + q : 53 + q, :].astype(F32)
        gather_forward(0)
        gather_forward(1)
        for s in range(2):
            away = 2 * s + side != place
            pl.when(away)(lambda s=s: token_copy(s).wait_send())
            pl.when(jnp.logical_not(away))(lambda s=s: token_keep(s).wait())
        for h in range(2):
            pl.when(2 * half_of + h != place)(lambda h=h: token_arrived(h).wait_recv())
        gather_forward(2)
        gather_forward(3)
        for rows in cuts(t):
            c, _ = normal(tokens[rows, :].astype(F32))
            v = (c * vec[0:1, :] + vec[1:2, :]).astype(BF)
            unit[rows, :] = v
            unit_t_ref[:, rows] = v.T
        tokens_ref[...] = tokens[...]
        small_out_ref[...] = small[...]
        for u in range(k):
            gather_far(u)

    def leave(u):
        return pltpu.make_async_copy(w.at[:, u], w_out_ref.at[:, u], w_leave.at[u])

    for u in range(k):

        @pl.when(j == u)
        def _(u=u):
            gather_end(u)
            leave(u).start()

    weights = w[:, j].reshape(d, d)
    for rows in cuts(t):
        s = dot(unit[rows, :], weights, 1, 0) + vec[pl.ds(2 + j, 1), :]
        inner_ref[rows, :] = s.astype(BF)
        a = (s * jax.nn.sigmoid(s)).astype(BF)
        act_ref[rows, :] = a
        act_t_ref[:, rows] = a.T

    @pl.when(j == k - 1)
    def _():
        for u in range(k + 1):
            gather_sent(u)
        for u in range(k):
            leave(u).wait()


def first_forward(x, w, gains, shifts, taps, bias):
    _, half, d = x.shape
    k, r, _ = w.shape
    n, t = 8, 2 * half
    rows = 64
    dma = pltpu.SemaphoreType.DMA
    anywhere = pl.BlockSpec(memory_space=pl.ANY)

    def whole(*shape):
        return pl.BlockSpec(shape, lambda j: (0,) * len(shape))

    return pl.pallas_call(
        first_kernel,
        grid=(k,),
        in_specs=[anywhere] * 2 + [whole(*a.shape) for a in (gains, shifts, taps, bias)],
        out_specs=[
            pl.BlockSpec((t, d), lambda j: (0, j)),
            pl.BlockSpec((t, d), lambda j: (0, j)),
            pl.BlockSpec((d, t), lambda j: (j, 0)),
            whole(d, t),
            whole(t, d),
            whole(n, rows, r),
            anywhere,
        ],
        out_shape=[
            jax.ShapeDtypeStruct((t, k * d), BF),
            jax.ShapeDtypeStruct((t, k * d), BF),
            jax.ShapeDtypeStruct((k * d, t), BF),
            jax.ShapeDtypeStruct((d, t), BF),
            jax.ShapeDtypeStruct((t, d), BF),
            jax.ShapeDtypeStruct((n, rows, r), BF),
            jax.ShapeDtypeStruct((n, k, r, d), BF),
        ],
        scratch_shapes=[
            scr((n, k, r, d), BF),
            scr((n, rows, r), BF),
            scr((rows, r), BF),
            scr((t, d), BF),
            scr((t, d), BF),
            scr((8, d), F32),
            dma((3, k + 1)),
            dma((3, k + 1)),
            dma((2, k + 1)),
            dma((2, k + 1)),
            dma((3, k + 1)),
            dma((3, k + 1)),
            dma((2,)),
            dma((2,)),
            dma((2 + k + 1,)),
            dma((k,)),
        ],
        compiler_params=pltpu.CompilerParams(vmem_limit_bytes=VMEM, collective_id=3, has_side_effects=True),
        cost_estimate=pl.CostEstimate(flops=30_000_000_000, bytes_accessed=100_000_000, transcendentals=0),
        name="first",
    )(x, w, gains, shifts, taps, bias)


def middle_kernel(
    g_ref, w_ref, w_attn_ref, taps_ref, vec_ref, dy_in, third_in, conv_in, val_in, sig_in, second_in, result_ref,
    d2_ref, dout_2_ref, mine_ref, other_ref, sums_4_ref, sums_3_ref, sums_2_ref, dconv_out, dout_3_out, dglu_out, outputs_ref,
    dy_ref, third_ref, conv_ref, val_ref, sig_ref, second_ref, dout_3_ref, dglu_ref,
    acc, d3, pad, load_sem, leave_sem, halo_send, halo_recv, out_send, out_recv, out_keep,
):
    s = pl.program_id(0)
    t, d = third_ref.shape

    def load(i):
        src = (dy_in, third_in, conv_in, val_in, sig_in, second_in)[i]
        dst = (dy_ref, third_ref, conv_ref, val_ref, sig_ref, second_ref)[i]
        return pltpu.make_async_copy(src, dst, load_sem.at[i])

    def leave(i):
        src = (pad.at[pl.ds(0, t)], dout_3_ref, dglu_ref)[i]
        return pltpu.make_async_copy(src, (dconv_out, dout_3_out, dglu_out)[i], leave_sem.at[i])

    place = lax.axis_index("seq")
    two = jnp.int32(2)
    odd, seq = lax.rem(place, two), lax.div(place, two)
    partner = {"seq": flipped_bit(place, 1)}
    half = d // 2

    def halo_copy():
        return pltpu.make_async_remote_copy(
            src_ref=pad.at[pl.ds(0, 32)],
            dst_ref=pad.at[pl.ds(t, 32)],
            send_sem=halo_send,
            recv_sem=halo_recv,
            device_id=partner,
            device_id_type=MESH,
        )

    def out_copy(h, to, s):
        return pltpu.make_async_remote_copy(
            src_ref=result_ref.at[pl.ds(h * (t // 2), t // 2)],
            dst_ref=outputs_ref.at[s],
            send_sem=out_send.at[h],
            recv_sem=out_recv.at[s],
            device_id={"seq": to},
            device_id_type=MESH,
        )

    def out_stay(h):
        return pltpu.make_async_copy(result_ref.at[pl.ds(h * (t // 2), t // 2)], outputs_ref.at[seq], out_keep)

    @pl.when(s == 0)
    def _():
        for i in range(6):
            load(i).start()
        barrier = pltpu.get_barrier_semaphore()
        for device in (partner, {"seq": flipped_bit(place, 2)}, {"seq": 3 - place}):
            pl.semaphore_signal(barrier, inc=1, device_id=device, device_id_type=MESH)
        pl.semaphore_wait(barrier, 3)
        for h in range(2):
            away = 2 * odd + h != place
            pl.when(away)(lambda h=h: out_copy(h, 2 * odd + h, seq).start())
            pl.when(jnp.logical_not(away))(lambda h=h: out_stay(h).start())
        for ref in (sums_4_ref, sums_3_ref, sums_2_ref):
            ref[...] = jnp.zeros_like(ref)

    w = flat(w_ref)

    @pl.when(s < 4)
    def _():
        for rows in cuts(t):
            p = dot(g_ref[rows, :], w, 1, 1)
            acc[rows, :] = p + jnp.where(s == 0, 0.0, acc[rows, :])

    @pl.when(s == 3)
    def _():
        load(0).wait()
        load(1).wait()
        for rows in cuts(t):
            n, r = normal(third_ref[rows, :])
            du = acc[rows, :]
            value = dy_ref[rows, :] + normal_back(du, n, r, vec_ref[0:1, :])
            d3[rows, :] = value
            dout = value.astype(BF)
            dout_3_ref[rows, :] = dout
            sums_4_ref[0:1, :] += total(du * n)
            sums_4_ref[1:2, :] += total(du)
            sums_3_ref[0:1, :] += total(dout.astype(F32))
        leave(1).start()

    @pl.when(s == 4)
    def _():
        load(2).wait()
        for i, rows in enumerate(cuts(t)):
            da = dot(dout_3_ref[rows, :], w, 1, 1)
            n, r = normal(conv_ref[rows, :])
            du = da * silu_slope(n * vec_ref[1:2, :] + vec_ref[2:3, :])
            dconv = normal_back(du, n, r, vec_ref[1:2, :])
            pad[rows, :] = dconv
            sums_3_ref[1:2, :] += total(du * n)
            sums_3_ref[2:3, :] += total(du)
            sums_3_ref[3:4, :] += total(dconv)
            if i == 0:

                @pl.when(odd == 1)
                def _():
                    halo_copy().start()
                    pad[t : t + 32, :] = jnp.zeros((32, d), F32)

        leave(0).start()

    @pl.when(s == 5)
    def _():
        load(3).wait()
        load(4).wait()
        pl.when(odd == 1)(lambda: halo_copy().wait_send())
        pl.when(odd == 0)(lambda: halo_copy().wait_recv())

        def write(rows, cols, dgated):
            sig = sig_ref[rows, cols].astype(F32)
            dval = dgated * sig
            dglu_ref[rows, cols] = dval.astype(BF)
            dgate = dval * val_ref[rows, cols].astype(F32) * (1.0 - sig)
            dglu_ref[rows, cols.start + d : cols.stop + d] = dgate.astype(BF)

        fir(pad, taps_ref, 0, t, d, lambda cols: jnp.zeros((FIR_ROWS, FIR_COLS), F32), write, turned=True)
        for rows in cuts(t):
            sums_2_ref[0:1, :] += total(dglu_ref[rows, :d].astype(F32))
            sums_2_ref[1:2, :] += total(dglu_ref[rows, d:].astype(F32))
            acc[rows, :] = dot(dglu_ref[rows, :d], w, 1, 1)
        leave(2).start()

    @pl.when(s == 6)
    def _():
        load(5).wait()
        w_attn = flat(w_attn_ref)
        for rows in cuts(t):
            du = acc[rows, :] + dot(dglu_ref[rows, d:], w, 1, 1)
            n, r = normal(second_ref[rows, :])
            d2 = d3[rows, :] + normal_back(du, n, r, vec_ref[3:4, :])
            sums_2_ref[2:3, :] += total(du * n)
            sums_2_ref[3:4, :] += total(du)
            d2_ref[rows, :] = d2
            dout = d2.astype(BF)
            dout_2_ref[rows, :] = dout
            sums_2_ref[4:5, :] += total(dout.astype(F32))
            dm = dot(dout, w_attn, 1, 1)
            low, high = dm[:, :half], dm[:, half:]
            mine = jnp.where(odd == 1, high, low).astype(BF)
            other = jnp.where(odd == 1, low, high).astype(BF)
            for part in range(half // 128):
                cols = slice(part * 128, part * 128 + 128)
                mine_ref[part, rows, :] = mine[:, cols]
                other_ref[part, rows, :] = other[:, cols]
        for i in range(3):
            leave(i).wait()
        for h in range(2):
            away = 2 * odd + h != place
            pl.when(away)(lambda h=h: out_copy(h, 2 * odd + h, seq).wait_send())
            pl.when(jnp.logical_not(away))(lambda h=h: out_stay(h).wait())
        for q in range(2):
            pl.when(2 * q + seq != place)(lambda q=q: out_copy(0, flipped_bit(place, 1), q).wait_recv())


def middle_back(dy, g, third, conv, val, sig, second, w, taps, vec, result):
    t, d = dy.shape
    n, _, r, _ = w.shape
    dma = pltpu.SemaphoreType.DMA

    def whole(*shape):
        return pl.BlockSpec(shape, lambda s: (0,) * len(shape))

    anywhere = pl.BlockSpec(memory_space=pl.ANY)
    outs = [
        ((t, d), F32), ((t, d), BF), ((d // 256, t, 128), BF), ((d // 256, t, 128), BF),
        ((8, d), F32), ((8, d), F32), ((8, d), F32),
    ]
    far = [((t, d), F32), ((t, d), BF), ((t, 2 * d), BF), ((2, t // 2, d), BF)]
    d2, dout_2, mine, other, sums_4, sums_3, sums_2, dconv, dout_3, dglu, result = pl.pallas_call(
        middle_kernel,
        grid=(7,),
        in_specs=[
            pl.BlockSpec((t, d), lambda s: (0, jnp.minimum(s, 3))),
            pl.BlockSpec((n, 1, r, d), lambda s: (0, jnp.where(s == 4, 7, s), 0, 0)),
            pl.BlockSpec((n, 1, r, d), lambda s: (0, 4, 0, 0)),
            whole(*taps.shape),
            whole(*vec.shape),
        ]
        + [anywhere] * 7,
        out_specs=[whole(*shape) for shape, _ in outs] + [anywhere] * 4,
        out_shape=[jax.ShapeDtypeStruct(shape, kind) for shape, kind in outs + far],
        scratch_shapes=[
            scr((t, d), F32), scr((t, d), F32), scr((t, d), F32), scr((t, d), BF), scr((t, d), BF), scr((t, d), F32),
            scr((t, d), BF), scr((t, 2 * d), BF),
            scr((t, d), F32), scr((t, d), F32), scr((t + 32, d), F32),
            dma((6,)), dma((3,)), dma, dma, dma((2,)), dma((2,)), dma,
        ],
        compiler_params=pltpu.CompilerParams(vmem_limit_bytes=58 << 20, collective_id=4, has_side_effects=True),
        cost_estimate=pl.CostEstimate(flops=40_000_000_000, bytes_accessed=120_000_000, transcendentals=0),
        name="middle_back",
    )(g, w, w, taps, vec, dy, third, conv, val, sig, second, result)
    return dconv, dout_3, d2, dout_2, dglu, mine, other, sums_4, sums_3, sums_2, result


ORDER = [
    ("q", 0), ("q", 1), ("q", 2), ("m", 0), ("m", 1), ("in", 0), ("m", 2), ("in", 1), ("m", 3),
    ("in", 2), ("out", 0), ("in", 3), ("out", 1), ("out", 2), ("out", 3),
]
N_CHUNK = len(ORDER)
FIRST_IN = 5
LAST_IN = 11
AHEAD = 2
HELD = 6


def thin(count):
    return [pl.ds(i, 128) for i in range(0, count, 128)]


def last_kernel(
    gain_ref, table_ref, sums_2_ref, sums_3_ref, sums_4_ref, sums_5_ref, sums_7_ref, dbias_ref,
    d2_ref, first_ref, x_ref, dconv_ref, gated_ref, halo_ref, part_ref, dqkv_ref, unit_q_ref, act_ref, unit_ref, inner_ref, w_out_ref, w_in_ref,
    mixed_ref, dout_2_ref, unit_2_ref, dglu_ref, act_c_ref, dout_3_ref,
    out_ref, out_part_ref, small_out_ref, table_out_ref, dx_ref,
    odd, even, core, first, second, whole, near, far,
    left, right, wo, wi, inner, dout, acc,
    small_0, small_y, small_x, small_c, small_z, table_got, d0, d1, some, dconv, gated, pad, taps,
    left_sem, right_sem, wo_sem, wi_sem, inner_sem, out_sem, part_sem, d1_sem, some_sem, taps_sem,
    core_send, core_recv, first_send, first_recv, second_send, second_recv,
    z_send, z_recv, small_send, small_recv, table_send, table_recv, dx_send, dx_recv, dx_sem, free_sem,
):
    r, d = out_ref.shape[1:]
    n_part = part_ref.shape[0]
    t = x_ref.shape[0]
    cut = r // 2
    me = lax.axis_index("fsdp")
    place = lax.axis_index("seq")
    two, four = jnp.int32(2), jnp.int32(4)
    chip = lax.div(me, two)
    bit_c, bit_x, bit_y = lax.rem(me, two), lax.rem(chip, two), lax.div(me, four)
    middle = lax.rem(lax.div(place + 1, two), two)
    to_c = {"fsdp": flipped_bit(me, 1)}
    to_x = {"fsdp": flipped_bit(me, 2)}
    to_y = {"fsdp": flipped_bit(me, 4)}
    to_1 = {"seq": flipped_bit(place, 1)}
    to_2 = {"seq": 3 - place}

    barrier = pltpu.get_barrier_semaphore()
    for device in (to_c, to_x, to_y, to_1, to_2, {"seq": flipped_bit(place, 2)}):
        pl.semaphore_signal(barrier, inc=1, device_id=device, device_id_type=MESH)

    def send(src, dst, send_sem, recv_sem, device):
        return pltpu.make_async_remote_copy(
            src_ref=src, dst_ref=dst, send_sem=send_sem, recv_sem=recv_sem, device_id=device, device_id_type=MESH
        )

    def at_2(c):
        return lax.rem(c, two)

    def at_3(c):
        return lax.rem(c, jnp.int32(3))

    def on(c, begin, end, work):
        pl.when((c >= begin) & (c < end))(lambda: work(c))

    def factor_copies(c, name, unit):
        cols = slice(unit * d, unit * d + d)
        lefts = {"q": unit_q_ref, "in": unit_ref, "m": (mixed_ref, unit_2_ref, unit_2_ref, act_c_ref)[unit % 4]}
        rights = {
            "q": lambda: dqkv_ref.at[:, cols],
            "m": lambda: (
                dout_2_ref if unit == 0 else dout_3_ref if unit == 3 else dglu_ref.at[:, (unit - 1) * d : unit * d]
            ),
        }
        src = act_ref.at[:, unit] if name == "out" else lefts[name]
        copies = [pltpu.make_async_copy(src, left.at[at_2(c)], left_sem.at[at_2(c)])]
        if name in rights:
            copies.append(pltpu.make_async_copy(rights[name](), right.at[at_3(c)], right_sem.at[at_3(c)]))
        return copies

    def fetch(c):
        for i, (name, unit) in enumerate(ORDER):

            @pl.when(c == i)
            def _(i=i, name=name, unit=unit):
                for copy in factor_copies(c, name, unit):
                    copy.start()

    def fetched(c):
        pltpu.make_async_copy(unit_ref, left.at[at_2(c)], left_sem.at[at_2(c)]).wait()
        has_right = functools.reduce(
            jnp.logical_or, [c == i for i, (name, _) in enumerate(ORDER) if name in ("q", "m")]
        )

        @pl.when(has_right)
        def _():
            pltpu.make_async_copy(dout_2_ref, right.at[at_3(c)], right_sem.at[at_3(c)]).wait()

    def is_in(c):
        return (c >= FIRST_IN) & (c <= LAST_IN) & (at_2(c) == FIRST_IN % 2)

    def wo_copy(j):
        return pltpu.make_async_copy(w_out_ref.at[pl.ds(2 * j, 2), pl.ds(0, 4)], wo, wo_sem)

    def wi_copy(j):
        return pltpu.make_async_copy(w_in_ref.at[:, j], wi, wi_sem)

    def wq_copy(i):
        return pltpu.make_async_copy(w_out_ref.at[:, 4 + i], wi, wi_sem)

    def inner_copy(j):
        return pltpu.make_async_copy(inner_ref.at[:, pl.ds(pl.multiple_of(j * d, d), d)], inner, inner_sem)

    def x_copy():
        return pltpu.make_async_copy(x_ref, inner, inner_sem)

    row = 53

    def hidden(c):
        j = lax.div(c - FIRST_IN, two)
        wo_copy(j).wait()
        inner_copy(j).wait()
        w = wo[...].reshape(d, d)
        dbias = jnp.zeros((1, d), F32)
        for rows in thin(t):
            da = dot(dout[rows, :], w, 1, 1)
            v = (da * silu_slope(inner[rows, :].astype(F32))).astype(BF)
            right[at_3(c), rows, :] = v
            dbias = dbias + total(v.astype(F32))
        for dev in range(2):
            for q in range(4):
                cols = pl.ds(pl.multiple_of((2 * j + dev) * r, r), r)
                small_0[row + 3 + q : row + 4 + q, cols] = dbias[:, dev * 4 * r + q * r : dev * 4 * r + (q + 1) * r]

        @pl.when(j < 3)
        def _():
            wo_copy(j + 1).start()
            inner_copy(j + 1).start()

        @pl.when(j == 3)
        def _():
            x_copy().start()

    def product(c):
        for i in range(4):
            value = dot(left[at_2(c), 2 * i : 2 * i + 2].reshape(2 * r, t), right[at_3(c)], 1, 0).astype(BF)
            low, high = value[:r], value[r:]
            p = i + bit_x - 2 * bit_x * (i % 2)
            p = p + 2 * bit_y - 4 * bit_y * lax.div(p, two)
            even[at_2(c), p] = jnp.where(bit_c == 0, low, high)
            odd[at_2(c), p] = jnp.where(bit_c == 0, high, low)

    def through(c, fresh):
        wi_copy(0).wait()
        w = wi[...].reshape(d, d)
        for rows in thin(t):
            p = dot(right[at_3(c), rows, :], w, 1, 1)
            acc[rows, :] = p + jnp.where(fresh, 0.0, acc[rows, :])

    def back(c):
        j = lax.div(c - FIRST_IN, two)
        through(c, j == 0)
        pl.when(j < 3)(lambda: wi_copy(j + 1).start())

    def back_q(c):
        through(c, c == 0)
        pl.when(c < 2)(lambda: wq_copy(c + 1).start())
        pl.when(c == 2)(lambda: wi_copy(0).start())
        column = total(right[at_3(c)].astype(F32))

        @pl.when(c == 0)
        def _():
            small_0[11:12, :] = column

        @pl.when(c == 2)
        def _():
            small_0[12:13, :] = column
            middle_gradient()

    def middle_gradient():
        pltpu.make_async_copy(d2_ref, d1, d1_sem).wait()
        copies = [
            pltpu.make_async_copy(first_ref.at[rows], some.at[i % 2], some_sem.at[i % 2]) for i, rows in enumerate(thin(t))
        ]
        for i, rows in enumerate(thin(t)):
            copies[i].wait()
            n, scale = normal(some[i % 2])
            du = acc[rows, :]
            value = d1[rows, :] + normal_back(du, n, scale, gain_ref[1:2, :])
            d1[rows, :] = value
            small_0[0:1, :] += total(du * n)
            small_0[5:6, :] += total(du)
            v = (HALF * value).astype(BF)
            dout[rows, :] = v
            small_0[row + 2 : row + 3, :] += total(v.astype(F32))
            if i + 2 < len(copies):
                copies[i + 2].start()

    def first_rows(i):
        return pltpu.make_async_copy(first_ref.at[pl.ds(128 * i, 128)], some.at[i], some_sem.at[i])

    def taps_copies(b):
        cols = pl.ds(pl.multiple_of(b * COLS, COLS), COLS)
        return [
            pltpu.make_async_copy(dconv_ref.at[:, cols], dconv, taps_sem.at[0]),
            pltpu.make_async_copy(halo_ref.at[:, cols], gated.at[pl.ds(0, 32)], taps_sem.at[1]),
            pltpu.make_async_copy(gated_ref.at[:, cols], gated.at[pl.ds(32, t)], taps_sem.at[2]),
        ]

    def taps_columns(b):
        for copy in taps_copies(b):
            copy.wait()
        pad[...] = gated[...].astype(F32)
        taps[...] = jnp.zeros_like(taps)
        reach = taps.shape[0] // 8

        def body(i, _):
            base = pl.multiple_of(i * ROWS, ROWS)
            window = pad[pl.ds(base, ROWS + 32), :]
            here = dconv[pl.ds(base, ROWS), :]
            for q in range(8):
                sh = shifted(window, q)
                for a in range(0, 5):
                    m = 8 * a + q - 2
                    if 0 <= m < reach:
                        v = here * sh[8 * a : 8 * a + ROWS]
                        taps[8 * m : 8 * m + 8, :] += (v[0:8] + v[8:16]) + (v[16:24] + v[24:32])
            return 0

        lax.fori_loop(0, t // ROWS, body, 0)
        cols = pl.ds(pl.multiple_of(b * COLS, COLS), COLS)
        for m in range(reach):
            small_0[18 + m : 19 + m, cols] = total(taps[8 * m : 8 * m + 8, :])

        @pl.when(b < d // COLS - 1)
        def _():
            for copy in taps_copies(b + 1):
                copy.start()

    def held_at(c):
        return lax.rem(c, jnp.int32(HELD))

    def core_copy(c):
        return send(odd.at[at_2(c)], core.at[held_at(c)], core_send.at[c], core_recv.at[c], to_c)

    def make(c):
        fetch(c + 1)
        fetched(c)

        is_out = functools.reduce(jnp.logical_or, [c == i for i, (name, _) in enumerate(ORDER) if name == "out"])

        @pl.when(is_out)
        def _():
            right[at_3(c)] = dout[...]

        pl.when(is_in(c))(lambda: hidden(c))
        product(c)
        pl.when(c >= HELD)(lambda: pl.semaphore_wait(free_sem, 1))
        core_copy(c).start()

    def make_back(c):
        pl.when(is_in(c))(lambda: back(c))
        pl.when(c < 3)(lambda: back_q(c))

    def first_copies(c):
        top, rest = pl.ds(0, cut), pl.ds(cut, cut)
        o = held_at(c)
        return [
            send(core.at[o, 1, top], first.at[o, 0, 0], first_send.at[c, 0], first_recv.at[c, 0], to_x),
            send(core.at[o, 3, top], first.at[o, 0, 1], first_send.at[c, 1], first_recv.at[c, 1], to_x),
            send(core.at[o, 2, rest], first.at[o, 1, 0], first_send.at[c, 2], first_recv.at[c, 2], to_y),
            send(core.at[o, 3, rest], first.at[o, 1, 1], first_send.at[c, 3], first_recv.at[c, 3], to_y),
        ]

    def second_copies(c):
        o = held_at(c)
        return [
            send(first.at[o, 0, 1], second.at[o, 0], second_send.at[c, 0], second_recv.at[c, 0], to_y),
            send(first.at[o, 1, 1], second.at[o, 1], second_send.at[c, 1], second_recv.at[c, 1], to_x),
        ]

    def add_core(c):
        core_copy(c).wait()
        o = held_at(c)

        def rows(i, _):
            at = pl.ds(pl.multiple_of(i * 32, 32), 32)
            for b in range(4):
                core[o, b, at] = (core[o, b, at].astype(F32) + even[at_2(c), b, at].astype(F32)).astype(BF)
            return 0

        lax.fori_loop(0, r // 32, rows, 0)
        for copy in first_copies(c):
            copy.start()

    def add_first(c):
        for copy in first_copies(c):
            copy.wait()
        o = held_at(c)

        def rows(i, _):
            at = pl.ds(pl.multiple_of(i * 32, 32), 32)
            low_at = pl.ds(pl.multiple_of(cut + i * 32, 32), 32)
            for b in range(2):
                first[o, 0, b, at] = (first[o, 0, b, at].astype(F32) + core[o, 2 * b, at].astype(F32)).astype(BF)
                first[o, 1, b, at] = (first[o, 1, b, at].astype(F32) + core[o, b, low_at].astype(F32)).astype(BF)
            return 0

        lax.fori_loop(0, cut // 32, rows, 0)

        @pl.when(c < N_CHUNK - HELD)
        def _():
            pl.semaphore_signal(free_sem, inc=1, device_id=to_c, device_id_type=MESH)

        for copy in second_copies(c):
            copy.start()

    def add_second(c):
        for copy in second_copies(c):
            copy.wait()
        o = held_at(c)
        whole[c, 0:cut] = (first[o, 0, 0].astype(F32) + second[o, 0].astype(F32)).astype(BF)
        whole[c, cut:r] = (first[o, 1, 0].astype(F32) + second[o, 1].astype(F32)).astype(BF)
        z_begin(c)

    z_begin, z_step = z_line(middle, to_1, to_2, whole, near, far, z_send, z_recv)

    def result_do(i, act):
        for is_middle, src in ((1, far), (0, near)):
            chunk = pltpu.make_async_copy(src.at[i], out_ref.at[i], out_sem.at[i])
            part = pltpu.make_async_copy(src.at[i], out_part_ref.at[i - N_CHUNK], out_sem.at[i])
            pl.when((middle == is_middle) & (i < N_CHUNK))(lambda chunk=chunk: act(chunk))
            pl.when((middle == is_middle) & (i >= N_CHUNK))(lambda part=part: act(part))

    def z_stage(i, stage):
        z_step(i, stage)
        if stage == 2:
            result_do(i, lambda copy: copy.start())

    wide = [d // 2, d // 4, d // 8]
    bits = [bit_y, bit_x, bit_c]
    held = [small_0, small_y, small_x, small_c]
    partner = [to_y, to_x, to_c, to_1, to_2]

    def columns(step, bit):
        return pl.ds(pl.multiple_of(bit * wide[step], wide[step]), wide[step])

    def small_copy(step):
        sems = (small_send.at[step], small_recv.at[step])
        if step < 3:
            return send(held[step].at[:, columns(step, 1 - bits[step])], held[step + 1], *sems, partner[step])
        if step == 3:
            return send(small_c, small_z.at[0], *sems, partner[step])
        return send(small_z.at[0], small_z.at[1], *sems, partner[step])

    def small_step(step):
        small_copy(step).wait()
        if step < 3:
            held[step + 1][...] += held[step][:, columns(step, bits[step])]
        elif step == 3:
            small_z[0] = small_z[0] + small_c[...]
        else:
            small_out_ref[...] = small_z[0] + small_z[1]
        if step < 4:
            small_copy(step + 1).start()

    def table_copy(step):
        src = table_ref if step == 0 else table_got.at[step - 1]
        return send(src, table_got.at[step], table_send.at[step], table_recv.at[step], partner[step])

    def table_step(step):
        table_copy(step).wait()
        before = table_ref[...] if step == 0 else table_got[step - 1]
        table_got[step] = table_got[step] + before
        if step < 4:
            table_copy(step + 1).start()
        else:
            table_out_ref[...] = table_got[step]

    mine, seq = lax.rem(place, two), lax.div(place, two)

    def dx_copy(h):
        return send(d0.at[pl.ds(h * (t // 2), t // 2)], dx_ref.at[seq], dx_send.at[h], dx_recv.at[seq], {"seq": 2 * mine + h})

    def dx_keep(h):
        return pltpu.make_async_copy(d0.at[pl.ds(h * (t // 2), t // 2)], dx_ref.at[seq], dx_sem)

    def dx_arrived(s):
        return send(d0.at[pl.ds(0, t // 2)], dx_ref.at[s], dx_send.at[0], dx_recv.at[s], to_1)

    def input_gradient():
        x_copy().wait()
        for rows in thin(t):
            n, scale = normal(inner[rows, :].astype(F32))
            du = acc[rows, :]
            d0[rows, :] = (d1[rows, :] + normal_back(du, n, scale, gain_ref[0:1, :])).astype(BF)
            small_0[row : row + 1, :] += total(du * n)
            small_0[row + 1 : row + 2, :] += total(du)
        for h in range(2):
            away = 2 * mine + h != place
            pl.when(away)(lambda h=h: dx_copy(h).start())
            pl.when(jnp.logical_not(away))(lambda h=h: dx_keep(h).start())
        small_copy(0).start()

    def part_copy(i):
        return pltpu.make_async_copy(part_ref.at[i], whole.at[N_CHUNK + i], part_sem.at[i])

    def part_begin(i):
        part_copy(i).wait()
        z_begin(N_CHUNK + i)

    fetch(jnp.int32(0))
    wq_copy(0).start()
    pltpu.make_async_copy(d2_ref, d1, d1_sem).start()
    for i in range(2):
        first_rows(i).start()
    for copy in taps_copies(jnp.int32(0)):
        copy.start()
    for i in range(n_part):
        part_copy(i).start()
    wo_copy(0).start()
    inner_copy(0).start()
    small_0[...] = jnp.zeros_like(small_0)
    here = {1: (sums_2_ref, 2), 2: (sums_3_ref, 1), 3: (sums_4_ref, 0), 4: (sums_5_ref, 0), 6: (sums_2_ref, 3)}
    here.update({7: (sums_3_ref, 2), 8: (sums_4_ref, 1), 9: (sums_5_ref, 1), 10: (sums_7_ref, 0), 13: (sums_2_ref, 4)})
    here.update({14: (sums_2_ref, 0), 15: (sums_2_ref, 1), 16: (sums_3_ref, 3), 17: (sums_3_ref, 0)})
    for at, (ref, i) in here.items():
        small_0[at : at + 1, :] = ref[i : i + 1, :]
    for j in range(4):
        for dev in range(2):
            for q in range(4):
                cols = slice((2 * j + dev) * r, (2 * j + dev + 1) * r)
                small_0[49 + q : 50 + q, cols] = dbias_ref[j, :, (4 * dev + q) * r : (4 * dev + q + 1) * r]
    pl.semaphore_wait(barrier, 6)
    table_copy(0).start()
    for c in range(AHEAD):
        make(jnp.int32(c))

    def slot(k, _):
        on(k, 0, N_CHUNK, add_core)
        on(k - 1, 0, N_CHUNK, add_first)
        on(k - 2, 0, N_CHUNK, add_second)
        for stage in range(3):
            on(k - 3 - stage, 0, N_CHUNK, lambda c, stage=stage: z_stage(c, stage))
        for h in range(2):
            on(2 * k + h, 0, n_part, part_begin)
            for stage in range(3):
                on(2 * (k - 1 - stage) + h, 0, n_part, lambda i, stage=stage: z_stage(N_CHUNK + i, stage))
        make_back(k)
        on(k + AHEAD, 0, N_CHUNK, make)
        pl.when(k == LAST_IN)(input_gradient)
        for b in range(d // COLS):
            pl.when(k == 4 + 2 * b)(lambda b=b: taps_columns(jnp.int32(b)))
        for step in range(5):
            pl.when(k == step)(lambda step=step: table_step(step))
            pl.when(k == LAST_IN + 1 + step)(lambda step=step: small_step(step))
        return 0

    lax.fori_loop(0, N_CHUNK + 5, slot, 0)
    for h in range(2):
        away = 2 * mine + h != place
        pl.when(away)(lambda h=h: dx_copy(h).wait_send())
        pl.when(jnp.logical_not(away))(lambda h=h: dx_keep(h).wait())
    for s in range(2):
        from_away = 2 * s + lax.div(place, two) != place
        pl.when(from_away)(lambda s=s: dx_arrived(s).wait_recv())

    def settle(i, _):
        result_do(i, lambda copy: copy.wait())
        return 0

    lax.fori_loop(0, N_CHUNK + n_part, settle, 0)


def last_reduced(
    gain, table, sums, dbias, d2, first, tokens, dconv, gated, halo, part, dqkv, unit_q, act_t, unit_t, inner, w_out, w_in, mixed_t, dout_2, unit_2, dglu, act_c, dout_3
):
    n, _, r, d = w_in.shape
    t = tokens.shape[0]
    rows = 64
    k = N_CHUNK
    m = part.shape[0]
    z = k + m
    dma = pltpu.SemaphoreType.DMA
    anywhere = pl.BlockSpec(memory_space=pl.ANY)
    vmem = pl.BlockSpec(memory_space=pltpu.VMEM)
    return pl.pallas_call(
        last_kernel,
        in_specs=[vmem] * 8 + [anywhere] * 20,
        out_specs=[anywhere, anywhere, vmem, vmem, anywhere],
        out_shape=[
            jax.ShapeDtypeStruct((k, r, d), BF),
            jax.ShapeDtypeStruct((m, r, d), BF),
            jax.ShapeDtypeStruct((rows, d // 8), F32),
            jax.ShapeDtypeStruct(table.shape, F32),
            jax.ShapeDtypeStruct((2, t // 2, d), BF),
        ],
        scratch_shapes=[
            scr((2, 4, r, d), BF),
            scr((2, 4, r, d), BF),
            scr((HELD, 4, r, d), BF),
            scr((HELD, 2, 2, r // 2, d), BF),
            scr((HELD, 2, r // 2, d), BF),
            scr((z, r, d), BF),
            scr((z, r, d), BF),
            scr((z, r, d), BF),
            scr((2, n, r, t), BF),
            scr((3, t, d), BF),
            scr((2, 4, r, d), BF),
            scr((n, r, d), BF),
            scr((t, d), BF),
            scr((t, d), BF),
            scr((t, d), F32),
            scr((rows, d), F32),
            scr((rows, d // 2), F32),
            scr((rows, d // 4), F32),
            scr((rows, d // 8), F32),
            scr((2, rows, d // 8), F32),
            scr((5,) + table.shape, F32),
            scr((t, d), BF),
            scr((t, d), F32),
            scr((2, 128, d), F32),
            scr((t, COLS), F32),
            scr((t + 32, COLS), BF),
            scr((t + 32, COLS), F32),
            scr((8 * 31, COLS), F32),
            dma((2,)),
            dma((3,)),
            dma,
            dma,
            dma,
            dma((z,)),
            dma((m,)),
            dma,
            dma((2,)),
            dma((3,)),
            dma((k,)),
            dma((k,)),
            dma((k, 4)),
            dma((k, 4)),
            dma((k, 2)),
            dma((k, 2)),
            dma((z, 3)),
            dma((z, 3)),
            dma((5,)),
            dma((5,)),
            dma((5,)),
            dma((5,)),
            dma((2,)),
            dma((2,)),
            dma,
            pltpu.SemaphoreType.REGULAR,
        ],
        compiler_params=pltpu.CompilerParams(vmem_limit_bytes=60 << 20, collective_id=0, has_side_effects=True),
        cost_estimate=pl.CostEstimate(flops=100_000_000_000, bytes_accessed=400_000_000, transcendentals=0),
        name="last",
    )(
        gain, table, *sums, dbias, d2, first, tokens, dconv, gated, halo, part, dqkv, unit_q.reshape(n, r, t), act_t.reshape(n, 4, r, t),
        unit_t.reshape(n, r, t), inner, w_out, w_in,
        mixed_t.reshape(n, r, t), dout_2, unit_2.reshape(n, r, t), dglu, act_c.reshape(n, r, t), dout_3,
    )


PLACE = {item: i for i, item in enumerate(ORDER)}


def finish_kernel(n_tap, main, in_b, out_b, small, table, result, dx, g_in, g_out, g_qkv, g_attn, g_conv_in, g_conv_out, g_taps, g_gain, g_shift, g_bias, g_table, g_result, g_dx):
    g_result[...] = result[...]
    g_dx[...] = dx[...]
    d = main.shape[-1]

    def of(name, unit):
        return main[PLACE[name, unit]].astype(F32)

    for u in range(4):
        cols = slice(u * d, (u + 1) * d)
        g_in[0, :, cols] = of("in", u)
        g_in[1, :, cols] = in_b[u].astype(F32)
        g_out[0, u] = of("out", u)
        g_out[1, u] = out_b[u].astype(F32)
    for u in range(3):
        g_qkv[u] = of("q", u)
    g_attn[...] = of("m", 0)
    g_conv_in[:, :d] = of("m", 1)
    g_conv_in[:, d:] = of("m", 2)
    g_conv_out[...] = of("m", 3)
    w = g_taps.shape[1]
    early, late = 0, 22 + n_tap
    g_taps[...] = small[18 : 18 + n_tap, :]
    g_gain[0:1, :] = small[late : late + 1, :]
    g_gain[1:6, :] = small[0:5, :]
    g_shift[0:1, :] = small[late + 1 : late + 2, :]
    g_shift[1:6, :] = small[5:10, :]
    g_shift[6:7, :] = small[late + 2 : late + 3, :]
    g_shift[7:15, :] = small[10:18, :]
    for u in range(4):
        g_bias[0:1, u * w : (u + 1) * w] = small[late + 3 + u : late + 4 + u, :]
        g_bias[1:2, u * w : (u + 1) * w] = small[18 + n_tap + u : 19 + n_tap + u, :]
    k, h = g_table.shape
    g_table[...] = table[0:k, 0:h] + table[0:k, h : 2 * h]


def finished(main, in_b, out_b, small, table, result, dx, n_tap, table_shape):
    k, r, d = main.shape
    w = small.shape[1]
    step = min(r, 32)

    def rows(count):
        return pl.BlockSpec((count, step, d), lambda i: (0, i, 0))

    def whole(*shape):
        return pl.BlockSpec(shape, lambda i: (0,) * len(shape))

    outs = [
        ((2, r, 4 * d), pl.BlockSpec((2, step, 4 * d), lambda i: (0, i, 0))),
        ((2, 4, r, d), pl.BlockSpec((2, 4, step, d), lambda i: (0, 0, i, 0))),
        ((3, r, d), rows(3)),
        ((r, d), pl.BlockSpec((step, d), lambda i: (i, 0))),
        ((r, 2 * d), pl.BlockSpec((step, 2 * d), lambda i: (i, 0))),
        ((r, d), pl.BlockSpec((step, d), lambda i: (i, 0))),
        ((n_tap, w), whole(n_tap, w)),
        ((6, w), whole(6, w)),
        ((15, w), whole(15, w)),
        ((2, 4 * w), whole(2, 4 * w)),
        (table_shape, whole(*table_shape)),
    ]
    count = result.shape[1] // (r // step)
    tokens = pl.BlockSpec((result.shape[0], count, d), lambda i: (0, i, 0))
    return pl.pallas_call(
        functools.partial(finish_kernel, n_tap),
        grid=(r // step,),
        in_specs=[rows(k), rows(4), rows(4), whole(*small.shape), whole(*table.shape), tokens, tokens],
        out_specs=[b for _, b in outs] + [tokens, tokens],
        out_shape=[jax.ShapeDtypeStruct(s, F32) for s, _ in outs] + [jax.ShapeDtypeStruct(result.shape, BF)] * 2,
        compiler_params=pltpu.CompilerParams(vmem_limit_bytes=VMEM),
        cost_estimate=pl.CostEstimate(flops=0, bytes_accessed=18_000_000, transcendentals=0),
        name="finish",
    )(main, in_b, out_b, small, table, result, dx)


def xor_route(axis, mask):
    return [(i, i ^ mask) for i in range(lax.axis_size(axis))]


def swapped(block, axis, mask):
    return lax.ppermute(block, axis, xor_route(axis, mask))


def after(value, *marks):
    return lax.optimization_barrier((value,) + marks)[0]


def over_seq(part):
    if lax.axis_size("seq") != 4 or part.shape[1] < 64:
        return lax.psum(part, "seq")
    place = lax.axis_index("seq")
    part = part.astype(F32)
    for mask in (1, 2):
        high = (place & mask) != 0
        half = part.shape[1] // 2
        first, second = part[:, :half], part[:, half:]
        sent = jnp.where(high, first, second).astype(BF)
        part = jnp.where(high, second, first) + swapped(sent, "seq", mask).astype(F32)
    part = part.astype(BF)
    for mask in (2, 1):
        high = (place & mask) != 0
        got = swapped(part, "seq", mask)
        part = jnp.where(high, jnp.concatenate([got, part], axis=1), jnp.concatenate([part, got], axis=1))
    return part


def reduced(g):
    return over_seq(lax.psum_scatter(g, "fsdp", scatter_dimension=0, tiled=False))


def small_reduced(rows):
    k, d = rows.shape
    n = lax.axis_size("fsdp")
    me = lax.axis_index("fsdp")
    rows = lax.psum(rows, ("seq", "fsdp"))
    return lax.dynamic_slice_in_dim(rows, me * (d // n), d // n, 1)


def to_pairs(array, place):
    one, two = array[0], array[1]
    got = lax.ppermute(jnp.where(place % 2 == 0, two, one), "seq", [(0, 2), (1, 0), (2, 3), (3, 1)])
    more = lax.ppermute(jnp.where(place == 1, two, one), "seq", [(1, 2), (2, 1)])
    first = jnp.where(place == 0, one, jnp.where(place == 1, more, got))
    second = jnp.where(place < 2, got, jnp.where(place == 2, more, two))
    return jnp.concatenate([first, second], axis=0)


def from_pairs(array, place):
    half = array.shape[0] // 2
    first, second = array[:half], array[half:]
    got = lax.ppermute(jnp.where(place < 2, second, first), "seq", [(2, 0), (0, 1), (3, 2), (1, 3)])
    more = lax.ppermute(jnp.where(place == 1, first, second), "seq", [(1, 2), (2, 1)])
    one = jnp.where(place == 0, first, jnp.where(place == 2, more, got))
    two = jnp.where(place == 3, second, jnp.where(place == 1, more, got))
    return jnp.stack([one, two])


def on_device(
    inputs,
    lengths,
    ffn_in,
    ffn_in_bias,
    ffn_out,
    qkv,
    attn_out,
    conv_in,
    conv_out,
    depthwise,
    gains,
    shifts,
    distance,
    grad_out,
):
    n = lax.axis_size("fsdp")
    me = lax.axis_index("fsdp")
    place = lax.axis_index("seq")
    odd = place % 2 == 1
    odd_word = (place % 2).astype(jnp.int32).reshape(1)
    me_word = me.astype(jnp.int32).reshape(1)
    width = inputs.shape[2]
    r = width // n
    inner_width = ffn_in.shape[2]
    n_gain, n_shift, n_tap = gains.shape[0], shifts.shape[0], depthwise.shape[0]
    cubed = n == 8 and lax.axis_size("seq") == 4

    def chunks(part):
        return [part[:, i : i + width] for i in range(0, part.shape[1], width)]

    shard_a = jnp.stack(chunks(ffn_in[0]))
    shard_b = jnp.concatenate([ffn_out[0].reshape(4, r, width), qkv], axis=0)
    shard_c = jnp.stack(chunks(ffn_in[1]) + [attn_out] + chunks(conv_in) + [conv_out])
    shard_d = ffn_out[1].reshape(4, r, width)
    if cubed:
        w_b = lax.all_gather(shard_b, "fsdp", axis=0)
        inner_a, act_a, act_t_a, unit_t_a, tokens, small, w_a = first_forward(
            inputs, after(shard_a, shard_b), gains, shifts, depthwise, ffn_in_bias
        )
        cotangent = to_pairs(after(grad_out, act_a), place)
    else:
        small = jnp.concatenate([gains, shifts, depthwise, ffn_in_bias.reshape(-1, r)], axis=0)
        small = lax.all_gather(small, "fsdp", axis=0)
        w_a = lax.all_gather(shard_a, "fsdp", axis=0)
        w_b = lax.all_gather(shard_b, "fsdp", axis=0)
        tokens, cotangent = to_pairs(inputs, place), to_pairs(grad_out, place)

    small = small.astype(F32)
    rows = jnp.transpose(small, (1, 0, 2))
    n_plain = n_gain + n_shift + n_tap
    gain = rows[:n_gain].reshape(n_gain, width)
    shift = rows[n_gain : n_gain + n_shift].reshape(n_shift, width)
    taps = rows[n_gain + n_shift : n_plain].reshape(n_tap, width)
    bias = small[:, n_plain : n_plain + 8].reshape(n, 2, -1).transpose(1, 0, 2).reshape(2, inner_width)

    length = jnp.where(place < 2, lengths[0], lengths[1]).reshape(1)
    wide, ends = tables(distance)
    pairs = [(0, 1), (2, 3)]

    if not cubed:
        inner_a, act_a, act_t_a, unit_t_a = ffn_in_forward(tokens, jnp.stack([gain[0], shift[0]]), bias[0], w_a, 0)
    w_c = lax.all_gather(after(shard_c, w_b, cotangent, act_a), "fsdp", axis=0)
    first, unit_t_1, mine, other = out_qkv_forward(
        odd_word, tokens, act_a, w_b, jnp.stack([shift[6], gain[1], shift[1], shift[8], shift[9]])
    )
    probs, heads, mixed = attend(mine, other, length, wide, ends)
    w_d = lax.all_gather(after(shard_d, w_c, mixed), "fsdp", axis=0)
    second, mixed_t, unit_t_2, val, sig, gated = mid_forward(
        first, mixed, w_c, 4, 5, jnp.stack([shift[10], gain[2], shift[2], shift[11], shift[12]])
    )
    count = gated.shape[0]
    halo = lax.ppermute(gated[count - 32 :], "seq", pairs)
    conv, act_t_c, third = conv_forward(
        gated, halo, taps, jnp.stack([shift[13], gain[3], shift[3], shift[14]]), second, w_c, 7
    )
    inner_b, act_b, act_t_b, unit_t_b = ffn_in_forward(third, jnp.stack([gain[4], shift[4]]), bias[1], w_c, 0)
    outputs, d4, dout, sums_5 = out_last(third, act_b, w_d, 0, cotangent, jnp.stack([shift[7], gain[5], shift[5]]))

    g_out_b = weight_grad(act_t_b, dout, n, 4, 0, True)
    part_out_b = lax.psum_scatter(g_out_b, "fsdp", scatter_dimension=0, tiled=False)
    dinner, dout, dbias_b, sums_7 = ffn_hidden_back(after(dout, g_out_b), inner_b, w_d, 0)
    g_in_b = weight_grad(unit_t_b, dinner, n, 4, 0, False)
    part_in_b = lax.psum_scatter(g_in_b, "fsdp", scatter_dimension=0, tiled=False)
    dinner = after(dinner, g_in_b)
    if cubed:
        vec = jnp.stack([gain[4], gain[3], shift[3], gain[2]])
        dconv, dout_3, d2, dout_2, dglu, mine, other, sums_4, sums_3, sums_2, outputs = middle_back(
            d4, dinner, third, conv, val, sig, second, w_c, taps, vec, outputs
        )
    else:
        outputs = from_pairs(outputs, place)
        d3, sums_4 = norm_input_back(d4, dinner, third, w_c, 0, gain[4:5])
        dconv, dout_3, sums_3 = conv_out_back(d3, conv, w_c, 7, jnp.stack([gain[3], shift[3]]))
        follow = lax.ppermute(dconv[:32], "seq", [(j, i) for i, j in pairs])
        d2, dout_2, dglu, mine, other, sums_2 = mid_back(
            odd_word, dconv, follow, taps, val, sig, second, d3, w_c, 4, 5, gain[2:3]
        )
    if cubed:
        dqkv, dtable, share_out_b = attend_back(heads, probs, wide, mine, other, part_out_b)
    else:
        dqkv, dtable = attend_back(heads, probs, wide, mine, other)
        share_out_b, share_in_b = over_seq(part_out_b), over_seq(part_in_b)

    def biases(part):
        return part.reshape(n, 4, r).transpose(1, 0, 2).reshape(4, width)

    if cubed:
        main, share_in_b, small, table, grad_tokens = last_reduced(
            gain[0:2], dtable, (sums_2, sums_3, sums_4, sums_5, sums_7), dbias_b, d2, first, tokens, dconv, gated, halo,
            part_in_b, dqkv, unit_t_1, act_t_a, unit_t_a, inner_a, w_b, w_a,
            mixed_t, dout_2, unit_t_2, dglu, act_t_c, dout_3,
        )
    else:
        d1, sums_1 = norm_input_back(d2, dqkv, first, w_b, 4, gain[1:2])
        bias_sums = jnp.sum(dqkv.astype(F32), axis=0)
        dtaps = taps_grad(dconv, gated, halo, n_tap)
        early = jnp.concatenate(
            [
                jnp.stack([sums_1[0], sums_2[2], sums_3[1], sums_4[0], sums_5[0]]),
                jnp.stack([sums_1[1], sums_2[3], sums_3[2], sums_4[1], sums_5[1]]),
                jnp.stack(
                    [
                        sums_7[0],
                        bias_sums[:width],
                        bias_sums[2 * width :],
                        sums_2[4],
                        sums_2[0],
                        sums_2[1],
                        sums_3[3],
                        sums_3[0],
                    ]
                ),
                dtaps,
                biases(dbias_b),
            ],
            axis=0,
        )
        dinner, dout, dbias_a, sums_6 = ffn_hidden_back(d1, inner_a, w_b, 0)
        g_m = weight_grad(unit_t_2, dglu, n, 4, 1, False)
        g_m = weight_grad(mixed_t, dout_2, n, 4, 0, False, into=g_m)
        g_m = weight_grad(act_t_c, dout_3, n, 4, 3, False, into=g_m)
        shares = {
            "m": reduced(g_m),
            "q": reduced(weight_grad(unit_t_1, dqkv, n, 3, 0, False)),
            "out": reduced(weight_grad(act_t_a, dout, n, 4, 0, True)),
            "in": reduced(weight_grad(unit_t_a, dinner, n, 4, 0, False)),
        }
        main = jnp.stack([shares[name][unit] for name, unit in ORDER])
        d0, sums_0 = norm_input_back(d1, dinner, tokens, w_a, 0, gain[0:1], BF)
        grad_tokens = from_pairs(d0, place)
        late = jnp.concatenate([jnp.stack([sums_0[0], sums_0[1], sums_6[0]]), biases(dbias_a)], axis=0)
        small = small_reduced(jnp.concatenate([early, late], axis=0))
        table = lax.psum(dtable, ("seq", "fsdp"))
    (
        g_in, g_out, g_qkv, g_attn, g_conv_in, g_conv_out, g_taps, g_gain, g_shift, g_bias, total_table, outputs, grad_tokens
    ) = finished(main, share_in_b, share_out_b, small, table, outputs, grad_tokens, n_tap, distance.shape)
    return (
        outputs,
        grad_tokens,
        g_in,
        g_bias,
        g_out.reshape(2, 4 * r, width),
        g_qkv,
        g_attn,
        g_conv_in,
        g_conv_out,
        g_taps,
        g_gain,
        g_shift,
        total_table,
    )


def solution(mesh):
    return jax.shard_map(
        on_device,
        mesh=mesh,
        in_specs=(
            P("fsdp", "seq", None),
            P("fsdp"),
            P(None, "fsdp", None),
            P(None, "fsdp"),
            P(None, "fsdp", None),
            P(None, "fsdp", None),
            P("fsdp", None),
            P("fsdp", None),
            P("fsdp", None),
            P(None, "fsdp"),
            P(None, "fsdp"),
            P(None, "fsdp"),
            P(),
            P("fsdp", "seq", None),
        ),
        out_specs=(
            P("fsdp", "seq", None),
            P("fsdp", "seq", None),
            P(None, "fsdp", None),
            P(None, "fsdp"),
            P(None, "fsdp", None),
            P(None, "fsdp", None),
            P("fsdp", None),
            P("fsdp", None),
            P("fsdp", None),
            P(None, "fsdp"),
            P(None, "fsdp"),
            P(None, "fsdp"),
            P(),
        ),
        check_vma=False,
    )
```

```python
import functools

import jax
import jax.numpy as jnp
from jax import lax
from jax.experimental import pallas as pl
from jax.experimental.pallas import tpu as pltpu
from jax.sharding import PartitionSpec as P

HEAD_DIM=64; LEFT=64; RIGHT=8
F32=jnp.float32; BF=jnp.bfloat16
RB=256
PADL=128
WIN=512

def dot(a,b,ca,cb):
    return lax.dot_general(a,b,(((ca,),(cb,)),((),())),preferred_element_type=F32)

def lanes(shape):
    return lax.broadcasted_iota(jnp.int32,shape,1)

def band_offset():
    row=lax.broadcasted_iota(jnp.int32,(RB,WIN),0)
    col=lax.broadcasted_iota(jnp.int32,(RB,WIN),1)
    return col-row-LEFT


MESH = pl.DeviceIdType.MESH
STEPS = 4


def pair_place():
    place = lax.axis_index("seq")
    half = lax.rem(place, jnp.int32(2))
    return half, {"seq": place + 1 - 2 * half}


def meet(partner):
    barrier = pltpu.get_barrier_semaphore()
    pl.semaphore_signal(barrier, inc=1, device_id=partner, device_id_type=MESH)
    pl.semaphore_wait(barrier, 1)


def block_at(step, half):
    return lax.rem(step + 2 * (1 - half), jnp.int32(STEPS))


def fwd_kernel(len_ref,wide_ref,ends_ref,mine_ref,other_ref,p_ref,heads_ref,mixed_ref,s_ref,kx_ref,buf,mixed,stage,in_send,in_recv,in_load,out_send,out_recv):
    n=buf.shape[2]; own=n//2
    pair=pl.program_id(0); step=pl.program_id(1)
    pairs=buf.shape[0]
    half,partner=pair_place()
    at=pl.multiple_of(half*own,own)
    def arrive(a):
        return pltpu.make_async_remote_copy(src_ref=other_ref.at[a],dst_ref=buf.at[a,:,pl.ds(at,own)],send_sem=in_send.at[a],recv_sem=in_recv.at[a],device_id=partner,device_id_type=MESH)
    def load(a):
        return pltpu.make_async_copy(mine_ref.at[a],buf.at[a,:,pl.ds(at,own)],in_load.at[a])
    def leave(a,b):
        cols=pl.ds(pl.multiple_of(half*own+a*128,128),128)
        return pltpu.make_async_remote_copy(src_ref=stage.at[a,b],dst_ref=mixed.at[pl.ds(pl.multiple_of(b*RB,RB),RB),cols],send_sem=out_send.at[a,b],recv_sem=out_recv.at[a,b],device_id=partner,device_id_type=MESH)
    @pl.when((pair==0)&(step==0))
    def _():
        meet(partner)
        for a in range(pairs):
            load(a).start()
            arrive(a).start()
    @pl.when(step==0)
    def _():
        load(pair).wait()
        arrive(pair).wait()
        heads_ref[0]=buf[pair]
        kx_ref[:,0:128]=buf[pair,1]
    i0=pl.multiple_of(block_at(step,half)*RB,RB)
    q2=buf[pair,0,pl.ds(i0,RB)]
    v2=buf[pair,2]
    lane=lanes((RB,128))
    t=lax.broadcasted_iota(jnp.int32,(n,128),0)
    c=lanes((n,128))
    left=(t<i0-128).astype(F32); right=(t>=i0+WIN-128).astype(F32)
    masked=jnp.where(t>=len_ref[0],-1e30,0.0)
    ext=jnp.where(c<2,left,jnp.where(c<4,right,jnp.where(c==4,masked,0.0)))
    kx_ref[:,128:256]=ext.astype(BF)
    qhs,qxs=[],[]
    for h in range(2):
        head=(lane<64) if h==0 else (lane>=64)
        qh=jnp.where(head,q2,jnp.zeros_like(q2))
        ends=dot(qh,ends_ref[...],1,0)
        hi=ends.astype(BF).astype(F32)
        qx=jnp.where((lane==0)|(lane==2),hi,jnp.where((lane==1)|(lane==3),ends-hi,jnp.where(lane==4,1.0,0.0))).astype(BF)
        qhs.append(qh); qxs.append(jnp.concatenate([qh,qx],axis=1))
    for h in range(2):
        s_ref[h,:,PADL:PADL+n]=dot(qxs[h],kx_ref[...],1,1)
    j=band_offset()
    w=pl.ds(i0,WIN)
    for h in range(2):
        wide=dot(qhs[h],wide_ref[...],1,0)
        band=pltpu.roll(wide,LEFT,1,stride=1,stride_axis=0)
        band=jnp.where(j>=LEFT+RIGHT,wide[:,LEFT+RIGHT:LEFT+RIGHT+1],band)
        s_ref[h,:,w]=s_ref[h,:,w]+band
    for h in range(2):
        s=s_ref[h,:,PADL:PADL+n]
        m=jnp.max(s,axis=1,keepdims=True)
        e=jnp.exp(s-m)
        z=jnp.sum(e,axis=1,keepdims=True)
        p_ref[h]=(e*(1.0/z)).astype(BF)
    outs=[dot(p_ref[h],v2,1,0) for h in range(2)]
    out=jnp.where(lane<64,outs[0],outs[1]).astype(BF)
    @pl.when(step<2)
    def _():
        stage[pair,step]=out
        leave(pair,step).start()
    @pl.when(step>=2)
    def _():
        cols=pl.ds(pl.multiple_of(half*own+pair*128,128),128)
        mixed[pl.ds(pl.multiple_of((step-2)*RB,RB),RB),cols]=out
    @pl.when((pair==pairs-1)&(step==STEPS-1))
    def _():
        for a in range(pairs):
            for b in range(2):
                leave(a,b).wait_send()
        for a in range(pairs):
            for b in range(2):
                arrived=pltpu.make_async_remote_copy(src_ref=stage.at[a,b],dst_ref=mixed.at[pl.ds(b*RB,RB),pl.ds(pl.multiple_of((1-half)*own+a*128,128),128)],send_sem=out_send.at[a,b],recv_sem=out_recv.at[a,b],device_id=partner,device_id_type=MESH)
                arrived.wait_recv()
        mixed_ref[...]=mixed[...]


def z_line(middle,to_1,to_2,whole,near,far,z_send,z_recv):
    def copy(i,stage):
        src=(whole,near,far)[stage]; dst=(near,far,near)[stage]
        return pltpu.make_async_remote_copy(src_ref=src.at[i],dst_ref=dst.at[i],send_sem=z_send.at[i,stage],recv_sem=z_recv.at[i,stage],device_id=to_2 if stage==1 else to_1,device_id_type=MESH)
    def begin(i):
        pl.when(middle==0)(lambda: copy(i,0).start())
    def step(i,stage):
        @pl.when(middle==1)
        def _():
            if stage==0:
                copy(i,0).wait_recv()
                near[i]=(whole[i].astype(F32)+near[i].astype(F32)).astype(BF)
                copy(i,1).start()
            elif stage==1:
                copy(i,1).wait()
                far[i]=(near[i].astype(F32)+far[i].astype(F32)).astype(BF)
                copy(i,2).start()
            else:
                copy(i,2).wait_send()
        if stage!=1:
            @pl.when(middle==0)
            def _():
                if stage==0:
                    copy(i,0).wait_send()
                else:
                    copy(i,2).wait_recv()
    return begin,step


def bwd_kernel(with_part,heads_ref,p_ref,wide_ref,mine_ref,other_ref,*rest):
    if with_part:
        part_ref,dqkv_ref,de_ref,out_ref,*rest=rest
        *rest,whole,near,far,part_sem,out_sem,z_send,z_recv=rest
    else:
        dqkv_ref,de_ref,*rest=rest
    ds_ref,kx_ref,dka,dva,dea,buf,dqkv,stage_q,stage_kv,in_send,in_recv,in_load,q_send,q_recv,kv_send,kv_recv=rest
    n=heads_ref.shape[2]; own=n//2
    pair=pl.program_id(0); step=pl.program_id(1)
    pairs=buf.shape[0]
    half,partner=pair_place()
    at=pl.multiple_of(half*own,own)
    width=2*own
    def columns(t,who,a):
        return pl.ds(pl.multiple_of(t*width+who*own+a*128,128),128)
    def arrive(a):
        return pltpu.make_async_remote_copy(src_ref=other_ref.at[a],dst_ref=buf.at[a,pl.ds(at,own)],send_sem=in_send.at[a],recv_sem=in_recv.at[a],device_id=partner,device_id_type=MESH)
    def load(a):
        return pltpu.make_async_copy(mine_ref.at[a],buf.at[a,pl.ds(at,own)],in_load.at[a])
    def leave_q(a,b,who):
        return pltpu.make_async_remote_copy(src_ref=stage_q.at[a,b],dst_ref=dqkv.at[pl.ds(pl.multiple_of(b*RB,RB),RB),columns(0,who,a)],send_sem=q_send.at[a,b],recv_sem=q_recv.at[a,b],device_id=partner,device_id_type=MESH)
    def leave_kv(a,t,who):
        return pltpu.make_async_remote_copy(src_ref=stage_kv.at[a,t],dst_ref=dqkv.at[:,columns(t+1,who,a)],send_sem=kv_send.at[a,t],recv_sem=kv_recv.at[a,t],device_id=partner,device_id_type=MESH)
    if with_part:
        n_part=part_ref.shape[0]
        place=lax.axis_index("seq")
        middle=lax.rem(lax.div(place+1,jnp.int32(2)),jnp.int32(2))
        across={"seq":3-place}
        z_begin,z_step=z_line(middle,partner,across,whole,near,far,z_send,z_recv)
        def part_copy(i):
            return pltpu.make_async_copy(part_ref.at[i],whole.at[i],part_sem.at[i])
        def result_do(i,act):
            for is_middle,src in ((1,far),(0,near)):
                copy=pltpu.make_async_copy(src.at[i],out_ref.at[i],out_sem.at[i])
                pl.when(middle==is_middle)(lambda copy=copy: act(copy))
        now=pair*STEPS+step
    @pl.when((pair==0)&(step==0))
    def _():
        if with_part:
            barrier=pltpu.get_barrier_semaphore()
            for device in (partner,across):
                pl.semaphore_signal(barrier,inc=1,device_id=device,device_id_type=MESH)
            pl.semaphore_wait(barrier,2)
        else:
            meet(partner)
        for a in range(pairs):
            load(a).start()
            arrive(a).start()
        if with_part:
            for i in range(n_part):
                part_copy(i).start()
        dea[...]=jnp.zeros_like(dea)
        for h in range(2):
            ds_ref[h,:,0:PADL]=jnp.zeros((RB,PADL),F32)
            ds_ref[h,:,PADL+n:]=jnp.zeros((RB,ds_ref.shape[2]-PADL-n),F32)
    @pl.when(step==0)
    def _():
        load(pair).wait()
        pl.when(pair>0)(lambda: arrive(pair).wait())
        kx_ref[:,0:128]=heads_ref[0,1]
        dka[...]=jnp.zeros_like(dka); dva[...]=jnp.zeros_like(dva)
    if with_part:
        for i in range(n_part):
            @pl.when(now==1+2*i)
            def _(i=i):
                part_copy(i).wait()
                z_begin(i)
            for stage in range(3):
                @pl.when(now==5+2*i+2*stage)
                def _(i=i,stage=stage):
                    z_step(i,stage)
                    if stage==2:
                        result_do(i,lambda copy: copy.start())
    @pl.when((pair==0)&(step==2))
    def _():
        arrive(pair).wait()
    turned=lax.rem(step+2*jnp.where(pair==0,1,0),jnp.int32(STEPS))
    i0=pl.multiple_of(block_at(turned,half)*RB,RB)
    q2=heads_ref[0,0,pl.ds(i0,RB)]
    v2=heads_ref[0,2]
    do2=buf[pair,pl.ds(i0,RB)]
    lane=lanes((RB,128))
    row=lax.broadcasted_iota(jnp.int32,(RB,128),0)
    t=lax.broadcasted_iota(jnp.int32,(n,128),0)
    c=lanes((n,128))
    left=(t<i0-128).astype(F32)
    kx_ref[:,128:256]=jnp.where(c==0,left,jnp.where(c==1,1.0,0.0)).astype(BF)
    heads=[]
    for h in range(2):
        head=(lane<64) if h==0 else (lane>=64)
        heads.append((jnp.where(head,do2,jnp.zeros_like(do2)),jnp.where(head,q2,jnp.zeros_like(q2))))
    dps=[dot(doh,v2,1,1) for doh,_ in heads]
    dss=[]
    for h in range(2):
        pf=p_ref[h].astype(F32)
        d=jnp.sum(pf*dps[h],axis=1,keepdims=True)
        dsf=pf*(dps[h]-d)
        ds_ref[h,:,PADL:PADL+n]=dsf
        dss.append(dsf.astype(BF))
    dva[...]+=dot(heads[0][0],p_ref[0],0,0)+dot(heads[1][0],p_ref[1],0,0)
    dka[...]+=dot(heads[0][1],dss[0],0,0)+dot(heads[1][1],dss[1],0,0)
    dqxs=[dot(ds,kx_ref[...],1,0) for ds in dss]
    j=band_offset()
    drels=[]
    for h in range(2):
        sums=dqxs[h][:,128:256]
        win=ds_ref[h,:,pl.ds(i0,WIN)]
        inleft=jnp.sum(jnp.where(j<=0,win,0.0),axis=1,keepdims=True)
        drel=jnp.concatenate([win[8*g:8*g+8,LEFT+8*g:LEFT+8*g+128] for g in range(RB//8)],axis=0)
        for bit in (1,2,4):
            drel=jnp.where((row&bit)!=0,pltpu.roll(drel,128-bit,1),drel)
        drel=jnp.where((lane>0)&(lane<LEFT+RIGHT),drel,0.0)
        bandsum=jnp.sum(drel,axis=1,keepdims=True)
        l=sums[:,0:1]+inleft
        r=sums[:,1:2]-l-bandsum
        drels.append(jnp.where(lane==0,l,jnp.where(lane==LEFT+RIGHT,r,drel)).astype(BF))
    dqs=[dqxs[h][:,0:128]+dot(drels[h],wide_ref[...],1,1) for h in range(2)]
    dea[...]+=dot(drels[0],heads[0][1],0,0)+dot(drels[1],heads[1][1],0,0)
    dq=(jnp.where(lane<64,dqs[0],dqs[1])*HEAD_DIM**-0.5).astype(BF)
    @pl.when(turned<2)
    def _():
        stage_q[pair,turned]=dq
        leave_q(pair,turned,half).start()
    @pl.when(turned>=2)
    def _():
        dqkv[pl.ds(pl.multiple_of((turned-2)*RB,RB),RB),columns(0,half,pair)]=dq
    @pl.when(step==STEPS-1)
    def _():
        for i,acc in enumerate((dka,dva)):
            mine=acc[:,pl.ds(at,own)]
            theirs=acc[:,pl.ds(pl.multiple_of((1-half)*own,own),own)]
            stage_kv[pair,i]=jnp.transpose(theirs).astype(BF)
            leave_kv(pair,i,half).start()
            dqkv[:,columns(i+1,half,pair)]=jnp.transpose(mine).astype(BF)
    @pl.when((pair==pairs-1)&(step==STEPS-1))
    def _():
        for a in range(pairs):
            for b in range(2):
                leave_q(a,b,half).wait_send()
                leave_kv(a,b,half).wait_send()
        for a in range(pairs):
            for b in range(2):
                leave_q(a,b,1-half).wait_recv()
                leave_kv(a,b,1-half).wait_recv()
        dqkv_ref[...]=dqkv[...]
        de_ref[...]=dea[...]
        if with_part:
            for i in range(n_part):
                result_do(i,lambda copy: copy.wait())


def tables(distance):
    e=distance.T
    wide=jnp.concatenate([e,jnp.broadcast_to(e[:,72:73],(64,120)),jnp.broadcast_to(e[:,0:1],(64,WIN-193))],axis=1)
    wide=jnp.concatenate([wide,wide],axis=0)
    ends=jnp.concatenate([e[:,0:1],e[:,0:1],e[:,72:73],e[:,72:73],jnp.zeros((64,124),e.dtype)],axis=1)
    ends=jnp.concatenate([ends,ends],axis=0)
    return wide,ends

def attend(mine,other,length,wide,ends):
    pairs,_,own,_=mine.shape; n=2*own
    dma=pltpu.SemaphoreType.DMA
    whole=lambda *shape: pl.BlockSpec(shape,lambda a,b:(0,)*len(shape))
    anywhere=pl.BlockSpec(memory_space=pl.ANY)
    return pl.pallas_call(fwd_kernel,
        grid=(pairs,STEPS),
        in_specs=[pl.BlockSpec(memory_space=pltpu.SMEM),whole(128,WIN),whole(128,128),anywhere,anywhere],
        out_specs=[pl.BlockSpec((2,RB,n),lambda a,b:(a,b,0)),pl.BlockSpec((1,3,n,128),lambda a,b:(a,0,0,0)),whole(own,2*own)],
        out_shape=[jax.ShapeDtypeStruct((2*pairs,n,n),BF),jax.ShapeDtypeStruct((pairs,3,n,128),BF),jax.ShapeDtypeStruct((own,2*own),BF)],
        scratch_shapes=[pltpu.VMEM((2,RB,PADL+n+256),F32),pltpu.VMEM((n,256),BF),pltpu.VMEM((pairs,3,n,128),BF),pltpu.VMEM((own,2*own),BF),pltpu.VMEM((pairs,2,RB,128),BF),
            dma((pairs,)),dma((pairs,)),dma((pairs,)),dma((pairs,2)),dma((pairs,2))],
        compiler_params=pltpu.CompilerParams(vmem_limit_bytes=58<<20,collective_id=1,has_side_effects=True),
        cost_estimate=pl.CostEstimate(flops=40_000_000_000,bytes_accessed=120_000_000,transcendentals=0),
        name="attend_fwd",
    )(length,wide,ends,mine,other)

def attend_back(heads,p,wide,mine,other,part=None):
    pairs,_,n,_=heads.shape; own=n//2
    dma=pltpu.SemaphoreType.DMA
    whole=lambda *shape: pl.BlockSpec(shape,lambda a,b:(0,)*len(shape))
    anywhere=pl.BlockSpec(memory_space=pl.ANY)
    with_part=part is not None
    extra=[pltpu.VMEM(part.shape,BF)]*3+[dma((part.shape[0],))]*2+[dma((part.shape[0],3))]*2 if with_part else []
    return pl.pallas_call(functools.partial(bwd_kernel,with_part),
        grid=(pairs,STEPS),
        in_specs=[pl.BlockSpec((1,3,n,128),lambda a,b:(a,0,0,0)),pl.BlockSpec((2,RB,n),lambda a,b:(a,jnp.where(a==0,lax.rem(b+2,STEPS),b),0)),whole(128,128),anywhere,anywhere]+[anywhere]*with_part,
        out_specs=[whole(own,6*own),whole(128,128)]+[anywhere]*with_part,
        out_shape=[jax.ShapeDtypeStruct((own,6*own),BF),jax.ShapeDtypeStruct((128,128),F32)]+([jax.ShapeDtypeStruct(part.shape,BF)] if with_part else []),
        scratch_shapes=[pltpu.VMEM((2,RB,PADL+n+256),F32),pltpu.VMEM((n,256),BF),pltpu.VMEM((128,n),F32),pltpu.VMEM((128,n),F32),pltpu.VMEM((128,128),F32),
            pltpu.VMEM((pairs,n,128),BF),pltpu.VMEM((own,6*own),BF),pltpu.VMEM((pairs,2,RB,128),BF),pltpu.VMEM((pairs,2,own,128),BF),
            dma((pairs,)),dma((pairs,)),dma((pairs,)),dma((pairs,2)),dma((pairs,2)),dma((pairs,2)),dma((pairs,2))]+extra,
        compiler_params=pltpu.CompilerParams(vmem_limit_bytes=58<<20,collective_id=2,has_side_effects=True),
        cost_estimate=pl.CostEstimate(flops=50_000_000_000,bytes_accessed=150_000_000,transcendentals=0),
        name="attend_bwd",
    )(heads,p,wide[:,0:128],mine,other,*([part] if with_part else []))


EPSILON = 1e-05
HALF = 0.5
CUT = 256
VMEM = 56 << 20


def flat(ref):
    value = ref[...]
    return value.reshape(-1, value.shape[-1])


def cuts(count):
    return [pl.ds(i, CUT) for i in range(0, count, CUT)]


def normal(v):
    c = v - jnp.mean(v, axis=-1, keepdims=True)
    r = lax.rsqrt(jnp.mean(c * c, axis=-1, keepdims=True) + EPSILON)
    return c * r, r


def normal_back(dy, unit, r, gain):
    a = dy * gain
    return (a - jnp.mean(a, axis=-1, keepdims=True) - unit * jnp.mean(a * unit, axis=-1, keepdims=True)) * r


def total(v):
    return jnp.sum(v, axis=0, keepdims=True)


def silu_slope(v):
    s = jax.nn.sigmoid(v)
    return s * (1.0 + v * (1.0 - s))


def call(kernel, grid, ins, outs, scratch=(), name=None, aliases=None, flops=0, moved=0):
    def spec(shape, block, where):
        if block is None:
            return pl.BlockSpec(shape, lambda *_: (0,) * len(shape))
        if block == "smem":
            return pl.BlockSpec(memory_space=pltpu.SMEM)
        if block == "any":
            return pl.BlockSpec(memory_space=pl.ANY)
        return pl.BlockSpec(block, where)

    return pl.pallas_call(
        kernel,
        grid=grid,
        in_specs=[spec(a.shape, b, w) for a, b, w in ins],
        out_specs=[spec(s, b, w) for s, _, b, w in outs],
        out_shape=[jax.ShapeDtypeStruct(s, d) for s, d, _, _ in outs],
        scratch_shapes=list(scratch),
        input_output_aliases=aliases or {},
        compiler_params=pltpu.CompilerParams(vmem_limit_bytes=VMEM),
        cost_estimate=pl.CostEstimate(flops=flops, bytes_accessed=moved, transcendentals=0),
        name=name,
    )(*[a for a, _, _ in ins])


def scr(shape, dtype):
    return pltpu.VMEM(shape, dtype)


def in_kernel(x_ref, vec_ref, bias_ref, w_ref, inner_ref, act_ref, act_t_ref, unit_t_ref, unit):
    @pl.when(pl.program_id(0) == 0)
    def _():
        for rows in cuts(x_ref.shape[0]):
            n, _ = normal(x_ref[rows, :].astype(F32))
            u = (n * vec_ref[0:1, :] + vec_ref[1:2, :]).astype(BF)
            unit[rows, :] = u
            unit_t_ref[:, rows] = u.T

    w = flat(w_ref)
    for rows in cuts(x_ref.shape[0]):
        s = dot(unit[rows, :], w, 1, 0) + bias_ref[0]
        inner_ref[rows, :] = s.astype(BF)
        a = (s * jax.nn.sigmoid(s)).astype(BF)
        act_ref[rows, :] = a
        act_t_ref[:, rows] = a.T


def ffn_in_forward(x, vec, bias, w, unit0):
    t, d = x.shape
    n, _, r, _ = w.shape
    k = bias.shape[0] // d
    bias = bias.reshape(k, 1, d)
    return call(
        in_kernel,
        (k,),
        [
            (x, None, None),
            (vec, None, None),
            (bias, (1, 1, d), lambda j: (j, 0, 0)),
            (w, (n, 1, r, d), lambda j: (0, unit0 + j, 0, 0)),
        ],
        [
            ((t, k * d), BF, (t, d), lambda j: (0, j)),
            ((t, k * d), BF, (t, d), lambda j: (0, j)),
            ((k * d, t), BF, (d, t), lambda j: (j, 0)),
            ((d, t), BF, None, None),
        ],
        [scr((t, d), BF)],
        name="ffn_in",
        flops=2 * t * d * d * k,
        moved=2 * d * d * k + 6 * t * d * k,
    )


def out_qkv_kernel(odd_ref, x_ref, act_ref, w_out_ref, w_qkv_ref, vec_ref, first_ref, unit_t_ref, mine_ref, other_ref, unit, acc):
    s = pl.program_id(0)
    t = x_ref.shape[0]

    @pl.when(s < 4)
    def _():
        w = flat(w_out_ref)
        for rows in cuts(t):
            p = dot(act_ref[rows, :], w, 1, 0)
            acc[rows, :] = p + jnp.where(s == 0, 0.0, acc[rows, :])

    @pl.when(s == 3)
    def _():
        for rows in cuts(t):
            first = x_ref[rows, :].astype(F32) + HALF * (acc[rows, :] + vec_ref[0:1, :])
            first_ref[rows, :] = first
            n, _ = normal(first)
            u = (n * vec_ref[1:2, :] + vec_ref[2:3, :]).astype(BF)
            unit[rows, :] = u
            unit_t_ref[:, rows] = u.T

    @pl.when(s >= 4)
    def _():
        w = flat(w_qkv_ref)
        odd = odd_ref[0] == 1
        half = w.shape[1] // 2
        scale = jnp.where(s == 4, HEAD_DIM**-0.5, 1.0)
        b = jnp.where(s == 4, vec_ref[3:4, :], jnp.where(s == 6, vec_ref[4:5, :], 0.0))
        for rows in cuts(t):
            y = (dot(unit[rows, :], w, 1, 0) + b) * scale
            low, high = y[:, :half], y[:, half:]
            mine = jnp.where(odd, high, low).astype(BF)
            other = jnp.where(odd, low, high).astype(BF)
            for part in range(half // 128):
                cols = slice(part * 128, part * 128 + 128)
                mine_ref[part, 0, rows, :] = mine[:, cols]
                other_ref[part, 0, rows, :] = other[:, cols]


def out_qkv_forward(odd, x, act, w, vec):
    t, d = x.shape
    n, _, r, _ = w.shape
    return call(
        out_qkv_kernel,
        (7,),
        [
            (odd, "smem", None),
            (x, None, None),
            (act, (t, d), lambda s: (0, jnp.minimum(s, 3))),
            (w, (n // 4, 4, r, d), lambda s: (jnp.minimum(s, 3), 0, 0, 0)),
            (w, (n, 1, r, d), lambda s: (0, jnp.maximum(s, 4), 0, 0)),
            (vec, None, None),
        ],
        [
            ((t, d), F32, None, None),
            ((d, t), BF, None, None),
            ((d // 256, 3, t, 128), BF, (d // 256, 1, t, 128), lambda s: (0, jnp.maximum(s - 4, 0), 0, 0)),
            ((d // 256, 3, t, 128), BF, (d // 256, 1, t, 128), lambda s: (0, jnp.maximum(s - 4, 0), 0, 0)),
        ],
        [scr((t, d), BF), scr((t, d), F32)],
        name="out_qkv",
        flops=14 * t * d * d,
        moved=14 * d * d + 20 * t * d,
    )


def mid_kernel(first_ref, mixed_ref, w_attn_ref, w_in_ref, vec_ref, second_ref, mixed_t_ref, unit_t_ref, val_ref, sig_ref, gated_ref, unit, val):
    s = pl.program_id(0)
    t = first_ref.shape[0]

    @pl.when(s == 0)
    def _():
        w = flat(w_attn_ref)
        for rows in cuts(t):
            m = mixed_ref[rows, :]
            mixed_t_ref[:, rows] = m.T
            second = first_ref[rows, :] + dot(m, w, 1, 0) + vec_ref[0:1, :]
            second_ref[rows, :] = second
            n, _ = normal(second)
            u = (n * vec_ref[1:2, :] + vec_ref[2:3, :]).astype(BF)
            unit[rows, :] = u
            unit_t_ref[:, rows] = u.T

    @pl.when(s == 1)
    def _():
        w = flat(w_in_ref)
        for rows in cuts(t):
            v = dot(unit[rows, :], w, 1, 0) + vec_ref[3:4, :]
            val[rows, :] = v
            val_ref[rows, :] = v.astype(BF)

    @pl.when(s == 2)
    def _():
        w = flat(w_in_ref)
        for rows in cuts(t):
            g = jax.nn.sigmoid(dot(unit[rows, :], w, 1, 0) + vec_ref[4:5, :])
            sig_ref[rows, :] = g.astype(BF)
            gated_ref[rows, :] = (val[rows, :] * g).astype(BF)


def mid_forward(first, mixed, w, u_attn, u_in, vec):
    t, d = first.shape
    n, _, r, _ = w.shape
    return call(
        mid_kernel,
        (3,),
        [
            (first, None, None),
            (mixed, None, None),
            (w, (n, 1, r, d), lambda s: (0, u_attn, 0, 0)),
            (w, (n, 1, r, d), lambda s: (0, u_in + jnp.maximum(s - 1, 0), 0, 0)),
            (vec, None, None),
        ],
        [((t, d), F32, None, None), ((d, t), BF, None, None), ((d, t), BF, None, None)]
        + [((t, d), BF, None, None)] * 3,
        [scr((t, d), BF), scr((t, d), F32)],
        name="mid",
        flops=6 * t * d * d,
        moved=6 * d * d + 20 * t * d,
    )


ROWS = 32
COLS = 256
FIR_ROWS = 64
FIR_COLS = 128


def shifted(window, b):
    return window if b == 0 else pltpu.roll(window, window.shape[0] - b, 0)


def fir(pad, taps, offset, count, width, start, write, turned=False):
    reach = taps.shape[0]
    for c in range(0, width, FIR_COLS):
        cols = slice(c, c + FIR_COLS)

        def body(i, _):
            base = pl.multiple_of(i * FIR_ROWS, FIR_ROWS)
            window = pad[pl.ds(base, FIR_ROWS + 32), cols]
            acc = start(cols)
            for b in range(8):
                sh = shifted(window, b)
                for a in range(0, 5):
                    m = 8 * a + b - offset
                    if 0 <= m < reach:
                        tap = reach - 1 - m if turned else m
                        acc = acc + taps[tap : tap + 1, cols] * sh[8 * a : 8 * a + FIR_ROWS]
            write(pl.ds(base, FIR_ROWS), cols, acc)
            return 0

        lax.fori_loop(0, count // FIR_ROWS, body, 0)


def conv_kernel(gated_ref, halo_ref, taps_ref, vec_ref, second_ref, w_ref, conv_ref, act_t_ref, third_ref, pad):
    t, d = gated_ref.shape
    pad[0:32, :] = halo_ref[...].astype(F32)
    for rows in cuts(t):
        pad[pl.ds(rows.start + 32, CUT), :] = gated_ref[rows, :].astype(F32)

    def write(rows, cols, acc):
        conv_ref[rows, cols] = acc

    fir(pad, taps_ref, 2, t, d, lambda cols: jnp.broadcast_to(vec_ref[0:1, cols], (FIR_ROWS, FIR_COLS)), write)
    w = flat(w_ref)
    for rows in cuts(t):
        n, _ = normal(conv_ref[rows, :])
        u = n * vec_ref[1:2, :] + vec_ref[2:3, :]
        a = (u * jax.nn.sigmoid(u)).astype(BF)
        act_t_ref[:, rows] = a.T
        third_ref[rows, :] = second_ref[rows, :] + dot(a, w, 1, 0) + vec_ref[3:4, :]


def conv_forward(gated, halo, taps, vec, second, w, unit0):
    t, d = gated.shape
    n, _, r, _ = w.shape
    return call(
        conv_kernel,
        (1,),
        [
            (gated, None, None),
            (halo, None, None),
            (taps, None, None),
            (vec, None, None),
            (second, None, None),
            (w, (n, 1, r, d), lambda s: (0, unit0, 0, 0)),
        ],
        [((t, d), F32, None, None), ((d, t), BF, None, None), ((t, d), F32, None, None)],
        [scr((t + 32, d), F32)],
        name="conv",
        flops=2 * t * d * d,
        moved=2 * d * d + 16 * t * d,
    )


def out_last_kernel(x_ref, act_ref, w_ref, cot_ref, vec_ref, out_ref, d_ref, dout_ref, sums_ref, acc):
    s = pl.program_id(0)
    t = x_ref.shape[0]
    w = flat(w_ref)
    for rows in cuts(t):
        p = dot(act_ref[rows, :], w, 1, 0)
        acc[rows, :] = p + jnp.where(s == 0, 0.0, acc[rows, :])

    @pl.when(s == 3)
    def _():
        sums_ref[...] = jnp.zeros_like(sums_ref)
        for rows in cuts(t):
            fourth = x_ref[rows, :] + HALF * (acc[rows, :] + vec_ref[0:1, :])
            n, r = normal(fourth)
            out_ref[rows, :] = (n * vec_ref[1:2, :] + vec_ref[2:3, :]).astype(BF)
            dy = cot_ref[rows, :].astype(F32)
            d = normal_back(dy, n, r, vec_ref[1:2, :])
            d_ref[rows, :] = d
            dout_ref[rows, :] = (HALF * d).astype(BF)
            sums_ref[0:1, :] += total(dy * n)
            sums_ref[1:2, :] += total(dy)


def out_last(x, act, w, block0, cot, vec):
    t, d = x.shape
    n, _, r, _ = w.shape
    return call(
        out_last_kernel,
        (4,),
        [
            (x, None, None),
            (act, (t, d), lambda s: (0, s)),
            (w, (n // 4, 4, r, d), lambda s: (s, block0, 0, 0)),
            (cot, None, None),
            (vec, None, None),
        ],
        [((t, d), BF, None, None), ((t, d), F32, None, None), ((t, d), BF, None, None), ((8, d), F32, None, None)],
        [scr((t, d), F32)],
        name="out_last",
        flops=8 * t * d * d,
        moved=8 * d * d + 20 * t * d,
    )


def ffn_hidden_kernel(d_ref, inner_ref, w_ref, dinner_ref, dout_ref, dbias_ref, sums_ref):
    t = d_ref.shape[0]

    @pl.when(pl.program_id(0) == 0)
    def _():
        sums_ref[...] = jnp.zeros_like(sums_ref)
        for rows in cuts(t):
            v = d_ref[rows, :] if d_ref.dtype == BF else (HALF * d_ref[rows, :]).astype(BF)
            dout_ref[rows, :] = v
            sums_ref[0:1, :] += total(v.astype(F32))

    w = flat(w_ref)
    dbias = 0.0
    for rows in cuts(t):
        da = dot(dout_ref[rows, :], w, 1, 1)
        v = (da * silu_slope(inner_ref[rows, :].astype(F32))).astype(BF)
        dinner_ref[rows, :] = v
        dbias = dbias + total(v.astype(F32))
    dbias_ref[0] = dbias


def ffn_hidden_back(dy, inner, w, block0):
    t, d = dy.shape
    n, _, r, _ = w.shape
    k = inner.shape[1] // d
    return call(
        ffn_hidden_kernel,
        (k,),
        [
            (dy, None, None),
            (inner, (t, d), lambda j: (0, j)),
            (w, (n // 4, 4, r, d), lambda j: (j, block0, 0, 0)),
        ],
        [
            ((t, k * d), BF, (t, d), lambda j: (0, j)),
            ((t, d), BF, None, None),
            ((k, 1, d), F32, (1, 1, d), lambda j: (j, 0, 0)),
            ((8, d), F32, None, None),
        ],
        name="ffn_hidden_back",
        flops=2 * t * d * d * k,
        moved=2 * d * d * k + 4 * t * d * k,
    )


def norm_input_kernel(k, dy_ref, g_ref, x_ref, w_ref, vec_ref, d_ref, sums_ref, acc):
    s = pl.program_id(0)
    t = x_ref.shape[0]
    w = flat(w_ref)
    for rows in cuts(t):
        p = dot(g_ref[rows, :], w, 1, 1)
        acc[rows, :] = p + jnp.where(s == 0, 0.0, acc[rows, :])

    @pl.when(s == k - 1)
    def _():
        sums_ref[...] = jnp.zeros_like(sums_ref)
        for rows in cuts(t):
            n, r = normal(x_ref[rows, :].astype(F32))
            du = acc[rows, :]
            d_ref[rows, :] = (dy_ref[rows, :] + normal_back(du, n, r, vec_ref[0:1, :])).astype(d_ref.dtype)
            sums_ref[0:1, :] += total(du * n)
            sums_ref[1:2, :] += total(du)


def norm_input_back(dy, g, x, w, unit0, gain, out_type=F32):
    t, d = dy.shape
    n, _, r, _ = w.shape
    k = g.shape[1] // d
    return call(
        functools.partial(norm_input_kernel, k),
        (k,),
        [
            (dy, None, None),
            (g, (t, d), lambda j: (0, j)),
            (x, None, None),
            (w, (n, 1, r, d), lambda j: (0, unit0 + j, 0, 0)),
            (gain, None, None),
        ],
        [((t, d), out_type, None, None), ((8, d), F32, None, None)],
        [scr((t, d), F32)],
        name="norm_input_back",
        flops=2 * t * d * d * k,
        moved=2 * d * d * k + 2 * t * d * k + 12 * t * d,
    )


def weight_kernel(left_ref, right_ref, *rest):
    out_ref = rest[-1]
    rows, d = left_ref.shape[0], out_ref.shape[-1]
    a, b, r, _ = out_ref.shape
    step = max(256, 4 * r)
    for i in range(0, rows, step):
        value = dot(left_ref[i : i + step, :], right_ref[...], 1, 0).astype(BF)
        if b == 1:
            out_ref[pl.ds(i // r, step // r), 0] = value.reshape(step // r, r, d)
        else:
            out_ref[pl.ds(i // (4 * r), step // (4 * r))] = value.reshape(step // (4 * r), 4, r, d)


def weight_grad(left_t, right, n, units, at, by_rows, into=None):
    d = 1024
    t = left_t.shape[1]
    r = d // n
    if by_rows:
        k = left_t.shape[0] // d
        ins = [(left_t, (d, t), lambda j: (j, 0)), (right, None, None)]
        block, where = (n // 4, 4, r, d), lambda j: (j, at // 4, 0, 0)
    else:
        k = right.shape[1] // d
        ins = [(left_t, None, None), (right, (t, d), lambda j: (0, j))]
        block, where = (n, 1, r, d), lambda j: (0, at + j, 0, 0)
    aliases = None
    if into is not None:
        ins.append((into, "any", None))
        aliases = {2: 0}
    return call(
        weight_kernel,
        (k,),
        ins,
        [((n, units, r, d), BF, block, where)],
        name="weight_grad",
        aliases=aliases,
        flops=2 * t * d * d * k,
        moved=2 * d * d * k + 2 * t * d * (k + 1),
    )[0]


def conv_out_kernel(d_ref, conv_ref, w_ref, vec_ref, dconv_ref, dout_ref, sums_ref):
    t = d_ref.shape[0]
    sums_ref[...] = jnp.zeros_like(sums_ref)
    w = flat(w_ref)
    for rows in cuts(t):
        dout = d_ref[rows, :].astype(BF)
        dout_ref[rows, :] = dout
        da = dot(dout, w, 1, 1)
        n, r = normal(conv_ref[rows, :])
        du = da * silu_slope(n * vec_ref[0:1, :] + vec_ref[1:2, :])
        dconv = normal_back(du, n, r, vec_ref[0:1, :])
        dconv_ref[rows, :] = dconv
        sums_ref[0:1, :] += total(dout.astype(F32))
        sums_ref[1:2, :] += total(du * n)
        sums_ref[2:3, :] += total(du)
        sums_ref[3:4, :] += total(dconv)


def conv_out_back(d3, conv, w, unit0, vec):
    t, d = d3.shape
    n, _, r, _ = w.shape
    return call(
        conv_out_kernel,
        (1,),
        [
            (d3, None, None),
            (conv, None, None),
            (w, (n, 1, r, d), lambda s: (0, unit0, 0, 0)),
            (vec, None, None),
        ],
        [((t, d), F32, None, None), ((t, d), BF, None, None), ((8, d), F32, None, None)],
        name="conv_out_back",
        flops=2 * t * d * d,
        moved=2 * d * d + 16 * t * d,
    )


def mid_back_kernel(odd_ref, dconv_ref, follow_ref, taps_ref, val_ref, sig_ref, second_ref, d3_ref, w_in_ref, w_attn_ref, vec_ref, d2_ref, dout_ref, dglu_ref, mine_ref, other_ref, sums_ref, pad, acc):
    s = pl.program_id(0)
    t, d = dconv_ref.shape

    @pl.when(s == 0)
    def _():
        for rows in cuts(t):
            pad[rows, :] = dconv_ref[rows, :]
        pad[t : t + 32, :] = follow_ref[...]

        def write(rows, cols, dgated):
            sig = sig_ref[rows, cols].astype(F32)
            dval = dgated * sig
            dglu_ref[rows, cols] = dval.astype(BF)
            dgate = dval * val_ref[rows, cols].astype(F32) * (1.0 - sig)
            dglu_ref[rows, cols.start + d : cols.stop + d] = dgate.astype(BF)

        fir(pad, taps_ref, 0, t, d, lambda cols: jnp.zeros((FIR_ROWS, FIR_COLS), F32), write, turned=True)
        sums_ref[...] = jnp.zeros_like(sums_ref)
        for rows in cuts(t):
            sums_ref[0:1, :] += total(dglu_ref[rows, :d].astype(F32))
            sums_ref[1:2, :] += total(dglu_ref[rows, d:].astype(F32))
        w = flat(w_in_ref)
        for rows in cuts(t):
            acc[rows, :] = dot(dglu_ref[rows, :d], w, 1, 1)

    @pl.when(s == 1)
    def _():
        w = flat(w_in_ref)
        w_attn = flat(w_attn_ref)
        odd = odd_ref[0] == 1
        half = d // 2
        for rows in cuts(t):
            du = acc[rows, :] + dot(dglu_ref[rows, d:], w, 1, 1)
            n, r = normal(second_ref[rows, :])
            d2 = d3_ref[rows, :] + normal_back(du, n, r, vec_ref[0:1, :])
            sums_ref[2:3, :] += total(du * n)
            sums_ref[3:4, :] += total(du)
            d2_ref[rows, :] = d2
            dout = d2.astype(BF)
            dout_ref[rows, :] = dout
            sums_ref[4:5, :] += total(dout.astype(F32))
            dm = dot(dout, w_attn, 1, 1)
            low, high = dm[:, :half], dm[:, half:]
            mine = jnp.where(odd, high, low).astype(BF)
            other = jnp.where(odd, low, high).astype(BF)
            for part in range(half // 128):
                cols = slice(part * 128, part * 128 + 128)
                mine_ref[part, rows, :] = mine[:, cols]
                other_ref[part, rows, :] = other[:, cols]


def mid_back(odd, dconv, follow, taps, val, sig, second, d3, w, u_attn, u_in, gain):
    t, d = d3.shape
    n, _, r, _ = w.shape
    return call(
        mid_back_kernel,
        (2,),
        [
            (odd, "smem", None),
            (dconv, None, None),
            (follow, None, None),
            (taps, None, None),
            (val, None, None),
            (sig, None, None),
            (second, None, None),
            (d3, None, None),
            (w, (n, 1, r, d), lambda s: (0, u_in + s, 0, 0)),
            (w, (n, 1, r, d), lambda s: (0, u_attn, 0, 0)),
            (gain, None, None),
        ],
        [
            ((t, d), F32, None, None),
            ((t, d), BF, None, None),
            ((t, 2 * d), BF, None, None),
            ((d // 256, t, 128), BF, None, None),
            ((d // 256, t, 128), BF, None, None),
            ((8, d), F32, None, None),
        ],
        [scr((t + 32, d), F32), scr((t, d), F32)],
        name="mid_back",
        flops=6 * t * d * d,
        moved=6 * d * d + 24 * t * d,
    )


def taps_kernel(dconv_ref, gated_ref, halo_ref, out_ref, pad, part):
    t, d = dconv_ref.shape
    reach = out_ref.shape[0]
    pad[0:32, :] = halo_ref[...].astype(F32)
    for rows in cuts(t):
        pad[pl.ds(rows.start + 32, CUT), :] = gated_ref[rows, :].astype(F32)
    part[...] = jnp.zeros_like(part)
    for c in range(0, d, COLS):
        cols = slice(c, c + COLS)

        def body(i, _):
            base = pl.multiple_of(i * ROWS, ROWS)
            window = pad[pl.ds(base, ROWS + 32), cols]
            here = dconv_ref[pl.ds(base, ROWS), cols]
            for b in range(8):
                sh = shifted(window, b)
                for a in range(0, 5):
                    m = 8 * a + b - 2
                    if 0 <= m < reach:
                        v = here * sh[8 * a : 8 * a + ROWS]
                        v = (v[0:8] + v[8:16]) + (v[16:24] + v[24:32])
                        part[8 * m : 8 * m + 8, cols] += v
            return 0

        lax.fori_loop(0, t // ROWS, body, 0)
    for m in range(reach):
        out_ref[m : m + 1, :] = total(part[8 * m : 8 * m + 8, :])


def taps_grad(dconv, gated, halo, reach):
    t, d = dconv.shape
    return call(
        taps_kernel,
        (1,),
        [(dconv, None, None), (gated, None, None), (halo, None, None)],
        [((reach, d), F32, None, None)],
        [scr((t + 32, d), F32), scr((8 * reach, d), F32)],
        name="taps_grad",
        flops=2 * t * d * reach,
        moved=6 * t * d,
    )[0]


def flipped_bit(index, mask):
    return index + mask - 2 * mask * lax.rem(lax.div(index, jnp.int32(mask)), jnp.int32(2))


def first_kernel(
    x_ref, w_ref, gains_ref, shifts_ref, taps_ref, bias_ref,
    inner_ref, act_ref, act_t_ref, unit_t_ref, tokens_ref, small_out_ref, w_out_ref,
    w, small, small_ref, tokens, unit, vec,
    own_send, own_recv, far_send, far_recv, core_send, core_recv, x_send, x_recv, x_load, w_leave,
):
    j = pl.program_id(0)
    n, k, r, d = w.shape
    t = tokens.shape[0]
    cut, thin_cut = r // 2, small.shape[1] // 2
    me, place = lax.axis_index("fsdp"), lax.axis_index("seq")
    two = jnp.int32(2)
    other_x, other_y, other_c = flipped_bit(me, 2), flipped_bit(me, 4), flipped_bit(me, 1)
    other_xy = flipped_bit(other_x, 4)
    to_x, to_y, to_c = {"fsdp": other_x}, {"fsdp": other_y}, {"fsdp": other_c}

    def send(src, dst, send_sem, recv_sem, device):
        return pltpu.make_async_remote_copy(
            src_ref=src, dst_ref=dst, send_sem=send_sem, recv_sem=recv_sem, device_id=device, device_id_type=MESH
        )

    def held(dev, u, rows=None):
        if u == k:
            return small.at[dev] if rows is None else small.at[dev, rows]
        return w.at[dev, u] if rows is None else w.at[dev, u, rows]

    def own(u):
        return small_ref if u == k else w_ref.at[u]

    def own_copies(u):
        return [
            send(own(u), held(me, u), own_send.at[i, u], own_recv.at[i, u], device)
            for i, device in enumerate((to_x, to_y, to_c))
        ]

    def keep_copy(u):
        return pltpu.make_async_copy(own(u), held(me, u), x_load.at[2 + u])

    def far_copies(u):
        half = thin_cut if u == k else cut
        top, low = pl.ds(0, half), pl.ds(half, half)
        return [
            send(held(other_x, u, top), held(other_x, u, top), far_send.at[0, u], far_recv.at[0, u], to_y),
            send(held(other_y, u, low), held(other_y, u, low), far_send.at[1, u], far_recv.at[1, u], to_x),
        ]

    def core_copy(i, u):
        dev = (other_x, other_y, other_xy)[i]
        return send(held(dev, u), held(dev, u), core_send.at[i, u], core_recv.at[i, u], to_c)

    def gather_begin(u):
        keep_copy(u).start()
        for copy in own_copies(u):
            copy.start()

    def gather_forward(u):
        across = own_copies(u)
        far = far_copies(u)
        across[0].wait_recv()
        far[0].start()
        core_copy(0, u).start()
        across[1].wait_recv()
        far[1].start()
        core_copy(1, u).start()

    def gather_far(u):
        for copy in far_copies(u):
            copy.wait_recv()
        core_copy(2, u).start()

    def gather_end(u):
        keep_copy(u).wait()
        own_copies(u)[2].wait_recv()
        for i in range(3):
            core_copy(i, u).wait_recv()

    def gather_sent(u):
        for copy in own_copies(u) + far_copies(u) + [core_copy(i, u) for i in range(3)]:
            copy.wait_send()

    side, half_of = lax.div(place, two), lax.rem(place, two)

    def token_rows(h):
        return pl.ds(pl.multiple_of(h * (t // 2), t // 2), t // 2)

    def token_copy(s):
        return send(x_ref.at[s], tokens.at[token_rows(half_of)], x_send.at[s], x_recv.at[half_of], {"seq": 2 * s + side})

    def token_keep(s):
        return pltpu.make_async_copy(x_ref.at[s], tokens.at[token_rows(half_of)], x_load.at[s])

    def token_arrived(h):
        return send(x_ref.at[0], tokens.at[token_rows(h)], x_send.at[0], x_recv.at[h], {"seq": flipped_bit(place, 1)})

    @pl.when(j == 0)
    def _():
        small_ref[...] = jnp.zeros_like(small_ref)
        at = 0
        for ref in (gains_ref, shifts_ref, taps_ref):
            small_ref[at : at + ref.shape[0], :] = ref[...]
            at += ref.shape[0]
        for layer in range(2):
            for q in range(4):
                row = at + 4 * layer + q
                small_ref[row : row + 1, :] = bias_ref[layer : layer + 1, q * r : (q + 1) * r]
        barrier = pltpu.get_barrier_semaphore()
        devices = [to_x, to_y, to_c, {"seq": flipped_bit(place, 1)}, {"seq": flipped_bit(place, 2)}, {"seq": 3 - place}]
        for device in devices:
            pl.semaphore_signal(barrier, inc=1, device_id=device, device_id_type=MESH)
        pl.semaphore_wait(barrier, 6)
        gather_begin(k)
        for s in range(2):
            away = 2 * s + side != place
            pl.when(away)(lambda s=s: token_copy(s).start())
            pl.when(jnp.logical_not(away))(lambda s=s: token_keep(s).start())
        for u in range(k):
            gather_begin(u)
        gather_forward(k)
        gather_far(k)
        gather_end(k)
        for dev in range(n):
            cols = slice(dev * r, (dev + 1) * r)
            vec[0:1, cols] = small[dev, 0:1, :].astype(F32)
            vec[1:2, cols] = small[dev, 6:7, :].astype(F32)
            for q in range(4):
                at = 4 * (dev % 2) + q
                vec[2 + dev // 2 : 3 + dev // 2, at * r : (at + 1) * r] = small[dev, 52 + q : 53 + q, :].astype(F32)
        gather_forward(0)
        gather_forward(1)
        for s in range(2):
            away = 2 * s + side != place
            pl.when(away)(lambda s=s: token_copy(s).wait_send())
            pl.when(jnp.logical_not(away))(lambda s=s: token_keep(s).wait())
        for h in range(2):
            pl.when(2 * half_of + h != place)(lambda h=h: token_arrived(h).wait_recv())
        gather_forward(2)
        gather_forward(3)
        for rows in cuts(t):
            c, _ = normal(tokens[rows, :].astype(F32))
            v = (c * vec[0:1, :] + vec[1:2, :]).astype(BF)
            unit[rows, :] = v
            unit_t_ref[:, rows] = v.T
        tokens_ref[...] = tokens[...]
        small_out_ref[...] = small[...]
        for u in range(k):
            gather_far(u)

    def leave(u):
        return pltpu.make_async_copy(w.at[:, u], w_out_ref.at[:, u], w_leave.at[u])

    for u in range(k):

        @pl.when(j == u)
        def _(u=u):
            gather_end(u)
            leave(u).start()

    weights = w[:, j].reshape(d, d)
    for rows in cuts(t):
        s = dot(unit[rows, :], weights, 1, 0) + vec[pl.ds(2 + j, 1), :]
        inner_ref[rows, :] = s.astype(BF)
        a = (s * jax.nn.sigmoid(s)).astype(BF)
        act_ref[rows, :] = a
        act_t_ref[:, rows] = a.T

    @pl.when(j == k - 1)
    def _():
        for u in range(k + 1):
            gather_sent(u)
        for u in range(k):
            leave(u).wait()


def first_forward(x, w, gains, shifts, taps, bias):
    _, half, d = x.shape
    k, r, _ = w.shape
    n, t = 8, 2 * half
    rows = 64
    dma = pltpu.SemaphoreType.DMA
    anywhere = pl.BlockSpec(memory_space=pl.ANY)

    def whole(*shape):
        return pl.BlockSpec(shape, lambda j: (0,) * len(shape))

    return pl.pallas_call(
        first_kernel,
        grid=(k,),
        in_specs=[anywhere] * 2 + [whole(*a.shape) for a in (gains, shifts, taps, bias)],
        out_specs=[
            pl.BlockSpec((t, d), lambda j: (0, j)),
            pl.BlockSpec((t, d), lambda j: (0, j)),
            pl.BlockSpec((d, t), lambda j: (j, 0)),
            whole(d, t),
            whole(t, d),
            whole(n, rows, r),
            anywhere,
        ],
        out_shape=[
            jax.ShapeDtypeStruct((t, k * d), BF),
            jax.ShapeDtypeStruct((t, k * d), BF),
            jax.ShapeDtypeStruct((k * d, t), BF),
            jax.ShapeDtypeStruct((d, t), BF),
            jax.ShapeDtypeStruct((t, d), BF),
            jax.ShapeDtypeStruct((n, rows, r), BF),
            jax.ShapeDtypeStruct((n, k, r, d), BF),
        ],
        scratch_shapes=[
            scr((n, k, r, d), BF),
            scr((n, rows, r), BF),
            scr((rows, r), BF),
            scr((t, d), BF),
            scr((t, d), BF),
            scr((8, d), F32),
            dma((3, k + 1)),
            dma((3, k + 1)),
            dma((2, k + 1)),
            dma((2, k + 1)),
            dma((3, k + 1)),
            dma((3, k + 1)),
            dma((2,)),
            dma((2,)),
            dma((2 + k + 1,)),
            dma((k,)),
        ],
        compiler_params=pltpu.CompilerParams(vmem_limit_bytes=VMEM, collective_id=3, has_side_effects=True),
        cost_estimate=pl.CostEstimate(flops=30_000_000_000, bytes_accessed=100_000_000, transcendentals=0),
        name="first",
    )(x, w, gains, shifts, taps, bias)


def middle_kernel(
    g_ref, w_ref, w_attn_ref, taps_ref, vec_ref, dy_in, third_in, conv_in, val_in, sig_in, second_in, result_ref,
    d2_ref, dout_2_ref, mine_ref, other_ref, sums_4_ref, sums_3_ref, sums_2_ref, dconv_out, dout_3_out, dglu_out, outputs_ref,
    dy_ref, third_ref, conv_ref, val_ref, sig_ref, second_ref, dout_3_ref, dglu_ref,
    acc, d3, pad, load_sem, leave_sem, halo_send, halo_recv, out_send, out_recv, out_keep,
):
    s = pl.program_id(0)
    t, d = third_ref.shape

    def load(i):
        src = (dy_in, third_in, conv_in, val_in, sig_in, second_in)[i]
        dst = (dy_ref, third_ref, conv_ref, val_ref, sig_ref, second_ref)[i]
        return pltpu.make_async_copy(src, dst, load_sem.at[i])

    def leave(i):
        src = (pad.at[pl.ds(0, t)], dout_3_ref, dglu_ref)[i]
        return pltpu.make_async_copy(src, (dconv_out, dout_3_out, dglu_out)[i], leave_sem.at[i])

    place = lax.axis_index("seq")
    two = jnp.int32(2)
    odd, seq = lax.rem(place, two), lax.div(place, two)
    partner = {"seq": flipped_bit(place, 1)}
    half = d // 2

    def halo_copy():
        return pltpu.make_async_remote_copy(
            src_ref=pad.at[pl.ds(0, 32)],
            dst_ref=pad.at[pl.ds(t, 32)],
            send_sem=halo_send,
            recv_sem=halo_recv,
            device_id=partner,
            device_id_type=MESH,
        )

    def out_copy(h, to, s):
        return pltpu.make_async_remote_copy(
            src_ref=result_ref.at[pl.ds(h * (t // 2), t // 2)],
            dst_ref=outputs_ref.at[s],
            send_sem=out_send.at[h],
            recv_sem=out_recv.at[s],
            device_id={"seq": to},
            device_id_type=MESH,
        )

    def out_stay(h):
        return pltpu.make_async_copy(result_ref.at[pl.ds(h * (t // 2), t // 2)], outputs_ref.at[seq], out_keep)

    @pl.when(s == 0)
    def _():
        for i in range(6):
            load(i).start()
        barrier = pltpu.get_barrier_semaphore()
        for device in (partner, {"seq": flipped_bit(place, 2)}, {"seq": 3 - place}):
            pl.semaphore_signal(barrier, inc=1, device_id=device, device_id_type=MESH)
        pl.semaphore_wait(barrier, 3)
        for h in range(2):
            away = 2 * odd + h != place
            pl.when(away)(lambda h=h: out_copy(h, 2 * odd + h, seq).start())
            pl.when(jnp.logical_not(away))(lambda h=h: out_stay(h).start())
        for ref in (sums_4_ref, sums_3_ref, sums_2_ref):
            ref[...] = jnp.zeros_like(ref)

    w = flat(w_ref)

    @pl.when(s < 4)
    def _():
        for rows in cuts(t):
            p = dot(g_ref[rows, :], w, 1, 1)
            acc[rows, :] = p + jnp.where(s == 0, 0.0, acc[rows, :])

    @pl.when(s == 3)
    def _():
        load(0).wait()
        load(1).wait()
        for rows in cuts(t):
            n, r = normal(third_ref[rows, :])
            du = acc[rows, :]
            value = dy_ref[rows, :] + normal_back(du, n, r, vec_ref[0:1, :])
            d3[rows, :] = value
            dout = value.astype(BF)
            dout_3_ref[rows, :] = dout
            sums_4_ref[0:1, :] += total(du * n)
            sums_4_ref[1:2, :] += total(du)
            sums_3_ref[0:1, :] += total(dout.astype(F32))
        leave(1).start()

    @pl.when(s == 4)
    def _():
        load(2).wait()
        for i, rows in enumerate(cuts(t)):
            da = dot(dout_3_ref[rows, :], w, 1, 1)
            n, r = normal(conv_ref[rows, :])
            du = da * silu_slope(n * vec_ref[1:2, :] + vec_ref[2:3, :])
            dconv = normal_back(du, n, r, vec_ref[1:2, :])
            pad[rows, :] = dconv
            sums_3_ref[1:2, :] += total(du * n)
            sums_3_ref[2:3, :] += total(du)
            sums_3_ref[3:4, :] += total(dconv)
            if i == 0:

                @pl.when(odd == 1)
                def _():
                    halo_copy().start()
                    pad[t : t + 32, :] = jnp.zeros((32, d), F32)

        leave(0).start()

    @pl.when(s == 5)
    def _():
        load(3).wait()
        load(4).wait()
        pl.when(odd == 1)(lambda: halo_copy().wait_send())
        pl.when(odd == 0)(lambda: halo_copy().wait_recv())

        def write(rows, cols, dgated):
            sig = sig_ref[rows, cols].astype(F32)
            dval = dgated * sig
            dglu_ref[rows, cols] = dval.astype(BF)
            dgate = dval * val_ref[rows, cols].astype(F32) * (1.0 - sig)
            dglu_ref[rows, cols.start + d : cols.stop + d] = dgate.astype(BF)

        fir(pad, taps_ref, 0, t, d, lambda cols: jnp.zeros((FIR_ROWS, FIR_COLS), F32), write, turned=True)
        for rows in cuts(t):
            sums_2_ref[0:1, :] += total(dglu_ref[rows, :d].astype(F32))
            sums_2_ref[1:2, :] += total(dglu_ref[rows, d:].astype(F32))
            acc[rows, :] = dot(dglu_ref[rows, :d], w, 1, 1)
        leave(2).start()

    @pl.when(s == 6)
    def _():
        load(5).wait()
        w_attn = flat(w_attn_ref)
        for rows in cuts(t):
            du = acc[rows, :] + dot(dglu_ref[rows, d:], w, 1, 1)
            n, r = normal(second_ref[rows, :])
            d2 = d3[rows, :] + normal_back(du, n, r, vec_ref[3:4, :])
            sums_2_ref[2:3, :] += total(du * n)
            sums_2_ref[3:4, :] += total(du)
            d2_ref[rows, :] = d2
            dout = d2.astype(BF)
            dout_2_ref[rows, :] = dout
            sums_2_ref[4:5, :] += total(dout.astype(F32))
            dm = dot(dout, w_attn, 1, 1)
            low, high = dm[:, :half], dm[:, half:]
            mine = jnp.where(odd == 1, high, low).astype(BF)
            other = jnp.where(odd == 1, low, high).astype(BF)
            for part in range(half // 128):
                cols = slice(part * 128, part * 128 + 128)
                mine_ref[part, rows, :] = mine[:, cols]
                other_ref[part, rows, :] = other[:, cols]
        for i in range(3):
            leave(i).wait()
        for h in range(2):
            away = 2 * odd + h != place
            pl.when(away)(lambda h=h: out_copy(h, 2 * odd + h, seq).wait_send())
            pl.when(jnp.logical_not(away))(lambda h=h: out_stay(h).wait())
        for q in range(2):
            pl.when(2 * q + seq != place)(lambda q=q: out_copy(0, flipped_bit(place, 1), q).wait_recv())


def middle_back(dy, g, third, conv, val, sig, second, w, taps, vec, result):
    t, d = dy.shape
    n, _, r, _ = w.shape
    dma = pltpu.SemaphoreType.DMA

    def whole(*shape):
        return pl.BlockSpec(shape, lambda s: (0,) * len(shape))

    anywhere = pl.BlockSpec(memory_space=pl.ANY)
    outs = [
        ((t, d), F32), ((t, d), BF), ((d // 256, t, 128), BF), ((d // 256, t, 128), BF),
        ((8, d), F32), ((8, d), F32), ((8, d), F32),
    ]
    far = [((t, d), F32), ((t, d), BF), ((t, 2 * d), BF), ((2, t // 2, d), BF)]
    d2, dout_2, mine, other, sums_4, sums_3, sums_2, dconv, dout_3, dglu, result = pl.pallas_call(
        middle_kernel,
        grid=(7,),
        in_specs=[
            pl.BlockSpec((t, d), lambda s: (0, jnp.minimum(s, 3))),
            pl.BlockSpec((n, 1, r, d), lambda s: (0, jnp.where(s == 4, 7, s), 0, 0)),
            pl.BlockSpec((n, 1, r, d), lambda s: (0, 4, 0, 0)),
            whole(*taps.shape),
            whole(*vec.shape),
        ]
        + [anywhere] * 7,
        out_specs=[whole(*shape) for shape, _ in outs] + [anywhere] * 4,
        out_shape=[jax.ShapeDtypeStruct(shape, kind) for shape, kind in outs + far],
        scratch_shapes=[
            scr((t, d), F32), scr((t, d), F32), scr((t, d), F32), scr((t, d), BF), scr((t, d), BF), scr((t, d), F32),
            scr((t, d), BF), scr((t, 2 * d), BF),
            scr((t, d), F32), scr((t, d), F32), scr((t + 32, d), F32),
            dma((6,)), dma((3,)), dma, dma, dma((2,)), dma((2,)), dma,
        ],
        compiler_params=pltpu.CompilerParams(vmem_limit_bytes=58 << 20, collective_id=4, has_side_effects=True),
        cost_estimate=pl.CostEstimate(flops=40_000_000_000, bytes_accessed=120_000_000, transcendentals=0),
        name="middle_back",
    )(g, w, w, taps, vec, dy, third, conv, val, sig, second, result)
    return dconv, dout_3, d2, dout_2, dglu, mine, other, sums_4, sums_3, sums_2, result


ORDER = [
    ("q", 0), ("q", 1), ("q", 2), ("m", 0), ("m", 1), ("in", 0), ("m", 2), ("in", 1), ("m", 3),
    ("in", 2), ("out", 0), ("in", 3), ("out", 1), ("out", 2), ("out", 3),
]
N_CHUNK = len(ORDER)
FIRST_IN = 5
LAST_IN = 11
AHEAD = 2
HELD = 6


def thin(count):
    return [pl.ds(i, 128) for i in range(0, count, 128)]


def last_kernel(
    gain_ref, table_ref, sums_2_ref, sums_3_ref, sums_4_ref, sums_5_ref, sums_7_ref, dbias_ref,
    d2_ref, first_ref, x_ref, dconv_ref, gated_ref, halo_ref, part_ref, dqkv_ref, unit_q_ref, act_ref, unit_ref, inner_ref, w_out_ref, w_in_ref,
    mixed_ref, dout_2_ref, unit_2_ref, dglu_ref, act_c_ref, dout_3_ref,
    out_ref, out_part_ref, small_out_ref, table_out_ref, dx_ref,
    odd, even, core, first, second, whole, near, far,
    left, right, wo, wi, inner, dout, acc,
    small_0, small_y, small_x, small_c, small_z, table_got, d0, d1, some, dconv, gated, pad, taps,
    left_sem, right_sem, wo_sem, wi_sem, inner_sem, out_sem, part_sem, d1_sem, some_sem, taps_sem,
    core_send, core_recv, first_send, first_recv, second_send, second_recv,
    z_send, z_recv, small_send, small_recv, table_send, table_recv, dx_send, dx_recv, dx_sem, free_sem,
):
    r, d = out_ref.shape[1:]
    n_part = part_ref.shape[0]
    t = x_ref.shape[0]
    cut = r // 2
    me = lax.axis_index("fsdp")
    place = lax.axis_index("seq")
    two, four = jnp.int32(2), jnp.int32(4)
    chip = lax.div(me, two)
    bit_c, bit_x, bit_y = lax.rem(me, two), lax.rem(chip, two), lax.div(me, four)
    middle = lax.rem(lax.div(place + 1, two), two)
    to_c = {"fsdp": flipped_bit(me, 1)}
    to_x = {"fsdp": flipped_bit(me, 2)}
    to_y = {"fsdp": flipped_bit(me, 4)}
    to_1 = {"seq": flipped_bit(place, 1)}
    to_2 = {"seq": 3 - place}

    barrier = pltpu.get_barrier_semaphore()
    for device in (to_c, to_x, to_y, to_1, to_2, {"seq": flipped_bit(place, 2)}):
        pl.semaphore_signal(barrier, inc=1, device_id=device, device_id_type=MESH)

    def send(src, dst, send_sem, recv_sem, device):
        return pltpu.make_async_remote_copy(
            src_ref=src, dst_ref=dst, send_sem=send_sem, recv_sem=recv_sem, device_id=device, device_id_type=MESH
        )

    def at_2(c):
        return lax.rem(c, two)

    def at_3(c):
        return lax.rem(c, jnp.int32(3))

    def on(c, begin, end, work):
        pl.when((c >= begin) & (c < end))(lambda: work(c))

    def factor_copies(c, name, unit):
        cols = slice(unit * d, unit * d + d)
        lefts = {"q": unit_q_ref, "in": unit_ref, "m": (mixed_ref, unit_2_ref, unit_2_ref, act_c_ref)[unit % 4]}
        rights = {
            "q": lambda: dqkv_ref.at[:, cols],
            "m": lambda: (
                dout_2_ref if unit == 0 else dout_3_ref if unit == 3 else dglu_ref.at[:, (unit - 1) * d : unit * d]
            ),
        }
        src = act_ref.at[:, unit] if name == "out" else lefts[name]
        copies = [pltpu.make_async_copy(src, left.at[at_2(c)], left_sem.at[at_2(c)])]
        if name in rights:
            copies.append(pltpu.make_async_copy(rights[name](), right.at[at_3(c)], right_sem.at[at_3(c)]))
        return copies

    def fetch(c):
        for i, (name, unit) in enumerate(ORDER):

            @pl.when(c == i)
            def _(i=i, name=name, unit=unit):
                for copy in factor_copies(c, name, unit):
                    copy.start()

    def fetched(c):
        pltpu.make_async_copy(unit_ref, left.at[at_2(c)], left_sem.at[at_2(c)]).wait()
        has_right = functools.reduce(
            jnp.logical_or, [c == i for i, (name, _) in enumerate(ORDER) if name in ("q", "m")]
        )

        @pl.when(has_right)
        def _():
            pltpu.make_async_copy(dout_2_ref, right.at[at_3(c)], right_sem.at[at_3(c)]).wait()

    def is_in(c):
        return (c >= FIRST_IN) & (c <= LAST_IN) & (at_2(c) == FIRST_IN % 2)

    def wo_copy(j):
        return pltpu.make_async_copy(w_out_ref.at[pl.ds(2 * j, 2), pl.ds(0, 4)], wo, wo_sem)

    def wi_copy(j):
        return pltpu.make_async_copy(w_in_ref.at[:, j], wi, wi_sem)

    def wq_copy(i):
        return pltpu.make_async_copy(w_out_ref.at[:, 4 + i], wi, wi_sem)

    def inner_copy(j):
        return pltpu.make_async_copy(inner_ref.at[:, pl.ds(pl.multiple_of(j * d, d), d)], inner, inner_sem)

    def x_copy():
        return pltpu.make_async_copy(x_ref, inner, inner_sem)

    row = 53

    def hidden(c):
        j = lax.div(c - FIRST_IN, two)
        wo_copy(j).wait()
        inner_copy(j).wait()
        w = wo[...].reshape(d, d)
        dbias = jnp.zeros((1, d), F32)
        for rows in thin(t):
            da = dot(dout[rows, :], w, 1, 1)
            v = (da * silu_slope(inner[rows, :].astype(F32))).astype(BF)
            right[at_3(c), rows, :] = v
            dbias = dbias + total(v.astype(F32))
        for dev in range(2):
            for q in range(4):
                cols = pl.ds(pl.multiple_of((2 * j + dev) * r, r), r)
                small_0[row + 3 + q : row + 4 + q, cols] = dbias[:, dev * 4 * r + q * r : dev * 4 * r + (q + 1) * r]

        @pl.when(j < 3)
        def _():
            wo_copy(j + 1).start()
            inner_copy(j + 1).start()

        @pl.when(j == 3)
        def _():
            x_copy().start()

    def product(c):
        for i in range(4):
            value = dot(left[at_2(c), 2 * i : 2 * i + 2].reshape(2 * r, t), right[at_3(c)], 1, 0).astype(BF)
            low, high = value[:r], value[r:]
            p = i + bit_x - 2 * bit_x * (i % 2)
            p = p + 2 * bit_y - 4 * bit_y * lax.div(p, two)
            even[at_2(c), p] = jnp.where(bit_c == 0, low, high)
            odd[at_2(c), p] = jnp.where(bit_c == 0, high, low)

    def through(c, fresh):
        wi_copy(0).wait()
        w = wi[...].reshape(d, d)
        for rows in thin(t):
            p = dot(right[at_3(c), rows, :], w, 1, 1)
            acc[rows, :] = p + jnp.where(fresh, 0.0, acc[rows, :])

    def back(c):
        j = lax.div(c - FIRST_IN, two)
        through(c, j == 0)
        pl.when(j < 3)(lambda: wi_copy(j + 1).start())

    def back_q(c):
        through(c, c == 0)
        pl.when(c < 2)(lambda: wq_copy(c + 1).start())
        pl.when(c == 2)(lambda: wi_copy(0).start())
        column = total(right[at_3(c)].astype(F32))

        @pl.when(c == 0)
        def _():
            small_0[11:12, :] = column

        @pl.when(c == 2)
        def _():
            small_0[12:13, :] = column
            middle_gradient()

    def middle_gradient():
        pltpu.make_async_copy(d2_ref, d1, d1_sem).wait()
        copies = [
            pltpu.make_async_copy(first_ref.at[rows], some.at[i % 2], some_sem.at[i % 2]) for i, rows in enumerate(thin(t))
        ]
        for i, rows in enumerate(thin(t)):
            copies[i].wait()
            n, scale = normal(some[i % 2])
            du = acc[rows, :]
            value = d1[rows, :] + normal_back(du, n, scale, gain_ref[1:2, :])
            d1[rows, :] = value
            small_0[0:1, :] += total(du * n)
            small_0[5:6, :] += total(du)
            v = (HALF * value).astype(BF)
            dout[rows, :] = v
            small_0[row + 2 : row + 3, :] += total(v.astype(F32))
            if i + 2 < len(copies):
                copies[i + 2].start()

    def first_rows(i):
        return pltpu.make_async_copy(first_ref.at[pl.ds(128 * i, 128)], some.at[i], some_sem.at[i])

    def taps_copies(b):
        cols = pl.ds(pl.multiple_of(b * COLS, COLS), COLS)
        return [
            pltpu.make_async_copy(dconv_ref.at[:, cols], dconv, taps_sem.at[0]),
            pltpu.make_async_copy(halo_ref.at[:, cols], gated.at[pl.ds(0, 32)], taps_sem.at[1]),
            pltpu.make_async_copy(gated_ref.at[:, cols], gated.at[pl.ds(32, t)], taps_sem.at[2]),
        ]

    def taps_columns(b):
        for copy in taps_copies(b):
            copy.wait()
        pad[...] = gated[...].astype(F32)
        taps[...] = jnp.zeros_like(taps)
        reach = taps.shape[0] // 8

        def body(i, _):
            base = pl.multiple_of(i * ROWS, ROWS)
            window = pad[pl.ds(base, ROWS + 32), :]
            here = dconv[pl.ds(base, ROWS), :]
            for q in range(8):
                sh = shifted(window, q)
                for a in range(0, 5):
                    m = 8 * a + q - 2
                    if 0 <= m < reach:
                        v = here * sh[8 * a : 8 * a + ROWS]
                        taps[8 * m : 8 * m + 8, :] += (v[0:8] + v[8:16]) + (v[16:24] + v[24:32])
            return 0

        lax.fori_loop(0, t // ROWS, body, 0)
        cols = pl.ds(pl.multiple_of(b * COLS, COLS), COLS)
        for m in range(reach):
            small_0[18 + m : 19 + m, cols] = total(taps[8 * m : 8 * m + 8, :])

        @pl.when(b < d // COLS - 1)
        def _():
            for copy in taps_copies(b + 1):
                copy.start()

    def held_at(c):
        return lax.rem(c, jnp.int32(HELD))

    def core_copy(c):
        return send(odd.at[at_2(c)], core.at[held_at(c)], core_send.at[c], core_recv.at[c], to_c)

    def make(c):
        fetch(c + 1)
        fetched(c)

        is_out = functools.reduce(jnp.logical_or, [c == i for i, (name, _) in enumerate(ORDER) if name == "out"])

        @pl.when(is_out)
        def _():
            right[at_3(c)] = dout[...]

        pl.when(is_in(c))(lambda: hidden(c))
        product(c)
        pl.when(c >= HELD)(lambda: pl.semaphore_wait(free_sem, 1))
        core_copy(c).start()

    def make_back(c):
        pl.when(is_in(c))(lambda: back(c))
        pl.when(c < 3)(lambda: back_q(c))

    def first_copies(c):
        top, rest = pl.ds(0, cut), pl.ds(cut, cut)
        o = held_at(c)
        return [
            send(core.at[o, 1, top], first.at[o, 0, 0], first_send.at[c, 0], first_recv.at[c, 0], to_x),
            send(core.at[o, 3, top], first.at[o, 0, 1], first_send.at[c, 1], first_recv.at[c, 1], to_x),
            send(core.at[o, 2, rest], first.at[o, 1, 0], first_send.at[c, 2], first_recv.at[c, 2], to_y),
            send(core.at[o, 3, rest], first.at[o, 1, 1], first_send.at[c, 3], first_recv.at[c, 3], to_y),
        ]

    def second_copies(c):
        o = held_at(c)
        return [
            send(first.at[o, 0, 1], second.at[o, 0], second_send.at[c, 0], second_recv.at[c, 0], to_y),
            send(first.at[o, 1, 1], second.at[o, 1], second_send.at[c, 1], second_recv.at[c, 1], to_x),
        ]

    def add_core(c):
        core_copy(c).wait()
        o = held_at(c)

        def rows(i, _):
            at = pl.ds(pl.multiple_of(i * 32, 32), 32)
            for b in range(4):
                core[o, b, at] = (core[o, b, at].astype(F32) + even[at_2(c), b, at].astype(F32)).astype(BF)
            return 0

        lax.fori_loop(0, r // 32, rows, 0)
        for copy in first_copies(c):
            copy.start()

    def add_first(c):
        for copy in first_copies(c):
            copy.wait()
        o = held_at(c)

        def rows(i, _):
            at = pl.ds(pl.multiple_of(i * 32, 32), 32)
            low_at = pl.ds(pl.multiple_of(cut + i * 32, 32), 32)
            for b in range(2):
                first[o, 0, b, at] = (first[o, 0, b, at].astype(F32) + core[o, 2 * b, at].astype(F32)).astype(BF)
                first[o, 1, b, at] = (first[o, 1, b, at].astype(F32) + core[o, b, low_at].astype(F32)).astype(BF)
            return 0

        lax.fori_loop(0, cut // 32, rows, 0)

        @pl.when(c < N_CHUNK - HELD)
        def _():
            pl.semaphore_signal(free_sem, inc=1, device_id=to_c, device_id_type=MESH)

        for copy in second_copies(c):
            copy.start()

    def add_second(c):
        for copy in second_copies(c):
            copy.wait()
        o = held_at(c)
        whole[c, 0:cut] = (first[o, 0, 0].astype(F32) + second[o, 0].astype(F32)).astype(BF)
        whole[c, cut:r] = (first[o, 1, 0].astype(F32) + second[o, 1].astype(F32)).astype(BF)
        z_begin(c)

    z_begin, z_step = z_line(middle, to_1, to_2, whole, near, far, z_send, z_recv)

    def result_do(i, act):
        for is_middle, src in ((1, far), (0, near)):
            chunk = pltpu.make_async_copy(src.at[i], out_ref.at[i], out_sem.at[i])
            part = pltpu.make_async_copy(src.at[i], out_part_ref.at[i - N_CHUNK], out_sem.at[i])
            pl.when((middle == is_middle) & (i < N_CHUNK))(lambda chunk=chunk: act(chunk))
            pl.when((middle == is_middle) & (i >= N_CHUNK))(lambda part=part: act(part))

    def z_stage(i, stage):
        z_step(i, stage)
        if stage == 2:
            result_do(i, lambda copy: copy.start())

    wide = [d // 2, d // 4, d // 8]
    bits = [bit_y, bit_x, bit_c]
    held = [small_0, small_y, small_x, small_c]
    partner = [to_y, to_x, to_c, to_1, to_2]

    def columns(step, bit):
        return pl.ds(pl.multiple_of(bit * wide[step], wide[step]), wide[step])

    def small_copy(step):
        sems = (small_send.at[step], small_recv.at[step])
        if step < 3:
            return send(held[step].at[:, columns(step, 1 - bits[step])], held[step + 1], *sems, partner[step])
        if step == 3:
            return send(small_c, small_z.at[0], *sems, partner[step])
        return send(small_z.at[0], small_z.at[1], *sems, partner[step])

    def small_step(step):
        small_copy(step).wait()
        if step < 3:
            held[step + 1][...] += held[step][:, columns(step, bits[step])]
        elif step == 3:
            small_z[0] = small_z[0] + small_c[...]
        else:
            small_out_ref[...] = small_z[0] + small_z[1]
        if step < 4:
            small_copy(step + 1).start()

    def table_copy(step):
        src = table_ref if step == 0 else table_got.at[step - 1]
        return send(src, table_got.at[step], table_send.at[step], table_recv.at[step], partner[step])

    def table_step(step):
        table_copy(step).wait()
        before = table_ref[...] if step == 0 else table_got[step - 1]
        table_got[step] = table_got[step] + before
        if step < 4:
            table_copy(step + 1).start()
        else:
            table_out_ref[...] = table_got[step]

    mine, seq = lax.rem(place, two), lax.div(place, two)

    def dx_copy(h):
        return send(d0.at[pl.ds(h * (t // 2), t // 2)], dx_ref.at[seq], dx_send.at[h], dx_recv.at[seq], {"seq": 2 * mine + h})

    def dx_keep(h):
        return pltpu.make_async_copy(d0.at[pl.ds(h * (t // 2), t // 2)], dx_ref.at[seq], dx_sem)

    def dx_arrived(s):
        return send(d0.at[pl.ds(0, t // 2)], dx_ref.at[s], dx_send.at[0], dx_recv.at[s], to_1)

    def input_gradient():
        x_copy().wait()
        for rows in thin(t):
            n, scale = normal(inner[rows, :].astype(F32))
            du = acc[rows, :]
            d0[rows, :] = (d1[rows, :] + normal_back(du, n, scale, gain_ref[0:1, :])).astype(BF)
            small_0[row : row + 1, :] += total(du * n)
            small_0[row + 1 : row + 2, :] += total(du)
        for h in range(2):
            away = 2 * mine + h != place
            pl.when(away)(lambda h=h: dx_copy(h).start())
            pl.when(jnp.logical_not(away))(lambda h=h: dx_keep(h).start())
        small_copy(0).start()

    def part_copy(i):
        return pltpu.make_async_copy(part_ref.at[i], whole.at[N_CHUNK + i], part_sem.at[i])

    def part_begin(i):
        part_copy(i).wait()
        z_begin(N_CHUNK + i)

    fetch(jnp.int32(0))
    wq_copy(0).start()
    pltpu.make_async_copy(d2_ref, d1, d1_sem).start()
    for i in range(2):
        first_rows(i).start()
    for copy in taps_copies(jnp.int32(0)):
        copy.start()
    for i in range(n_part):
        part_copy(i).start()
    wo_copy(0).start()
    inner_copy(0).start()
    small_0[...] = jnp.zeros_like(small_0)
    here = {1: (sums_2_ref, 2), 2: (sums_3_ref, 1), 3: (sums_4_ref, 0), 4: (sums_5_ref, 0), 6: (sums_2_ref, 3)}
    here.update({7: (sums_3_ref, 2), 8: (sums_4_ref, 1), 9: (sums_5_ref, 1), 10: (sums_7_ref, 0), 13: (sums_2_ref, 4)})
    here.update({14: (sums_2_ref, 0), 15: (sums_2_ref, 1), 16: (sums_3_ref, 3), 17: (sums_3_ref, 0)})
    for at, (ref, i) in here.items():
        small_0[at : at + 1, :] = ref[i : i + 1, :]
    for j in range(4):
        for dev in range(2):
            for q in range(4):
                cols = slice((2 * j + dev) * r, (2 * j + dev + 1) * r)
                small_0[49 + q : 50 + q, cols] = dbias_ref[j, :, (4 * dev + q) * r : (4 * dev + q + 1) * r]
    pl.semaphore_wait(barrier, 6)
    table_copy(0).start()
    for c in range(AHEAD):
        make(jnp.int32(c))

    def slot(k, _):
        on(k, 0, N_CHUNK, add_core)
        on(k - 1, 0, N_CHUNK, add_first)
        on(k - 2, 0, N_CHUNK, add_second)
        for stage in range(3):
            on(k - 3 - stage, 0, N_CHUNK, lambda c, stage=stage: z_stage(c, stage))
        for h in range(2):
            on(2 * k + h, 0, n_part, part_begin)
            for stage in range(3):
                on(2 * (k - 1 - stage) + h, 0, n_part, lambda i, stage=stage: z_stage(N_CHUNK + i, stage))
        make_back(k)
        on(k + AHEAD, 0, N_CHUNK, make)
        pl.when(k == LAST_IN)(input_gradient)
        for b in range(d // COLS):
            pl.when(k == 4 + 2 * b)(lambda b=b: taps_columns(jnp.int32(b)))
        for step in range(5):
            pl.when(k == step)(lambda step=step: table_step(step))
            pl.when(k == LAST_IN + 1 + step)(lambda step=step: small_step(step))
        return 0

    lax.fori_loop(0, N_CHUNK + 5, slot, 0)
    for h in range(2):
        away = 2 * mine + h != place
        pl.when(away)(lambda h=h: dx_copy(h).wait_send())
        pl.when(jnp.logical_not(away))(lambda h=h: dx_keep(h).wait())
    for s in range(2):
        from_away = 2 * s + lax.div(place, two) != place
        pl.when(from_away)(lambda s=s: dx_arrived(s).wait_recv())

    def settle(i, _):
        result_do(i, lambda copy: copy.wait())
        return 0

    lax.fori_loop(0, N_CHUNK + n_part, settle, 0)


def last_reduced(
    gain, table, sums, dbias, d2, first, tokens, dconv, gated, halo, part, dqkv, unit_q, act_t, unit_t, inner, w_out, w_in, mixed_t, dout_2, unit_2, dglu, act_c, dout_3
):
    n, _, r, d = w_in.shape
    t = tokens.shape[0]
    rows = 64
    k = N_CHUNK
    m = part.shape[0]
    z = k + m
    dma = pltpu.SemaphoreType.DMA
    anywhere = pl.BlockSpec(memory_space=pl.ANY)
    vmem = pl.BlockSpec(memory_space=pltpu.VMEM)
    return pl.pallas_call(
        last_kernel,
        in_specs=[vmem] * 8 + [anywhere] * 20,
        out_specs=[anywhere, anywhere, vmem, vmem, anywhere],
        out_shape=[
            jax.ShapeDtypeStruct((k, r, d), BF),
            jax.ShapeDtypeStruct((m, r, d), BF),
            jax.ShapeDtypeStruct((rows, d // 8), F32),
            jax.ShapeDtypeStruct(table.shape, F32),
            jax.ShapeDtypeStruct((2, t // 2, d), BF),
        ],
        scratch_shapes=[
            scr((2, 4, r, d), BF),
            scr((2, 4, r, d), BF),
            scr((HELD, 4, r, d), BF),
            scr((HELD, 2, 2, r // 2, d), BF),
            scr((HELD, 2, r // 2, d), BF),
            scr((z, r, d), BF),
            scr((z, r, d), BF),
            scr((z, r, d), BF),
            scr((2, n, r, t), BF),
            scr((3, t, d), BF),
            scr((2, 4, r, d), BF),
            scr((n, r, d), BF),
            scr((t, d), BF),
            scr((t, d), BF),
            scr((t, d), F32),
            scr((rows, d), F32),
            scr((rows, d // 2), F32),
            scr((rows, d // 4), F32),
            scr((rows, d // 8), F32),
            scr((2, rows, d // 8), F32),
            scr((5,) + table.shape, F32),
            scr((t, d), BF),
            scr((t, d), F32),
            scr((2, 128, d), F32),
            scr((t, COLS), F32),
            scr((t + 32, COLS), BF),
            scr((t + 32, COLS), F32),
            scr((8 * 31, COLS), F32),
            dma((2,)),
            dma((3,)),
            dma,
            dma,
            dma,
            dma((z,)),
            dma((m,)),
            dma,
            dma((2,)),
            dma((3,)),
            dma((k,)),
            dma((k,)),
            dma((k, 4)),
            dma((k, 4)),
            dma((k, 2)),
            dma((k, 2)),
            dma((z, 3)),
            dma((z, 3)),
            dma((5,)),
            dma((5,)),
            dma((5,)),
            dma((5,)),
            dma((2,)),
            dma((2,)),
            dma,
            pltpu.SemaphoreType.REGULAR,
        ],
        compiler_params=pltpu.CompilerParams(vmem_limit_bytes=60 << 20, collective_id=0, has_side_effects=True),
        cost_estimate=pl.CostEstimate(flops=100_000_000_000, bytes_accessed=400_000_000, transcendentals=0),
        name="last",
    )(
        gain, table, *sums, dbias, d2, first, tokens, dconv, gated, halo, part, dqkv, unit_q.reshape(n, r, t), act_t.reshape(n, 4, r, t),
        unit_t.reshape(n, r, t), inner, w_out, w_in,
        mixed_t.reshape(n, r, t), dout_2, unit_2.reshape(n, r, t), dglu, act_c.reshape(n, r, t), dout_3,
    )


PLACE = {item: i for i, item in enumerate(ORDER)}


def finish_kernel(n_tap, main, in_b, out_b, small, table, result, dx, g_in, g_out, g_qkv, g_attn, g_conv_in, g_conv_out, g_taps, g_gain, g_shift, g_bias, g_table, g_result, g_dx):
    g_result[...] = result[...]
    g_dx[...] = dx[...]
    d = main.shape[-1]

    def of(name, unit):
        return main[PLACE[name, unit]].astype(F32)

    for u in range(4):
        cols = slice(u * d, (u + 1) * d)
        g_in[0, :, cols] = of("in", u)
        g_in[1, :, cols] = in_b[u].astype(F32)
        g_out[0, u] = of("out", u)
        g_out[1, u] = out_b[u].astype(F32)
    for u in range(3):
        g_qkv[u] = of("q", u)
    g_attn[...] = of("m", 0)
    g_conv_in[:, :d] = of("m", 1)
    g_conv_in[:, d:] = of("m", 2)
    g_conv_out[...] = of("m", 3)
    w = g_taps.shape[1]
    early, late = 0, 22 + n_tap
    g_taps[...] = small[18 : 18 + n_tap, :]
    g_gain[0:1, :] = small[late : late + 1, :]
    g_gain[1:6, :] = small[0:5, :]
    g_shift[0:1, :] = small[late + 1 : late + 2, :]
    g_shift[1:6, :] = small[5:10, :]
    g_shift[6:7, :] = small[late + 2 : late + 3, :]
    g_shift[7:15, :] = small[10:18, :]
    for u in range(4):
        g_bias[0:1, u * w : (u + 1) * w] = small[late + 3 + u : late + 4 + u, :]
        g_bias[1:2, u * w : (u + 1) * w] = small[18 + n_tap + u : 19 + n_tap + u, :]
    k, h = g_table.shape
    g_table[...] = table[0:k, 0:h] + table[0:k, h : 2 * h]


def finished(main, in_b, out_b, small, table, result, dx, n_tap, table_shape):
    k, r, d = main.shape
    w = small.shape[1]
    step = min(r, 32)

    def rows(count):
        return pl.BlockSpec((count, step, d), lambda i: (0, i, 0))

    def whole(*shape):
        return pl.BlockSpec(shape, lambda i: (0,) * len(shape))

    outs = [
        ((2, r, 4 * d), pl.BlockSpec((2, step, 4 * d), lambda i: (0, i, 0))),
        ((2, 4, r, d), pl.BlockSpec((2, 4, step, d), lambda i: (0, 0, i, 0))),
        ((3, r, d), rows(3)),
        ((r, d), pl.BlockSpec((step, d), lambda i: (i, 0))),
        ((r, 2 * d), pl.BlockSpec((step, 2 * d), lambda i: (i, 0))),
        ((r, d), pl.BlockSpec((step, d), lambda i: (i, 0))),
        ((n_tap, w), whole(n_tap, w)),
        ((6, w), whole(6, w)),
        ((15, w), whole(15, w)),
        ((2, 4 * w), whole(2, 4 * w)),
        (table_shape, whole(*table_shape)),
    ]
    count = result.shape[1] // (r // step)
    tokens = pl.BlockSpec((result.shape[0], count, d), lambda i: (0, i, 0))
    return pl.pallas_call(
        functools.partial(finish_kernel, n_tap),
        grid=(r // step,),
        in_specs=[rows(k), rows(4), rows(4), whole(*small.shape), whole(*table.shape), tokens, tokens],
        out_specs=[b for _, b in outs] + [tokens, tokens],
        out_shape=[jax.ShapeDtypeStruct(s, F32) for s, _ in outs] + [jax.ShapeDtypeStruct(result.shape, BF)] * 2,
        compiler_params=pltpu.CompilerParams(vmem_limit_bytes=VMEM),
        cost_estimate=pl.CostEstimate(flops=0, bytes_accessed=18_000_000, transcendentals=0),
        name="finish",
    )(main, in_b, out_b, small, table, result, dx)


def xor_route(axis, mask):
    return [(i, i ^ mask) for i in range(lax.axis_size(axis))]


def swapped(block, axis, mask):
    return lax.ppermute(block, axis, xor_route(axis, mask))


def after(value, *marks):
    return lax.optimization_barrier((value,) + marks)[0]


def over_seq(part):
    if lax.axis_size("seq") != 4 or part.shape[1] < 64:
        return lax.psum(part, "seq")
    place = lax.axis_index("seq")
    part = part.astype(F32)
    for mask in (1, 2):
        high = (place & mask) != 0
        half = part.shape[1] // 2
        first, second = part[:, :half], part[:, half:]
        sent = jnp.where(high, first, second).astype(BF)
        part = jnp.where(high, second, first) + swapped(sent, "seq", mask).astype(F32)
    part = part.astype(BF)
    for mask in (2, 1):
        high = (place & mask) != 0
        got = swapped(part, "seq", mask)
        part = jnp.where(high, jnp.concatenate([got, part], axis=1), jnp.concatenate([part, got], axis=1))
    return part


def reduced(g):
    return over_seq(lax.psum_scatter(g, "fsdp", scatter_dimension=0, tiled=False))


def small_reduced(rows):
    k, d = rows.shape
    n = lax.axis_size("fsdp")
    me = lax.axis_index("fsdp")
    rows = lax.psum(rows, ("seq", "fsdp"))
    return lax.dynamic_slice_in_dim(rows, me * (d // n), d // n, 1)


def to_pairs(array, place):
    one, two = array[0], array[1]
    got = lax.ppermute(jnp.where(place % 2 == 0, two, one), "seq", [(0, 2), (1, 0), (2, 3), (3, 1)])
    more = lax.ppermute(jnp.where(place == 1, two, one), "seq", [(1, 2), (2, 1)])
    first = jnp.where(place == 0, one, jnp.where(place == 1, more, got))
    second = jnp.where(place < 2, got, jnp.where(place == 2, more, two))
    return jnp.concatenate([first, second], axis=0)


def from_pairs(array, place):
    half = array.shape[0] // 2
    first, second = array[:half], array[half:]
    got = lax.ppermute(jnp.where(place < 2, second, first), "seq", [(2, 0), (0, 1), (3, 2), (1, 3)])
    more = lax.ppermute(jnp.where(place == 1, first, second), "seq", [(1, 2), (2, 1)])
    one = jnp.where(place == 0, first, jnp.where(place == 2, more, got))
    two = jnp.where(place == 3, second, jnp.where(place == 1, more, got))
    return jnp.stack([one, two])


def on_device(
    inputs,
    lengths,
    ffn_in,
    ffn_in_bias,
    ffn_out,
    qkv,
    attn_out,
    conv_in,
    conv_out,
    depthwise,
    gains,
    shifts,
    distance,
    grad_out,
):
    n = lax.axis_size("fsdp")
    me = lax.axis_index("fsdp")
    place = lax.axis_index("seq")
    odd = place % 2 == 1
    odd_word = (place % 2).astype(jnp.int32).reshape(1)
    me_word = me.astype(jnp.int32).reshape(1)
    width = inputs.shape[2]
    r = width // n
    inner_width = ffn_in.shape[2]
    n_gain, n_shift, n_tap = gains.shape[0], shifts.shape[0], depthwise.shape[0]
    cubed = n == 8 and lax.axis_size("seq") == 4

    def chunks(part):
        return [part[:, i : i + width] for i in range(0, part.shape[1], width)]

    shard_a = jnp.stack(chunks(ffn_in[0]))
    shard_b = jnp.concatenate([ffn_out[0].reshape(4, r, width), qkv], axis=0)
    if cubed:
        w_b = lax.all_gather(shard_b, "fsdp", axis=0)
        inner_a, act_a, act_t_a, unit_t_a, tokens, small, w_a = first_forward(
            inputs, after(shard_a, shard_b), gains, shifts, depthwise, ffn_in_bias
        )
        cotangent = to_pairs(after(grad_out, act_a), place)
    else:
        small = jnp.concatenate([gains, shifts, depthwise, ffn_in_bias.reshape(-1, r)], axis=0)
        small = lax.all_gather(small, "fsdp", axis=0)
        w_a = lax.all_gather(shard_a, "fsdp", axis=0)
        w_b = lax.all_gather(shard_b, "fsdp", axis=0)
        tokens, cotangent = to_pairs(inputs, place), to_pairs(grad_out, place)

    small = small.astype(F32)
    rows = jnp.transpose(small, (1, 0, 2))
    n_plain = n_gain + n_shift + n_tap
    gain = rows[:n_gain].reshape(n_gain, width)
    shift = rows[n_gain : n_gain + n_shift].reshape(n_shift, width)
    taps = rows[n_gain + n_shift : n_plain].reshape(n_tap, width)
    bias = small[:, n_plain : n_plain + 8].reshape(n, 2, -1).transpose(1, 0, 2).reshape(2, inner_width)

    length = jnp.where(place < 2, lengths[0], lengths[1]).reshape(1)
    wide, ends = tables(distance)
    pairs = [(0, 1), (2, 3)]

    if not cubed:
        inner_a, act_a, act_t_a, unit_t_a = ffn_in_forward(tokens, jnp.stack([gain[0], shift[0]]), bias[0], w_a, 0)
    later_in, later_out, attn_out, conv_in, conv_out, _ = lax.optimization_barrier(
        (ffn_in, ffn_out, attn_out, conv_in, conv_out, act_a)
    )
    shard_c = jnp.stack(chunks(later_in[1]) + [attn_out] + chunks(conv_in) + [conv_out])
    shard_d = later_out[1].reshape(4, r, width)
    w_c = lax.all_gather(after(shard_c, w_b, cotangent), "fsdp", axis=0)
    first, unit_t_1, mine, other = out_qkv_forward(
        odd_word, tokens, act_a, w_b, jnp.stack([shift[6], gain[1], shift[1], shift[8], shift[9]])
    )
    probs, heads, mixed = attend(mine, other, length, wide, ends)
    w_d = lax.all_gather(after(shard_d, w_c, mixed), "fsdp", axis=0)
    second, mixed_t, unit_t_2, val, sig, gated = mid_forward(
        first, mixed, w_c, 4, 5, jnp.stack([shift[10], gain[2], shift[2], shift[11], shift[12]])
    )
    count = gated.shape[0]
    halo = lax.ppermute(gated[count - 32 :], "seq", pairs)
    conv, act_t_c, third = conv_forward(
        gated, halo, taps, jnp.stack([shift[13], gain[3], shift[3], shift[14]]), second, w_c, 7
    )
    inner_b, act_b, act_t_b, unit_t_b = ffn_in_forward(third, jnp.stack([gain[4], shift[4]]), bias[1], w_c, 0)
    outputs, d4, dout, sums_5 = out_last(third, act_b, w_d, 0, cotangent, jnp.stack([shift[7], gain[5], shift[5]]))

    g_out_b = weight_grad(act_t_b, dout, n, 4, 0, True)
    part_out_b = lax.psum_scatter(g_out_b, "fsdp", scatter_dimension=0, tiled=False)
    dinner, dout, dbias_b, sums_7 = ffn_hidden_back(after(dout, g_out_b), inner_b, w_d, 0)
    g_in_b = weight_grad(unit_t_b, dinner, n, 4, 0, False)
    part_in_b = lax.psum_scatter(g_in_b, "fsdp", scatter_dimension=0, tiled=False)
    dinner = after(dinner, g_in_b)
    if cubed:
        vec = jnp.stack([gain[4], gain[3], shift[3], gain[2]])
        dconv, dout_3, d2, dout_2, dglu, mine, other, sums_4, sums_3, sums_2, outputs = middle_back(
            d4, dinner, third, conv, val, sig, second, w_c, taps, vec, outputs
        )
    else:
        outputs = from_pairs(outputs, place)
        d3, sums_4 = norm_input_back(d4, dinner, third, w_c, 0, gain[4:5])
        dconv, dout_3, sums_3 = conv_out_back(d3, conv, w_c, 7, jnp.stack([gain[3], shift[3]]))
        follow = lax.ppermute(dconv[:32], "seq", [(j, i) for i, j in pairs])
        d2, dout_2, dglu, mine, other, sums_2 = mid_back(
            odd_word, dconv, follow, taps, val, sig, second, d3, w_c, 4, 5, gain[2:3]
        )
    if cubed:
        dqkv, dtable, share_out_b = attend_back(heads, probs, wide, mine, other, part_out_b)
    else:
        dqkv, dtable = attend_back(heads, probs, wide, mine, other)
        share_out_b, share_in_b = over_seq(part_out_b), over_seq(part_in_b)

    def biases(part):
        return part.reshape(n, 4, r).transpose(1, 0, 2).reshape(4, width)

    if cubed:
        main, share_in_b, small, table, grad_tokens = last_reduced(
            gain[0:2], dtable, (sums_2, sums_3, sums_4, sums_5, sums_7), dbias_b, d2, first, tokens, dconv, gated, halo,
            part_in_b, dqkv, unit_t_1, act_t_a, unit_t_a, inner_a, w_b, w_a,
            mixed_t, dout_2, unit_t_2, dglu, act_t_c, dout_3,
        )
    else:
        d1, sums_1 = norm_input_back(d2, dqkv, first, w_b, 4, gain[1:2])
        bias_sums = jnp.sum(dqkv.astype(F32), axis=0)
        dtaps = taps_grad(dconv, gated, halo, n_tap)
        early = jnp.concatenate(
            [
                jnp.stack([sums_1[0], sums_2[2], sums_3[1], sums_4[0], sums_5[0]]),
                jnp.stack([sums_1[1], sums_2[3], sums_3[2], sums_4[1], sums_5[1]]),
                jnp.stack(
                    [
                        sums_7[0],
                        bias_sums[:width],
                        bias_sums[2 * width :],
                        sums_2[4],
                        sums_2[0],
                        sums_2[1],
                        sums_3[3],
                        sums_3[0],
                    ]
                ),
                dtaps,
                biases(dbias_b),
            ],
            axis=0,
        )
        dinner, dout, dbias_a, sums_6 = ffn_hidden_back(d1, inner_a, w_b, 0)
        g_m = weight_grad(unit_t_2, dglu, n, 4, 1, False)
        g_m = weight_grad(mixed_t, dout_2, n, 4, 0, False, into=g_m)
        g_m = weight_grad(act_t_c, dout_3, n, 4, 3, False, into=g_m)
        shares = {
            "m": reduced(g_m),
            "q": reduced(weight_grad(unit_t_1, dqkv, n, 3, 0, False)),
            "out": reduced(weight_grad(act_t_a, dout, n, 4, 0, True)),
            "in": reduced(weight_grad(unit_t_a, dinner, n, 4, 0, False)),
        }
        main = jnp.stack([shares[name][unit] for name, unit in ORDER])
        d0, sums_0 = norm_input_back(d1, dinner, tokens, w_a, 0, gain[0:1], BF)
        grad_tokens = from_pairs(d0, place)
        late = jnp.concatenate([jnp.stack([sums_0[0], sums_0[1], sums_6[0]]), biases(dbias_a)], axis=0)
        small = small_reduced(jnp.concatenate([early, late], axis=0))
        table = lax.psum(dtable, ("seq", "fsdp"))
    (
        g_in, g_out, g_qkv, g_attn, g_conv_in, g_conv_out, g_taps, g_gain, g_shift, g_bias, total_table, outputs, grad_tokens
    ) = finished(main, share_in_b, share_out_b, small, table, outputs, grad_tokens, n_tap, distance.shape)
    return (
        outputs,
        grad_tokens,
        g_in,
        g_bias,
        g_out.reshape(2, 4 * r, width),
        g_qkv,
        g_attn,
        g_conv_in,
        g_conv_out,
        g_taps,
        g_gain,
        g_shift,
        total_table,
    )


def solution(mesh):
    return jax.shard_map(
        on_device,
        mesh=mesh,
        in_specs=(
            P("fsdp", "seq", None),
            P("fsdp"),
            P(None, "fsdp", None),
            P(None, "fsdp"),
            P(None, "fsdp", None),
            P(None, "fsdp", None),
            P("fsdp", None),
            P("fsdp", None),
            P("fsdp", None),
            P(None, "fsdp"),
            P(None, "fsdp"),
            P(None, "fsdp"),
            P(),
            P("fsdp", "seq", None),
        ),
        out_specs=(
            P("fsdp", "seq", None),
            P("fsdp", "seq", None),
            P(None, "fsdp", None),
            P(None, "fsdp"),
            P(None, "fsdp", None),
            P(None, "fsdp", None),
            P("fsdp", None),
            P("fsdp", None),
            P("fsdp", None),
            P(None, "fsdp"),
            P(None, "fsdp"),
            P(None, "fsdp"),
            P(),
        ),
        check_vma=False,
    )
```
